32 devices in a mesh: tm: 8 (over y, x, core), zone: 4 (over z).
Axes of the slice: x: 2, y: 2, z: 4, core: 2. Of those that a mesh axis runs over, the one named last changes fastest.
Arguments:
- states: bfloat16 [32, 512, 512], P('tm', 'zone'), may hold values from -6 to 6
- gain_attn: float32 [512], replicated, may hold values from 0.1 to 1.9
- w_qkv: bfloat16 [512, 1536], P('zone')
- w_out_attn: bfloat16 [512, 512], P('zone'), may hold values from -0.25 to 0.25
- pattern: int32 [8, 2], P('tm'), may hold values from 0 to 1, as said below
- gain_mix: float32 [512], replicated, may hold values from 0.1 to 1.9
- neighbours: int32 [4, 3], replicated, may hold values from 0 to 3, as said below
- degree: int32 [4], replicated, may hold values from 1 to 3
- mix: bfloat16 [4, 3, 128, 128], replicated, may hold values from -0.3125 to 0.3125
- gain_ffn: float32 [512], replicated, may hold values from 0.1 to 1.9
- w_in: bfloat16 [512, 2048], P('zone'), may hold values from -0.25 to 0.25
- w_out: bfloat16 [2048, 512], P('zone'), may hold values from -0.125 to 0.125
Outputs:
- evolved: bfloat16 [32, 512, 512], P('tm', 'zone')
The draws below stay inside these ranges and needn't reach their ends.
Inputs may be any that keep to these rules, and one draw needn't show every extreme that they name: `pattern`: time blocks 1 to 2 each attend to time block 0. `neighbours`: each row names 3 different zone blocks.
All inputs are finite; a program needn't handle non-finite values.
Results may differ from the reference program's by a relative error of at most 0.008.
Values may be sent and summed in bfloat16 or wider, within the bound.
No kernel may reach another device: no remote copies, remote signals or barrier semaphores. Data moves between devices by JAX's collectives and lax.ppermute only.
A program may use at most 64 MiB of HBM per device.

```python
import math
import jax
import jax.numpy as jnp
from jax import lax

D = 512
HEADS = 4
FF = 2048
ZB = 128
T_DEV = 4
REACH = 2
KMAX = 3
HD = 128
TBLOCKS = 8
ZBLOCKS = 4
TIME = 32
ZONES = 512


def draw_w_qkv(key, part):
    first = jax.random.fold_in(key, 0)
    base = jax.random.normal(first, (D, 3 * D), jnp.float32) / math.sqrt(D)
    return base.astype(jnp.bfloat16)


def draw_pattern(key, part):
    bits = jax.random.randint(jax.random.fold_in(key, 37), (TBLOCKS, REACH), 0, 2, jnp.int32)
    block_ids = jnp.arange(TBLOCKS, dtype=jnp.int32)[:, None]
    back_ids = jnp.arange(REACH, dtype=jnp.int32)[None, :] + 1
    return jnp.where(block_ids == back_ids, 1, bits).astype(jnp.int32)


def draw_neighbours(key, part):
    row_keys = jax.random.split(jax.random.fold_in(key, 11), ZBLOCKS)
    rows = jax.vmap(lambda row_key: jax.random.permutation(row_key, ZBLOCKS)[:KMAX])(row_keys)
    return rows.astype(jnp.int32)


def draw_degree(key, part):
    first, second = jax.random.split(jax.random.fold_in(key, 23))
    counts = jax.random.randint(first, (ZBLOCKS,), 1, KMAX + 1, jnp.int32)
    chosen = jax.random.randint(second, (), 0, ZBLOCKS, jnp.int32)
    return jnp.where(jnp.arange(ZBLOCKS, dtype=jnp.int32) == chosen, KMAX, counts).astype(jnp.int32)


def block_scale(rng, dims, shards, low, high):
    level, own = 1.0, jax.random.fold_in(rng, 6)
    for position, parts in shards:
        draws = jnp.exp(jax.random.uniform(jax.random.fold_in(own, position), (parts,), jnp.float32, low / len(shards), high / len(shards)))
        level = level * jnp.repeat(draws, dims[position] // parts).reshape([-1 if axis == position else 1 for axis in range(len(dims))])
    return level


def noise(own_key, shape, width, most, cuts=(), kind=jnp.bfloat16):
    level = block_scale(own_key, shape, cuts, -0.22, 0.18) if cuts else 1.0
    drawn = jax.random.normal(own_key, shape, jnp.float32) * width * level
    return jnp.minimum(jnp.maximum(drawn, -most), most).astype(kind)


def setup_inputs(seed: int = 0) -> dict:
    key_of = jax.random.split(jax.random.key(seed), 13)
    states = noise(key_of[0], (TIME, ZONES, D), 1.0, 6.0, ((0, 8), (1, 4)))
    gain_attn = jnp.clip(1.0 + 0.18 * jax.random.normal(key_of[1], (D,), jnp.float32), 0.1, 1.9)
    w_qkv = draw_w_qkv(jax.random.fold_in(key_of[12], 71), 0)
    w_out_attn = noise(key_of[3], (D, D), D ** -0.5, 0.25, ((0, 4),))
    pattern = draw_pattern(jax.random.fold_in(key_of[12], 71), 0)
    gain_mix = jnp.clip(1.0 + 0.18 * jax.random.normal(key_of[5], (D,), jnp.float32), 0.1, 1.9)
    neighbours = draw_neighbours(jax.random.fold_in(key_of[12], 71), 0)
    degree = draw_degree(jax.random.fold_in(key_of[12], 71), 0)
    mix = noise(key_of[8], (ZBLOCKS, KMAX, ZB, ZB), (ZB * KMAX) ** -0.5, 0.3125)
    gain_ffn = jnp.clip(1.0 + 0.18 * jax.random.normal(key_of[9], (D,), jnp.float32), 0.1, 1.9)
    w_in = noise(key_of[10], (D, FF), D ** -0.5, 0.25, ((0, 4),))
    w_out = noise(key_of[11], (FF, D), FF ** -0.5, 0.125, ((0, 4),))
    return dict(states=states, gain_attn=gain_attn, w_qkv=w_qkv, w_out_attn=w_out_attn, pattern=pattern, gain_mix=gain_mix, neighbours=neighbours, degree=degree, mix=mix, gain_ffn=gain_ffn, w_in=w_in, w_out=w_out)


def rms_scale(values, gain):
    mean_sq = lax.optimization_barrier(jnp.mean(values * values, axis=-1, keepdims=True))
    return values * lax.rsqrt(mean_sq + 1e-06) * gain

def attend_block(x_block, gain_attn, w_qkv, w_out_attn, pattern):
    steps = x_block.shape[0]
    x_wide = x_block.astype(jnp.float32)
    normed = rms_scale(x_wide, gain_attn).astype(jnp.bfloat16)
    projected = jnp.dot(normed.reshape(-1, D), w_qkv, preferred_element_type=jnp.float32).astype(jnp.bfloat16)
    projected = projected.reshape(steps, ZB, 3, HEADS, HD)
    queries = projected[:, :, 0].astype(jnp.float32)
    keys = projected[:, :, 1].astype(jnp.float32)
    values = projected[:, :, 2].astype(jnp.float32)
    scores = jnp.einsum('tzhd,szhd->zhts', queries, keys) * HD ** (-0.5)
    tpos = jnp.arange(steps, dtype=jnp.int32)
    qblock = tpos // T_DEV
    offset = qblock[:, None] - qblock[None, :]
    pattern_ext = jnp.concatenate([jnp.ones((TBLOCKS, 1), jnp.int32), pattern.astype(jnp.int32), jnp.zeros((TBLOCKS, 1), jnp.int32)], axis=1)
    clipped = jnp.clip(offset, 0, REACH + 1)
    allowed = (tpos[None, :] <= tpos[:, None]) & (offset <= REACH) & (pattern_ext[qblock[:, None], clipped] == 1)
    masked = jnp.where(allowed, scores, -1e+30)
    top = lax.optimization_barrier(jnp.max(masked, axis=-1, keepdims=True))
    expw = jnp.where(allowed, jnp.exp(masked - top), 0.0)
    total = lax.optimization_barrier(jnp.sum(expw, axis=-1))
    probs = expw.astype(jnp.bfloat16).astype(jnp.float32)
    context = jnp.einsum('zhts,szhd->tzhd', probs, values) / jnp.transpose(total, (2, 0, 1))[..., None]
    context = context.astype(jnp.bfloat16).reshape(-1, D)
    return x_wide + jnp.dot(context, w_out_attn, preferred_element_type=jnp.float32).reshape(steps, ZB, D)

def reference(states, gain_attn, w_qkv, w_out_attn, pattern, gain_mix, neighbours, degree, mix, gain_ffn, w_in, w_out):

    def section_one(block):
        x_block = lax.dynamic_slice_in_dim(states, (block * ZB).astype(jnp.int32), ZB, 1)
        return attend_block(x_block, gain_attn, w_qkv, w_out_attn, pattern)
    blocks = lax.map(section_one, jnp.arange(ZBLOCKS, dtype=jnp.int32))
    after_attn = jnp.transpose(blocks, (1, 0, 2, 3)).reshape(TIME, ZONES, D)
    slot_live = jnp.arange(KMAX, dtype=jnp.int32)[None, :] < degree[:, None]
    live_mix = jnp.where(slot_live[:, :, None, None], mix.astype(jnp.float32), 0.0)

    def section_two(row):
        mixin = rms_scale(row, gain_mix).astype(jnp.bfloat16).reshape(ZBLOCKS, ZB, D)
        nearby = mixin[neighbours].astype(jnp.float32)
        spatial = jnp.einsum('bkzy,bkyd->bzd', live_mix, nearby).astype(jnp.bfloat16).reshape(ZONES, D)
        after_mix = row + spatial.astype(jnp.float32)
        ffn_in = rms_scale(after_mix, gain_ffn).astype(jnp.bfloat16)
        hidden = jax.nn.gelu(jnp.dot(ffn_in, w_in, preferred_element_type=jnp.float32), approximate=True).astype(jnp.bfloat16)
        return (after_mix + jnp.dot(hidden, w_out, preferred_element_type=jnp.float32)).astype(jnp.bfloat16)
    return lax.map(section_two, after_attn)
```

```python
import jax
import jax.numpy as jnp
from jax import lax
from jax.sharding import PartitionSpec as P

HEADS = 4


def shifted(value, axis, steps):
    count = lax.axis_size(axis)
    first, last = (max(0, -steps), min(count, count - steps))
    return lax.ppermute(value, axis, [(source, source + steps) for source in range(first, last)])


def tm_slice(weight, spread):
    rows = weight.shape[0] // spread
    return lax.dynamic_slice_in_dim(weight, lax.axis_index("tm") * rows, rows, axis=0)


def rms_scale(values, gain):
    mean_sq = jnp.mean(values * values, axis=-1, keepdims=True)
    return values * lax.rsqrt(mean_sq + 1e-06) * gain


def on_device(
    states,
    gain_attn,
    w_qkv,
    w_out_attn,
    pattern,
    gain_mix,
    neighbours,
    degree,
    mix,
    gain_ffn,
    w_in,
    w_out,
):
    steps, zone_rows, width = states.shape
    head_size = width // HEADS
    reach = pattern.shape[1]
    spread = lax.axis_size("tm")
    first = jnp.concatenate([tm_slice(w_qkv, spread), tm_slice(w_out_attn, spread)], axis=1)
    full_first = lax.all_gather(first, ("zone", "tm"), axis=0, tiled=True)
    full_qkv, full_attn = full_first[:, : 3 * width], full_first[:, 3 * width :]
    full_in = lax.all_gather(tm_slice(w_in, spread), ("zone", "tm"), axis=0, tiled=True)
    full_out = lax.all_gather(tm_slice(w_out, spread), ("zone", "tm"), axis=0, tiled=True)
    earlier = []
    for offset in range(reach, 0, -1):
        earlier.append(shifted(states, "tm", offset))
    all_states = jnp.concatenate(earlier + [states], axis=0).astype(jnp.float32)
    input_wide = states.astype(jnp.float32)
    normed = rms_scale(all_states, gain_attn).astype(jnp.bfloat16)
    key_count = normed.shape[0]
    projected = jnp.dot(
        normed.reshape(-1, width), full_qkv, preferred_element_type=jnp.float32
    ).astype(jnp.bfloat16)
    projected = projected.reshape(key_count, zone_rows, 3 * width)
    queries = projected[-steps:, :, :width].reshape(steps, zone_rows, HEADS, head_size)
    keys_all = projected[..., width : 2 * width].reshape(key_count, zone_rows, HEADS, head_size)
    values_all = projected[..., 2 * width :].reshape(key_count, zone_rows, HEADS, head_size)
    scores = jnp.einsum(
        "tzhd,szhd->zhts", queries, keys_all, preferred_element_type=jnp.float32
    ) * head_size ** (-0.5)
    my_block = lax.axis_index("tm")
    key_index = jnp.arange(key_count, dtype=jnp.int32)
    back = reach - key_index // steps
    pattern_row = jnp.concatenate([jnp.ones((1,), jnp.int32), pattern[0]])
    live_back = jnp.sum(
        jnp.where(
            back[:, None] == jnp.arange(reach + 1, dtype=jnp.int32)[None, :],
            pattern_row[None, :],
            0,
        ),
        axis=1,
    )
    query_pos = jnp.arange(steps, dtype=jnp.int32)
    local_key = key_index - reach * steps
    earlier_ok = (back > 0) & (live_back == 1) & (my_block - back >= 0)
    allowed = earlier_ok[None, :] | (back[None, :] == 0) & (
        local_key[None, :] <= query_pos[:, None]
    )
    masked = jnp.where(allowed, scores, -1e30)
    top = jnp.max(masked, axis=-1, keepdims=True)
    expw = jnp.where(allowed, jnp.exp(masked - top), 0.0)
    total = jnp.sum(expw, axis=-1)
    probs = expw.astype(jnp.bfloat16)
    context = jnp.einsum("zhts,szhd->tzhd", probs, values_all, preferred_element_type=jnp.float32)
    context = (
        (context / jnp.transpose(total, (2, 0, 1))[..., None])
        .astype(jnp.bfloat16)
        .reshape(-1, width)
    )
    after_attn = input_wide + jnp.dot(
        context, full_attn, preferred_element_type=jnp.float32
    ).reshape(steps, zone_rows, width)
    mixin = jnp.transpose(rms_scale(after_attn, gain_mix).astype(jnp.bfloat16), (0, 2, 1))
    slot_live = jnp.arange(mix.shape[1], dtype=jnp.int32)[None, :] < degree[:, None]
    live_mix = jnp.where(slot_live[:, :, None, None], mix, jnp.zeros_like(mix))
    items = lax.all_to_all(mixin, "zone", split_axis=1, concat_axis=2, tiled=True)
    count, channels, zones_all = items.shape
    block_count = neighbours.shape[0]
    grid = items.reshape(count, channels, block_count, zones_all // block_count)
    nearby = grid[:, :, neighbours, :]
    spatial = jnp.einsum("ncbky,bkzy->ncbz", nearby, live_mix, preferred_element_type=jnp.float32)
    spatial = spatial.astype(jnp.bfloat16).reshape(count, channels, zones_all)
    returned = lax.all_to_all(spatial, "zone", split_axis=2, concat_axis=1, tiled=True)
    after_mix = after_attn + jnp.transpose(returned, (0, 2, 1)).astype(jnp.float32)
    ffn_in = rms_scale(after_mix, gain_ffn).astype(jnp.bfloat16).reshape(-1, width)
    hidden = jax.nn.gelu(
        jnp.dot(ffn_in, full_in, preferred_element_type=jnp.float32), approximate=True
    ).astype(jnp.bfloat16)
    evolved = after_mix + jnp.dot(hidden, full_out, preferred_element_type=jnp.float32).reshape(
        steps, zone_rows, width
    )
    return evolved.astype(jnp.bfloat16)


def solution(mesh):
    return jax.shard_map(
        on_device,
        mesh=mesh,
        in_specs=(
            P("tm", "zone", None),
            P(),
            P("zone", None),
            P("zone", None),
            P("tm", None),
            P(),
            P(),
            P(),
            P(),
            P(),
            P("zone", None),
            P("zone", None),
        ),
        out_specs=P("tm", "zone", None),
        check_vma=False,
    )
```

```python
import functools

import jax
import jax.numpy as jnp
from jax import lax
from jax.experimental import pallas as pl
from jax.experimental.pallas import tpu as pltpu
from jax.sharding import PartitionSpec as P

HEADS = 4
SPREAD = 8
LANES = 128
F32 = jnp.float32
BF16 = jnp.bfloat16
VMEM_LIMIT = 48 * 1024 * 1024


def shifted(value, axis, steps):
    count = lax.axis_size(axis)
    return lax.ppermute(value, axis, [(source, source + steps) for source in range(count - steps)])


def rotated(value, axis, steps):
    count = lax.axis_size(axis)
    return lax.ppermute(value, axis, [(source, (source + steps) % count) for source in range(count)])


def swapped(value, axis, bits):
    count = lax.axis_size(axis)
    return lax.ppermute(value, axis, [(source, source ^ bits) for source in range(count)])


def rms_scale(values, gain):
    mean_sq = jnp.mean(values * values, axis=-1, keepdims=True)
    return values * lax.rsqrt(mean_sq + 1e-06) * gain


def row_sum(value):
    return jnp.sum(value, axis=0, keepdims=True)


def attention_kernel(zones, reach, place, pattern, states, *refs):
    earlier, refs = refs[:reach], refs[reach:]
    (gain_attn, gain_mix, own_qkv, own_attn), refs = refs[:4], refs[4:]
    direct, refs = refs[: zones - 1], refs[zones - 1 :]
    partner, refs = refs[: zones - 1], refs[zones - 1 :]
    after_out, mixin_out, w_qkv, w_attn, w_turned, normed, projected, context = refs
    steps, zone_rows, width = states.shape
    head_size = width // HEADS
    key_count = (reach + 1) * steps
    my_block, my_zone = place[0], place[1]
    my_half = lax.rem(my_block, 2)
    shard = own_qkv.shape[0]
    half = shard // 2

    def put(rows, qkv, attn):
        w_qkv[rows, :] = qkv
        w_attn[rows, :] = attn

    put(pl.ds(pl.multiple_of(my_zone * shard, shard), shard), own_qkv[...], own_attn[...])
    for step in range(1, zones):
        source = lax.rem(my_zone - step + zones, zones)
        for pieces, which in ((direct, my_half), (partner, 1 - my_half)):
            start = pl.multiple_of(source * shard + which * half, half)
            piece = pieces[step - 1]
            put(pl.ds(start, half), piece[:, : 3 * width], piece[:, 3 * width :])
    for block in range(3 * width // LANES):
        cols = slice(block * LANES, (block + 1) * LANES)
        w_turned[cols, :] = w_qkv[:, cols].T

    blocks = list(earlier) + [states]
    gain = gain_attn[...]
    for index, block in enumerate(blocks):
        for step in range(steps):
            row = (index * steps + step) * zone_rows
            normed[row : row + zone_rows, :] = rms_scale(block[step].astype(F32), gain).astype(BF16)

    def project(first, last, weight_rows):
        return lax.dot_general(
            w_turned[weight_rows, :],
            normed[first:last, :],
            (((1,), (1,)), ((), ())),
            preferred_element_type=F32,
        ).astype(BF16).astype(F32)

    span = 2 * zone_rows
    for first in range(0, key_count * zone_rows, span):
        own = first >= reach * steps * zone_rows
        rows = slice(0 if own else width, 3 * width)
        projected[rows, first : first + span] = project(first, first + span, rows)

    allowed_back = [
        (pattern[0, back - 1] == 1) & (my_block >= back) for back in range(reach, 0, -1)
    ]
    chunks = head_size // 8

    def usable(query):
        return range(reach * steps + query + 1)

    def head_body(head, carry):
        base = head * head_size

        def tile(kind, chunk, key):
            row = pl.multiple_of(kind * width + base + chunk * 8, 8)
            return projected[pl.ds(row, 8), key * zone_rows : (key + 1) * zone_rows]

        for pair in range(0, steps, 2):
            queries = range(pair, min(pair + 2, steps))
            sums = {}
            for chunk in range(chunks):
                q_tiles = {q: tile(0, chunk, reach * steps + q) for q in queries}
                for key in usable(queries[-1]):
                    k_tile = tile(1, chunk, key)
                    for q in queries:
                        if key in usable(q):
                            term = q_tiles[q] * k_tile
                            sums[q, key] = term if chunk == 0 else sums[q, key] + term
            weights, scales = {}, {}
            for q in queries:
                scores = jnp.concatenate([row_sum(sums[q, key]) for key in usable(q)], axis=0)
                scores = scores * head_size ** (-0.5)
                row_id = lax.broadcasted_iota(jnp.int32, scores.shape, 0)
                allowed = row_id >= reach * steps
                for index, live in enumerate(allowed_back):
                    inside = (row_id >= index * steps) & (row_id < (index + 1) * steps)
                    allowed = allowed | (inside & live)
                masked = jnp.where(allowed, scores, -1e30)
                top = jnp.max(masked, axis=0, keepdims=True)
                expw = jnp.where(allowed, jnp.exp(masked - top), 0.0)
                scales[q] = jnp.broadcast_to(1.0 / row_sum(expw), (8, zone_rows))
                probs = expw.astype(BF16).astype(F32)
                for key in usable(q):
                    weights[q, key] = jnp.broadcast_to(probs[key : key + 1, :], (8, zone_rows))
            for chunk in range(chunks):
                sums = {}
                for key in usable(queries[-1]):
                    v_tile = tile(2, chunk, key)
                    for q in queries:
                        if key in usable(q):
                            term = weights[q, key] * v_tile
                            sums[q] = term if key == 0 else sums[q] + term
                for q in queries:
                    row = pl.multiple_of(base + chunk * 8, 8)
                    context[pl.ds(row, 8), q * zone_rows : (q + 1) * zone_rows] = sums[q] * scales[q]
        return carry

    lax.fori_loop(0, HEADS, head_body, 0)

    mix_gain = gain_mix[...]
    for step in range(steps):
        rows = slice(step * zone_rows, (step + 1) * zone_rows)
        turned = context[:, rows].T.astype(BF16)
        after = states[step].astype(F32) + jnp.dot(turned, w_attn[...], preferred_element_type=F32)
        after_out[rows, :] = after
        mixin = rms_scale(after, mix_gain).astype(BF16)
        if len(mixin_out.shape) == 2:
            mixin_out[rows, :] = mixin
        else:
            part = mixin_out.shape[-1]
            for index in range(mixin_out.shape[0]):
                mixin_out[index, rows, :] = mixin[:, index * part : (index + 1) * part]


def mixing_kernel(steps, neighbours, degree, mix, items, out):
    block_count, slots, zone_rows, _ = mix.shape
    part = items.shape[-1]
    group = 2 if part % LANES == 0 and steps % 2 == 0 else 1

    def block_body(block, carry):
        left = []
        for slot in range(slots):
            tile = mix[block, slot]
            left.append(jnp.where(degree[block] > slot, tile, jnp.zeros_like(tile)))
        left = jnp.concatenate(left, axis=1)
        for step in range(0, steps, group):
            right = []
            for slot in range(slots):
                source = neighbours[block, slot]
                right.append(
                    jnp.concatenate(
                        [
                            items[source, (step + index) * zone_rows : (step + index + 1) * zone_rows, :]
                            for index in range(group)
                        ],
                        axis=1,
                    )
                )
            result = jnp.dot(left, jnp.concatenate(right, axis=0), preferred_element_type=F32)
            for index in range(group):
                rows = slice((step + index) * zone_rows, (step + index + 1) * zone_rows)
                out[block, rows, :] = result[:, index * part : (index + 1) * part].astype(BF16)
        return carry

    lax.fori_loop(0, block_count, block_body, 0)


def ffn_kernel(zones, place, spatial, after_attn, gain_ffn, own_in, own_out, *refs):
    pieces, (out, w_in, w_out, after_mix, ffn_in) = refs[:SPREAD], refs[SPREAD:]
    rows_all, width = after_attn.shape
    my_block, my_zone = place[0], place[1]
    in_shard, hidden = own_in.shape
    out_shard = own_out.shape[0]
    in_cols, out_rows = hidden // SPREAD, out_shard // SPREAD
    folds = width // in_cols

    start = pl.multiple_of(my_zone * in_shard, in_shard)
    for index in range(SPREAD):
        w_in[index, pl.ds(start, in_shard), :] = own_in[:, index * in_cols : (index + 1) * in_cols]
    w_out[pl.ds(pl.multiple_of(my_zone * out_shard, out_shard), out_shard), :] = own_out[...]
    for bits in range(SPREAD):
        slot = lax.rem(my_block, SPREAD) ^ bits
        for step in range(1, zones):
            source = lax.rem(my_zone - step + zones, zones)
            piece = pieces[bits]
            w_in[slot, pl.ds(pl.multiple_of(source * in_shard, in_shard), in_shard), :] = piece[
                step - 1, :in_shard, :
            ]
            start = pl.multiple_of(source * out_shard + slot * out_rows, out_rows)
            for fold in range(folds):
                first = in_shard + fold * out_rows
                w_out[pl.ds(start, out_rows), fold * in_cols : (fold + 1) * in_cols] = piece[
                    step - 1, first : first + out_rows, :
                ]

    gain = gain_ffn[...]
    span = 128
    for first in range(0, rows_all, span):
        rows = slice(first, first + span)
        if len(spatial.shape) == 2:
            moved = spatial[rows, :]
        else:
            moved = jnp.concatenate([spatial[index, rows, :] for index in range(spatial.shape[0])], axis=1)
        total = after_attn[rows, :] + moved.astype(F32)
        after_mix[rows, :] = total
        ffn_in[rows, :] = rms_scale(total, gain).astype(BF16)
    span = 256
    for first in range(0, rows_all, span):
        rows = slice(first, first + span)
        total = after_mix[rows, :]
        for index in range(SPREAD):
            hidden_part = jnp.dot(ffn_in[rows, :], w_in[index], preferred_element_type=F32)
            hidden_part = jax.nn.gelu(hidden_part, approximate=True).astype(BF16)
            total = total + jnp.dot(
                hidden_part,
                w_out[index * in_cols : (index + 1) * in_cols, :],
                preferred_element_type=F32,
            )
        out[rows, :] = total.astype(BF16)


def call(kernel, out_shape, scratch, flops, smem, args):
    in_specs = [
        pl.BlockSpec(memory_space=pltpu.SMEM if index in smem else pltpu.VMEM)
        for index in range(len(args))
    ]
    moved = sum(arg.size * arg.dtype.itemsize for arg in args)
    return pl.pallas_call(
        kernel,
        out_shape=out_shape,
        in_specs=in_specs,
        out_specs=jax.tree.map(lambda _: pl.BlockSpec(memory_space=pltpu.VMEM), out_shape),
        scratch_shapes=scratch,
        cost_estimate=pl.CostEstimate(flops=flops, bytes_accessed=moved, transcendentals=0),
        compiler_params=pltpu.CompilerParams(vmem_limit_bytes=VMEM_LIMIT),
    )(*args)


def on_device(
    states,
    gain_attn,
    w_qkv,
    w_out_attn,
    pattern,
    gain_mix,
    neighbours,
    degree,
    mix,
    gain_ffn,
    w_in,
    w_out,
):
    steps, zone_rows, width = states.shape
    rows = steps * zone_rows
    reach = pattern.shape[1]
    zones = lax.axis_size("zone")
    my_block, my_zone = lax.axis_index("tm"), lax.axis_index("zone")
    place = jnp.stack([my_block, my_zone]).astype(jnp.int32)
    key_count = (reach + 1) * steps

    half = w_qkv.shape[0] // 2
    first = lax.dynamic_slice_in_dim(
        jnp.concatenate([w_qkv, w_out_attn], axis=1), (my_block % 2) * half, half, axis=0
    )
    direct = [rotated(first, "zone", step) for step in range(1, zones)]
    earlier = [shifted(states, "tm", offset) for offset in range(reach, 0, -1)]
    partner = [swapped(piece, "tm", 1) for piece in direct]

    in_cols = w_in.shape[1] // SPREAD
    out_rows = w_out.shape[0] // SPREAD
    slot = my_block % SPREAD
    out_slice = lax.dynamic_slice_in_dim(w_out, slot * out_rows, out_rows, axis=0)
    second = jnp.concatenate(
        [lax.dynamic_slice_in_dim(w_in, slot * in_cols, in_cols, axis=1)]
        + [out_slice[:, at : at + in_cols] for at in range(0, width, in_cols)],
        axis=0,
    )
    across = jnp.stack([rotated(second, "zone", step) for step in range(1, zones)])
    pieces = {0: across}
    for bits in range(2, SPREAD, 2):
        pieces[bits] = swapped(across, "tm", bits)
    for bits in range(0, SPREAD, 2):
        pieces[bits + 1] = swapped(pieces[bits], "tm", 1)

    part = width // zones
    wide = part % LANES == 0
    mixin_shape = (zones, rows, part) if wide else (rows, width)
    after_attn, mixin = call(
        functools.partial(attention_kernel, zones, reach),
        (jax.ShapeDtypeStruct((rows, width), F32), jax.ShapeDtypeStruct(mixin_shape, BF16)),
        [
            pltpu.VMEM((width, 3 * width), BF16),
            pltpu.VMEM((width, width), BF16),
            pltpu.VMEM((3 * width, width), BF16),
            pltpu.VMEM((key_count * zone_rows, width), BF16),
            pltpu.VMEM((3 * width, key_count * zone_rows), F32),
            pltpu.VMEM((width, rows), F32),
        ],
        2 * rows * width * width * 10,
        (0, 1),
        [place, pattern, states]
        + earlier
        + [gain_attn.reshape(1, -1), gain_mix.reshape(1, -1), w_qkv, w_out_attn]
        + direct
        + partner,
    )
    if not wide:
        mixin = jnp.transpose(mixin.reshape(rows, zones, part), (1, 0, 2))
    items = lax.all_to_all(mixin, "zone", split_axis=0, concat_axis=0, tiled=True)
    spatial = call(
        functools.partial(mixing_kernel, steps),
        jax.ShapeDtypeStruct((zones, rows, part), BF16),
        [],
        2 * rows * width * zone_rows * 3,
        (0, 1),
        [neighbours, degree, mix, items],
    )
    spatial = lax.all_to_all(spatial, "zone", split_axis=0, concat_axis=0, tiled=True)
    if not wide:
        spatial = jnp.transpose(spatial, (1, 0, 2)).reshape(rows, width)
    hidden = w_in.shape[1]
    evolved = call(
        functools.partial(ffn_kernel, zones),
        jax.ShapeDtypeStruct((rows, width), BF16),
        [
            pltpu.VMEM((SPREAD, width, in_cols), BF16),
            pltpu.VMEM((hidden, width), BF16),
            pltpu.VMEM((rows, width), F32),
            pltpu.VMEM((rows, width), BF16),
        ],
        4 * rows * width * hidden,
        (0,),
        [place, spatial, after_attn, gain_ffn.reshape(1, -1), w_in, w_out]
        + [pieces[bits] for bits in range(SPREAD)],
    )
    return evolved.reshape(steps, zone_rows, width)


def solution(mesh):
    return jax.shard_map(
        on_device,
        mesh=mesh,
        in_specs=(
            P("tm", "zone", None),
            P(),
            P("zone", None),
            P("zone", None),
            P("tm", None),
            P(),
            P(),
            P(),
            P(),
            P(),
            P("zone", None),
            P("zone", None),
        ),
        out_specs=P("tm", "zone", None),
        check_vma=False,
    )
```

```python
import functools

import jax
import jax.numpy as jnp
from jax import lax
from jax.experimental import pallas as pl
from jax.experimental.pallas import tpu as pltpu
from jax.sharding import PartitionSpec as P

HEADS = 4
SPREAD = 8
LANES = 128
F32 = jnp.float32
BF16 = jnp.bfloat16
MIB = 1024 * 1024


def shifted(value, axis, steps):
    count = lax.axis_size(axis)
    return lax.ppermute(value, axis, [(source, source + steps) for source in range(count - steps)])


def rotated(value, axis, steps):
    count = lax.axis_size(axis)
    return lax.ppermute(value, axis, [(source, (source + steps) % count) for source in range(count)])


def swapped(value, axis, bits):
    count = lax.axis_size(axis)
    return lax.ppermute(value, axis, [(source, source ^ bits) for source in range(count)])


def rms_scale(values, gain):
    mean_sq = jnp.mean(values * values, axis=-1, keepdims=True)
    return values * lax.rsqrt(mean_sq + 1e-06) * gain


def quarter_of(block):
    return lax.rem(block, 2) + 2 * lax.rem(lax.div(block, 4), 2)


def row_sum(value):
    return jnp.sum(value, axis=0, keepdims=True)


def attention_kernel(zones, reach, place, pattern, states, *refs):
    earlier, refs = refs[:reach], refs[reach:]
    (gain_attn, gain_mix, own_qkv, own_attn), refs = refs[:4], refs[4:]
    pieces, refs = refs[:4], refs[4:]
    after_out, mixin_out, weights, w_turned, normed, projected, context = refs
    steps, zone_rows, width = states.shape
    head_size = width // HEADS
    key_count = (reach + 1) * steps
    my_block, my_zone = place[0], place[1]
    shard = own_qkv.shape[0]

    own_rows = pl.ds(pl.multiple_of(my_zone * shard, shard), shard)
    for index in range(3):
        weights[index, own_rows, :] = own_qkv[:, index * width : (index + 1) * width]
    weights[3, own_rows, :] = own_attn[...]
    my_quarter = quarter_of(my_block)
    for bits in range(4):
        for step in range(1, zones):
            source = lax.rem(my_zone - step + zones, zones)
            rows = pl.ds(pl.multiple_of(source * shard, shard), shard)
            weights[my_quarter ^ bits, rows, :] = pieces[bits][step - 1]
    for index in range(3):
        for block in range(width // LANES):
            first = block * LANES
            rows = slice(index * width + first, index * width + first + LANES)
            w_turned[rows, :] = weights[index, :, first : first + LANES].T

    blocks = list(earlier) + [states]
    gain = gain_attn[...]
    for index, block in enumerate(blocks):
        for step in range(steps):
            row = (index * steps + step) * zone_rows
            normed[row : row + zone_rows, :] = rms_scale(block[step].astype(F32), gain).astype(BF16)

    def project(first, last, weight_rows):
        return lax.dot_general(
            w_turned[weight_rows, :],
            normed[first:last, :],
            (((1,), (1,)), ((), ())),
            preferred_element_type=F32,
        ).astype(BF16).astype(F32)

    span = 2 * zone_rows
    for first in range(0, key_count * zone_rows, span):
        own = first >= reach * steps * zone_rows
        rows = slice(0 if own else width, 3 * width)
        projected[rows, first : first + span] = project(first, first + span, rows)

    allowed_back = [
        (pattern[0, back - 1] == 1) & (my_block >= back) for back in range(reach, 0, -1)
    ]
    chunks = head_size // 8

    def usable(query):
        return range(reach * steps + query + 1)

    def head_body(head, carry):
        base = head * head_size

        def tile(kind, chunk, key):
            row = pl.multiple_of(kind * width + base + chunk * 8, 8)
            return projected[pl.ds(row, 8), key * zone_rows : (key + 1) * zone_rows]

        for pair in range(0, steps, 2):
            queries = range(pair, min(pair + 2, steps))
            sums = {}
            for chunk in range(chunks):
                q_tiles = {q: tile(0, chunk, reach * steps + q) for q in queries}
                for key in usable(queries[-1]):
                    k_tile = tile(1, chunk, key)
                    for q in queries:
                        if key in usable(q):
                            term = q_tiles[q] * k_tile
                            sums[q, key] = term if chunk == 0 else sums[q, key] + term
            weights, scales = {}, {}
            for q in queries:
                scores = jnp.concatenate([row_sum(sums[q, key]) for key in usable(q)], axis=0)
                scores = scores * head_size ** (-0.5)
                row_id = lax.broadcasted_iota(jnp.int32, scores.shape, 0)
                allowed = row_id >= reach * steps
                for index, live in enumerate(allowed_back):
                    inside = (row_id >= index * steps) & (row_id < (index + 1) * steps)
                    allowed = allowed | (inside & live)
                masked = jnp.where(allowed, scores, -1e30)
                top = jnp.max(masked, axis=0, keepdims=True)
                expw = jnp.where(allowed, jnp.exp(masked - top), 0.0)
                scales[q] = jnp.broadcast_to(1.0 / row_sum(expw), (8, zone_rows))
                probs = expw.astype(BF16).astype(F32)
                for key in usable(q):
                    weights[q, key] = jnp.broadcast_to(probs[key : key + 1, :], (8, zone_rows))
            for chunk in range(chunks):
                sums = {}
                for key in usable(queries[-1]):
                    v_tile = tile(2, chunk, key)
                    for q in queries:
                        if key in usable(q):
                            term = weights[q, key] * v_tile
                            sums[q] = term if key == 0 else sums[q] + term
                for q in queries:
                    row = pl.multiple_of(base + chunk * 8, 8)
                    context[pl.ds(row, 8), q * zone_rows : (q + 1) * zone_rows] = sums[q] * scales[q]
        return carry

    lax.fori_loop(0, HEADS, head_body, 0)

    mix_gain = gain_mix[...]
    for step in range(steps):
        rows = slice(step * zone_rows, (step + 1) * zone_rows)
        turned = context[:, rows].T.astype(BF16)
        after = states[step].astype(F32) + jnp.dot(turned, weights[3], preferred_element_type=F32)
        after_out[rows, :] = after
        mixin = rms_scale(after, mix_gain).astype(BF16)
        if len(mixin_out.shape) == 2:
            mixin_out[rows, :] = mixin
        else:
            part = mixin_out.shape[-1]
            for index in range(mixin_out.shape[0]):
                mixin_out[index, rows, :] = mixin[:, index * part : (index + 1) * part]


def mixing_kernel(steps, neighbours, degree, mix, items, out):
    block_count, slots, zone_rows, _ = mix.shape
    part = items.shape[-1]
    group = 2 if part % LANES == 0 and steps % 2 == 0 else 1

    def block_body(block, carry):
        left = []
        for slot in range(slots):
            tile = mix[block, slot]
            left.append(jnp.where(degree[block] > slot, tile, jnp.zeros_like(tile)))
        left = jnp.concatenate(left, axis=1)
        for step in range(0, steps, group):
            right = []
            for slot in range(slots):
                source = neighbours[block, slot]
                right.append(
                    jnp.concatenate(
                        [
                            items[source, (step + index) * zone_rows : (step + index + 1) * zone_rows, :]
                            for index in range(group)
                        ],
                        axis=1,
                    )
                )
            result = jnp.dot(left, jnp.concatenate(right, axis=0), preferred_element_type=F32)
            for index in range(group):
                rows = slice((step + index) * zone_rows, (step + index + 1) * zone_rows)
                out[block, rows, :] = result[:, index * part : (index + 1) * part].astype(BF16)
        return carry

    lax.fori_loop(0, block_count, block_body, 0)


def ffn_kernel(zones, place, spatial, after_attn, gain_ffn, own_in, own_out, *refs):
    pieces, (out, w_in, w_out, after_mix, ffn_in) = refs[:SPREAD], refs[SPREAD:]
    rows_all, width = after_attn.shape
    my_block, my_zone = place[0], place[1]
    in_shard, hidden = own_in.shape
    out_shard = own_out.shape[0]
    in_cols, out_rows = hidden // SPREAD, out_shard // SPREAD
    folds = width // in_cols

    start = pl.multiple_of(my_zone * in_shard, in_shard)
    for index in range(SPREAD):
        w_in[index, pl.ds(start, in_shard), :] = own_in[:, index * in_cols : (index + 1) * in_cols]
    w_out[pl.ds(pl.multiple_of(my_zone * out_shard, out_shard), out_shard), :] = own_out[...]
    for bits in range(SPREAD):
        slot = lax.rem(my_block, SPREAD) ^ bits
        for step in range(1, zones):
            source = lax.rem(my_zone - step + zones, zones)
            piece = pieces[bits]
            w_in[slot, pl.ds(pl.multiple_of(source * in_shard, in_shard), in_shard), :] = piece[
                step - 1, :in_shard, :
            ]
            start = pl.multiple_of(source * out_shard + slot * out_rows, out_rows)
            for fold in range(folds):
                first = in_shard + fold * out_rows
                w_out[pl.ds(start, out_rows), fold * in_cols : (fold + 1) * in_cols] = piece[
                    step - 1, first : first + out_rows, :
                ]

    gain = gain_ffn[...]
    span = 128
    for first in range(0, rows_all, span):
        rows = slice(first, first + span)
        if len(spatial.shape) == 2:
            moved = spatial[rows, :]
        else:
            moved = jnp.concatenate([spatial[index, rows, :] for index in range(spatial.shape[0])], axis=1)
        total = after_attn[rows, :] + moved.astype(F32)
        after_mix[rows, :] = total
        ffn_in[rows, :] = rms_scale(total, gain).astype(BF16)
    span = 256
    for first in range(0, rows_all, span):
        rows = slice(first, first + span)
        total = after_mix[rows, :]
        for index in range(SPREAD):
            hidden_part = jnp.dot(ffn_in[rows, :], w_in[index], preferred_element_type=F32)
            hidden_part = jax.nn.gelu(hidden_part, approximate=True).astype(BF16)
            total = total + jnp.dot(
                hidden_part,
                w_out[index * in_cols : (index + 1) * in_cols, :],
                preferred_element_type=F32,
            )
        out[rows, :] = total.astype(BF16)


def call(kernel, out_shape, scratch, flops, smem, limit, args):
    in_specs = [
        pl.BlockSpec(memory_space=pltpu.SMEM if index in smem else pltpu.VMEM)
        for index in range(len(args))
    ]
    moved = sum(arg.size * arg.dtype.itemsize for arg in args)
    return pl.pallas_call(
        kernel,
        out_shape=out_shape,
        in_specs=in_specs,
        out_specs=jax.tree.map(lambda _: pl.BlockSpec(memory_space=pltpu.VMEM), out_shape),
        scratch_shapes=scratch,
        cost_estimate=pl.CostEstimate(flops=flops, bytes_accessed=moved, transcendentals=0),
        compiler_params=pltpu.CompilerParams(vmem_limit_bytes=limit * MIB),
    )(*args)


def on_device(
    states,
    gain_attn,
    w_qkv,
    w_out_attn,
    pattern,
    gain_mix,
    neighbours,
    degree,
    mix,
    gain_ffn,
    w_in,
    w_out,
):
    steps, zone_rows, width = states.shape
    rows = steps * zone_rows
    reach = pattern.shape[1]
    zones = lax.axis_size("zone")
    my_block, my_zone = lax.axis_index("tm"), lax.axis_index("zone")
    place = jnp.stack([my_block, my_zone]).astype(jnp.int32)
    key_count = (reach + 1) * steps

    first = lax.dynamic_slice_in_dim(
        jnp.concatenate([w_qkv, w_out_attn], axis=1), quarter_of(my_block) * width, width, axis=1
    )
    direct = [rotated(first, "zone", step) for step in range(1, zones)]
    earlier = [shifted(states, "tm", offset) for offset in range(reach, 0, -1)]
    direct = jnp.stack(direct)
    over = swapped(direct, "tm", 4)
    quarters = [direct, swapped(direct, "tm", 1), over, swapped(over, "tm", 1)]

    in_cols = w_in.shape[1] // SPREAD
    out_rows = w_out.shape[0] // SPREAD
    slot = my_block % SPREAD
    out_slice = lax.dynamic_slice_in_dim(w_out, slot * out_rows, out_rows, axis=0)
    second = jnp.concatenate(
        [lax.dynamic_slice_in_dim(w_in, slot * in_cols, in_cols, axis=1)]
        + [out_slice[:, at : at + in_cols] for at in range(0, width, in_cols)],
        axis=0,
    )
    second, _ = lax.optimization_barrier((second, direct))
    across = jnp.stack([rotated(second, "zone", step) for step in range(1, zones)])
    across, quarters = lax.optimization_barrier((across, quarters))
    pieces = {0: across}
    for bits in range(2, SPREAD, 2):
        pieces[bits] = swapped(across, "tm", bits)
    for bits in range(0, SPREAD, 2):
        pieces[bits + 1] = swapped(pieces[bits], "tm", 1)

    part = width // zones
    wide = part % LANES == 0
    mixin_shape = (zones, rows, part) if wide else (rows, width)
    after_attn, mixin = call(
        functools.partial(attention_kernel, zones, reach),
        (jax.ShapeDtypeStruct((rows, width), F32), jax.ShapeDtypeStruct(mixin_shape, BF16)),
        [
            pltpu.VMEM((4, width, width), BF16),
            pltpu.VMEM((3 * width, width), BF16),
            pltpu.VMEM((key_count * zone_rows, width), BF16),
            pltpu.VMEM((3 * width, key_count * zone_rows), F32),
            pltpu.VMEM((width, rows), F32),
        ],
        2 * rows * width * width * 10,
        (0, 1),
        24,
        [place, pattern, states]
        + earlier
        + [gain_attn.reshape(1, -1), gain_mix.reshape(1, -1), w_qkv, w_out_attn]
        + quarters,
    )
    if not wide:
        mixin = jnp.transpose(mixin.reshape(rows, zones, part), (1, 0, 2))
    items = lax.all_to_all(mixin, "zone", split_axis=0, concat_axis=0, tiled=True)
    spatial = call(
        functools.partial(mixing_kernel, steps),
        jax.ShapeDtypeStruct((zones, rows, part), BF16),
        [],
        2 * rows * width * zone_rows * 3,
        (0, 1),
        8,
        [neighbours, degree, mix, items],
    )
    spatial = lax.all_to_all(spatial, "zone", split_axis=0, concat_axis=0, tiled=True)
    if not wide:
        spatial = jnp.transpose(spatial, (1, 0, 2)).reshape(rows, width)
    hidden = w_in.shape[1]
    evolved = call(
        functools.partial(ffn_kernel, zones),
        jax.ShapeDtypeStruct((rows, width), BF16),
        [
            pltpu.VMEM((SPREAD, width, in_cols), BF16),
            pltpu.VMEM((hidden, width), BF16),
            pltpu.VMEM((rows, width), F32),
            pltpu.VMEM((rows, width), BF16),
        ],
        4 * rows * width * hidden,
        (0,),
        16,
        [place, spatial, after_attn, gain_ffn.reshape(1, -1), w_in, w_out]
        + [pieces[bits] for bits in range(SPREAD)],
    )
    return evolved.reshape(steps, zone_rows, width)


def solution(mesh):
    return jax.shard_map(
        on_device,
        mesh=mesh,
        in_specs=(
            P("tm", "zone", None),
            P(),
            P("zone", None),
            P("zone", None),
            P("tm", None),
            P(),
            P(),
            P(),
            P(),
            P(),
            P("zone", None),
            P("zone", None),
        ),
        out_specs=P("tm", "zone", None),
        check_vma=False,
    )
```

```python
import functools

import jax
import jax.numpy as jnp
from jax import lax
from jax.experimental import pallas as pl
from jax.experimental.pallas import tpu as pltpu
from jax.sharding import PartitionSpec as P

HEADS = 4
SPREAD = 8
FIRST_BITS = (0, 2, 4, 6, 1, 3, 5, 7)
SECOND_BITS = (0, 4, 2, 6, 1, 5, 3, 7)
LANES = 128
F32 = jnp.float32
BF16 = jnp.bfloat16
MIB = 1024 * 1024


def shifted(value, axis, steps):
    count = lax.axis_size(axis)
    return lax.ppermute(value, axis, [(source, source + steps) for source in range(count - steps)])


def rotated(value, axis, steps):
    count = lax.axis_size(axis)
    return lax.ppermute(value, axis, [(source, (source + steps) % count) for source in range(count)])


def swapped(value, axis, bits):
    count = lax.axis_size(axis)
    return lax.ppermute(value, axis, [(source, source ^ bits) for source in range(count)])


def rms_scale(values, gain):
    mean_sq = jnp.mean(values * values, axis=-1, keepdims=True)
    return values * lax.rsqrt(mean_sq + 1e-06) * gain


def quarter_of(block):
    parity = lax.rem(lax.div(block, 2) + lax.div(block, 4), 2)
    return lax.rem(block, 2) + 2 * parity


def row_sum(value):
    return jnp.sum(value, axis=0, keepdims=True)


def norm_kernel(*refs):
    blocks, (gain_attn, normed) = refs[:-2], refs[-2:]
    steps, zone_rows, _ = blocks[0].shape
    gain = gain_attn[...]
    for index, block in enumerate(blocks):
        for step in range(steps):
            row = (index * steps + step) * zone_rows
            normed[row : row + zone_rows, :] = rms_scale(block[step].astype(F32), gain).astype(BF16)


def attention_kernel(zones, reach, steps, place, pattern, normed, own_qkv, own_attn, *refs):
    pieces, (context_out, attn_out, weights, w_turned, projected, context) = refs[:-6], refs[-6:]
    key_count = (reach + 1) * steps
    zone_rows = normed.shape[0] // key_count
    width = normed.shape[1]
    head_size = width // HEADS
    my_block, my_zone = place[0], place[1]
    shard = own_qkv.shape[0]

    own_rows = pl.ds(pl.multiple_of(my_zone * shard, shard), shard)
    for index in range(3):
        weights[index, own_rows, :] = own_qkv[:, index * width : (index + 1) * width]
    weights[3, own_rows, :] = own_attn[...]
    my_quarter = quarter_of(my_block)
    half = shard // 2
    for step in range(1, zones):
        source = lax.rem(my_zone - step + zones, zones)
        for piece, bits, part in zip(pieces, (0, 1, 2, 2, 3, 3), (0, 0, 0, 1, 0, 1)):
            rows = pl.ds(pl.multiple_of(source * shard + part * half, half), piece.shape[1])
            weights[my_quarter ^ bits, rows, :] = piece[step - 1]
    attn_out[...] = weights[3]
    for index in range(3):
        for block in range(width // LANES):
            first = block * LANES
            rows = slice(index * width + first, index * width + first + LANES)
            w_turned[rows, :] = weights[index, :, first : first + LANES].T

    def project(first, last, weight_rows):
        return lax.dot_general(
            w_turned[weight_rows, :],
            normed[first:last, :],
            (((1,), (1,)), ((), ())),
            preferred_element_type=F32,
        ).astype(BF16).astype(F32)

    span = 2 * zone_rows
    for first in range(0, key_count * zone_rows, span):
        own = first >= reach * steps * zone_rows
        rows = slice(0 if own else width, 3 * width)
        projected[rows, first : first + span] = project(first, first + span, rows)

    allowed_back = [
        (pattern[0, back - 1] == 1) & (my_block >= back) for back in range(reach, 0, -1)
    ]
    chunks = head_size // 8

    def usable(query):
        return range(reach * steps + query + 1)

    def head_body(head, carry):
        base = head * head_size

        def tile(kind, chunk, key):
            row = pl.multiple_of(kind * width + base + chunk * 8, 8)
            return projected[pl.ds(row, 8), key * zone_rows : (key + 1) * zone_rows]

        for pair in range(0, steps, 2):
            queries = range(pair, min(pair + 2, steps))
            sums = {}
            for chunk in range(chunks):
                q_tiles = {q: tile(0, chunk, reach * steps + q) for q in queries}
                for key in usable(queries[-1]):
                    k_tile = tile(1, chunk, key)
                    for q in queries:
                        if key in usable(q):
                            term = q_tiles[q] * k_tile
                            sums[q, key] = term if chunk == 0 else sums[q, key] + term
            weights, scales = {}, {}
            for q in queries:
                scores = jnp.concatenate([row_sum(sums[q, key]) for key in usable(q)], axis=0)
                scores = scores * head_size ** (-0.5)
                row_id = lax.broadcasted_iota(jnp.int32, scores.shape, 0)
                allowed = row_id >= reach * steps
                for index, live in enumerate(allowed_back):
                    inside = (row_id >= index * steps) & (row_id < (index + 1) * steps)
                    allowed = allowed | (inside & live)
                masked = jnp.where(allowed, scores, -1e30)
                top = jnp.max(masked, axis=0, keepdims=True)
                expw = jnp.where(allowed, jnp.exp(masked - top), 0.0)
                scales[q] = jnp.broadcast_to(1.0 / row_sum(expw), (8, zone_rows))
                probs = expw.astype(BF16).astype(F32)
                for key in usable(q):
                    weights[q, key] = jnp.broadcast_to(probs[key : key + 1, :], (8, zone_rows))
            for chunk in range(chunks):
                sums = {}
                for key in usable(queries[-1]):
                    v_tile = tile(2, chunk, key)
                    for q in queries:
                        if key in usable(q):
                            term = weights[q, key] * v_tile
                            sums[q] = term if key == 0 else sums[q] + term
                for q in queries:
                    row = pl.multiple_of(base + chunk * 8, 8)
                    context[pl.ds(row, 8), q * zone_rows : (q + 1) * zone_rows] = sums[q] * scales[q]
        return carry

    lax.fori_loop(0, HEADS, head_body, 0)

    for step in range(steps):
        rows = slice(step * zone_rows, (step + 1) * zone_rows)
        context_out[rows, :] = context[:, rows].T.astype(BF16)


def project_kernel(place, states, context, w_attn, gain_mix, *refs):
    (after_out, *outs), parts = refs[:-1], refs[-1]
    steps, zone_rows, _ = states.shape
    zones, _, part = parts.shape
    my_zone = place[1]
    gain = gain_mix[...]
    for step in range(steps):
        rows = slice(step * zone_rows, (step + 1) * zone_rows)
        after = states[step].astype(F32) + jnp.dot(
            context[rows, :], w_attn[...], preferred_element_type=F32
        )
        after_out[rows, :] = after
        mixin = rms_scale(after, gain).astype(BF16)
        for index in range(zones):
            parts[index, rows, :] = mixin[:, index * part : (index + 1) * part]
    for step in range(zones):
        outs[step][...] = parts[lax.rem(my_zone + step, zones)]


def mixing_kernel(steps, zones, place, neighbours, degree, mix, *refs):
    arrived, outs, items = refs[:zones], refs[zones : 2 * zones], refs[-1]
    _, slots, zone_rows, _ = mix.shape
    part = items.shape[-1]
    my_zone = place[1]
    group = 2 if part % LANES == 0 and steps % 2 == 0 else 1
    for step in range(zones):
        items[lax.rem(my_zone - step + zones, zones)] = arrived[step][...]

    for target in range(zones):
        block = lax.rem(my_zone + target, zones)
        left = []
        for slot in range(slots):
            tile = mix[block, slot]
            left.append(jnp.where(degree[block] > slot, tile, jnp.zeros_like(tile)))
        left = jnp.concatenate(left, axis=1)
        for step in range(0, steps, group):
            right = []
            for slot in range(slots):
                source = neighbours[block, slot]
                right.append(
                    jnp.concatenate(
                        [
                            items[source, (step + index) * zone_rows : (step + index + 1) * zone_rows, :]
                            for index in range(group)
                        ],
                        axis=1,
                    )
                )
            result = jnp.dot(left, jnp.concatenate(right, axis=0), preferred_element_type=F32)
            for index in range(group):
                rows = slice((step + index) * zone_rows, (step + index + 1) * zone_rows)
                outs[target][rows, :] = result[:, index * part : (index + 1) * part].astype(BF16)


def ffn_kernel(zones, place, after_attn, gain_ffn, own_in, own_out, *refs):
    arrived, refs = refs[:zones], refs[zones:]
    pieces, (out, w_in, w_out, after_mix, ffn_in, parts) = refs[:-6], refs[-6:]
    rows_all, width = after_attn.shape
    my_block, my_zone = place[0], place[1]
    in_shard, hidden = own_in.shape
    out_shard = own_out.shape[0]
    in_cols, out_rows = hidden // SPREAD, out_shard // SPREAD

    for step in range(zones):
        parts[lax.rem(my_zone - step + zones, zones)] = arrived[step][...]
    start = pl.multiple_of(my_zone * in_shard, in_shard)
    for index in range(SPREAD):
        w_in[index, pl.ds(start, in_shard), :] = own_in[:, index * in_cols : (index + 1) * in_cols]
    w_out[pl.ds(pl.multiple_of(my_zone * out_shard, out_shard), out_shard), :] = own_out[...]
    for index, bits in enumerate(FIRST_BITS + SECOND_BITS):
        slot = lax.rem(my_block, SPREAD) ^ bits
        piece = pieces[index]
        for step in range(1, zones):
            source = lax.rem(my_zone - step + zones, zones)
            if index < SPREAD:
                rows = pl.ds(pl.multiple_of(source * in_shard, in_shard), in_shard)
                w_in[slot, rows, :] = piece[step - 1]
            else:
                rows = pl.ds(pl.multiple_of(source * out_shard + slot * out_rows, out_rows), out_rows)
                w_out[rows, :] = piece[step - 1]

    gain = gain_ffn[...]
    span = 128
    part = parts.shape[-1]
    for first in range(0, rows_all, span):
        rows = slice(first, first + span)
        for index in range(zones):
            cols = slice(index * part, (index + 1) * part)
            after_mix[rows, cols] = after_attn[rows, cols] + parts[index, rows, :].astype(F32)
        ffn_in[rows, :] = rms_scale(after_mix[rows, :], gain).astype(BF16)
    span = 256
    for first in range(0, rows_all, span):
        rows = slice(first, first + span)
        total = after_mix[rows, :]
        for index in range(SPREAD):
            hidden_part = jnp.dot(ffn_in[rows, :], w_in[index], preferred_element_type=F32)
            hidden_part = jax.nn.gelu(hidden_part, approximate=True).astype(BF16)
            total = total + jnp.dot(
                hidden_part,
                w_out[index * in_cols : (index + 1) * in_cols, :],
                preferred_element_type=F32,
            )
        out[rows, :] = total.astype(BF16)


def call(kernel, out_shape, scratch, flops, smem, limit, args):
    in_specs = [
        pl.BlockSpec(memory_space=pltpu.SMEM if index in smem else pltpu.VMEM)
        for index in range(len(args))
    ]
    moved = sum(arg.size * arg.dtype.itemsize for arg in args)
    return pl.pallas_call(
        kernel,
        out_shape=out_shape,
        in_specs=in_specs,
        out_specs=jax.tree.map(lambda _: pl.BlockSpec(memory_space=pltpu.VMEM), out_shape),
        scratch_shapes=scratch,
        cost_estimate=pl.CostEstimate(flops=flops, bytes_accessed=moved, transcendentals=0),
        compiler_params=pltpu.CompilerParams(vmem_limit_bytes=limit * MIB),
    )(*args)


def on_device(
    states,
    gain_attn,
    w_qkv,
    w_out_attn,
    pattern,
    gain_mix,
    neighbours,
    degree,
    mix,
    gain_ffn,
    w_in,
    w_out,
):
    steps, zone_rows, width = states.shape
    rows = steps * zone_rows
    reach = pattern.shape[1]
    zones = lax.axis_size("zone")
    my_block, my_zone = lax.axis_index("tm"), lax.axis_index("zone")
    place = jnp.stack([my_block, my_zone]).astype(jnp.int32)
    key_count = (reach + 1) * steps
    hidden = w_in.shape[1]
    in_cols = hidden // SPREAD
    out_rows = w_out.shape[0] // SPREAD
    part = width // zones
    rotations = range(1, zones)

    before = shifted(states, "tm", 2)
    first = lax.dynamic_slice_in_dim(
        jnp.concatenate([w_qkv, w_out_attn], axis=1), quarter_of(my_block) * width, width, axis=1
    )
    direct = [rotated(first, "zone", step) for step in rotations]
    slot = my_block % SPREAD
    slice_in = lax.dynamic_slice_in_dim(w_in, slot * in_cols, in_cols, axis=1)
    slice_out = lax.dynamic_slice_in_dim(w_out, slot * out_rows, out_rows, axis=0)

    half = first.shape[0] // 2
    upper = jnp.stack([piece[:half] for piece in direct])
    lower = jnp.stack([piece[half:] for piece in direct])
    direct = jnp.concatenate([upper, lower], axis=1)
    over_x, over_y = swapped(upper, "tm", 2), swapped(lower, "tm", 4)
    quarters = [direct, swapped(direct, "tm", 1), over_x, over_y]
    quarters += [swapped(over_x, "tm", 1), swapped(over_y, "tm", 1)]

    last = swapped(jnp.where(my_block % 2 == 1, before, states), "tm", 1)
    normed = call(
        norm_kernel,
        jax.ShapeDtypeStruct((key_count * zone_rows, width), BF16),
        [],
        8 * key_count * zone_rows * width,
        (),
        8,
        [before, last, states, gain_attn.reshape(1, -1)],
    )

    packed = jnp.concatenate(
        [slice_in] + [slice_out[:, at : at + in_cols] for at in range(0, width, in_cols)], axis=0
    )
    packed, _ = lax.optimization_barrier((packed, direct))
    across = jnp.stack([rotated(packed, "zone", step) for step in rotations])

    context, w_attn = call(
        functools.partial(attention_kernel, zones, reach, steps),
        (
            jax.ShapeDtypeStruct((rows, width), BF16),
            jax.ShapeDtypeStruct((width, width), BF16),
        ),
        [
            pltpu.VMEM((4, width, width), BF16),
            pltpu.VMEM((3 * width, width), BF16),
            pltpu.VMEM((3 * width, key_count * zone_rows), F32),
            pltpu.VMEM((width, rows), F32),
        ],
        2 * rows * width * width * 20,
        (0, 1),
        22,
        [place, pattern, normed, w_qkv, w_out_attn] + quarters,
    )
    context, across = lax.optimization_barrier((context, across))

    chunk = jax.ShapeDtypeStruct((rows, part), BF16)
    after_attn, *chunks = call(
        project_kernel,
        (jax.ShapeDtypeStruct((rows, width), F32),) + (chunk,) * zones,
        [pltpu.VMEM((zones, rows, part), BF16)],
        2 * rows * width * width,
        (0,),
        8,
        [place, states, context, w_attn, gain_mix.reshape(1, -1)],
    )
    arrived = [chunks[0]] + [rotated(chunks[step], "zone", step) for step in rotations]

    in_shard = w_in.shape[0]
    from_in = across[:, :in_shard]
    from_out = jnp.concatenate(
        [
            across[:, in_shard + fold * out_rows : in_shard + (fold + 1) * out_rows]
            for fold in range(width // in_cols)
        ],
        axis=2,
    )
    ins, outs = [from_in], [from_out]
    for bits_in, bits_out in ((2, 4), (4, 2)):
        ins += [swapped(value, "tm", bits_in) for value in ins]
        outs += [swapped(value, "tm", bits_out) for value in outs]
    pieces = ins + [swapped(value, "tm", 1) for value in ins]
    pieces += outs + [swapped(value, "tm", 1) for value in outs]

    spatial = call(
        functools.partial(mixing_kernel, steps, zones),
        (chunk,) * zones,
        [pltpu.VMEM((zones, rows, part), BF16)],
        2 * rows * width * zone_rows * 3,
        (0, 1, 2),
        8,
        [place, neighbours, degree, mix] + arrived,
    )
    arrived = [spatial[0]] + [rotated(spatial[step], "zone", step) for step in rotations]
    evolved = call(
        functools.partial(ffn_kernel, zones),
        jax.ShapeDtypeStruct((rows, width), BF16),
        [
            pltpu.VMEM((SPREAD, width, in_cols), BF16),
            pltpu.VMEM((hidden, width), BF16),
            pltpu.VMEM((rows, width), F32),
            pltpu.VMEM((rows, width), BF16),
            pltpu.VMEM((zones, rows, part), BF16),
        ],
        4 * rows * width * hidden,
        (0,),
        16,
        [place, after_attn, gain_ffn.reshape(1, -1), w_in, w_out] + arrived + pieces,
    )
    return evolved.reshape(steps, zone_rows, width)


def solution(mesh):
    return jax.shard_map(
        on_device,
        mesh=mesh,
        in_specs=(
            P("tm", "zone", None),
            P(),
            P("zone", None),
            P("zone", None),
            P("tm", None),
            P(),
            P(),
            P(),
            P(),
            P(),
            P("zone", None),
            P("zone", None),
        ),
        out_specs=P("tm", "zone", None),
        check_vma=False,
    )
```

```python
import functools

import jax
import jax.numpy as jnp
from jax import lax
from jax.experimental import pallas as pl
from jax.experimental.pallas import tpu as pltpu
from jax.sharding import PartitionSpec as P

HEADS = 4
SPREAD = 8
LANES = 128
F32 = jnp.float32
BF16 = jnp.bfloat16
MIB = 1024 * 1024


def shifted(value, axis, steps):
    count = lax.axis_size(axis)
    return lax.ppermute(value, axis, [(source, source + steps) for source in range(count - steps)])


def rotated(value, axis, steps):
    count = lax.axis_size(axis)
    return lax.ppermute(value, axis, [(source, (source + steps) % count) for source in range(count)])


def swapped(value, axis, bits):
    count = lax.axis_size(axis)
    return lax.ppermute(value, axis, [(source, source ^ bits) for source in range(count)])


def rms_scale(values, gain):
    mean_sq = jnp.mean(values * values, axis=-1, keepdims=True)
    return values * lax.rsqrt(mean_sq + 1e-06) * gain


def quarter_of(block):
    return lax.rem(block, 2) + 2 * lax.rem(lax.div(block, 4), 2)


def row_sum(value):
    return jnp.sum(value, axis=0, keepdims=True)


def norm_kernel(*refs):
    blocks, (gain_attn, normed) = refs[:-2], refs[-2:]
    steps, zone_rows, _ = blocks[0].shape
    gain = gain_attn[...]
    for index, block in enumerate(blocks):
        for step in range(steps):
            row = (index * steps + step) * zone_rows
            normed[row : row + zone_rows, :] = rms_scale(block[step].astype(F32), gain).astype(BF16)


def pack_kernel(place, own_in, own_out, *refs):
    arrived, (stacked, packed) = refs[:-2], refs[-2:]
    in_shard, hidden = own_in.shape
    out_shard, width = own_out.shape
    in_cols, out_rows = hidden // SPREAD, out_shard // SPREAD
    slot = lax.rem(place[0], SPREAD)
    for index, piece in enumerate(arrived):
        stacked[index] = piece[...]
    packed[:in_shard, :] = own_in[:, pl.ds(pl.multiple_of(slot * in_cols, in_cols), in_cols)]
    rows = pl.ds(pl.multiple_of(slot * out_rows, out_rows), out_rows)
    for fold in range(width // in_cols):
        first = in_shard + fold * out_rows
        packed[first : first + out_rows, :] = own_out[rows, fold * in_cols : (fold + 1) * in_cols]


def attention_kernel(zones, reach, steps, place, pattern, normed, own_qkv, own_attn, *refs):
    pieces, (context_out, attn_out, weights, w_turned, projected, context) = refs[:-6], refs[-6:]
    key_count = (reach + 1) * steps
    zone_rows = normed.shape[0] // key_count
    width = normed.shape[1]
    head_size = width // HEADS
    my_block, my_zone = place[0], place[1]
    shard = own_qkv.shape[0]

    own_rows = pl.ds(pl.multiple_of(my_zone * shard, shard), shard)
    for index in range(3):
        weights[index, own_rows, :] = own_qkv[:, index * width : (index + 1) * width]
    weights[3, own_rows, :] = own_attn[...]
    my_quarter = quarter_of(my_block)
    for step in range(1, zones):
        source = lax.rem(my_zone - step + zones, zones)
        rows = pl.ds(pl.multiple_of(source * shard, shard), shard)
        for bits, piece in enumerate(pieces):
            weights[my_quarter ^ bits, rows, :] = piece[step - 1]
    attn_out[...] = weights[3]
    for index in range(3):
        for block in range(width // LANES):
            first = block * LANES
            rows = slice(index * width + first, index * width + first + LANES)
            w_turned[rows, :] = weights[index, :, first : first + LANES].T

    def project(first, last, weight_rows):
        return lax.dot_general(
            w_turned[weight_rows, :],
            normed[first:last, :],
            (((1,), (1,)), ((), ())),
            preferred_element_type=F32,
        ).astype(BF16).astype(F32)

    span = 2 * zone_rows
    for first in range(0, key_count * zone_rows, span):
        own = first >= reach * steps * zone_rows
        rows = slice(0 if own else width, 3 * width)
        projected[rows, first : first + span] = project(first, first + span, rows)

    allowed_back = [
        (pattern[0, back - 1] == 1) & (my_block >= back) for back in range(reach, 0, -1)
    ]
    chunks = head_size // 8

    def usable(query):
        return range(reach * steps + query + 1)

    def head_body(head, carry):
        base = head * head_size

        def tile(kind, chunk, key):
            row = pl.multiple_of(kind * width + base + chunk * 8, 8)
            return projected[pl.ds(row, 8), key * zone_rows : (key + 1) * zone_rows]

        for pair in range(0, steps, 2):
            queries = range(pair, min(pair + 2, steps))
            sums = {}
            for chunk in range(chunks):
                q_tiles = {q: tile(0, chunk, reach * steps + q) for q in queries}
                for key in usable(queries[-1]):
                    k_tile = tile(1, chunk, key)
                    for q in queries:
                        if key in usable(q):
                            term = q_tiles[q] * k_tile
                            sums[q, key] = term if chunk == 0 else sums[q, key] + term
            weights, scales = {}, {}
            for q in queries:
                scores = jnp.concatenate([row_sum(sums[q, key]) for key in usable(q)], axis=0)
                scores = scores * head_size ** (-0.5)
                row_id = lax.broadcasted_iota(jnp.int32, scores.shape, 0)
                allowed = row_id >= reach * steps
                for index, live in enumerate(allowed_back):
                    inside = (row_id >= index * steps) & (row_id < (index + 1) * steps)
                    allowed = allowed | (inside & live)
                masked = jnp.where(allowed, scores, -1e30)
                top = jnp.max(masked, axis=0, keepdims=True)
                expw = jnp.where(allowed, jnp.exp(masked - top), 0.0)
                scales[q] = jnp.broadcast_to(1.0 / row_sum(expw), (8, zone_rows))
                probs = expw.astype(BF16).astype(F32)
                for key in usable(q):
                    weights[q, key] = jnp.broadcast_to(probs[key : key + 1, :], (8, zone_rows))
            for chunk in range(chunks):
                sums = {}
                for key in usable(queries[-1]):
                    v_tile = tile(2, chunk, key)
                    for q in queries:
                        if key in usable(q):
                            term = weights[q, key] * v_tile
                            sums[q] = term if key == 0 else sums[q] + term
                for q in queries:
                    row = pl.multiple_of(base + chunk * 8, 8)
                    context[pl.ds(row, 8), q * zone_rows : (q + 1) * zone_rows] = sums[q] * scales[q]
        return carry

    lax.fori_loop(0, HEADS, head_body, 0)

    for step in range(steps):
        rows = slice(step * zone_rows, (step + 1) * zone_rows)
        context_out[rows, :] = context[:, rows].T.astype(BF16)


def project_kernel(place, states, context, w_attn, gain_mix, *refs):
    parts = refs[-1]
    steps, zone_rows, _ = states.shape
    zones, _, part = parts.shape
    across, (after_out, *outs, across_out) = refs[: zones - 1], refs[zones - 1 : -1]
    for index, piece in enumerate(across):
        across_out[index] = piece[...]
    my_zone = place[1]
    gain = gain_mix[...]
    for step in range(steps):
        rows = slice(step * zone_rows, (step + 1) * zone_rows)
        after = states[step].astype(F32) + jnp.dot(
            context[rows, :], w_attn[...], preferred_element_type=F32
        )
        after_out[rows, :] = after
        mixin = rms_scale(after, gain).astype(BF16)
        for index in range(zones):
            parts[index, rows, :] = mixin[:, index * part : (index + 1) * part]
    for step in range(zones):
        outs[step][...] = parts[lax.rem(my_zone + step, zones)]


def mixing_kernel(steps, zones, place, neighbours, degree, mix, *refs):
    arrived, outs, items = refs[:zones], refs[zones : 2 * zones], refs[-1]
    _, slots, zone_rows, _ = mix.shape
    part = items.shape[-1]
    my_zone = place[1]
    group = 2 if part % LANES == 0 and steps % 2 == 0 else 1
    for step in range(zones):
        items[lax.rem(my_zone - step + zones, zones)] = arrived[step][...]

    for target in range(zones):
        block = lax.rem(my_zone + target, zones)
        left = []
        for slot in range(slots):
            tile = mix[block, slot]
            left.append(jnp.where(degree[block] > slot, tile, jnp.zeros_like(tile)))
        left = jnp.concatenate(left, axis=1)
        for step in range(0, steps, group):
            right = []
            for slot in range(slots):
                source = neighbours[block, slot]
                right.append(
                    jnp.concatenate(
                        [
                            items[source, (step + index) * zone_rows : (step + index + 1) * zone_rows, :]
                            for index in range(group)
                        ],
                        axis=1,
                    )
                )
            result = jnp.dot(left, jnp.concatenate(right, axis=0), preferred_element_type=F32)
            for index in range(group):
                rows = slice((step + index) * zone_rows, (step + index + 1) * zone_rows)
                outs[target][rows, :] = result[:, index * part : (index + 1) * part].astype(BF16)


def ffn_kernel(zones, place, after_attn, gain_ffn, own_in, own_out, *refs):
    arrived, refs = refs[:zones], refs[zones:]
    pieces, (out, w_in, w_out, after_mix, ffn_in, parts) = refs[:-6], refs[-6:]
    rows_all, width = after_attn.shape
    my_block, my_zone = place[0], place[1]
    in_shard, hidden = own_in.shape
    out_shard = own_out.shape[0]
    in_cols, out_rows = hidden // SPREAD, out_shard // SPREAD

    for step in range(zones):
        parts[lax.rem(my_zone - step + zones, zones)] = arrived[step][...]
    start = pl.multiple_of(my_zone * in_shard, in_shard)
    for index in range(SPREAD):
        w_in[index, pl.ds(start, in_shard), :] = own_in[:, index * in_cols : (index + 1) * in_cols]
    w_out[pl.ds(pl.multiple_of(my_zone * out_shard, out_shard), out_shard), :] = own_out[...]
    for bits, piece in enumerate(pieces):
        slot = lax.rem(my_block, SPREAD) ^ bits
        for step in range(1, zones):
            source = lax.rem(my_zone - step + zones, zones)
            rows = pl.ds(pl.multiple_of(source * in_shard, in_shard), in_shard)
            w_in[slot, rows, :] = piece[step - 1, :in_shard, :]
            rows = pl.ds(pl.multiple_of(source * out_shard + slot * out_rows, out_rows), out_rows)
            for fold in range(width // in_cols):
                first = in_shard + fold * out_rows
                cols = slice(fold * in_cols, (fold + 1) * in_cols)
                w_out[rows, cols] = piece[step - 1, first : first + out_rows, :]

    gain = gain_ffn[...]
    span = 128
    part = parts.shape[-1]
    for first in range(0, rows_all, span):
        rows = slice(first, first + span)
        for index in range(zones):
            cols = slice(index * part, (index + 1) * part)
            after_mix[rows, cols] = after_attn[rows, cols] + parts[index, rows, :].astype(F32)
        ffn_in[rows, :] = rms_scale(after_mix[rows, :], gain).astype(BF16)
    span = 256
    for first in range(0, rows_all, span):
        rows = slice(first, first + span)
        total = after_mix[rows, :]
        for index in range(SPREAD):
            hidden_part = jnp.dot(ffn_in[rows, :], w_in[index], preferred_element_type=F32)
            hidden_part = jax.nn.gelu(hidden_part, approximate=True).astype(BF16)
            total = total + jnp.dot(
                hidden_part,
                w_out[index * in_cols : (index + 1) * in_cols, :],
                preferred_element_type=F32,
            )
        out[rows, :] = total.astype(BF16)


def call(kernel, out_shape, scratch, flops, smem, limit, args):
    in_specs = [
        pl.BlockSpec(memory_space=pltpu.SMEM if index in smem else pltpu.VMEM)
        for index in range(len(args))
    ]
    moved = sum(arg.size * arg.dtype.itemsize for arg in args)
    return pl.pallas_call(
        kernel,
        out_shape=out_shape,
        in_specs=in_specs,
        out_specs=jax.tree.map(lambda _: pl.BlockSpec(memory_space=pltpu.VMEM), out_shape),
        scratch_shapes=scratch,
        cost_estimate=pl.CostEstimate(flops=flops, bytes_accessed=moved, transcendentals=0),
        compiler_params=pltpu.CompilerParams(vmem_limit_bytes=limit * MIB),
    )(*args)


def on_device(
    states,
    gain_attn,
    w_qkv,
    w_out_attn,
    pattern,
    gain_mix,
    neighbours,
    degree,
    mix,
    gain_ffn,
    w_in,
    w_out,
):
    steps, zone_rows, width = states.shape
    rows = steps * zone_rows
    reach = pattern.shape[1]
    zones = lax.axis_size("zone")
    my_block, my_zone = lax.axis_index("tm"), lax.axis_index("zone")
    place = jnp.stack([my_block, my_zone]).astype(jnp.int32)
    key_count = (reach + 1) * steps
    hidden = w_in.shape[1]
    in_cols = hidden // SPREAD
    out_rows = w_out.shape[0] // SPREAD
    part = width // zones
    rotations = range(1, zones)

    before = shifted(states, "tm", 2)
    first = lax.dynamic_slice_in_dim(
        jnp.concatenate([w_qkv, w_out_attn], axis=1), quarter_of(my_block) * width, width, axis=1
    )
    direct = [rotated(first, "zone", step) for step in rotations]
    in_shard = w_in.shape[0]
    packed_shape = (in_shard + out_rows * (width // in_cols), in_cols)
    direct, packed = call(
        pack_kernel,
        (
            jax.ShapeDtypeStruct((zones - 1,) + first.shape, BF16),
            jax.ShapeDtypeStruct(packed_shape, BF16),
        ),
        [],
        0,
        (0,),
        8,
        [place, w_in, w_out] + direct,
    )
    over = swapped(direct, "tm", 4)
    quarters = [direct, swapped(direct, "tm", 1), over, swapped(over, "tm", 1)]
    across = [rotated(packed, "zone", step) for step in rotations]

    last = swapped(jnp.where(my_block % 2 == 1, before, states), "tm", 1)
    normed = call(
        norm_kernel,
        jax.ShapeDtypeStruct((key_count * zone_rows, width), BF16),
        [],
        8 * key_count * zone_rows * width,
        (),
        8,
        [before, last, states, gain_attn.reshape(1, -1)],
    )

    context, w_attn = call(
        functools.partial(attention_kernel, zones, reach, steps),
        (
            jax.ShapeDtypeStruct((rows, width), BF16),
            jax.ShapeDtypeStruct((width, width), BF16),
        ),
        [
            pltpu.VMEM((4, width, width), BF16),
            pltpu.VMEM((3 * width, width), BF16),
            pltpu.VMEM((3 * width, key_count * zone_rows), F32),
            pltpu.VMEM((width, rows), F32),
        ],
        2 * rows * width * width * 20,
        (0, 1),
        22,
        [place, pattern, normed, w_qkv, w_out_attn] + quarters,
    )

    chunk = jax.ShapeDtypeStruct((rows, part), BF16)
    after_attn, *chunks, across = call(
        project_kernel,
        (jax.ShapeDtypeStruct((rows, width), F32),)
        + (chunk,) * zones
        + (jax.ShapeDtypeStruct((zones - 1,) + packed_shape, BF16),),
        [pltpu.VMEM((zones, rows, part), BF16)],
        2 * rows * width * width,
        (0,),
        8,
        [place, states, context, w_attn, gain_mix.reshape(1, -1)] + across,
    )
    arrived = [chunks[0]] + [rotated(chunks[step], "zone", step) for step in rotations]

    pieces = {bits: swapped(across, "tm", bits) for bits in range(2, SPREAD, 2)}
    pieces[0] = across
    for bits in range(0, SPREAD, 2):
        pieces[bits + 1] = swapped(pieces[bits], "tm", 1)

    spatial = call(
        functools.partial(mixing_kernel, steps, zones),
        (chunk,) * zones,
        [pltpu.VMEM((zones, rows, part), BF16)],
        2 * rows * width * zone_rows * 3,
        (0, 1, 2),
        8,
        [place, neighbours, degree, mix] + arrived,
    )
    arrived = [spatial[0]] + [rotated(spatial[step], "zone", step) for step in rotations]
    evolved = call(
        functools.partial(ffn_kernel, zones),
        jax.ShapeDtypeStruct((rows, width), BF16),
        [
            pltpu.VMEM((SPREAD, width, in_cols), BF16),
            pltpu.VMEM((hidden, width), BF16),
            pltpu.VMEM((rows, width), F32),
            pltpu.VMEM((rows, width), BF16),
            pltpu.VMEM((zones, rows, part), BF16),
        ],
        4 * rows * width * hidden,
        (0,),
        16,
        [place, after_attn, gain_ffn.reshape(1, -1), w_in, w_out]
        + arrived
        + [pieces[bits] for bits in range(SPREAD)],
    )
    return evolved.reshape(steps, zone_rows, width)


def solution(mesh):
    return jax.shard_map(
        on_device,
        mesh=mesh,
        in_specs=(
            P("tm", "zone", None),
            P(),
            P("zone", None),
            P("zone", None),
            P("tm", None),
            P(),
            P(),
            P(),
            P(),
            P(),
            P("zone", None),
            P("zone", None),
        ),
        out_specs=P("tm", "zone", None),
        check_vma=False,
    )
```

```python
import functools

import jax
import jax.numpy as jnp
from jax import lax
from jax.experimental import pallas as pl
from jax.experimental.pallas import tpu as pltpu
from jax.sharding import PartitionSpec as P

HEADS = 4
SPREAD = 8
IN_BITS = ((0, 2), (4, 6), (1, 3), (5, 7))
OUT_BITS = ((0, 4), (2, 6), (1, 5), (3, 7))
LANES = 128
F32 = jnp.float32
BF16 = jnp.bfloat16
MIB = 1024 * 1024


def shifted(value, axis, steps):
    count = lax.axis_size(axis)
    return lax.ppermute(value, axis, [(source, source + steps) for source in range(count - steps)])


def rotated(value, axis, steps):
    count = lax.axis_size(axis)
    return lax.ppermute(value, axis, [(source, (source + steps) % count) for source in range(count)])


def swapped(value, axis, bits):
    count = lax.axis_size(axis)
    return lax.ppermute(value, axis, [(source, source ^ bits) for source in range(count)])


def rms_scale(values, gain):
    mean_sq = jnp.mean(values * values, axis=-1, keepdims=True)
    return values * lax.rsqrt(mean_sq + 1e-06) * gain


def quarter_of(block):
    return lax.rem(block, 2) + 2 * lax.rem(lax.div(block, 4), 2)


def row_sum(value):
    return jnp.sum(value, axis=0, keepdims=True)


def norm_kernel(*refs):
    blocks, (gain_attn, normed) = refs[:-2], refs[-2:]
    steps, zone_rows, _ = blocks[0].shape
    gain = gain_attn[...]
    for index, block in enumerate(blocks):
        for step in range(steps):
            row = (index * steps + step) * zone_rows
            normed[row : row + zone_rows, :] = rms_scale(block[step].astype(F32), gain).astype(BF16)


def pack_kernel(place, own_in, own_out, *refs):
    arrived, (stacked, packed, sems) = refs[:-3], refs[-3:]
    in_shard, hidden = own_in.shape
    out_shard, width = own_out.shape
    in_cols, out_rows = hidden // SPREAD, out_shard // SPREAD
    slot = lax.rem(place[0], SPREAD)
    cols = pl.ds(pl.multiple_of(slot * in_cols, in_cols), in_cols)
    rows = pl.ds(pl.multiple_of(slot * out_rows, out_rows), out_rows)
    copies = [pltpu.make_async_copy(own_in.at[:, cols], packed.at[:in_shard, :], sems.at[0])]
    for fold in range(width // in_cols):
        first = in_shard + fold * out_rows
        copies.append(
            pltpu.make_async_copy(
                own_out.at[rows, fold * in_cols : (fold + 1) * in_cols],
                packed.at[first : first + out_rows, :],
                sems.at[1 + fold],
            )
        )
    for copy in copies:
        copy.start()
    for index, piece in enumerate(arrived):
        stacked[index] = piece[...]
    for copy in copies:
        copy.wait()


def pair_kernel(*refs):
    ins, outs = refs[:4], refs[4:]
    for index, value in enumerate(ins):
        outs[index // 2][index % 2] = value[...]


def attention_kernel(zones, reach, steps, place, pattern, normed, own_qkv, own_attn, *refs):
    pieces, (context_out, attn_out, weights, w_turned, projected, context, sems) = refs[:-7], refs[-7:]
    key_count = (reach + 1) * steps
    zone_rows = normed.shape[0] // key_count
    width = normed.shape[1]
    head_size = width // HEADS
    my_block, my_zone = place[0], place[1]
    shard = own_qkv.shape[0]

    own_rows = pl.ds(pl.multiple_of(my_zone * shard, shard), shard)
    copies = [
        pltpu.make_async_copy(
            own_qkv.at[:, index * width : (index + 1) * width],
            weights.at[index, own_rows, :],
            sems.at[index],
        )
        for index in range(3)
    ]
    copies.append(pltpu.make_async_copy(own_attn, weights.at[3, own_rows, :], sems.at[3]))
    for copy in copies:
        copy.start()
    my_quarter = quarter_of(my_block)
    for step in range(1, zones):
        source = lax.rem(my_zone - step + zones, zones)
        rows = pl.ds(pl.multiple_of(source * shard, shard), shard)
        for bits, piece in enumerate(pieces):
            weights[my_quarter ^ bits, rows, :] = piece[step - 1]
    for copy in copies:
        copy.wait()
    attn_out[...] = weights[3]
    for index in range(3):
        for block in range(width // LANES):
            first = block * LANES
            rows = slice(index * width + first, index * width + first + LANES)
            w_turned[rows, :] = weights[index, :, first : first + LANES].T

    def project(first, last, weight_rows):
        return lax.dot_general(
            w_turned[weight_rows, :],
            normed[first:last, :],
            (((1,), (1,)), ((), ())),
            preferred_element_type=F32,
        ).astype(BF16).astype(F32)

    span = 2 * zone_rows
    for first in range(0, key_count * zone_rows, span):
        own = first >= reach * steps * zone_rows
        rows = slice(0 if own else width, 3 * width)
        projected[rows, first : first + span] = project(first, first + span, rows)

    allowed_back = [
        (pattern[0, back - 1] == 1) & (my_block >= back) for back in range(reach, 0, -1)
    ]
    chunks = head_size // 8

    def usable(query):
        return range(reach * steps + query + 1)

    def head_body(head, carry):
        base = head * head_size

        def tile(kind, chunk, key):
            row = pl.multiple_of(kind * width + base + chunk * 8, 8)
            return projected[pl.ds(row, 8), key * zone_rows : (key + 1) * zone_rows]

        for pair in range(0, steps, 2):
            queries = range(pair, min(pair + 2, steps))
            sums = {}
            for chunk in range(chunks):
                q_tiles = {q: tile(0, chunk, reach * steps + q) for q in queries}
                for key in usable(queries[-1]):
                    k_tile = tile(1, chunk, key)
                    for q in queries:
                        if key in usable(q):
                            term = q_tiles[q] * k_tile
                            sums[q, key] = term if chunk == 0 else sums[q, key] + term
            weights, scales = {}, {}
            for q in queries:
                scores = jnp.concatenate([row_sum(sums[q, key]) for key in usable(q)], axis=0)
                scores = scores * head_size ** (-0.5)
                row_id = lax.broadcasted_iota(jnp.int32, scores.shape, 0)
                allowed = row_id >= reach * steps
                for index, live in enumerate(allowed_back):
                    inside = (row_id >= index * steps) & (row_id < (index + 1) * steps)
                    allowed = allowed | (inside & live)
                masked = jnp.where(allowed, scores, -1e30)
                top = jnp.max(masked, axis=0, keepdims=True)
                expw = jnp.where(allowed, jnp.exp(masked - top), 0.0)
                scales[q] = jnp.broadcast_to(1.0 / row_sum(expw), (8, zone_rows))
                probs = expw.astype(BF16).astype(F32)
                for key in usable(q):
                    weights[q, key] = jnp.broadcast_to(probs[key : key + 1, :], (8, zone_rows))
            for chunk in range(chunks):
                sums = {}
                for key in usable(queries[-1]):
                    v_tile = tile(2, chunk, key)
                    for q in queries:
                        if key in usable(q):
                            term = weights[q, key] * v_tile
                            sums[q] = term if key == 0 else sums[q] + term
                for q in queries:
                    row = pl.multiple_of(base + chunk * 8, 8)
                    context[pl.ds(row, 8), q * zone_rows : (q + 1) * zone_rows] = sums[q] * scales[q]
        return carry

    lax.fori_loop(0, HEADS, head_body, 0)

    for step in range(steps):
        rows = slice(step * zone_rows, (step + 1) * zone_rows)
        context_out[rows, :] = context[:, rows].T.astype(BF16)


def project_kernel(place, states, context, w_attn, gain_mix, *refs):
    parts = refs[-1]
    steps, zone_rows, _ = states.shape
    zones, _, part = parts.shape
    across, (after_out, *outs, first_out, second_out) = refs[: zones - 1], refs[zones - 1 : -1]
    split = first_out.shape[1]
    for index, piece in enumerate(across):
        first_out[index] = piece[:split, :]
        second_out[index] = piece[split:, :]
    my_zone = place[1]
    gain = gain_mix[...]
    for step in range(steps):
        rows = slice(step * zone_rows, (step + 1) * zone_rows)
        after = states[step].astype(F32) + jnp.dot(
            context[rows, :], w_attn[...], preferred_element_type=F32
        )
        after_out[rows, :] = after
        mixin = rms_scale(after, gain).astype(BF16)
        for index in range(zones):
            parts[index, rows, :] = mixin[:, index * part : (index + 1) * part]
    for step in range(zones):
        outs[step][...] = parts[lax.rem(my_zone + step, zones)]


def mixing_kernel(steps, zones, place, neighbours, degree, mix, *refs):
    arrived, outs, items = refs[:zones], refs[-1 - zones : -1], refs[-1]
    _, slots, zone_rows, _ = mix.shape
    part = items.shape[-1]
    my_zone = place[1]
    group = 2 if part % LANES == 0 and steps % 2 == 0 else 1
    for step in range(zones):
        items[lax.rem(my_zone - step + zones, zones)] = arrived[step][...]

    for target in range(zones):
        block = lax.rem(my_zone + target, zones)
        left = []
        for slot in range(slots):
            tile = mix[block, slot]
            left.append(jnp.where(degree[block] > slot, tile, jnp.zeros_like(tile)))
        left = jnp.concatenate(left, axis=1)
        for step in range(0, steps, group):
            right = []
            for slot in range(slots):
                source = neighbours[block, slot]
                right.append(
                    jnp.concatenate(
                        [
                            items[source, (step + index) * zone_rows : (step + index + 1) * zone_rows, :]
                            for index in range(group)
                        ],
                        axis=1,
                    )
                )
            result = jnp.dot(left, jnp.concatenate(right, axis=0), preferred_element_type=F32)
            for index in range(group):
                rows = slice((step + index) * zone_rows, (step + index + 1) * zone_rows)
                outs[target][rows, :] = result[:, index * part : (index + 1) * part].astype(BF16)


def ffn_kernel(zones, place, after_attn, gain_ffn, own_in, own_out, *refs):
    arrived, refs = refs[:zones], refs[zones:]
    pieces, (out, w_in, w_out, after_mix, ffn_in, parts, sems) = refs[:-7], refs[-7:]
    rows_all, width = after_attn.shape
    my_block, my_zone = place[0], place[1]
    in_shard, hidden = own_in.shape
    out_shard = own_out.shape[0]
    in_cols, out_rows = hidden // SPREAD, out_shard // SPREAD

    own_rows = pl.ds(pl.multiple_of(my_zone * in_shard, in_shard), in_shard)
    copies = [
        pltpu.make_async_copy(
            own_in.at[:, index * in_cols : (index + 1) * in_cols],
            w_in.at[index, own_rows, :],
            sems.at[index],
        )
        for index in range(SPREAD)
    ]
    own_rows = pl.ds(pl.multiple_of(my_zone * out_shard, out_shard), out_shard)
    copies.append(pltpu.make_async_copy(own_out, w_out.at[own_rows, :], sems.at[SPREAD]))
    for copy in copies:
        copy.start()
    for step in range(zones):
        parts[lax.rem(my_zone - step + zones, zones)] = arrived[step][...]
    for piece, bits_pair in zip(pieces[:4], IN_BITS):
        for index, bits in enumerate(bits_pair):
            slot = lax.rem(my_block, SPREAD) ^ bits
            for step in range(1, zones):
                source = lax.rem(my_zone - step + zones, zones)
                rows = pl.ds(pl.multiple_of(source * in_shard, in_shard), in_shard)
                w_in[slot, rows, :] = piece[index, step - 1]
    for piece, bits_pair in zip(pieces[4:], OUT_BITS):
        for index, bits in enumerate(bits_pair):
            slot = lax.rem(my_block, SPREAD) ^ bits
            for step in range(1, zones):
                source = lax.rem(my_zone - step + zones, zones)
                first = pl.multiple_of(source * out_shard + slot * out_rows, out_rows)
                for fold in range(width // in_cols):
                    cols = slice(fold * in_cols, (fold + 1) * in_cols)
                    rows = slice(fold * out_rows, (fold + 1) * out_rows)
                    w_out[pl.ds(first, out_rows), cols] = piece[index, step - 1, rows, :]
    for copy in copies:
        copy.wait()

    gain = gain_ffn[...]
    span = 128
    part = parts.shape[-1]
    for first in range(0, rows_all, span):
        rows = slice(first, first + span)
        for index in range(zones):
            cols = slice(index * part, (index + 1) * part)
            after_mix[rows, cols] = after_attn[rows, cols] + parts[index, rows, :].astype(F32)
        ffn_in[rows, :] = rms_scale(after_mix[rows, :], gain).astype(BF16)
    span = 256
    for first in range(0, rows_all, span):
        rows = slice(first, first + span)
        total = after_mix[rows, :]
        for index in range(SPREAD):
            hidden_part = jnp.dot(ffn_in[rows, :], w_in[index], preferred_element_type=F32)
            hidden_part = jax.nn.gelu(hidden_part, approximate=True).astype(BF16)
            total = total + jnp.dot(
                hidden_part,
                w_out[index * in_cols : (index + 1) * in_cols, :],
                preferred_element_type=F32,
            )
        out[rows, :] = total.astype(BF16)


def call(kernel, out_shape, scratch, smem, hbm, limit, args):
    spaces = {index: pltpu.SMEM for index in smem} | {index: pltpu.HBM for index in hbm}
    return pl.pallas_call(
        kernel,
        out_shape=out_shape,
        in_specs=[
            pl.BlockSpec(memory_space=spaces.get(index, pltpu.VMEM)) for index in range(len(args))
        ],
        out_specs=jax.tree.map(lambda _: pl.BlockSpec(memory_space=pltpu.VMEM), out_shape),
        scratch_shapes=scratch,
        cost_estimate=pl.CostEstimate(flops=0, bytes_accessed=0, transcendentals=0),
        compiler_params=pltpu.CompilerParams(vmem_limit_bytes=limit * MIB),
    )(*args)


def on_device(
    states,
    gain_attn,
    w_qkv,
    w_out_attn,
    pattern,
    gain_mix,
    neighbours,
    degree,
    mix,
    gain_ffn,
    w_in,
    w_out,
):
    steps, zone_rows, width = states.shape
    rows = steps * zone_rows
    reach = pattern.shape[1]
    zones = lax.axis_size("zone")
    my_block, my_zone = lax.axis_index("tm"), lax.axis_index("zone")
    place = jnp.stack([my_block, my_zone]).astype(jnp.int32)
    key_count = (reach + 1) * steps
    hidden = w_in.shape[1]
    in_cols = hidden // SPREAD
    out_rows = w_out.shape[0] // SPREAD
    part = width // zones
    rotations = range(1, zones)

    before = shifted(states, "tm", 2)
    first = lax.dynamic_slice_in_dim(
        jnp.concatenate([w_qkv, w_out_attn], axis=1), quarter_of(my_block) * width, width, axis=1
    )
    direct = [rotated(first, "zone", step) for step in rotations]
    in_shard = w_in.shape[0]
    sizes = (in_shard, out_rows * (width // in_cols))
    packed_shape = (sum(sizes), in_cols)
    direct, packed = call(
        pack_kernel,
        (
            jax.ShapeDtypeStruct((zones - 1,) + first.shape, BF16),
            jax.ShapeDtypeStruct(packed_shape, BF16),
        ),
        [pltpu.SemaphoreType.DMA((1 + width // in_cols,))],
        (0,),
        (1, 2),
        8,
        [place, w_in, w_out] + direct,
    )
    over = swapped(direct, "tm", 4)
    quarters = [direct, swapped(direct, "tm", 1), over, swapped(over, "tm", 1)]
    across = [rotated(packed, "zone", step) for step in rotations]

    last = swapped(jnp.where(my_block % 2 == 1, before, states), "tm", 1)
    normed = call(
        norm_kernel,
        jax.ShapeDtypeStruct((key_count * zone_rows, width), BF16),
        [],
        (),
        (),
        8,
        [before, last, states, gain_attn.reshape(1, -1)],
    )

    context, w_attn = call(
        functools.partial(attention_kernel, zones, reach, steps),
        (
            jax.ShapeDtypeStruct((rows, width), BF16),
            jax.ShapeDtypeStruct((width, width), BF16),
        ),
        [
            pltpu.VMEM((4, width, width), BF16),
            pltpu.VMEM((3 * width, width), BF16),
            pltpu.VMEM((3 * width, key_count * zone_rows), F32),
            pltpu.VMEM((width, rows), F32),
            pltpu.SemaphoreType.DMA((4,)),
        ],
        (0, 1),
        (3, 4),
        22,
        [place, pattern, normed, w_qkv, w_out_attn] + quarters,
    )

    chunk = jax.ShapeDtypeStruct((rows, part), BF16)
    after_attn, *chunks, part_in, part_out = call(
        project_kernel,
        (jax.ShapeDtypeStruct((rows, width), F32),)
        + (chunk,) * zones
        + tuple(jax.ShapeDtypeStruct((zones - 1, size, in_cols), BF16) for size in sizes),
        [pltpu.VMEM((zones, rows, part), BF16)],
        (0,),
        (),
        8,
        [place, states, context, w_attn, gain_mix.reshape(1, -1)] + across,
    )
    arrived = [chunks[0]] + [rotated(chunks[step], "zone", step) for step in rotations]

    over_in, over_out = swapped(part_in, "tm", 2), swapped(part_out, "tm", 4)
    pair_in, pair_out = call(
        pair_kernel,
        tuple(jax.ShapeDtypeStruct((2,) + value.shape, BF16) for value in (part_in, part_out)),
        [],
        (),
        (),
        8,
        [part_in, over_in, part_out, over_out],
    )
    pieces_in = [pair_in, swapped(pair_in, "tm", 4)]
    pieces_out = [pair_out, swapped(pair_out, "tm", 2)]
    pieces = pieces_in + [swapped(value, "tm", 1) for value in pieces_in]
    pieces += pieces_out + [swapped(value, "tm", 1) for value in pieces_out]

    spatial = call(
        functools.partial(mixing_kernel, steps, zones),
        (chunk,) * zones,
        [pltpu.VMEM((zones, rows, part), BF16)],
        (0, 1, 2),
        (),
        8,
        [place, neighbours, degree, mix] + arrived + [pair_in],
    )
    arrived = [spatial[0]] + [rotated(spatial[step], "zone", step) for step in rotations]
    evolved = call(
        functools.partial(ffn_kernel, zones),
        jax.ShapeDtypeStruct((rows, width), BF16),
        [
            pltpu.VMEM((SPREAD, width, in_cols), BF16),
            pltpu.VMEM((hidden, width), BF16),
            pltpu.VMEM((rows, width), F32),
            pltpu.VMEM((rows, width), BF16),
            pltpu.VMEM((zones, rows, part), BF16),
            pltpu.SemaphoreType.DMA((SPREAD + 1,)),
        ],
        (0,),
        (3, 4),
        16,
        [place, after_attn, gain_ffn.reshape(1, -1), w_in, w_out]
        + arrived
        + pieces,
    )
    return evolved.reshape(steps, zone_rows, width)


def solution(mesh):
    return jax.shard_map(
        on_device,
        mesh=mesh,
        in_specs=(
            P("tm", "zone", None),
            P(),
            P("zone", None),
            P("zone", None),
            P("tm", None),
            P(),
            P(),
            P(),
            P(),
            P(),
            P("zone", None),
            P("zone", None),
        ),
        out_specs=P("tm", "zone", None),
        check_vma=False,
    )
```

```python
import functools

import jax
import jax.numpy as jnp
from jax import lax
from jax.experimental import pallas as pl
from jax.experimental.pallas import tpu as pltpu
from jax.sharding import PartitionSpec as P

HEADS = 4
SPREAD = 8
IN_BITS = (0, 2, 4, 6)
OUT_BITS = (0, 4, 2, 6)
LANES = 128
F32 = jnp.float32
BF16 = jnp.bfloat16
MIB = 1024 * 1024


def shifted(value, axis, steps):
    count = lax.axis_size(axis)
    return lax.ppermute(value, axis, [(source, source + steps) for source in range(count - steps)])


def rotated(value, axis, steps):
    count = lax.axis_size(axis)
    return lax.ppermute(value, axis, [(source, (source + steps) % count) for source in range(count)])


def swapped(value, axis, bits):
    count = lax.axis_size(axis)
    return lax.ppermute(value, axis, [(source, source ^ bits) for source in range(count)])


def rms_scale(values, gain):
    mean_sq = jnp.mean(values * values, axis=-1, keepdims=True)
    return values * lax.rsqrt(mean_sq + 1e-06) * gain


def quarter_of(block):
    parity = lax.rem(lax.div(block, 2) + lax.div(block, 4), 2)
    return lax.rem(block, 2) + 2 * parity


def row_sum(value):
    return jnp.sum(value, axis=0, keepdims=True)


def norm_kernel(*refs):
    blocks, (gain_attn, normed) = refs[:-2], refs[-2:]
    steps, zone_rows, _ = blocks[0].shape
    gain = gain_attn[...]
    for index, block in enumerate(blocks):
        for step in range(steps):
            row = (index * steps + step) * zone_rows
            normed[row : row + zone_rows, :] = rms_scale(block[step].astype(F32), gain).astype(BF16)


def split_kernel(packed, before, *refs):
    arrived, (upper, lower, packed_out) = refs[:-3], refs[-3:]
    half = upper.shape[1]
    for index, piece in enumerate(arrived):
        upper[index] = piece[:half, :]
        lower[index] = piece[half:, :]
    packed_out[...] = packed[...]


def gather_kernel(place, states, before, upper, lower, over_x, over_y, *refs):
    across, (quarters, last, first_out, second_out) = refs[:-4], refs[-4:]
    half = upper.shape[1]
    for index, (top, bottom) in enumerate(((upper, lower), (over_x, over_y))):
        quarters[index, :, :half, :] = top[...]
        quarters[index, :, half:, :] = bottom[...]
    last[...] = jnp.where(lax.rem(place[0], 2) == 1, before[...], states[...])
    split = first_out.shape[1]
    for index, piece in enumerate(across):
        first_out[index] = piece[:split, :]
        second_out[index] = piece[split:, :]


def attention_kernel(zones, reach, steps, place, pattern, normed, own_qkv, own_attn, *refs):
    quarters, (context_out, attn_out, weights, w_turned, projected, context, sems) = refs[:-7], refs[-7:]
    key_count = (reach + 1) * steps
    zone_rows = normed.shape[0] // key_count
    width = normed.shape[1]
    head_size = width // HEADS
    my_block, my_zone = place[0], place[1]
    shard = own_qkv.shape[0]

    own_rows = pl.ds(pl.multiple_of(my_zone * shard, shard), shard)
    copies = [
        pltpu.make_async_copy(
            own_qkv.at[:, index * width : (index + 1) * width],
            weights.at[index, own_rows, :],
            sems.at[index],
        )
        for index in range(3)
    ]
    copies.append(pltpu.make_async_copy(own_attn, weights.at[3, own_rows, :], sems.at[3]))
    for copy in copies:
        copy.start()
    my_quarter = quarter_of(my_block)
    for step in range(1, zones):
        source = lax.rem(my_zone - step + zones, zones)
        rows = pl.ds(pl.multiple_of(source * shard, shard), shard)
        for core, pair in enumerate(quarters):
            for index in range(2):
                weights[my_quarter ^ (core + 2 * index), rows, :] = pair[index, step - 1]
    for copy in copies:
        copy.wait()
    attn_out[...] = weights[3]
    for index in range(3):
        for block in range(width // LANES):
            first = block * LANES
            rows = slice(index * width + first, index * width + first + LANES)
            w_turned[rows, :] = weights[index, :, first : first + LANES].T

    def project(first, last, weight_rows):
        return lax.dot_general(
            w_turned[weight_rows, :],
            normed[first:last, :],
            (((1,), (1,)), ((), ())),
            preferred_element_type=F32,
        ).astype(BF16).astype(F32)

    span = 2 * zone_rows
    for first in range(0, key_count * zone_rows, span):
        own = first >= reach * steps * zone_rows
        rows = slice(0 if own else width, 3 * width)
        projected[rows, first : first + span] = project(first, first + span, rows)

    allowed_back = [
        (pattern[0, back - 1] == 1) & (my_block >= back) for back in range(reach, 0, -1)
    ]
    chunks = head_size // 8

    def usable(query):
        return range(reach * steps + query + 1)

    def head_body(head, carry):
        base = head * head_size

        def tile(kind, chunk, key):
            row = pl.multiple_of(kind * width + base + chunk * 8, 8)
            return projected[pl.ds(row, 8), key * zone_rows : (key + 1) * zone_rows]

        for pair in range(0, steps, 2):
            queries = range(pair, min(pair + 2, steps))
            sums = {}
            for chunk in range(chunks):
                q_tiles = {q: tile(0, chunk, reach * steps + q) for q in queries}
                for key in usable(queries[-1]):
                    k_tile = tile(1, chunk, key)
                    for q in queries:
                        if key in usable(q):
                            term = q_tiles[q] * k_tile
                            sums[q, key] = term if chunk == 0 else sums[q, key] + term
            weights, scales = {}, {}
            for q in queries:
                scores = jnp.concatenate([row_sum(sums[q, key]) for key in usable(q)], axis=0)
                scores = scores * head_size ** (-0.5)
                row_id = lax.broadcasted_iota(jnp.int32, scores.shape, 0)
                allowed = row_id >= reach * steps
                for index, live in enumerate(allowed_back):
                    inside = (row_id >= index * steps) & (row_id < (index + 1) * steps)
                    allowed = allowed | (inside & live)
                masked = jnp.where(allowed, scores, -1e30)
                top = jnp.max(masked, axis=0, keepdims=True)
                expw = jnp.where(allowed, jnp.exp(masked - top), 0.0)
                scales[q] = jnp.broadcast_to(1.0 / row_sum(expw), (8, zone_rows))
                probs = expw.astype(BF16).astype(F32)
                for key in usable(q):
                    weights[q, key] = jnp.broadcast_to(probs[key : key + 1, :], (8, zone_rows))
            for chunk in range(chunks):
                sums = {}
                for key in usable(queries[-1]):
                    v_tile = tile(2, chunk, key)
                    for q in queries:
                        if key in usable(q):
                            term = weights[q, key] * v_tile
                            sums[q] = term if key == 0 else sums[q] + term
                for q in queries:
                    row = pl.multiple_of(base + chunk * 8, 8)
                    context[pl.ds(row, 8), q * zone_rows : (q + 1) * zone_rows] = sums[q] * scales[q]
        return carry

    lax.fori_loop(0, HEADS, head_body, 0)

    for step in range(steps):
        rows = slice(step * zone_rows, (step + 1) * zone_rows)
        context_out[rows, :] = context[:, rows].T.astype(BF16)


def project_kernel(place, states, context, w_attn, gain_mix, *refs):
    halves, (after_out, *outs, pair_in, pair_out, parts) = refs[:4], refs[4:]
    steps, zone_rows, _ = states.shape
    zones, _, part = parts.shape
    for index, value in enumerate(halves):
        (pair_in, pair_out)[index // 2][index % 2] = value[...]
    my_zone = place[1]
    gain = gain_mix[...]
    for step in range(steps):
        rows = slice(step * zone_rows, (step + 1) * zone_rows)
        after = states[step].astype(F32) + jnp.dot(
            context[rows, :], w_attn[...], preferred_element_type=F32
        )
        after_out[rows, :] = after
        mixin = rms_scale(after, gain).astype(BF16)
        for index in range(zones):
            parts[index, rows, :] = mixin[:, index * part : (index + 1) * part]
    for step in range(zones):
        outs[step][...] = parts[lax.rem(my_zone + step, zones)]


def mixing_kernel(steps, zones, place, neighbours, degree, mix, *refs):
    arrived, pairs, (*outs, gathered, items) = refs[:zones], refs[zones : zones + 4], refs[zones + 4 :]
    for index, pair in enumerate(pairs):
        gathered[2 * index : 2 * index + 2] = pair[...]
    _, slots, zone_rows, _ = mix.shape
    part = items.shape[-1]
    my_zone = place[1]
    group = 2 if part % LANES == 0 and steps % 2 == 0 else 1
    for step in range(zones):
        items[lax.rem(my_zone - step + zones, zones)] = arrived[step][...]

    for target in range(zones):
        block = lax.rem(my_zone + target, zones)
        left = []
        for slot in range(slots):
            tile = mix[block, slot]
            left.append(jnp.where(degree[block] > slot, tile, jnp.zeros_like(tile)))
        left = jnp.concatenate(left, axis=1)
        for step in range(0, steps, group):
            right = []
            for slot in range(slots):
                source = neighbours[block, slot]
                right.append(
                    jnp.concatenate(
                        [
                            items[source, (step + index) * zone_rows : (step + index + 1) * zone_rows, :]
                            for index in range(group)
                        ],
                        axis=1,
                    )
                )
            result = jnp.dot(left, jnp.concatenate(right, axis=0), preferred_element_type=F32)
            for index in range(group):
                rows = slice((step + index) * zone_rows, (step + index + 1) * zone_rows)
                outs[target][rows, :] = result[:, index * part : (index + 1) * part].astype(BF16)


def order_kernel(zones, place, own_in, own_out, *refs):
    gathered, (w_in, w_out, sems) = refs[:2], refs[2:]
    width = own_out.shape[1]
    my_block, my_zone = place[0], place[1]
    in_shard, hidden = own_in.shape
    out_shard = own_out.shape[0]
    in_cols, out_rows = hidden // SPREAD, out_shard // SPREAD

    own_rows = pl.ds(pl.multiple_of(my_zone * in_shard, in_shard), in_shard)
    copies = [
        pltpu.make_async_copy(
            own_in.at[:, index * in_cols : (index + 1) * in_cols],
            w_in.at[index, own_rows, :],
            sems.at[index],
        )
        for index in range(SPREAD)
    ]
    own_rows = pl.ds(pl.multiple_of(my_zone * out_shard, out_shard), out_shard)
    copies.append(pltpu.make_async_copy(own_out, w_out.at[own_rows, :], sems.at[SPREAD]))
    for copy in copies:
        copy.start()
    for core, pieces in enumerate(gathered):
        for index in range(4):
            slot_in = lax.rem(my_block, SPREAD) ^ (IN_BITS[index] + core)
            slot_out = lax.rem(my_block, SPREAD) ^ (OUT_BITS[index] + core)
            for step in range(1, zones):
                source = lax.rem(my_zone - step + zones, zones)
                rows = pl.ds(pl.multiple_of(source * in_shard, in_shard), in_shard)
                w_in[slot_in, rows, :] = pieces[index, step - 1]
                first = pl.multiple_of(source * out_shard + slot_out * out_rows, out_rows)
                for fold in range(width // in_cols):
                    cols = slice(fold * in_cols, (fold + 1) * in_cols)
                    rows = slice(fold * out_rows, (fold + 1) * out_rows)
                    w_out[pl.ds(first, out_rows), cols] = pieces[4 + index, step - 1, rows, :]
    for copy in copies:
        copy.wait()


def ffn_kernel(zones, place, after_attn, gain_ffn, w_in, w_out, *refs):
    arrived, (out, after_mix, ffn_in, parts) = refs[:zones], refs[zones:]
    rows_all, width = after_attn.shape
    my_zone = place[1]
    in_cols = w_in.shape[2]
    for step in range(zones):
        parts[lax.rem(my_zone - step + zones, zones)] = arrived[step][...]

    gain = gain_ffn[...]
    span = 128
    part = parts.shape[-1]
    for first in range(0, rows_all, span):
        rows = slice(first, first + span)
        for index in range(zones):
            cols = slice(index * part, (index + 1) * part)
            after_mix[rows, cols] = after_attn[rows, cols] + parts[index, rows, :].astype(F32)
        ffn_in[rows, :] = rms_scale(after_mix[rows, :], gain).astype(BF16)
    span = 256
    for first in range(0, rows_all, span):
        rows = slice(first, first + span)
        total = after_mix[rows, :]
        for index in range(SPREAD):
            hidden_part = jnp.dot(ffn_in[rows, :], w_in[index], preferred_element_type=F32)
            hidden_part = jax.nn.gelu(hidden_part, approximate=True).astype(BF16)
            total = total + jnp.dot(
                hidden_part,
                w_out[index * in_cols : (index + 1) * in_cols, :],
                preferred_element_type=F32,
            )
        out[rows, :] = total.astype(BF16)


def call(kernel, out_shape, scratch, smem, hbm, limit, args):
    spaces = {index: pltpu.SMEM for index in smem} | {index: pltpu.HBM for index in hbm}
    return pl.pallas_call(
        kernel,
        out_shape=out_shape,
        in_specs=[
            pl.BlockSpec(memory_space=spaces.get(index, pltpu.VMEM)) for index in range(len(args))
        ],
        out_specs=jax.tree.map(lambda _: pl.BlockSpec(memory_space=pltpu.VMEM), out_shape),
        scratch_shapes=scratch,
        cost_estimate=pl.CostEstimate(flops=0, bytes_accessed=0, transcendentals=0),
        compiler_params=pltpu.CompilerParams(vmem_limit_bytes=limit * MIB),
    )(*args)


def on_device(
    states,
    gain_attn,
    w_qkv,
    w_out_attn,
    pattern,
    gain_mix,
    neighbours,
    degree,
    mix,
    gain_ffn,
    w_in,
    w_out,
):
    steps, zone_rows, width = states.shape
    rows = steps * zone_rows
    reach = pattern.shape[1]
    zones = lax.axis_size("zone")
    my_block, my_zone = lax.axis_index("tm"), lax.axis_index("zone")
    place = jnp.stack([my_block, my_zone]).astype(jnp.int32)
    key_count = (reach + 1) * steps
    hidden = w_in.shape[1]
    in_cols = hidden // SPREAD
    out_rows = w_out.shape[0] // SPREAD
    part = width // zones
    rotations = range(1, zones)

    before = shifted(states, "tm", 2)
    first = lax.dynamic_slice_in_dim(
        jnp.concatenate([w_qkv, w_out_attn], axis=1), quarter_of(my_block) * width, width, axis=1
    )
    direct = [rotated(first, "zone", step) for step in rotations]
    slot = my_block % SPREAD
    slice_in = lax.dynamic_slice_in_dim(w_in, slot * in_cols, in_cols, axis=1)
    slice_out = lax.dynamic_slice_in_dim(w_out, slot * out_rows, out_rows, axis=0)
    in_shard = w_in.shape[0]
    sizes = (in_shard, out_rows * (width // in_cols))
    packed = jnp.concatenate(
        [slice_in] + [slice_out[:, at : at + in_cols] for at in range(0, width, in_cols)], axis=0
    )
    half = first.shape[0] // 2
    half_shape = jax.ShapeDtypeStruct((zones - 1, half, width), BF16)
    upper, lower, packed = call(
        split_kernel,
        (half_shape, half_shape, jax.ShapeDtypeStruct(packed.shape, BF16)),
        [],
        (),
        (),
        4,
        [packed, before] + direct,
    )
    over_x, over_y = swapped(upper, "tm", 2), swapped(lower, "tm", 4)
    across = [rotated(packed, "zone", step) for step in rotations]
    quarters, last, part_in, part_out = call(
        gather_kernel,
        (
            jax.ShapeDtypeStruct((2, zones - 1) + first.shape, BF16),
            jax.ShapeDtypeStruct(states.shape, BF16),
        )
        + tuple(jax.ShapeDtypeStruct((zones - 1, size, in_cols), BF16) for size in sizes),
        [],
        (0,),
        (),
        4,
        [place, states, before, upper, lower, over_x, over_y] + across,
    )
    quarters = [quarters, swapped(quarters, "tm", 1)]
    last = swapped(last, "tm", 1)
    over_in, over_out = swapped(part_in, "tm", 2), swapped(part_out, "tm", 4)
    normed = call(
        norm_kernel,
        jax.ShapeDtypeStruct((key_count * zone_rows, width), BF16),
        [],
        (),
        (),
        4,
        [before, last, states, gain_attn.reshape(1, -1)],
    )

    context, w_attn = call(
        functools.partial(attention_kernel, zones, reach, steps),
        (
            jax.ShapeDtypeStruct((rows, width), BF16),
            jax.ShapeDtypeStruct((width, width), BF16),
        ),
        [
            pltpu.VMEM((4, width, width), BF16),
            pltpu.VMEM((3 * width, width), BF16),
            pltpu.VMEM((3 * width, key_count * zone_rows), F32),
            pltpu.VMEM((width, rows), F32),
            pltpu.SemaphoreType.DMA((4,)),
        ],
        (0, 1),
        (3, 4),
        22,
        [place, pattern, normed, w_qkv, w_out_attn] + quarters,
    )

    chunk = jax.ShapeDtypeStruct((rows, part), BF16)
    after_attn, *chunks, pair_in, pair_out = call(
        project_kernel,
        (jax.ShapeDtypeStruct((rows, width), F32),)
        + (chunk,) * zones
        + tuple(jax.ShapeDtypeStruct((2, zones - 1, size, in_cols), BF16) for size in sizes),
        [pltpu.VMEM((zones, rows, part), BF16)],
        (0,),
        (),
        8,
        [place, states, context, w_attn, gain_mix.reshape(1, -1)]
        + [part_in, over_in, part_out, over_out],
    )
    arrived = [chunks[0]] + [rotated(chunks[step], "zone", step) for step in rotations]

    pairs = [pair_in, swapped(pair_in, "tm", 4), pair_out, swapped(pair_out, "tm", 2)]

    *spatial, gathered = call(
        functools.partial(mixing_kernel, steps, zones),
        (chunk,) * zones
        + (jax.ShapeDtypeStruct((SPREAD, zones - 1, in_shard, in_cols), BF16),),
        [pltpu.VMEM((zones, rows, part), BF16)],
        (0, 1, 2),
        (),
        8,
        [place, neighbours, degree, mix] + arrived + pairs,
    )
    full_in, full_out = call(
        functools.partial(order_kernel, zones),
        (
            jax.ShapeDtypeStruct((SPREAD, width, in_cols), BF16),
            jax.ShapeDtypeStruct((hidden, width), BF16),
        ),
        [pltpu.SemaphoreType.DMA((SPREAD + 1,))],
        (0,),
        (1, 2),
        8,
        [place, w_in, w_out, gathered, swapped(gathered, "tm", 1)],
    )
    arrived = [spatial[0]] + [rotated(spatial[step], "zone", step) for step in rotations]
    evolved = call(
        functools.partial(ffn_kernel, zones),
        jax.ShapeDtypeStruct((rows, width), BF16),
        [
            pltpu.VMEM((rows, width), F32),
            pltpu.VMEM((rows, width), BF16),
            pltpu.VMEM((zones, rows, part), BF16),
        ],
        (0,),
        (),
        10,
        [place, after_attn, gain_ffn.reshape(1, -1), full_in, full_out] + arrived,
    )
    return evolved.reshape(steps, zone_rows, width)


def solution(mesh):
    return jax.shard_map(
        on_device,
        mesh=mesh,
        in_specs=(
            P("tm", "zone", None),
            P(),
            P("zone", None),
            P("zone", None),
            P("tm", None),
            P(),
            P(),
            P(),
            P(),
            P(),
            P("zone", None),
            P("zone", None),
        ),
        out_specs=P("tm", "zone", None),
        check_vma=False,
    )
```

```python
import functools

import jax
import jax.numpy as jnp
from jax import lax
from jax.experimental import pallas as pl
from jax.experimental.pallas import tpu as pltpu
from jax.sharding import PartitionSpec as P

HEADS = 4
SPREAD = 8
IN_BITS = (0, 2, 4, 6)
OUT_BITS = (0, 4, 2, 6)
LANES = 128
F32 = jnp.float32
BF16 = jnp.bfloat16
MIB = 1024 * 1024


def shifted(value, axis, steps):
    count = lax.axis_size(axis)
    return lax.ppermute(value, axis, [(source, source + steps) for source in range(count - steps)])


def swapped(value, axis, bits):
    count = lax.axis_size(axis)
    return lax.ppermute(value, axis, [(source, source ^ bits) for source in range(count)])


def steps_over(count):
    half = count // 2
    return tuple(range(half, count)) + tuple(range(1, half))


def rms_scale(values, gain):
    mean_sq = jnp.mean(values * values, axis=-1, keepdims=True)
    return values * lax.rsqrt(mean_sq + 1e-06) * gain


def quarter_of(block):
    return lax.rem(block, 2) + 2 * lax.rem(lax.div(block, 4), 2)


def row_sum(value):
    return jnp.sum(value, axis=0, keepdims=True)


def norm_kernel(*refs):
    blocks, (gain_attn, normed) = refs[:-2], refs[-2:]
    steps, zone_rows, _ = blocks[0].shape
    gain = gain_attn[...]
    for index, block in enumerate(blocks):
        for step in range(steps):
            row = (index * steps + step) * zone_rows
            normed[row : row + zone_rows, :] = rms_scale(block[step].astype(F32), gain).astype(BF16)


def split_kernel(place, packed, states, before, *refs):
    arrived, (direct, packed_out, last) = refs[:-3], refs[-3:]
    for index, piece in enumerate(arrived):
        direct[index] = piece[...]
    packed_out[...] = packed[...]
    last[...] = jnp.where(lax.rem(place[0], 2) == 1, before[...], states[...])


def gather_kernel(normed, direct, over, *refs):
    across, (quarters, first_out, second_out) = refs[:-3], refs[-3:]
    quarters[0] = direct[...]
    quarters[1] = over[...]
    split = first_out.shape[1]
    for index, piece in enumerate(across):
        first_out[index] = piece[:split, :]
        second_out[index] = piece[split:, :]


def attention_kernel(zones, reach, steps, place, pattern, normed, own_qkv, own_attn, *refs):
    quarters, (context_out, attn_out, weights, w_turned, projected, context, sems) = refs[:-7], refs[-7:]
    key_count = (reach + 1) * steps
    zone_rows = normed.shape[0] // key_count
    width = normed.shape[1]
    head_size = width // HEADS
    my_block, my_zone = place[0], place[1]
    shard = own_qkv.shape[0]

    own_rows = pl.ds(pl.multiple_of(my_zone * shard, shard), shard)
    copies = [
        pltpu.make_async_copy(
            own_qkv.at[:, index * width : (index + 1) * width],
            weights.at[index, own_rows, :],
            sems.at[index],
        )
        for index in range(3)
    ]
    copies.append(pltpu.make_async_copy(own_attn, weights.at[3, own_rows, :], sems.at[3]))
    for copy in copies:
        copy.start()
    my_quarter = quarter_of(my_block)
    for place_in, step in enumerate(steps_over(zones)):
        rows = pl.ds(pl.multiple_of((my_zone ^ step) * shard, shard), shard)
        for core, pair in enumerate(quarters):
            for index in range(2):
                weights[my_quarter ^ (core + 2 * index), rows, :] = pair[index, place_in]
    for copy in copies:
        copy.wait()
    attn_out[...] = weights[3]
    for index in range(3):
        for block in range(width // LANES):
            first = block * LANES
            rows = slice(index * width + first, index * width + first + LANES)
            w_turned[rows, :] = weights[index, :, first : first + LANES].T

    def project(first, last, weight_rows):
        return lax.dot_general(
            w_turned[weight_rows, :],
            normed[first:last, :],
            (((1,), (1,)), ((), ())),
            preferred_element_type=F32,
        ).astype(BF16).astype(F32)

    span = 2 * zone_rows
    for first in range(0, key_count * zone_rows, span):
        own = first >= reach * steps * zone_rows
        rows = slice(0 if own else width, 3 * width)
        projected[rows, first : first + span] = project(first, first + span, rows)

    allowed_back = [
        (pattern[0, back - 1] == 1) & (my_block >= back) for back in range(reach, 0, -1)
    ]
    chunks = head_size // 8

    def usable(query):
        return range(reach * steps + query + 1)

    def head_body(head, carry):
        base = head * head_size

        def tile(kind, chunk, key):
            row = pl.multiple_of(kind * width + base + chunk * 8, 8)
            return projected[pl.ds(row, 8), key * zone_rows : (key + 1) * zone_rows]

        for pair in range(0, steps, 2):
            queries = range(pair, min(pair + 2, steps))
            sums = {}
            for chunk in range(chunks):
                q_tiles = {q: tile(0, chunk, reach * steps + q) for q in queries}
                for key in usable(queries[-1]):
                    k_tile = tile(1, chunk, key)
                    for q in queries:
                        if key in usable(q):
                            term = q_tiles[q] * k_tile
                            sums[q, key] = term if chunk == 0 else sums[q, key] + term
            weights, scales = {}, {}
            for q in queries:
                scores = jnp.concatenate([row_sum(sums[q, key]) for key in usable(q)], axis=0)
                scores = scores * head_size ** (-0.5)
                row_id = lax.broadcasted_iota(jnp.int32, scores.shape, 0)
                allowed = row_id >= reach * steps
                for index, live in enumerate(allowed_back):
                    inside = (row_id >= index * steps) & (row_id < (index + 1) * steps)
                    allowed = allowed | (inside & live)
                masked = jnp.where(allowed, scores, -1e30)
                top = jnp.max(masked, axis=0, keepdims=True)
                expw = jnp.where(allowed, jnp.exp(masked - top), 0.0)
                scales[q] = jnp.broadcast_to(1.0 / row_sum(expw), (8, zone_rows))
                probs = expw.astype(BF16).astype(F32)
                for key in usable(q):
                    weights[q, key] = jnp.broadcast_to(probs[key : key + 1, :], (8, zone_rows))
            for chunk in range(chunks):
                sums = {}
                for key in usable(queries[-1]):
                    v_tile = tile(2, chunk, key)
                    for q in queries:
                        if key in usable(q):
                            term = weights[q, key] * v_tile
                            sums[q] = term if key == 0 else sums[q] + term
                for q in queries:
                    row = pl.multiple_of(base + chunk * 8, 8)
                    context[pl.ds(row, 8), q * zone_rows : (q + 1) * zone_rows] = sums[q] * scales[q]
        return carry

    lax.fori_loop(0, HEADS, head_body, 0)

    for step in range(steps):
        rows = slice(step * zone_rows, (step + 1) * zone_rows)
        context_out[rows, :] = context[:, rows].T.astype(BF16)


def project_kernel(place, states, context, w_attn, gain_mix, *refs):
    halves, (after_out, *outs, pair_in, pair_out, parts) = refs[:4], refs[4:]
    steps, zone_rows, _ = states.shape
    zones, _, part = parts.shape
    for index, value in enumerate(halves):
        (pair_in, pair_out)[index // 2][index % 2] = value[...]
    my_zone = place[1]
    gain = gain_mix[...]
    for step in range(steps):
        rows = slice(step * zone_rows, (step + 1) * zone_rows)
        after = states[step].astype(F32) + jnp.dot(
            context[rows, :], w_attn[...], preferred_element_type=F32
        )
        after_out[rows, :] = after
        mixin = rms_scale(after, gain).astype(BF16)
        for index in range(zones):
            parts[index, rows, :] = mixin[:, index * part : (index + 1) * part]
    for index, step in enumerate((0,) + steps_over(zones)):
        outs[index][...] = parts[my_zone ^ step]


def mixing_kernel(steps, zones, place, neighbours, degree, mix, *refs):
    arrived, pairs, (*outs, gathered, items) = refs[:zones], refs[zones : zones + 4], refs[zones + 4 :]
    for index, pair in enumerate(pairs):
        gathered[2 * index : 2 * index + 2] = pair[...]
    _, slots, zone_rows, _ = mix.shape
    part = items.shape[-1]
    my_zone = place[1]
    group = 2 if part % LANES == 0 and steps % 2 == 0 else 1
    for index, step in enumerate((0,) + steps_over(zones)):
        items[my_zone ^ step] = arrived[index][...]

    for target, target_step in enumerate((0,) + steps_over(zones)):
        block = my_zone ^ target_step
        left = []
        for slot in range(slots):
            tile = mix[block, slot]
            left.append(jnp.where(degree[block] > slot, tile, jnp.zeros_like(tile)))
        left = jnp.concatenate(left, axis=1)
        for step in range(0, steps, group):
            right = []
            for slot in range(slots):
                source = neighbours[block, slot]
                right.append(
                    jnp.concatenate(
                        [
                            items[source, (step + index) * zone_rows : (step + index + 1) * zone_rows, :]
                            for index in range(group)
                        ],
                        axis=1,
                    )
                )
            result = jnp.dot(left, jnp.concatenate(right, axis=0), preferred_element_type=F32)
            for index in range(group):
                rows = slice((step + index) * zone_rows, (step + index + 1) * zone_rows)
                outs[target][rows, :] = result[:, index * part : (index + 1) * part].astype(BF16)


def order_kernel(zones, place, own_in, own_out, *refs):
    gathered, (w_in, w_out, sems) = refs[:2], refs[2:]
    width = own_out.shape[1]
    my_block, my_zone = place[0], place[1]
    in_shard, hidden = own_in.shape
    out_shard = own_out.shape[0]
    in_cols, out_rows = hidden // SPREAD, out_shard // SPREAD

    own_rows = pl.ds(pl.multiple_of(my_zone * in_shard, in_shard), in_shard)
    copies = [
        pltpu.make_async_copy(
            own_in.at[:, index * in_cols : (index + 1) * in_cols],
            w_in.at[index, own_rows, :],
            sems.at[index],
        )
        for index in range(SPREAD)
    ]
    own_rows = pl.ds(pl.multiple_of(my_zone * out_shard, out_shard), out_shard)
    copies.append(pltpu.make_async_copy(own_out, w_out.at[own_rows, :], sems.at[SPREAD]))
    for copy in copies:
        copy.start()
    for core, pieces in enumerate(gathered):
        for index in range(4):
            slot_in = lax.rem(my_block, SPREAD) ^ (IN_BITS[index] + core)
            slot_out = lax.rem(my_block, SPREAD) ^ (OUT_BITS[index] + core)
            for place_in, step in enumerate(steps_over(zones)):
                source = my_zone ^ step
                rows = pl.ds(pl.multiple_of(source * in_shard, in_shard), in_shard)
                w_in[slot_in, rows, :] = pieces[index, place_in]
                first = pl.multiple_of(source * out_shard + slot_out * out_rows, out_rows)
                for fold in range(width // in_cols):
                    cols = slice(fold * in_cols, (fold + 1) * in_cols)
                    rows = slice(fold * out_rows, (fold + 1) * out_rows)
                    w_out[pl.ds(first, out_rows), cols] = pieces[4 + index, place_in, rows, :]
    for copy in copies:
        copy.wait()


def ffn_kernel(zones, place, after_attn, gain_ffn, w_in, w_out, *refs):
    arrived, (out, after_mix, ffn_in, parts, hidden) = refs[:zones], refs[zones:]
    rows_all, width = after_attn.shape
    my_zone = place[1]
    in_cols = w_in.shape[2]
    for index, step in enumerate((0,) + steps_over(zones)):
        parts[my_zone ^ step] = arrived[index][...]

    gain = gain_ffn[...]
    span = 128
    part = parts.shape[-1]
    for first in range(0, rows_all, span):
        rows = slice(first, first + span)
        for index in range(zones):
            cols = slice(index * part, (index + 1) * part)
            after_mix[rows, cols] = after_attn[rows, cols] + parts[index, rows, :].astype(F32)
        ffn_in[rows, :] = rms_scale(after_mix[rows, :], gain).astype(BF16)
    span = 256
    for first in range(0, rows_all, span):
        rows = slice(first, first + span)
        for index in range(SPREAD):
            grown = jnp.dot(ffn_in[rows, :], w_in[index], preferred_element_type=F32)
            cols = slice(index * in_cols, (index + 1) * in_cols)
            hidden[rows, cols] = jax.nn.gelu(grown, approximate=True).astype(BF16)
        shrunk = jnp.dot(hidden[rows, :], w_out[...], preferred_element_type=F32)
        out[rows, :] = (after_mix[rows, :] + shrunk).astype(BF16)


def call(kernel, out_shape, scratch, smem, hbm, limit, args):
    spaces = {index: pltpu.SMEM for index in smem} | {index: pltpu.HBM for index in hbm}
    return pl.pallas_call(
        kernel,
        out_shape=out_shape,
        in_specs=[
            pl.BlockSpec(memory_space=spaces.get(index, pltpu.VMEM)) for index in range(len(args))
        ],
        out_specs=jax.tree.map(lambda _: pl.BlockSpec(memory_space=pltpu.VMEM), out_shape),
        scratch_shapes=scratch,
        cost_estimate=pl.CostEstimate(flops=0, bytes_accessed=0, transcendentals=0),
        compiler_params=pltpu.CompilerParams(vmem_limit_bytes=limit * MIB),
    )(*args)


def on_device(
    states,
    gain_attn,
    w_qkv,
    w_out_attn,
    pattern,
    gain_mix,
    neighbours,
    degree,
    mix,
    gain_ffn,
    w_in,
    w_out,
):
    steps, zone_rows, width = states.shape
    rows = steps * zone_rows
    reach = pattern.shape[1]
    zones = lax.axis_size("zone")
    my_block, my_zone = lax.axis_index("tm"), lax.axis_index("zone")
    place = jnp.stack([my_block, my_zone]).astype(jnp.int32)
    key_count = (reach + 1) * steps
    hidden = w_in.shape[1]
    in_cols = hidden // SPREAD
    out_rows = w_out.shape[0] // SPREAD
    part = width // zones
    exchanges = steps_over(zones)

    before = shifted(states, "tm", 2)
    first = lax.dynamic_slice_in_dim(
        jnp.concatenate([w_qkv, w_out_attn], axis=1), quarter_of(my_block) * width, width, axis=1
    )
    direct = [swapped(first, "zone", step) for step in exchanges]
    slot = my_block % SPREAD
    slice_in = lax.dynamic_slice_in_dim(w_in, slot * in_cols, in_cols, axis=1)
    slice_out = lax.dynamic_slice_in_dim(w_out, slot * out_rows, out_rows, axis=0)
    in_shard = w_in.shape[0]
    sizes = (in_shard, out_rows * (width // in_cols))
    packed = jnp.concatenate(
        [slice_in] + [slice_out[:, at : at + in_cols] for at in range(0, width, in_cols)], axis=0
    )
    direct, packed, last = call(
        split_kernel,
        (
            jax.ShapeDtypeStruct((zones - 1,) + first.shape, BF16),
            jax.ShapeDtypeStruct(packed.shape, BF16),
            jax.ShapeDtypeStruct(states.shape, BF16),
        ),
        [],
        (0,),
        (),
        4,
        [place, packed, states, before] + direct,
    )
    over = swapped(direct, "tm", 4)
    last = swapped(last, "tm", 1)
    across = [swapped(packed, "zone", step) for step in exchanges]
    normed = call(
        norm_kernel,
        jax.ShapeDtypeStruct((key_count * zone_rows, width), BF16),
        [],
        (),
        (),
        4,
        [before, last, states, gain_attn.reshape(1, -1)],
    )

    quarters, part_in, part_out = call(
        gather_kernel,
        (jax.ShapeDtypeStruct((2,) + direct.shape, BF16),)
        + tuple(jax.ShapeDtypeStruct((zones - 1, size, in_cols), BF16) for size in sizes),
        [],
        (),
        (),
        4,
        [normed, direct, over] + across,
    )
    quarters = [quarters, swapped(quarters, "tm", 1)]
    over_in, over_out = swapped(part_in, "tm", 2), swapped(part_out, "tm", 4)
    context, w_attn = call(
        functools.partial(attention_kernel, zones, reach, steps),
        (
            jax.ShapeDtypeStruct((rows, width), BF16),
            jax.ShapeDtypeStruct((width, width), BF16),
        ),
        [
            pltpu.VMEM((4, width, width), BF16),
            pltpu.VMEM((3 * width, width), BF16),
            pltpu.VMEM((3 * width, key_count * zone_rows), F32),
            pltpu.VMEM((width, rows), F32),
            pltpu.SemaphoreType.DMA((4,)),
        ],
        (0, 1),
        (3, 4),
        22,
        [place, pattern, normed, w_qkv, w_out_attn] + quarters,
    )

    chunk = jax.ShapeDtypeStruct((rows, part), BF16)
    after_attn, *chunks, pair_in, pair_out = call(
        project_kernel,
        (jax.ShapeDtypeStruct((rows, width), F32),)
        + (chunk,) * zones
        + tuple(jax.ShapeDtypeStruct((2, zones - 1, size, in_cols), BF16) for size in sizes),
        [pltpu.VMEM((zones, rows, part), BF16)],
        (0,),
        (),
        8,
        [place, states, context, w_attn, gain_mix.reshape(1, -1)]
        + [part_in, over_in, part_out, over_out],
    )
    arrived = [chunks[0]] + [
        swapped(value, "zone", step) for value, step in zip(chunks[1:], exchanges)
    ]

    pairs = [pair_in, swapped(pair_in, "tm", 4), pair_out, swapped(pair_out, "tm", 2)]

    *spatial, gathered = call(
        functools.partial(mixing_kernel, steps, zones),
        (chunk,) * zones
        + (jax.ShapeDtypeStruct((SPREAD, zones - 1, in_shard, in_cols), BF16),),
        [pltpu.VMEM((zones, rows, part), BF16)],
        (0, 1, 2),
        (),
        8,
        [place, neighbours, degree, mix] + arrived + pairs,
    )
    full_in, full_out = call(
        functools.partial(order_kernel, zones),
        (
            jax.ShapeDtypeStruct((SPREAD, width, in_cols), BF16),
            jax.ShapeDtypeStruct((hidden, width), BF16),
        ),
        [pltpu.SemaphoreType.DMA((SPREAD + 1,))],
        (0,),
        (1, 2),
        8,
        [place, w_in, w_out, gathered, swapped(gathered, "tm", 1)],
    )
    arrived = [spatial[0]] + [
        swapped(value, "zone", step) for value, step in zip(spatial[1:], exchanges)
    ]
    evolved = call(
        functools.partial(ffn_kernel, zones),
        jax.ShapeDtypeStruct((rows, width), BF16),
        [
            pltpu.VMEM((rows, width), F32),
            pltpu.VMEM((rows, width), BF16),
            pltpu.VMEM((zones, rows, part), BF16),
            pltpu.VMEM((rows, hidden), BF16),
        ],
        (0,),
        (),
        10,
        [place, after_attn, gain_ffn.reshape(1, -1), full_in, full_out] + arrived,
    )
    return evolved.reshape(steps, zone_rows, width)


def solution(mesh):
    return jax.shard_map(
        on_device,
        mesh=mesh,
        in_specs=(
            P("tm", "zone", None),
            P(),
            P("zone", None),
            P("zone", None),
            P("tm", None),
            P(),
            P(),
            P(),
            P(),
            P(),
            P("zone", None),
            P("zone", None),
        ),
        out_specs=P("tm", "zone", None),
        check_vma=False,
    )
```

```python
import functools

import jax
import jax.numpy as jnp
from jax import lax
from jax.experimental import pallas as pl
from jax.experimental.pallas import tpu as pltpu
from jax.sharding import PartitionSpec as P

HEADS = 4
SPREAD = 8
LANES = 128
F32 = jnp.float32
BF16 = jnp.bfloat16
MIB = 1024 * 1024


def shifted(value, axis, steps):
    count = lax.axis_size(axis)
    return lax.ppermute(value, axis, [(source, source + steps) for source in range(count - steps)])


def swapped(value, axis, bits):
    count = lax.axis_size(axis)
    return lax.ppermute(value, axis, [(source, source ^ bits) for source in range(count)])


def crossed(value, axis, even_bits, odd_bits):
    count = lax.axis_size(axis)
    pairs = [(source, source ^ (odd_bits if source % 2 else even_bits)) for source in range(count)]
    return lax.ppermute(value, axis, pairs)


def steps_over(count):
    half = count // 2
    return tuple(range(half, count)) + tuple(range(1, half))


def rms_scale(values, gain):
    mean_sq = jnp.mean(values * values, axis=-1, keepdims=True)
    return values * lax.rsqrt(mean_sq + 1e-06) * gain


def quarter_of(block):
    core = lax.rem(block, 2)
    return (1 - core) * lax.rem(lax.div(block, 2), 2) + core * (2 + lax.rem(lax.div(block, 4), 2))


def row_sum(value):
    return jnp.sum(value, axis=0, keepdims=True)


def norm_kernel(*refs):
    blocks, (gain_attn, normed) = refs[:-2], refs[-2:]
    steps, zone_rows, _ = blocks[0].shape
    gain = gain_attn[...]
    for index, block in enumerate(blocks):
        for step in range(steps):
            row = (index * steps + step) * zone_rows
            normed[row : row + zone_rows, :] = rms_scale(block[step].astype(F32), gain).astype(BF16)


def split_kernel(place, packed, beside, states, before, *refs):
    arrived, (direct, upper, lower, doubled, last) = refs[:-5], refs[-5:]
    half = upper.shape[1]
    for index, piece in enumerate(arrived):
        direct[index] = piece[...]
        upper[index] = piece[:half, :]
        lower[index] = piece[half:, :]
    doubled[0] = packed[...]
    doubled[1] = beside[...]
    last[...] = jnp.where(lax.rem(place[0], 2) == 1, before[...], states[...])


def stack_kernel(doubled, arrived, *refs):
    out = refs[-1]
    near = doubled.shape[0]
    out[: near - 1] = doubled[1:]
    out[near - 1 :] = arrived[...]


def attention_kernel(zones, reach, steps, place, pattern, normed, own_qkv, own_attn, *refs):
    pieces, (context_out, attn_out, weights, w_turned, projected, context, sems) = refs[:-7], refs[-7:]
    key_count = (reach + 1) * steps
    zone_rows = normed.shape[0] // key_count
    width = normed.shape[1]
    head_size = width // HEADS
    my_block, my_zone = place[0], place[1]
    shard = own_qkv.shape[0]

    own_rows = pl.ds(pl.multiple_of(my_zone * shard, shard), shard)
    copies = [
        pltpu.make_async_copy(
            own_qkv.at[:, index * width : (index + 1) * width],
            weights.at[index, own_rows, :],
            sems.at[index],
        )
        for index in range(3)
    ]
    copies.append(pltpu.make_async_copy(own_attn, weights.at[3, own_rows, :], sems.at[3]))
    for copy in copies:
        copy.start()
    half = shard // 2
    mine, other = quarter_of(my_block), quarter_of(my_block ^ 1)
    for place_in, step in enumerate(steps_over(zones)):
        start = (my_zone ^ step) * shard
        for piece, quarter, low in zip(
            pieces, (mine, mine ^ 1, mine ^ 1, other, other ^ 1, other ^ 1), (0, 0, half, 0, 0, half)
        ):
            rows = pl.ds(pl.multiple_of(start + low, half), piece.shape[1])
            weights[quarter, rows, :] = piece[place_in]
    for copy in copies:
        copy.wait()
    attn_out[...] = weights[3]
    for index in range(3):
        for block in range(width // LANES):
            first = block * LANES
            rows = slice(index * width + first, index * width + first + LANES)
            w_turned[rows, :] = weights[index, :, first : first + LANES].T

    def project(first, last, weight_rows):
        return lax.dot_general(
            w_turned[weight_rows, :],
            normed[first:last, :],
            (((1,), (1,)), ((), ())),
            preferred_element_type=F32,
        ).astype(BF16).astype(F32)

    span = 2 * zone_rows
    for first in range(0, key_count * zone_rows, span):
        own = first >= reach * steps * zone_rows
        rows = slice(0 if own else width, 3 * width)
        projected[rows, first : first + span] = project(first, first + span, rows)

    allowed_back = [
        (pattern[0, back - 1] == 1) & (my_block >= back) for back in range(reach, 0, -1)
    ]
    chunks = head_size // 8

    def usable(query):
        return range(reach * steps + query + 1)

    def head_body(head, carry):
        base = head * head_size

        def tile(kind, chunk, key):
            row = pl.multiple_of(kind * width + base + chunk * 8, 8)
            return projected[pl.ds(row, 8), key * zone_rows : (key + 1) * zone_rows]

        for pair in range(0, steps, 2):
            queries = range(pair, min(pair + 2, steps))
            sums = {}
            for chunk in range(chunks):
                q_tiles = {q: tile(0, chunk, reach * steps + q) for q in queries}
                for key in usable(queries[-1]):
                    k_tile = tile(1, chunk, key)
                    for q in queries:
                        if key in usable(q):
                            term = q_tiles[q] * k_tile
                            sums[q, key] = term if chunk == 0 else sums[q, key] + term
            weights, scales = {}, {}
            for q in queries:
                scores = jnp.concatenate([row_sum(sums[q, key]) for key in usable(q)], axis=0)
                scores = scores * head_size ** (-0.5)
                row_id = lax.broadcasted_iota(jnp.int32, scores.shape, 0)
                allowed = row_id >= reach * steps
                for index, live in enumerate(allowed_back):
                    inside = (row_id >= index * steps) & (row_id < (index + 1) * steps)
                    allowed = allowed | (inside & live)
                masked = jnp.where(allowed, scores, -1e30)
                top = jnp.max(masked, axis=0, keepdims=True)
                expw = jnp.where(allowed, jnp.exp(masked - top), 0.0)
                scales[q] = jnp.broadcast_to(1.0 / row_sum(expw), (8, zone_rows))
                probs = expw.astype(BF16).astype(F32)
                for key in usable(q):
                    weights[q, key] = jnp.broadcast_to(probs[key : key + 1, :], (8, zone_rows))
            for chunk in range(chunks):
                sums = {}
                for key in usable(queries[-1]):
                    v_tile = tile(2, chunk, key)
                    for q in queries:
                        if key in usable(q):
                            term = weights[q, key] * v_tile
                            sums[q] = term if key == 0 else sums[q] + term
                for q in queries:
                    row = pl.multiple_of(base + chunk * 8, 8)
                    context[pl.ds(row, 8), q * zone_rows : (q + 1) * zone_rows] = sums[q] * scales[q]
        return carry

    lax.fori_loop(0, HEADS, head_body, 0)

    for step in range(steps):
        rows = slice(step * zone_rows, (step + 1) * zone_rows)
        context_out[rows, :] = context[:, rows].T.astype(BF16)


def project_kernel(place, states, context, w_attn, gain_mix, *refs):
    halves, (after_out, *outs, pair, parts) = refs[:2], refs[2:]
    steps, zone_rows, _ = states.shape
    zones, _, part = parts.shape
    for index, value in enumerate(halves):
        pair[index] = value[...]
    my_zone = place[1]
    gain = gain_mix[...]
    for step in range(steps):
        rows = slice(step * zone_rows, (step + 1) * zone_rows)
        after = states[step].astype(F32) + jnp.dot(
            context[rows, :], w_attn[...], preferred_element_type=F32
        )
        after_out[rows, :] = after
        mixin = rms_scale(after, gain).astype(BF16)
        for index in range(zones):
            parts[index, rows, :] = mixin[:, index * part : (index + 1) * part]
    for index, step in enumerate((0,) + steps_over(zones)):
        outs[index][...] = parts[my_zone ^ step]


def mixing_kernel(steps, zones, place, neighbours, degree, mix, *refs):
    arrived, pairs, (*outs, gathered, items) = refs[:zones], refs[zones : zones + 2], refs[zones + 2 :]
    for index, pair in enumerate(pairs):
        gathered[2 * index : 2 * index + 2] = pair[...]
    _, slots, zone_rows, _ = mix.shape
    part = items.shape[-1]
    my_zone = place[1]
    group = 2 if part % LANES == 0 and steps % 2 == 0 else 1
    for index, step in enumerate((0,) + steps_over(zones)):
        items[my_zone ^ step] = arrived[index][...]

    for target, target_step in enumerate((0,) + steps_over(zones)):
        block = my_zone ^ target_step
        left = []
        for slot in range(slots):
            tile = mix[block, slot]
            left.append(jnp.where(degree[block] > slot, tile, jnp.zeros_like(tile)))
        left = jnp.concatenate(left, axis=1)
        for step in range(0, steps, group):
            right = []
            for slot in range(slots):
                source = neighbours[block, slot]
                right.append(
                    jnp.concatenate(
                        [
                            items[source, (step + index) * zone_rows : (step + index + 1) * zone_rows, :]
                            for index in range(group)
                        ],
                        axis=1,
                    )
                )
            result = jnp.dot(left, jnp.concatenate(right, axis=0), preferred_element_type=F32)
            for index in range(group):
                rows = slice((step + index) * zone_rows, (step + index + 1) * zone_rows)
                outs[target][rows, :] = result[:, index * part : (index + 1) * part].astype(BF16)


def order_kernel(zones, place, own_in, own_out, *refs):
    gathered, (w_in, w_out, sems) = refs[:2], refs[2:]
    width = own_out.shape[1]
    my_block, my_zone = place[0], place[1]
    in_shard, hidden = own_in.shape
    out_shard = own_out.shape[0]
    in_cols, out_rows = hidden // SPREAD, out_shard // SPREAD

    own_rows = pl.ds(pl.multiple_of(my_zone * in_shard, in_shard), in_shard)
    copies = [
        pltpu.make_async_copy(
            own_in.at[:, index * in_cols : (index + 1) * in_cols],
            w_in.at[index, own_rows, :],
            sems.at[index],
        )
        for index in range(SPREAD)
    ]
    own_rows = pl.ds(pl.multiple_of(my_zone * out_shard, out_shard), out_shard)
    copies.append(pltpu.make_async_copy(own_out, w_out.at[own_rows, :], sems.at[SPREAD]))
    for copy in copies:
        copy.start()
    for pieces, block in zip(gathered, (my_block, my_block ^ 1)):
        near = 2 + 2 * lax.rem(block, 2)
        for index, bits in enumerate((0, near, 6 - near, 6)):
            slot = lax.rem(block, SPREAD) ^ bits
            for step in range(1, zones):
                source = my_zone ^ step
                piece = pieces.at[index, step - 1]
                rows = pl.ds(pl.multiple_of(source * in_shard, in_shard), in_shard)
                w_in[slot, rows, :] = piece[:in_shard, :]
                first = pl.multiple_of(source * out_shard + slot * out_rows, out_rows)
                for fold in range(width // in_cols):
                    cols = slice(fold * in_cols, (fold + 1) * in_cols)
                    low = in_shard + fold * out_rows
                    w_out[pl.ds(first, out_rows), cols] = piece[low : low + out_rows, :]
    for copy in copies:
        copy.wait()


def ffn_kernel(zones, place, after_attn, gain_ffn, w_in, w_out, *refs):
    arrived, (out, after_mix, ffn_in, parts, hidden) = refs[:zones], refs[zones:]
    rows_all, width = after_attn.shape
    my_zone = place[1]
    in_cols = w_in.shape[2]
    for index, step in enumerate((0,) + steps_over(zones)):
        parts[my_zone ^ step] = arrived[index][...]

    gain = gain_ffn[...]
    span = 128
    part = parts.shape[-1]
    for first in range(0, rows_all, span):
        rows = slice(first, first + span)
        for index in range(zones):
            cols = slice(index * part, (index + 1) * part)
            after_mix[rows, cols] = after_attn[rows, cols] + parts[index, rows, :].astype(F32)
        ffn_in[rows, :] = rms_scale(after_mix[rows, :], gain).astype(BF16)
    span = 256
    for first in range(0, rows_all, span):
        rows = slice(first, first + span)
        for index in range(SPREAD):
            grown = jnp.dot(ffn_in[rows, :], w_in[index], preferred_element_type=F32)
            cols = slice(index * in_cols, (index + 1) * in_cols)
            hidden[rows, cols] = jax.nn.gelu(grown, approximate=True).astype(BF16)
        shrunk = jnp.dot(hidden[rows, :], w_out[...], preferred_element_type=F32)
        out[rows, :] = (after_mix[rows, :] + shrunk).astype(BF16)


def call(kernel, out_shape, scratch, smem, hbm, limit, args):
    spaces = {index: pltpu.SMEM for index in smem} | {index: pltpu.HBM for index in hbm}
    return pl.pallas_call(
        kernel,
        out_shape=out_shape,
        in_specs=[
            pl.BlockSpec(memory_space=spaces.get(index, pltpu.VMEM)) for index in range(len(args))
        ],
        out_specs=jax.tree.map(lambda _: pl.BlockSpec(memory_space=pltpu.VMEM), out_shape),
        scratch_shapes=scratch,
        cost_estimate=pl.CostEstimate(flops=0, bytes_accessed=0, transcendentals=0),
        compiler_params=pltpu.CompilerParams(vmem_limit_bytes=limit * MIB),
    )(*args)


def on_device(
    states,
    gain_attn,
    w_qkv,
    w_out_attn,
    pattern,
    gain_mix,
    neighbours,
    degree,
    mix,
    gain_ffn,
    w_in,
    w_out,
):
    steps, zone_rows, width = states.shape
    rows = steps * zone_rows
    reach = pattern.shape[1]
    zones = lax.axis_size("zone")
    my_block, my_zone = lax.axis_index("tm"), lax.axis_index("zone")
    place = jnp.stack([my_block, my_zone]).astype(jnp.int32)
    key_count = (reach + 1) * steps
    hidden = w_in.shape[1]
    in_cols = hidden // SPREAD
    out_rows = w_out.shape[0] // SPREAD
    part = width // zones
    exchanges = steps_over(zones)

    before = shifted(states, "tm", 2)
    first = lax.dynamic_slice_in_dim(
        jnp.concatenate([w_qkv, w_out_attn], axis=1), quarter_of(my_block) * width, width, axis=1
    )
    direct = [swapped(first, "zone", step) for step in exchanges]
    slot = my_block % SPREAD
    slice_in = lax.dynamic_slice_in_dim(w_in, slot * in_cols, in_cols, axis=1)
    slice_out = lax.dynamic_slice_in_dim(w_out, slot * out_rows, out_rows, axis=0)
    packed = jnp.concatenate(
        [slice_in] + [slice_out[:, at : at + in_cols] for at in range(0, width, in_cols)], axis=0
    )
    beside = swapped(packed, "zone", 1)
    half_shape = jax.ShapeDtypeStruct((zones - 1, first.shape[0] // 2, width), BF16)
    direct, upper, lower, doubled, last = call(
        split_kernel,
        (
            jax.ShapeDtypeStruct((zones - 1,) + first.shape, BF16),
            half_shape,
            half_shape,
            jax.ShapeDtypeStruct((2,) + packed.shape, BF16),
            jax.ShapeDtypeStruct(states.shape, BF16),
        ),
        [],
        (0,),
        (),
        4,
        [place, packed, beside, states, before] + direct,
    )
    over = [crossed(value, "tm", 2, 4) for value in (upper, lower)]
    last = swapped(last, "tm", 1)
    pieces = [direct] + over + [swapped(value, "tm", 1) for value in [direct] + over]
    normed = call(
        norm_kernel,
        jax.ShapeDtypeStruct((key_count * zone_rows, width), BF16),
        [],
        (),
        (),
        4,
        [before, last, states, gain_attn.reshape(1, -1)],
    )
    bits = 2
    while 2 * bits < zones:
        doubled = jnp.concatenate([doubled, swapped(doubled, "zone", bits)], axis=0)
        bits *= 2
    across = call(
        stack_kernel,
        jax.ShapeDtypeStruct((zones - 1,) + packed.shape, BF16),
        [],
        (),
        (),
        4,
        [doubled, swapped(doubled, "zone", bits), normed] + pieces[3:],
    )
    nearest = crossed(across, "tm", 2, 4)

    context, w_attn = call(
        functools.partial(attention_kernel, zones, reach, steps),
        (
            jax.ShapeDtypeStruct((rows, width), BF16),
            jax.ShapeDtypeStruct((width, width), BF16),
        ),
        [
            pltpu.VMEM((4, width, width), BF16),
            pltpu.VMEM((3 * width, width), BF16),
            pltpu.VMEM((3 * width, key_count * zone_rows), F32),
            pltpu.VMEM((width, rows), F32),
            pltpu.SemaphoreType.DMA((4,)),
        ],
        (0, 1),
        (3, 4),
        22,
        [place, pattern, normed, w_qkv, w_out_attn] + pieces,
    )

    chunk = jax.ShapeDtypeStruct((rows, part), BF16)
    after_attn, *chunks, pair = call(
        project_kernel,
        (jax.ShapeDtypeStruct((rows, width), F32),)
        + (chunk,) * zones
        + (jax.ShapeDtypeStruct((2,) + across.shape, BF16),),
        [pltpu.VMEM((zones, rows, part), BF16)],
        (0,),
        (),
        8,
        [place, states, context, w_attn, gain_mix.reshape(1, -1)]
        + [across, nearest],
    )
    arrived = [chunks[0]] + [
        swapped(value, "zone", step) for value, step in zip(chunks[1:], exchanges)
    ]

    *spatial, gathered = call(
        functools.partial(mixing_kernel, steps, zones),
        (chunk,) * zones
        + (jax.ShapeDtypeStruct((4,) + across.shape, BF16),),
        [pltpu.VMEM((zones, rows, part), BF16)],
        (0, 1, 2),
        (),
        8,
        [place, neighbours, degree, mix] + arrived + [pair, crossed(pair, "tm", 4, 2)],
    )
    full_in, full_out = call(
        functools.partial(order_kernel, zones),
        (
            jax.ShapeDtypeStruct((SPREAD, width, in_cols), BF16),
            jax.ShapeDtypeStruct((hidden, width), BF16),
        ),
        [pltpu.SemaphoreType.DMA((SPREAD + 1,))],
        (0,),
        (1, 2),
        8,
        [place, w_in, w_out, gathered, swapped(gathered, "tm", 1)],
    )
    arrived = [spatial[0]] + [
        swapped(value, "zone", step) for value, step in zip(spatial[1:], exchanges)
    ]
    evolved = call(
        functools.partial(ffn_kernel, zones),
        jax.ShapeDtypeStruct((rows, width), BF16),
        [
            pltpu.VMEM((rows, width), F32),
            pltpu.VMEM((rows, width), BF16),
            pltpu.VMEM((zones, rows, part), BF16),
            pltpu.VMEM((rows, hidden), BF16),
        ],
        (0,),
        (),
        10,
        [place, after_attn, gain_ffn.reshape(1, -1), full_in, full_out] + arrived,
    )
    return evolved.reshape(steps, zone_rows, width)


def solution(mesh):
    return jax.shard_map(
        on_device,
        mesh=mesh,
        in_specs=(
            P("tm", "zone", None),
            P(),
            P("zone", None),
            P("zone", None),
            P("tm", None),
            P(),
            P(),
            P(),
            P(),
            P(),
            P("zone", None),
            P("zone", None),
        ),
        out_specs=P("tm", "zone", None),
        check_vma=False,
    )
```

```python
import functools

import jax
import jax.numpy as jnp
from jax import lax
from jax.experimental import pallas as pl
from jax.experimental.pallas import tpu as pltpu
from jax.sharding import PartitionSpec as P

HEADS = 4
SPREAD = 8
LANES = 128
F32 = jnp.float32
BF16 = jnp.bfloat16
MIB = 1024 * 1024


def shifted(value, axis, steps):
    count = lax.axis_size(axis)
    return lax.ppermute(value, axis, [(source, source + steps) for source in range(count - steps)])


def swapped(value, axis, bits):
    count = lax.axis_size(axis)
    return lax.ppermute(value, axis, [(source, source ^ bits) for source in range(count)])


def crossed(value, axis, even_bits, odd_bits):
    count = lax.axis_size(axis)
    pairs = [(source, source ^ (odd_bits if source % 2 else even_bits)) for source in range(count)]
    return lax.ppermute(value, axis, pairs)


def steps_over(count):
    half = count // 2
    return tuple(range(half, count)) + tuple(range(1, half))


def rms_scale(values, gain):
    mean_sq = jnp.mean(values * values, axis=-1, keepdims=True)
    return values * lax.rsqrt(mean_sq + 1e-06) * gain


def quarter_of(block):
    core = lax.rem(block, 2)
    return (1 - core) * lax.rem(lax.div(block, 2), 2) + core * (2 + lax.rem(lax.div(block, 4), 2))


def row_sum(value):
    return jnp.sum(value, axis=0, keepdims=True)


def norm_kernel(*refs):
    blocks, (gain_attn, normed) = refs[:-2], refs[-2:]
    steps, zone_rows, _ = blocks[0].shape
    gain = gain_attn[...]
    for index, block in enumerate(blocks):
        for step in range(steps):
            row = (index * steps + step) * zone_rows
            normed[row : row + zone_rows, :] = rms_scale(block[step].astype(F32), gain).astype(BF16)


def group_kernel(zones, place, w_in, w_out, own_in, packed):
    in_shard, hidden = w_in.shape
    out_rows = w_out.shape[0] // SPREAD
    in_cols = hidden // SPREAD
    width = w_out.shape[1]
    for index in range(SPREAD):
        for source in range(zones):
            low = (source * SPREAD + index) * out_rows
            to = slice(source * out_rows, (source + 1) * out_rows)
            own_in[index, :, to] = w_in[:, low : low + out_rows]
    slot = lax.rem(place[0], SPREAD)
    packed[:in_shard, :] = own_in[slot]
    rows = pl.ds(pl.multiple_of(slot * out_rows, out_rows), out_rows)
    for fold in range(width // in_cols):
        low = in_shard + fold * out_rows
        packed[low : low + out_rows, :] = w_out[rows, fold * in_cols : (fold + 1) * in_cols]


def split_kernel(place, packed, beside, states, before, *refs):
    arrived, (direct, upper, lower, doubled, last) = refs[:-5], refs[-5:]
    half = upper.shape[1]
    for index, piece in enumerate(arrived):
        direct[index] = piece[...]
        upper[index] = piece[:half, :]
        lower[index] = piece[half:, :]
    doubled[0] = packed[...]
    doubled[1] = beside[...]
    last[...] = jnp.where(lax.rem(place[0], 2) == 1, before[...], states[...])


def stack_kernel(doubled, arrived, *refs):
    out = refs[-1]
    near = doubled.shape[0]
    out[: near - 1] = doubled[1:]
    out[near - 1 :] = arrived[...]


def attention_kernel(zones, reach, steps, place, pattern, normed, own_qkv, own_attn, *refs):
    pieces, (context_out, attn_out, weights, w_turned, projected, context, sems) = refs[:-7], refs[-7:]
    key_count = (reach + 1) * steps
    zone_rows = normed.shape[0] // key_count
    width = normed.shape[1]
    head_size = width // HEADS
    my_block, my_zone = place[0], place[1]
    shard = own_qkv.shape[0]

    own_rows = pl.ds(pl.multiple_of(my_zone * shard, shard), shard)
    copies = [
        pltpu.make_async_copy(
            own_qkv.at[:, index * width : (index + 1) * width],
            weights.at[index, own_rows, :],
            sems.at[index],
        )
        for index in range(3)
    ]
    copies.append(pltpu.make_async_copy(own_attn, weights.at[3, own_rows, :], sems.at[3]))
    for copy in copies:
        copy.start()
    half = shard // 2
    mine, other = quarter_of(my_block), quarter_of(my_block ^ 1)
    for place_in, step in enumerate(steps_over(zones)):
        start = (my_zone ^ step) * shard
        for piece, quarter, low in zip(
            pieces, (mine, mine ^ 1, mine ^ 1, other, other ^ 1, other ^ 1), (0, 0, half, 0, 0, half)
        ):
            rows = pl.ds(pl.multiple_of(start + low, half), piece.shape[1])
            weights[quarter, rows, :] = piece[place_in]
    for copy in copies:
        copy.wait()
    attn_out[...] = weights[3]
    for index in range(3):
        for block in range(width // LANES):
            first = block * LANES
            rows = slice(index * width + first, index * width + first + LANES)
            w_turned[rows, :] = weights[index, :, first : first + LANES].T

    def project(first, last, weight_rows):
        return lax.dot_general(
            w_turned[weight_rows, :],
            normed[first:last, :],
            (((1,), (1,)), ((), ())),
            preferred_element_type=F32,
        ).astype(BF16).astype(F32)

    span = 2 * zone_rows
    for first in range(0, key_count * zone_rows, span):
        own = first >= reach * steps * zone_rows
        rows = slice(0 if own else width, 3 * width)
        projected[rows, first : first + span] = project(first, first + span, rows)

    allowed_back = [
        (pattern[0, back - 1] == 1) & (my_block >= back) for back in range(reach, 0, -1)
    ]
    chunks = head_size // 8

    def usable(query):
        return range(reach * steps + query + 1)

    def head_body(head, carry):
        base = head * head_size

        def tile(kind, chunk, key):
            row = pl.multiple_of(kind * width + base + chunk * 8, 8)
            return projected[pl.ds(row, 8), key * zone_rows : (key + 1) * zone_rows]

        for pair in range(0, steps, 2):
            queries = range(pair, min(pair + 2, steps))
            sums = {}
            for chunk in range(chunks):
                q_tiles = {q: tile(0, chunk, reach * steps + q) for q in queries}
                for key in usable(queries[-1]):
                    k_tile = tile(1, chunk, key)
                    for q in queries:
                        if key in usable(q):
                            term = q_tiles[q] * k_tile
                            sums[q, key] = term if chunk == 0 else sums[q, key] + term
            weights, scales = {}, {}
            for q in queries:
                scores = jnp.concatenate([row_sum(sums[q, key]) for key in usable(q)], axis=0)
                scores = scores * head_size ** (-0.5)
                row_id = lax.broadcasted_iota(jnp.int32, scores.shape, 0)
                allowed = row_id >= reach * steps
                for index, live in enumerate(allowed_back):
                    inside = (row_id >= index * steps) & (row_id < (index + 1) * steps)
                    allowed = allowed | (inside & live)
                masked = jnp.where(allowed, scores, -1e30)
                top = jnp.max(masked, axis=0, keepdims=True)
                expw = jnp.where(allowed, jnp.exp(masked - top), 0.0)
                scales[q] = jnp.broadcast_to(1.0 / row_sum(expw), (8, zone_rows))
                probs = expw.astype(BF16).astype(F32)
                for key in usable(q):
                    weights[q, key] = jnp.broadcast_to(probs[key : key + 1, :], (8, zone_rows))
            for chunk in range(chunks):
                sums = {}
                for key in usable(queries[-1]):
                    v_tile = tile(2, chunk, key)
                    for q in queries:
                        if key in usable(q):
                            term = weights[q, key] * v_tile
                            sums[q] = term if key == 0 else sums[q] + term
                for q in queries:
                    row = pl.multiple_of(base + chunk * 8, 8)
                    context[pl.ds(row, 8), q * zone_rows : (q + 1) * zone_rows] = sums[q] * scales[q]
        return carry

    lax.fori_loop(0, HEADS, head_body, 0)

    for step in range(steps):
        rows = slice(step * zone_rows, (step + 1) * zone_rows)
        context_out[rows, :] = context[:, rows].T.astype(BF16)


def project_kernel(place, states, context, w_attn, gain_mix, after_out, *refs):
    *outs, parts = refs
    steps, zone_rows, _ = states.shape
    zones, _, part = parts.shape
    my_zone = place[1]
    gain = gain_mix[...]
    for step in range(steps):
        rows = slice(step * zone_rows, (step + 1) * zone_rows)
        after = states[step].astype(F32) + jnp.dot(
            context[rows, :], w_attn[...], preferred_element_type=F32
        )
        after_out[rows, :] = after
        mixin = rms_scale(after, gain).astype(BF16)
        for index in range(zones):
            parts[index, rows, :] = mixin[:, index * part : (index + 1) * part]
    for index, step in enumerate((0,) + steps_over(zones)):
        outs[index][...] = parts[my_zone ^ step]


def mixing_kernel(steps, zones, place, neighbours, degree, mix, *refs):
    arrived, halves, (*outs, pair, items) = refs[:zones], refs[zones : zones + 2], refs[zones + 2 :]
    for index, value in enumerate(halves):
        pair[index] = value[...]
    _, slots, zone_rows, _ = mix.shape
    part = items.shape[-1]
    my_zone = place[1]
    group = 2 if part % LANES == 0 and steps % 2 == 0 else 1
    for index, step in enumerate((0,) + steps_over(zones)):
        items[my_zone ^ step] = arrived[index][...]

    for target, target_step in enumerate((0,) + steps_over(zones)):
        block = my_zone ^ target_step
        left = []
        for slot in range(slots):
            tile = mix[block, slot]
            left.append(jnp.where(degree[block] > slot, tile, jnp.zeros_like(tile)))
        left = jnp.concatenate(left, axis=1)
        for step in range(0, steps, group):
            right = []
            for slot in range(slots):
                source = neighbours[block, slot]
                right.append(
                    jnp.concatenate(
                        [
                            items[source, (step + index) * zone_rows : (step + index + 1) * zone_rows, :]
                            for index in range(group)
                        ],
                        axis=1,
                    )
                )
            result = jnp.dot(left, jnp.concatenate(right, axis=0), preferred_element_type=F32)
            for index in range(group):
                rows = slice((step + index) * zone_rows, (step + index + 1) * zone_rows)
                outs[target][rows, :] = result[:, index * part : (index + 1) * part].astype(BF16)


def slots_of(block):
    near = 2 + 2 * lax.rem(block, 2)
    return [lax.rem(block, SPREAD) ^ bits for bits in (0, near, 6 - near, 6)]


def fill_slots(zones, place, own_in, own_out, slots, pieces, w_in, w_out, sems):
    my_zone = place[1]
    in_shard = own_in.shape[1]
    out_rows = own_out.shape[0] // SPREAD
    in_cols, width = own_in.shape[2], own_out.shape[1]
    own_rows = pl.ds(pl.multiple_of(my_zone * in_shard, in_shard), in_shard)
    own_out_rows = pl.ds(pl.multiple_of(my_zone * out_rows, out_rows), out_rows)
    copies = []
    for index, slot in enumerate(slots):
        from_rows = pl.ds(pl.multiple_of(slot * out_rows, out_rows), out_rows)
        copies += [
            pltpu.make_async_copy(own_in.at[slot], w_in.at[index, own_rows, :], sems.at[2 * index]),
            pltpu.make_async_copy(
                own_out.at[from_rows, :], w_out.at[index, own_out_rows, :], sems.at[2 * index + 1]
            ),
        ]
    for copy in copies:
        copy.start()
    for index, piece in enumerate(pieces):
        for step in range(1, zones):
            source = my_zone ^ step
            part = piece[step - 1]
            rows = pl.ds(pl.multiple_of(source * in_shard, in_shard), in_shard)
            w_in[index, rows, :] = part[:in_shard, :]
            rows = pl.ds(pl.multiple_of(source * out_rows, out_rows), out_rows)
            for fold in range(width // in_cols):
                low = in_shard + fold * out_rows
                w_out[index, rows, fold * in_cols : (fold + 1) * in_cols] = part[low : low + out_rows, :]
    for copy in copies:
        copy.wait()


def order_kernel(zones, place, own_in, own_out, pair, far, swapped_pair, w_in, w_out, sems):
    my_block = place[0]
    slots = slots_of(my_block) + slots_of(my_block ^ 1)[:2]
    pieces = [group.at[index] for group in (pair, far, swapped_pair) for index in range(2)]
    fill_slots(zones, place, own_in, own_out, slots, pieces, w_in, w_out, sems)


def after_kernel(zones, place, after_attn, gain_ffn, ready, far, *refs):
    arrived, (after_mix, ffn_in, far_out, parts) = refs[:zones], refs[zones:]
    rows_all, width = after_attn.shape
    my_zone = place[1]
    far_out[...] = far[...]
    for index, step in enumerate((0,) + steps_over(zones)):
        parts[my_zone ^ step] = arrived[index][...]
    gain = gain_ffn[...]
    span = 128
    part = parts.shape[-1]
    for first in range(0, rows_all, span):
        rows = slice(first, first + span)
        for index in range(zones):
            cols = slice(index * part, (index + 1) * part)
            after_mix[rows, cols] = after_attn[rows, cols] + parts[index, rows, :].astype(F32)
        ffn_in[rows, :] = rms_scale(after_mix[rows, :], gain).astype(BF16)


def ffn_rows(ffn_in, w_in, w_out, total):
    for index in range(w_in.shape[0]):
        grown = jnp.dot(ffn_in, w_in[index], preferred_element_type=F32)
        grown = jax.nn.gelu(grown, approximate=True).astype(BF16)
        total = total + jnp.dot(grown, w_out[index], preferred_element_type=F32)
    return total


def ffn_kernel(after_mix, ffn_in, w_in, w_out, out):
    span = 256
    for first in range(0, after_mix.shape[0], span):
        rows = slice(first, first + span)
        out[rows, :] = ffn_rows(ffn_in[rows, :], w_in, w_out, after_mix[rows, :])


def last_kernel(zones, place, own_in, own_out, total, ffn_in, swapped_far, out, w_in, w_out, sems):
    slots = slots_of(place[0] ^ 1)[2:]
    pieces = [swapped_far.at[index] for index in range(2)]
    fill_slots(zones, place, own_in, own_out, slots, pieces, w_in, w_out, sems)
    span = 256
    for first in range(0, total.shape[0], span):
        rows = slice(first, first + span)
        out[rows, :] = ffn_rows(ffn_in[rows, :], w_in, w_out, total[rows, :]).astype(BF16)


def call(kernel, out_shape, scratch, smem, hbm, limit, args):
    spaces = {index: pltpu.SMEM for index in smem} | {index: pltpu.HBM for index in hbm}
    return pl.pallas_call(
        kernel,
        out_shape=out_shape,
        in_specs=[
            pl.BlockSpec(memory_space=spaces.get(index, pltpu.VMEM)) for index in range(len(args))
        ],
        out_specs=jax.tree.map(lambda _: pl.BlockSpec(memory_space=pltpu.VMEM), out_shape),
        scratch_shapes=scratch,
        cost_estimate=pl.CostEstimate(flops=0, bytes_accessed=0, transcendentals=0),
        compiler_params=pltpu.CompilerParams(vmem_limit_bytes=limit * MIB),
    )(*args)


def on_device(
    states,
    gain_attn,
    w_qkv,
    w_out_attn,
    pattern,
    gain_mix,
    neighbours,
    degree,
    mix,
    gain_ffn,
    w_in,
    w_out,
):
    steps, zone_rows, width = states.shape
    rows = steps * zone_rows
    reach = pattern.shape[1]
    zones = lax.axis_size("zone")
    my_block, my_zone = lax.axis_index("tm"), lax.axis_index("zone")
    place = jnp.stack([my_block, my_zone]).astype(jnp.int32)
    key_count = (reach + 1) * steps
    hidden = w_in.shape[1]
    in_cols = hidden // SPREAD
    out_rows = w_out.shape[0] // SPREAD
    part = width // zones
    exchanges = steps_over(zones)

    before = shifted(states, "tm", 2)
    first = lax.dynamic_slice_in_dim(
        jnp.concatenate([w_qkv, w_out_attn], axis=1), quarter_of(my_block) * width, width, axis=1
    )
    direct = [swapped(first, "zone", step) for step in exchanges]
    packed_rows = w_in.shape[0] + out_rows * (width // in_cols)
    own_in, packed = call(
        functools.partial(group_kernel, zones),
        (
            jax.ShapeDtypeStruct((SPREAD, w_in.shape[0], in_cols), BF16),
            jax.ShapeDtypeStruct((packed_rows, in_cols), BF16),
        ),
        [],
        (0,),
        (),
        4,
        [place, w_in, w_out],
    )
    beside = swapped(packed, "zone", 1)
    half_shape = jax.ShapeDtypeStruct((zones - 1, first.shape[0] // 2, width), BF16)
    direct, upper, lower, doubled, last = call(
        split_kernel,
        (
            jax.ShapeDtypeStruct((zones - 1,) + first.shape, BF16),
            half_shape,
            half_shape,
            jax.ShapeDtypeStruct((2,) + packed.shape, BF16),
            jax.ShapeDtypeStruct(states.shape, BF16),
        ),
        [],
        (0,),
        (),
        4,
        [place, packed, beside, states, before] + direct,
    )
    over = [crossed(value, "tm", 2, 4) for value in (upper, lower)]
    last = swapped(last, "tm", 1)
    pieces = [direct] + over + [swapped(value, "tm", 1) for value in [direct] + over]
    normed = call(
        norm_kernel,
        jax.ShapeDtypeStruct((key_count * zone_rows, width), BF16),
        [],
        (),
        (),
        4,
        [before, last, states, gain_attn.reshape(1, -1)],
    )
    bits = 2
    while 2 * bits < zones:
        doubled = jnp.concatenate([doubled, swapped(doubled, "zone", bits)], axis=0)
        bits *= 2
    context, w_attn = call(
        functools.partial(attention_kernel, zones, reach, steps),
        (
            jax.ShapeDtypeStruct((rows, width), BF16),
            jax.ShapeDtypeStruct((width, width), BF16),
        ),
        [
            pltpu.VMEM((4, width, width), BF16),
            pltpu.VMEM((3 * width, width), BF16),
            pltpu.VMEM((3 * width, key_count * zone_rows), F32),
            pltpu.VMEM((width, rows), F32),
            pltpu.SemaphoreType.DMA((4,)),
        ],
        (0, 1),
        (3, 4),
        22,
        [place, pattern, normed, w_qkv, w_out_attn] + pieces,
    )

    chunk = jax.ShapeDtypeStruct((rows, part), BF16)
    after_attn, *chunks = call(
        project_kernel,
        (jax.ShapeDtypeStruct((rows, width), F32),)
        + (chunk,) * zones,
        [pltpu.VMEM((zones, rows, part), BF16)],
        (0,),
        (),
        8,
        [place, states, context, w_attn, gain_mix.reshape(1, -1)],
    )
    across = call(
        stack_kernel,
        jax.ShapeDtypeStruct((zones - 1,) + packed.shape, BF16),
        [],
        (),
        (),
        4,
        [doubled, swapped(doubled, "zone", bits), after_attn],
    )
    nearest = crossed(across, "tm", 2, 4)

    arrived = [chunks[0]] + [
        swapped(value, "zone", step) for value, step in zip(chunks[1:], exchanges)
    ]

    *spatial, pair = call(
        functools.partial(mixing_kernel, steps, zones),
        (chunk,) * zones
        + (jax.ShapeDtypeStruct((2,) + across.shape, BF16),),
        [pltpu.VMEM((zones, rows, part), BF16)],
        (0, 1, 2),
        (),
        8,
        [place, neighbours, degree, mix] + arrived + [across, nearest],
    )
    far = crossed(pair, "tm", 4, 2)
    full_in, full_out = call(
        functools.partial(order_kernel, zones),
        (
            jax.ShapeDtypeStruct((6, width, in_cols), BF16),
            jax.ShapeDtypeStruct((6, in_cols, width), BF16),
        ),
        [pltpu.SemaphoreType.DMA((12,))],
        (0,),
        (1, 2),
        8,
        [place, own_in, w_out, pair, far, swapped(pair, "tm", 1)],
    )
    arrived = [spatial[0]] + [
        swapped(value, "zone", step) for value, step in zip(spatial[1:], exchanges)
    ]
    after_mix, ffn_in, far = call(
        functools.partial(after_kernel, zones),
        (
            jax.ShapeDtypeStruct((rows, width), F32),
            jax.ShapeDtypeStruct((rows, width), BF16),
            jax.ShapeDtypeStruct(far.shape, BF16),
        ),
        [pltpu.VMEM((zones, rows, part), BF16)],
        (0,),
        (),
        8,
        [place, after_attn, gain_ffn.reshape(1, -1), full_out, far] + arrived,
    )
    total = call(
        ffn_kernel,
        jax.ShapeDtypeStruct((rows, width), F32),
        [],
        (),
        (),
        8,
        [after_mix, ffn_in, full_in, full_out],
    )
    evolved = call(
        functools.partial(last_kernel, zones),
        jax.ShapeDtypeStruct((rows, width), BF16),
        [
            pltpu.VMEM((2, width, in_cols), BF16),
            pltpu.VMEM((2, in_cols, width), BF16),
            pltpu.SemaphoreType.DMA((4,)),
        ],
        (0,),
        (1, 2),
        8,
        [place, own_in, w_out, total, ffn_in, swapped(far, "tm", 1)],
    )
    return evolved.reshape(steps, zone_rows, width)


def solution(mesh):
    return jax.shard_map(
        on_device,
        mesh=mesh,
        in_specs=(
            P("tm", "zone", None),
            P(),
            P("zone", None),
            P("zone", None),
            P("tm", None),
            P(),
            P(),
            P(),
            P(),
            P(),
            P("zone", None),
            P("zone", None),
        ),
        out_specs=P("tm", "zone", None),
        check_vma=False,
    )
```

```python
import functools

import jax
import jax.numpy as jnp
from jax import lax
from jax.experimental import pallas as pl
from jax.experimental.pallas import tpu as pltpu
from jax.sharding import PartitionSpec as P

HEADS = 4
SPREAD = 8
LANES = 128
F32 = jnp.float32
BF16 = jnp.bfloat16
MIB = 1024 * 1024


def shifted(value, axis, steps):
    count = lax.axis_size(axis)
    return lax.ppermute(value, axis, [(source, source + steps) for source in range(count - steps)])


def swapped(value, axis, bits):
    count = lax.axis_size(axis)
    return lax.ppermute(value, axis, [(source, source ^ bits) for source in range(count)])


def crossed(value, axis, even_bits, odd_bits):
    count = lax.axis_size(axis)
    pairs = [(source, source ^ (odd_bits if source % 2 else even_bits)) for source in range(count)]
    return lax.ppermute(value, axis, pairs)


def steps_over(count):
    half = count // 2
    return tuple(range(half, count)) + tuple(range(1, half))


def rms_scale(values, gain):
    mean_sq = jnp.mean(values * values, axis=-1, keepdims=True)
    return values * lax.rsqrt(mean_sq + 1e-06) * gain


def quarter_of(block):
    core = lax.rem(block, 2)
    return (1 - core) * lax.rem(lax.div(block, 2), 2) + core * (2 + lax.rem(lax.div(block, 4), 2))


def row_sum(value):
    return jnp.sum(value, axis=0, keepdims=True)


def norm_kernel(*refs):
    blocks, (gain_attn, normed) = refs[:-2], refs[-2:]
    steps, zone_rows, _ = blocks[0].shape
    gain = gain_attn[...]
    for index, block in enumerate(blocks):
        for step in range(steps):
            row = (index * steps + step) * zone_rows
            normed[row : row + zone_rows, :] = rms_scale(block[step].astype(F32), gain).astype(BF16)


def group_kernel(zones, place, w_in, w_out, own_in, packed):
    in_shard, hidden = w_in.shape
    out_rows = w_out.shape[0] // SPREAD
    in_cols = hidden // SPREAD
    width = w_out.shape[1]
    for index in range(SPREAD):
        for source in range(zones):
            low = (source * SPREAD + index) * out_rows
            to = slice(source * out_rows, (source + 1) * out_rows)
            own_in[index, :, to] = w_in[:, low : low + out_rows]
    slot = lax.rem(place[0], SPREAD)
    packed[:in_shard, :] = own_in[slot]
    rows = pl.ds(pl.multiple_of(slot * out_rows, out_rows), out_rows)
    for fold in range(width // in_cols):
        low = in_shard + fold * out_rows
        packed[low : low + out_rows, :] = w_out[rows, fold * in_cols : (fold + 1) * in_cols]


def split_kernel(place, packed, beside, states, before, *refs):
    arrived, (direct, upper, lower, doubled, last) = refs[:-5], refs[-5:]
    half = upper.shape[1]
    for index, piece in enumerate(arrived):
        direct[index] = piece[...]
        upper[index] = piece[:half, :]
        lower[index] = piece[half:, :]
    doubled[0] = packed[...]
    doubled[1] = beside[...]
    last[...] = jnp.where(lax.rem(place[0], 2) == 1, before[...], states[...])


def stack_kernel(doubled, arrived, *refs):
    out = refs[-1]
    near = doubled.shape[0]
    out[: near - 1] = doubled[1:]
    out[near - 1 :] = arrived[...]


def attention_kernel(zones, reach, steps, place, pattern, normed, own_qkv, own_attn, *refs):
    pieces, (context_out, attn_out, weights, w_turned, projected, context, sems) = refs[:-7], refs[-7:]
    key_count = (reach + 1) * steps
    zone_rows = normed.shape[0] // key_count
    width = normed.shape[1]
    head_size = width // HEADS
    my_block, my_zone = place[0], place[1]
    shard = own_qkv.shape[0]

    own_rows = pl.ds(pl.multiple_of(my_zone * shard, shard), shard)
    copies = [
        pltpu.make_async_copy(
            own_qkv.at[:, index * width : (index + 1) * width],
            weights.at[index, own_rows, :],
            sems.at[index],
        )
        for index in range(3)
    ]
    copies.append(pltpu.make_async_copy(own_attn, weights.at[3, own_rows, :], sems.at[3]))
    for copy in copies:
        copy.start()
    half = shard // 2
    mine, other = quarter_of(my_block), quarter_of(my_block ^ 1)
    for place_in, step in enumerate(steps_over(zones)):
        start = (my_zone ^ step) * shard
        for piece, quarter, low in zip(
            pieces, (mine, mine ^ 1, mine ^ 1, other, other ^ 1, other ^ 1), (0, 0, half, 0, 0, half)
        ):
            rows = pl.ds(pl.multiple_of(start + low, half), piece.shape[1])
            weights[quarter, rows, :] = piece[place_in]
    for copy in copies:
        copy.wait()
    attn_out[...] = weights[3]
    group = 3 * head_size
    for head in range(HEADS):
        for kind in range(3):
            rows = slice(head * group + kind * head_size, head * group + (kind + 1) * head_size)
            w_turned[rows, :] = weights[kind, :, head * head_size : (head + 1) * head_size].T

    def project(head, first, span):
        skip = 0 if first >= reach * steps * zone_rows else head_size
        projected[head, skip:, first : first + span] = lax.dot_general(
            w_turned[head * group + skip : (head + 1) * group, :],
            normed[first : first + span, :],
            (((1,), (1,)), ((), ())),
            preferred_element_type=F32,
        )

    span = 2 * zone_rows
    pending = [(head, first) for head in range(HEADS) for first in range(0, key_count * zone_rows, span)]

    def project_some(count):
        for _ in range(min(count, len(pending))):
            head, first = pending.pop(0)
            project(head, first, span)

    allowed_back = [
        (pattern[0, back - 1] == 1) & (my_block >= back) for back in range(reach, 0, -1)
    ]
    chunks = head_size // 8

    def usable(query):
        return range(reach * steps + query + 1)

    def attend(head, queries):
        def tile(kind, chunk, key):
            row = kind * head_size + chunk * 8
            return projected[head, row : row + 8, key * zone_rows : (key + 1) * zone_rows]

        sums = {}
        for chunk in range(chunks):
            q_tiles = {q: tile(0, chunk, reach * steps + q) for q in queries}
            for key in usable(queries[-1]):
                k_tile = tile(1, chunk, key)
                for q in queries:
                    if key in usable(q):
                        term = q_tiles[q] * k_tile
                        sums[q, key] = term if chunk == 0 else sums[q, key] + term
        weights_of, scales = {}, {}
        for q in queries:
            scores = jnp.concatenate([row_sum(sums[q, key]) for key in usable(q)], axis=0)
            scores = scores * head_size ** (-0.5)
            row_id = lax.broadcasted_iota(jnp.int32, scores.shape, 0)
            allowed = row_id >= reach * steps
            for index, live in enumerate(allowed_back):
                inside = (row_id >= index * steps) & (row_id < (index + 1) * steps)
                allowed = allowed | (inside & live)
            masked = jnp.where(allowed, scores, -1e30)
            top = jnp.max(masked, axis=0, keepdims=True)
            expw = jnp.where(allowed, jnp.exp(masked - top), 0.0)
            scales[q] = jnp.broadcast_to(1.0 / row_sum(expw), (8, zone_rows))
            probs = expw.astype(BF16).astype(F32)
            for key in usable(q):
                weights_of[q, key] = jnp.broadcast_to(probs[key : key + 1, :], (8, zone_rows))
        for chunk in range(chunks):
            sums = {}
            for key in usable(queries[-1]):
                v_tile = tile(2, chunk, key)
                for q in queries:
                    if key in usable(q):
                        term = weights_of[q, key] * v_tile
                        sums[q] = term if key == 0 else sums[q] + term
            for q in queries:
                row = head * head_size + chunk * 8
                context[row : row + 8, q * zone_rows : (q + 1) * zone_rows] = sums[q] * scales[q]

    spans = key_count * zone_rows // span
    project_some(spans)
    pairs = range(0, steps, 2)
    for head in range(HEADS):
        for pair in pairs:
            project_some(-(-spans // len(pairs)))
            attend(head, range(pair, min(pair + 2, steps)))

    for step in range(steps):
        rows = slice(step * zone_rows, (step + 1) * zone_rows)
        context_out[rows, :] = context[:, rows].T.astype(BF16)


def project_kernel(place, states, context, w_attn, gain_mix, after_out, *refs):
    *outs, parts = refs
    steps, zone_rows, _ = states.shape
    zones, _, part = parts.shape
    my_zone = place[1]
    gain = gain_mix[...]
    for step in range(steps):
        rows = slice(step * zone_rows, (step + 1) * zone_rows)
        after = states[step].astype(F32) + jnp.dot(
            context[rows, :], w_attn[...], preferred_element_type=F32
        )
        after_out[rows, :] = after
        mixin = rms_scale(after, gain).astype(BF16)
        for index in range(zones):
            parts[index, rows, :] = mixin[:, index * part : (index + 1) * part]
    for index, step in enumerate((0,) + steps_over(zones)):
        outs[index][...] = parts[my_zone ^ step]


def mixing_kernel(steps, zones, place, neighbours, degree, mix, *refs):
    arrived, halves, (*outs, pair, items) = refs[:zones], refs[zones : zones + 2], refs[zones + 2 :]
    for index, value in enumerate(halves):
        pair[index] = value[...]
    _, slots, zone_rows, _ = mix.shape
    part = items.shape[-1]
    my_zone = place[1]
    group = 2 if part % LANES == 0 and steps % 2 == 0 else 1
    for index, step in enumerate((0,) + steps_over(zones)):
        items[my_zone ^ step] = arrived[index][...]

    for target, target_step in enumerate((0,) + steps_over(zones)):
        block = my_zone ^ target_step
        left = []
        for slot in range(slots):
            tile = mix[block, slot]
            left.append(jnp.where(degree[block] > slot, tile, jnp.zeros_like(tile)))
        left = jnp.concatenate(left, axis=1)
        for step in range(0, steps, group):
            right = []
            for slot in range(slots):
                source = neighbours[block, slot]
                right.append(
                    jnp.concatenate(
                        [
                            items[source, (step + index) * zone_rows : (step + index + 1) * zone_rows, :]
                            for index in range(group)
                        ],
                        axis=1,
                    )
                )
            result = jnp.dot(left, jnp.concatenate(right, axis=0), preferred_element_type=F32)
            for index in range(group):
                rows = slice((step + index) * zone_rows, (step + index + 1) * zone_rows)
                outs[target][rows, :] = result[:, index * part : (index + 1) * part].astype(BF16)


def slots_of(block):
    near = 2 + 2 * lax.rem(block, 2)
    return [lax.rem(block, SPREAD) ^ bits for bits in (0, near, 6 - near, 6)]


def fill_slots(zones, place, own_in, own_out, slots, pieces, w_in, w_out):
    my_zone = place[1]
    in_shard = own_in.shape[1]
    out_rows = own_out.shape[0] // SPREAD
    in_cols, width = own_in.shape[2], own_out.shape[1]
    own_rows = pl.ds(pl.multiple_of(my_zone * in_shard, in_shard), in_shard)
    own_out_rows = pl.ds(pl.multiple_of(my_zone * out_rows, out_rows), out_rows)
    for index, (slot, piece) in enumerate(zip(slots, pieces)):
        from_rows = pl.ds(pl.multiple_of(slot * out_rows, out_rows), out_rows)
        w_in[index, own_rows, :] = own_in[slot]
        w_out[index, own_out_rows, :] = own_out[from_rows, :]
        for step in range(1, zones):
            source = my_zone ^ step
            part = piece[step - 1]
            rows = pl.ds(pl.multiple_of(source * in_shard, in_shard), in_shard)
            w_in[index, rows, :] = part[:in_shard, :]
            rows = pl.ds(pl.multiple_of(source * out_rows, out_rows), out_rows)
            for fold in range(width // in_cols):
                low = in_shard + fold * out_rows
                w_out[index, rows, fold * in_cols : (fold + 1) * in_cols] = part[low : low + out_rows, :]


def order_kernel(zones, place, own_in, own_out, pair, far, swapped_pair, w_in, w_out):
    my_block = place[0]
    slots = slots_of(my_block) + slots_of(my_block ^ 1)[:2]
    pieces = [group.at[index] for group in (pair, far, swapped_pair) for index in range(2)]
    fill_slots(zones, place, own_in, own_out, slots, pieces, w_in, w_out)


def after_kernel(zones, place, after_attn, gain_ffn, ready, far, *refs):
    arrived, (after_mix, ffn_in, far_out, parts) = refs[:zones], refs[zones:]
    rows_all, width = after_attn.shape
    my_zone = place[1]
    far_out[...] = far[...]
    for index, step in enumerate((0,) + steps_over(zones)):
        parts[my_zone ^ step] = arrived[index][...]
    gain = gain_ffn[...]
    span = 128
    part = parts.shape[-1]
    for first in range(0, rows_all, span):
        rows = slice(first, first + span)
        for index in range(zones):
            cols = slice(index * part, (index + 1) * part)
            after_mix[rows, cols] = after_attn[rows, cols] + parts[index, rows, :].astype(F32)
        ffn_in[rows, :] = rms_scale(after_mix[rows, :], gain).astype(BF16)


def ffn_rows(ffn_in, w_in, w_out, total):
    for index in range(w_in.shape[0]):
        grown = jnp.dot(ffn_in, w_in[index], preferred_element_type=F32)
        grown = jax.nn.gelu(grown, approximate=True).astype(BF16)
        total = total + jnp.dot(grown, w_out[index], preferred_element_type=F32)
    return total


def ffn_kernel(after_mix, ffn_in, w_in, w_out, out):
    span = 256
    for first in range(0, after_mix.shape[0], span):
        rows = slice(first, first + span)
        out[rows, :] = ffn_rows(ffn_in[rows, :], w_in, w_out, after_mix[rows, :])


def last_kernel(zones, place, own_in, own_out, total, ffn_in, swapped_far, out, w_in, w_out):
    slots = slots_of(place[0] ^ 1)[2:]
    pieces = [swapped_far.at[index] for index in range(2)]
    fill_slots(zones, place, own_in, own_out, slots, pieces, w_in, w_out)
    span = 256
    for first in range(0, total.shape[0], span):
        rows = slice(first, first + span)
        out[rows, :] = ffn_rows(ffn_in[rows, :], w_in, w_out, total[rows, :]).astype(BF16)


def call(kernel, out_shape, scratch, smem, hbm, limit, args):
    spaces = {index: pltpu.SMEM for index in smem} | {index: pltpu.HBM for index in hbm}
    return pl.pallas_call(
        kernel,
        out_shape=out_shape,
        in_specs=[
            pl.BlockSpec(memory_space=spaces.get(index, pltpu.VMEM)) for index in range(len(args))
        ],
        out_specs=jax.tree.map(lambda _: pl.BlockSpec(memory_space=pltpu.VMEM), out_shape),
        scratch_shapes=scratch,
        cost_estimate=pl.CostEstimate(flops=0, bytes_accessed=0, transcendentals=0),
        compiler_params=pltpu.CompilerParams(vmem_limit_bytes=limit * MIB),
    )(*args)


def on_device(
    states,
    gain_attn,
    w_qkv,
    w_out_attn,
    pattern,
    gain_mix,
    neighbours,
    degree,
    mix,
    gain_ffn,
    w_in,
    w_out,
):
    steps, zone_rows, width = states.shape
    rows = steps * zone_rows
    reach = pattern.shape[1]
    zones = lax.axis_size("zone")
    my_block, my_zone = lax.axis_index("tm"), lax.axis_index("zone")
    place = jnp.stack([my_block, my_zone]).astype(jnp.int32)
    key_count = (reach + 1) * steps
    hidden = w_in.shape[1]
    in_cols = hidden // SPREAD
    out_rows = w_out.shape[0] // SPREAD
    part = width // zones
    exchanges = steps_over(zones)

    before = shifted(states, "tm", 2)
    first = lax.dynamic_slice_in_dim(
        jnp.concatenate([w_qkv, w_out_attn], axis=1), quarter_of(my_block) * width, width, axis=1
    )
    direct = [swapped(first, "zone", step) for step in exchanges]
    packed_rows = w_in.shape[0] + out_rows * (width // in_cols)
    own_in, packed = call(
        functools.partial(group_kernel, zones),
        (
            jax.ShapeDtypeStruct((SPREAD, w_in.shape[0], in_cols), BF16),
            jax.ShapeDtypeStruct((packed_rows, in_cols), BF16),
        ),
        [],
        (0,),
        (),
        4,
        [place, w_in, w_out],
    )
    beside = swapped(packed, "zone", 1)
    half_shape = jax.ShapeDtypeStruct((zones - 1, first.shape[0] // 2, width), BF16)
    direct, upper, lower, doubled, last = call(
        split_kernel,
        (
            jax.ShapeDtypeStruct((zones - 1,) + first.shape, BF16),
            half_shape,
            half_shape,
            jax.ShapeDtypeStruct((2,) + packed.shape, BF16),
            jax.ShapeDtypeStruct(states.shape, BF16),
        ),
        [],
        (0,),
        (),
        4,
        [place, packed, beside, states, before] + direct,
    )
    over = [crossed(value, "tm", 2, 4) for value in (upper, lower)]
    last = swapped(last, "tm", 1)
    pieces = [direct] + over + [swapped(value, "tm", 1) for value in [direct] + over]
    normed = call(
        norm_kernel,
        jax.ShapeDtypeStruct((key_count * zone_rows, width), BF16),
        [],
        (),
        (),
        4,
        [before, last, states, gain_attn.reshape(1, -1)],
    )
    bits = 2
    while 2 * bits < zones:
        doubled = jnp.concatenate([doubled, swapped(doubled, "zone", bits)], axis=0)
        bits *= 2
    context, w_attn = call(
        functools.partial(attention_kernel, zones, reach, steps),
        (
            jax.ShapeDtypeStruct((rows, width), BF16),
            jax.ShapeDtypeStruct((width, width), BF16),
        ),
        [
            pltpu.VMEM((4, width, width), BF16),
            pltpu.VMEM((3 * width, width), BF16),
            pltpu.VMEM((HEADS, 3 * (width // HEADS), key_count * zone_rows), F32),
            pltpu.VMEM((width, rows), F32),
            pltpu.SemaphoreType.DMA((4,)),
        ],
        (0, 1),
        (3, 4),
        22,
        [place, pattern, normed, w_qkv, w_out_attn] + pieces,
    )

    chunk = jax.ShapeDtypeStruct((rows, part), BF16)
    after_attn, *chunks = call(
        project_kernel,
        (jax.ShapeDtypeStruct((rows, width), F32),)
        + (chunk,) * zones,
        [pltpu.VMEM((zones, rows, part), BF16)],
        (0,),
        (),
        8,
        [place, states, context, w_attn, gain_mix.reshape(1, -1)],
    )
    across = call(
        stack_kernel,
        jax.ShapeDtypeStruct((zones - 1,) + packed.shape, BF16),
        [],
        (),
        (),
        4,
        [doubled, swapped(doubled, "zone", bits), after_attn],
    )
    nearest = crossed(across, "tm", 2, 4)

    arrived = [chunks[0]] + [
        swapped(value, "zone", step) for value, step in zip(chunks[1:], exchanges)
    ]

    *spatial, pair = call(
        functools.partial(mixing_kernel, steps, zones),
        (chunk,) * zones
        + (jax.ShapeDtypeStruct((2,) + across.shape, BF16),),
        [pltpu.VMEM((zones, rows, part), BF16)],
        (0, 1, 2),
        (),
        8,
        [place, neighbours, degree, mix] + arrived + [across, nearest],
    )
    far = crossed(pair, "tm", 4, 2)
    full_in, full_out = call(
        functools.partial(order_kernel, zones),
        (
            jax.ShapeDtypeStruct((6, width, in_cols), BF16),
            jax.ShapeDtypeStruct((6, in_cols, width), BF16),
        ),
        [],
        (0,),
        (),
        8,
        [place, own_in, w_out, pair, far, swapped(pair, "tm", 1)],
    )
    arrived = [spatial[0]] + [
        swapped(value, "zone", step) for value, step in zip(spatial[1:], exchanges)
    ]
    after_mix, ffn_in, far = call(
        functools.partial(after_kernel, zones),
        (
            jax.ShapeDtypeStruct((rows, width), F32),
            jax.ShapeDtypeStruct((rows, width), BF16),
            jax.ShapeDtypeStruct(far.shape, BF16),
        ),
        [pltpu.VMEM((zones, rows, part), BF16)],
        (0,),
        (),
        8,
        [place, after_attn, gain_ffn.reshape(1, -1), full_out, far] + arrived,
    )
    total = call(
        ffn_kernel,
        jax.ShapeDtypeStruct((rows, width), F32),
        [],
        (),
        (),
        8,
        [after_mix, ffn_in, full_in, full_out],
    )
    evolved = call(
        functools.partial(last_kernel, zones),
        jax.ShapeDtypeStruct((rows, width), BF16),
        [
            pltpu.VMEM((2, width, in_cols), BF16),
            pltpu.VMEM((2, in_cols, width), BF16),
        ],
        (0,),
        (),
        8,
        [place, own_in, w_out, total, ffn_in, swapped(far, "tm", 1)],
    )
    return evolved.reshape(steps, zone_rows, width)


def solution(mesh):
    return jax.shard_map(
        on_device,
        mesh=mesh,
        in_specs=(
            P("tm", "zone", None),
            P(),
            P("zone", None),
            P("zone", None),
            P("tm", None),
            P(),
            P(),
            P(),
            P(),
            P(),
            P("zone", None),
            P("zone", None),
        ),
        out_specs=P("tm", "zone", None),
        check_vma=False,
    )
```

```python
import functools

import jax
import jax.numpy as jnp
from jax import lax
from jax.experimental import pallas as pl
from jax.experimental.pallas import tpu as pltpu
from jax.sharding import PartitionSpec as P

HEADS = 4
SPREAD = 8
LANES = 128
F32 = jnp.float32
BF16 = jnp.bfloat16
MIB = 1024 * 1024


def shifted(value, axis, steps):
    count = lax.axis_size(axis)
    return lax.ppermute(value, axis, [(source, source + steps) for source in range(count - steps)])


def swapped(value, axis, bits):
    count = lax.axis_size(axis)
    return lax.ppermute(value, axis, [(source, source ^ bits) for source in range(count)])


def crossed(value, axis, even_bits, odd_bits):
    count = lax.axis_size(axis)
    pairs = [(source, source ^ (odd_bits if source % 2 else even_bits)) for source in range(count)]
    return lax.ppermute(value, axis, pairs)


def steps_over(count):
    half = count // 2
    return tuple(range(half, count)) + tuple(range(1, half))


def rms_scale(values, gain):
    mean_sq = jnp.mean(values * values, axis=-1, keepdims=True)
    return values * lax.rsqrt(mean_sq + 1e-06) * gain


def quarter_of(block):
    core = lax.rem(block, 2)
    return (1 - core) * lax.rem(lax.div(block, 2), 2) + core * (2 + lax.rem(lax.div(block, 4), 2))


def row_sum(value):
    return jnp.sum(value, axis=0, keepdims=True)


def norm_kernel(*refs):
    blocks, (gain_attn, normed) = refs[:-2], refs[-2:]
    steps, zone_rows, _ = blocks[0].shape
    gain = gain_attn[...]
    for index, block in enumerate(blocks):
        for step in range(steps):
            row = (index * steps + step) * zone_rows
            normed[row : row + zone_rows, :] = rms_scale(block[step].astype(F32), gain).astype(BF16)


def group_kernel(zones, place, w_in, w_out, own_in, packed):
    in_shard, hidden = w_in.shape
    out_rows = w_out.shape[0] // SPREAD
    in_cols = hidden // SPREAD
    width = w_out.shape[1]
    for index in range(SPREAD):
        for source in range(zones):
            low = (source * SPREAD + index) * out_rows
            to = slice(source * out_rows, (source + 1) * out_rows)
            own_in[index, :, to] = w_in[:, low : low + out_rows]
    slot = lax.rem(place[0], SPREAD)
    packed[:in_shard, :] = own_in[slot]
    rows = pl.ds(pl.multiple_of(slot * out_rows, out_rows), out_rows)
    for fold in range(width // in_cols):
        low = in_shard + fold * out_rows
        packed[low : low + out_rows, :] = w_out[rows, fold * in_cols : (fold + 1) * in_cols]


def split_kernel(place, packed, beside, states, before, *refs):
    arrived, (direct, upper, lower, doubled, last) = refs[:-5], refs[-5:]
    half = upper.shape[1]
    for index, piece in enumerate(arrived):
        direct[index] = piece[...]
        upper[index] = piece[:half, :]
        lower[index] = piece[half:, :]
    doubled[0] = packed[...]
    doubled[1] = beside[...]
    last[...] = jnp.where(lax.rem(place[0], 2) == 1, before[...], states[...])


def stack_kernel(doubled, arrived, *refs):
    out = refs[-1]
    near = doubled.shape[0]
    out[: near - 1] = doubled[1:]
    out[near - 1 :] = arrived[...]


def attention_kernel(zones, reach, steps, place, pattern, normed, own_qkv, own_attn, *refs):
    pieces, (context_out, attn_out, weights, w_turned, projected, context, sems) = refs[:-7], refs[-7:]
    key_count = (reach + 1) * steps
    zone_rows = normed.shape[0] // key_count
    width = normed.shape[1]
    head_size = width // HEADS
    my_block, my_zone = place[0], place[1]
    shard = own_qkv.shape[0]

    own_rows = pl.ds(pl.multiple_of(my_zone * shard, shard), shard)
    copies = [
        pltpu.make_async_copy(
            own_qkv.at[:, index * width : (index + 1) * width],
            weights.at[index, own_rows, :],
            sems.at[index],
        )
        for index in range(3)
    ]
    copies.append(pltpu.make_async_copy(own_attn, weights.at[3, own_rows, :], sems.at[3]))
    for copy in copies:
        copy.start()
    half = shard // 2
    mine, other = quarter_of(my_block), quarter_of(my_block ^ 1)
    for place_in, step in enumerate(steps_over(zones)):
        start = (my_zone ^ step) * shard
        for piece, quarter, low in zip(
            pieces, (mine, mine ^ 1, mine ^ 1, other, other ^ 1, other ^ 1), (0, 0, half, 0, 0, half)
        ):
            rows = pl.ds(pl.multiple_of(start + low, half), piece.shape[1])
            weights[quarter, rows, :] = piece[place_in]
    for copy in copies:
        copy.wait()
    attn_out[...] = weights[3]
    group = 3 * head_size
    def turn(head):
        for kind in range(3):
            rows = slice(head * group + kind * head_size, head * group + (kind + 1) * head_size)
            w_turned[rows, :] = weights[kind, :, head * head_size : (head + 1) * head_size].T

    def project(head, first, span):
        skip = 0 if first >= reach * steps * zone_rows else head_size
        projected[head, skip:, first : first + span] = lax.dot_general(
            w_turned[head * group + skip : (head + 1) * group, :],
            normed[first : first + span, :],
            (((1,), (1,)), ((), ())),
            preferred_element_type=F32,
        )

    span = 2 * zone_rows
    pending = [(head, first) for head in range(HEADS) for first in range(0, key_count * zone_rows, span)]

    def project_some(count):
        for _ in range(min(count, len(pending))):
            head, first = pending.pop(0)
            if first == 0:
                turn(head)
            project(head, first, span)

    allowed_back = [
        (pattern[0, back - 1] == 1) & (my_block >= back) for back in range(reach, 0, -1)
    ]
    chunks = head_size // 8

    def usable(query):
        return range(reach * steps + query + 1)

    def attend(head, queries):
        def tile(kind, chunk, key):
            row = kind * head_size + chunk * 8
            return projected[head, row : row + 8, key * zone_rows : (key + 1) * zone_rows]

        sums = {}
        for chunk in range(chunks):
            q_tiles = {q: tile(0, chunk, reach * steps + q) for q in queries}
            for key in usable(queries[-1]):
                k_tile = tile(1, chunk, key)
                for q in queries:
                    if key in usable(q):
                        term = q_tiles[q] * k_tile
                        sums[q, key] = term if chunk == 0 else sums[q, key] + term
        weights_of, scales = {}, {}
        for q in queries:
            scores = jnp.concatenate([row_sum(sums[q, key]) for key in usable(q)], axis=0)
            scores = scores * head_size ** (-0.5)
            row_id = lax.broadcasted_iota(jnp.int32, scores.shape, 0)
            allowed = row_id >= reach * steps
            for index, live in enumerate(allowed_back):
                inside = (row_id >= index * steps) & (row_id < (index + 1) * steps)
                allowed = allowed | (inside & live)
            masked = jnp.where(allowed, scores, -1e30)
            top = jnp.max(masked, axis=0, keepdims=True)
            expw = jnp.where(allowed, jnp.exp(masked - top), 0.0)
            scales[q] = jnp.broadcast_to(1.0 / row_sum(expw), (8, zone_rows))
            probs = expw.astype(BF16).astype(F32)
            for key in usable(q):
                weights_of[q, key] = jnp.broadcast_to(probs[key : key + 1, :], (8, zone_rows))
        for chunk in range(chunks):
            sums = {}
            for key in usable(queries[-1]):
                v_tile = tile(2, chunk, key)
                for q in queries:
                    if key in usable(q):
                        term = weights_of[q, key] * v_tile
                        sums[q] = term if key == 0 else sums[q] + term
            for q in queries:
                row = head * head_size + chunk * 8
                context[row : row + 8, q * zone_rows : (q + 1) * zone_rows] = sums[q] * scales[q]

    spans = key_count * zone_rows // span
    project_some(spans)
    pairs = range(0, steps, 2)
    for head in range(HEADS):
        for pair in pairs:
            project_some(-(-spans // len(pairs)))
            attend(head, range(pair, min(pair + 2, steps)))

    for step in range(steps):
        rows = slice(step * zone_rows, (step + 1) * zone_rows)
        context_out[rows, :] = context[:, rows].T.astype(BF16)


def project_kernel(place, states, context, w_attn, gain_mix, after_out, *refs):
    *outs, parts = refs
    steps, zone_rows, _ = states.shape
    zones, _, part = parts.shape
    my_zone = place[1]
    gain = gain_mix[...]
    for step in range(steps):
        rows = slice(step * zone_rows, (step + 1) * zone_rows)
        after = states[step].astype(F32) + jnp.dot(
            context[rows, :], w_attn[...], preferred_element_type=F32
        )
        after_out[rows, :] = after
        mixin = rms_scale(after, gain).astype(BF16)
        for index in range(zones):
            parts[index, rows, :] = mixin[:, index * part : (index + 1) * part]
    for index, step in enumerate((0,) + steps_over(zones)):
        outs[index][...] = parts[my_zone ^ step]


def mixing_kernel(steps, zones, place, neighbours, degree, mix, *refs):
    arrived, halves, (*outs, pair, items) = refs[:zones], refs[zones : zones + 2], refs[zones + 2 :]
    for index, value in enumerate(halves):
        pair[index] = value[...]
    _, slots, zone_rows, _ = mix.shape
    part = items.shape[-1]
    my_zone = place[1]
    group = 2 if part % LANES == 0 and steps % 2 == 0 else 1
    for index, step in enumerate((0,) + steps_over(zones)):
        items[my_zone ^ step] = arrived[index][...]

    for target, target_step in enumerate((0,) + steps_over(zones)):
        block = my_zone ^ target_step
        left = []
        for slot in range(slots):
            tile = mix[block, slot]
            left.append(jnp.where(degree[block] > slot, tile, jnp.zeros_like(tile)))
        left = jnp.concatenate(left, axis=1)
        for step in range(0, steps, group):
            right = []
            for slot in range(slots):
                source = neighbours[block, slot]
                right.append(
                    jnp.concatenate(
                        [
                            items[source, (step + index) * zone_rows : (step + index + 1) * zone_rows, :]
                            for index in range(group)
                        ],
                        axis=1,
                    )
                )
            result = jnp.dot(left, jnp.concatenate(right, axis=0), preferred_element_type=F32)
            for index in range(group):
                rows = slice((step + index) * zone_rows, (step + index + 1) * zone_rows)
                outs[target][rows, :] = result[:, index * part : (index + 1) * part].astype(BF16)


def slots_of(block):
    near = 2 + 2 * lax.rem(block, 2)
    return [lax.rem(block, SPREAD) ^ bits for bits in (0, near, 6 - near, 6)]


def fill_slots(zones, place, own_in, own_out, slots, pieces, w_in, w_out):
    my_zone = place[1]
    in_shard = own_in.shape[1]
    out_rows = own_out.shape[0] // SPREAD
    in_cols, width = own_in.shape[2], own_out.shape[1]
    own_rows = pl.ds(pl.multiple_of(my_zone * in_shard, in_shard), in_shard)
    own_out_rows = pl.ds(pl.multiple_of(my_zone * out_rows, out_rows), out_rows)
    for index, (slot, piece) in enumerate(zip(slots, pieces)):
        from_rows = pl.ds(pl.multiple_of(slot * out_rows, out_rows), out_rows)
        w_in[index, own_rows, :] = own_in[slot]
        w_out[index, own_out_rows, :] = own_out[from_rows, :]
        for step in range(1, zones):
            source = my_zone ^ step
            part = piece[step - 1]
            rows = pl.ds(pl.multiple_of(source * in_shard, in_shard), in_shard)
            w_in[index, rows, :] = part[:in_shard, :]
            rows = pl.ds(pl.multiple_of(source * out_rows, out_rows), out_rows)
            for fold in range(width // in_cols):
                low = in_shard + fold * out_rows
                w_out[index, rows, fold * in_cols : (fold + 1) * in_cols] = part[low : low + out_rows, :]


def order_kernel(zones, place, own_in, own_out, pair, far, swapped_pair, w_in, w_out):
    my_block = place[0]
    slots = slots_of(my_block) + slots_of(my_block ^ 1)[:2]
    pieces = [group.at[index] for group in (pair, far, swapped_pair) for index in range(2)]
    fill_slots(zones, place, own_in, own_out, slots, pieces, w_in, w_out)


def after_kernel(zones, place, after_attn, gain_ffn, ready, far, *refs):
    arrived, (after_mix, ffn_in, far_out, parts) = refs[:zones], refs[zones:]
    rows_all, width = after_attn.shape
    my_zone = place[1]
    far_out[...] = far[...]
    for index, step in enumerate((0,) + steps_over(zones)):
        parts[my_zone ^ step] = arrived[index][...]
    gain = gain_ffn[...]
    span = 128
    part = parts.shape[-1]
    for first in range(0, rows_all, span):
        rows = slice(first, first + span)
        for index in range(zones):
            cols = slice(index * part, (index + 1) * part)
            after_mix[rows, cols] = after_attn[rows, cols] + parts[index, rows, :].astype(F32)
        ffn_in[rows, :] = rms_scale(after_mix[rows, :], gain).astype(BF16)


def ffn_rows(ffn_in, w_in, w_out, total):
    for index in range(w_in.shape[0]):
        grown = jnp.dot(ffn_in, w_in[index], preferred_element_type=F32)
        grown = jax.nn.gelu(grown, approximate=True).astype(BF16)
        total = total + jnp.dot(grown, w_out[index], preferred_element_type=F32)
    return total


def ffn_kernel(after_mix, ffn_in, w_in, w_out, out):
    span = 256
    for first in range(0, after_mix.shape[0], span):
        rows = slice(first, first + span)
        out[rows, :] = ffn_rows(ffn_in[rows, :], w_in, w_out, after_mix[rows, :])


def last_kernel(zones, place, own_in, own_out, total, ffn_in, swapped_far, out, w_in, w_out, rows_out, sems):
    slots = slots_of(place[0] ^ 1)[2:]
    pieces = [swapped_far.at[index] for index in range(2)]
    fill_slots(zones, place, own_in, own_out, slots, pieces, w_in, w_out)
    span = total.shape[0] // sems.shape[0]
    copies = []
    for index in range(sems.shape[0]):
        rows = slice(index * span, (index + 1) * span)
        rows_out[rows, :] = ffn_rows(ffn_in[rows, :], w_in, w_out, total[rows, :]).astype(BF16)
        copies.append(pltpu.make_async_copy(rows_out.at[rows, :], out.at[rows, :], sems.at[index]))
        copies[-1].start()
    for copy in copies:
        copy.wait()


def call(kernel, out_shape, scratch, smem, hbm, limit, args, out_space=pltpu.VMEM):
    spaces = {index: pltpu.SMEM for index in smem} | {index: pltpu.HBM for index in hbm}
    return pl.pallas_call(
        kernel,
        out_shape=out_shape,
        in_specs=[
            pl.BlockSpec(memory_space=spaces.get(index, pltpu.VMEM)) for index in range(len(args))
        ],
        out_specs=jax.tree.map(lambda _: pl.BlockSpec(memory_space=out_space), out_shape),
        scratch_shapes=scratch,
        cost_estimate=pl.CostEstimate(flops=0, bytes_accessed=0, transcendentals=0),
        compiler_params=pltpu.CompilerParams(vmem_limit_bytes=limit * MIB),
    )(*args)


def on_device(
    states,
    gain_attn,
    w_qkv,
    w_out_attn,
    pattern,
    gain_mix,
    neighbours,
    degree,
    mix,
    gain_ffn,
    w_in,
    w_out,
):
    steps, zone_rows, width = states.shape
    rows = steps * zone_rows
    reach = pattern.shape[1]
    zones = lax.axis_size("zone")
    my_block, my_zone = lax.axis_index("tm"), lax.axis_index("zone")
    place = jnp.stack([my_block, my_zone]).astype(jnp.int32)
    key_count = (reach + 1) * steps
    hidden = w_in.shape[1]
    in_cols = hidden // SPREAD
    out_rows = w_out.shape[0] // SPREAD
    part = width // zones
    exchanges = steps_over(zones)

    before = shifted(states, "tm", 2)
    first = lax.dynamic_slice_in_dim(
        jnp.concatenate([w_qkv, w_out_attn], axis=1), quarter_of(my_block) * width, width, axis=1
    )
    direct = [swapped(first, "zone", step) for step in exchanges]
    packed_rows = w_in.shape[0] + out_rows * (width // in_cols)
    own_in, packed = call(
        functools.partial(group_kernel, zones),
        (
            jax.ShapeDtypeStruct((SPREAD, w_in.shape[0], in_cols), BF16),
            jax.ShapeDtypeStruct((packed_rows, in_cols), BF16),
        ),
        [],
        (0,),
        (),
        4,
        [place, w_in, w_out],
    )
    beside = swapped(packed, "zone", 1)
    half_shape = jax.ShapeDtypeStruct((zones - 1, first.shape[0] // 2, width), BF16)
    direct, upper, lower, doubled, last = call(
        split_kernel,
        (
            jax.ShapeDtypeStruct((zones - 1,) + first.shape, BF16),
            half_shape,
            half_shape,
            jax.ShapeDtypeStruct((2,) + packed.shape, BF16),
            jax.ShapeDtypeStruct(states.shape, BF16),
        ),
        [],
        (0,),
        (),
        4,
        [place, packed, beside, states, before] + direct,
    )
    over = [crossed(value, "tm", 2, 4) for value in (upper, lower)]
    last = swapped(last, "tm", 1)
    pieces = [direct] + over + [swapped(value, "tm", 1) for value in [direct] + over]
    normed = call(
        norm_kernel,
        jax.ShapeDtypeStruct((key_count * zone_rows, width), BF16),
        [],
        (),
        (),
        4,
        [before, last, states, gain_attn.reshape(1, -1)],
    )
    bits = 2
    while 2 * bits < zones:
        doubled = jnp.concatenate([doubled, swapped(doubled, "zone", bits)], axis=0)
        bits *= 2
    context, w_attn = call(
        functools.partial(attention_kernel, zones, reach, steps),
        (
            jax.ShapeDtypeStruct((rows, width), BF16),
            jax.ShapeDtypeStruct((width, width), BF16),
        ),
        [
            pltpu.VMEM((4, width, width), BF16),
            pltpu.VMEM((3 * width, width), BF16),
            pltpu.VMEM((HEADS, 3 * (width // HEADS), key_count * zone_rows), F32),
            pltpu.VMEM((width, rows), F32),
            pltpu.SemaphoreType.DMA((4,)),
        ],
        (0, 1),
        (3, 4),
        22,
        [place, pattern, normed, w_qkv, w_out_attn] + pieces,
    )

    chunk = jax.ShapeDtypeStruct((rows, part), BF16)
    after_attn, *chunks = call(
        project_kernel,
        (jax.ShapeDtypeStruct((rows, width), F32),)
        + (chunk,) * zones,
        [pltpu.VMEM((zones, rows, part), BF16)],
        (0,),
        (),
        8,
        [place, states, context, w_attn, gain_mix.reshape(1, -1)],
    )
    across = call(
        stack_kernel,
        jax.ShapeDtypeStruct((zones - 1,) + packed.shape, BF16),
        [],
        (),
        (),
        4,
        [doubled, swapped(doubled, "zone", bits), after_attn],
    )
    nearest = crossed(across, "tm", 2, 4)

    arrived = [chunks[0]] + [
        swapped(value, "zone", step) for value, step in zip(chunks[1:], exchanges)
    ]

    *spatial, pair = call(
        functools.partial(mixing_kernel, steps, zones),
        (chunk,) * zones
        + (jax.ShapeDtypeStruct((2,) + across.shape, BF16),),
        [pltpu.VMEM((zones, rows, part), BF16)],
        (0, 1, 2),
        (),
        8,
        [place, neighbours, degree, mix] + arrived + [across, nearest],
    )
    far = crossed(pair, "tm", 4, 2)
    full_in, full_out = call(
        functools.partial(order_kernel, zones),
        (
            jax.ShapeDtypeStruct((6, width, in_cols), BF16),
            jax.ShapeDtypeStruct((6, in_cols, width), BF16),
        ),
        [],
        (0,),
        (),
        8,
        [place, own_in, w_out, pair, far, swapped(pair, "tm", 1)],
    )
    arrived = [spatial[0]] + [
        swapped(value, "zone", step) for value, step in zip(spatial[1:], exchanges)
    ]
    after_mix, ffn_in, far = call(
        functools.partial(after_kernel, zones),
        (
            jax.ShapeDtypeStruct((rows, width), F32),
            jax.ShapeDtypeStruct((rows, width), BF16),
            jax.ShapeDtypeStruct(far.shape, BF16),
        ),
        [pltpu.VMEM((zones, rows, part), BF16)],
        (0,),
        (),
        8,
        [place, after_attn, gain_ffn.reshape(1, -1), full_out, far] + arrived,
    )
    total = call(
        ffn_kernel,
        jax.ShapeDtypeStruct((rows, width), F32),
        [],
        (),
        (),
        8,
        [after_mix, ffn_in, full_in, full_out],
    )
    evolved = call(
        functools.partial(last_kernel, zones),
        jax.ShapeDtypeStruct((rows, width), BF16),
        [
            pltpu.VMEM((2, width, in_cols), BF16),
            pltpu.VMEM((2, in_cols, width), BF16),
            pltpu.VMEM((rows, width), BF16),
            pltpu.SemaphoreType.DMA((4,)),
        ],
        (0,),
        (),
        8,
        [place, own_in, w_out, total, ffn_in, swapped(far, "tm", 1)],
        pl.ANY,
    )
    return evolved.reshape(steps, zone_rows, width)


def solution(mesh):
    return jax.shard_map(
        on_device,
        mesh=mesh,
        in_specs=(
            P("tm", "zone", None),
            P(),
            P("zone", None),
            P("zone", None),
            P("tm", None),
            P(),
            P(),
            P(),
            P(),
            P(),
            P("zone", None),
            P("zone", None),
        ),
        out_specs=P("tm", "zone", None),
        check_vma=False,
    )
```

```python
import functools

import jax
import jax.numpy as jnp
from jax import lax
from jax.experimental import pallas as pl
from jax.experimental.pallas import tpu as pltpu
from jax.sharding import PartitionSpec as P

HEADS = 4
SPREAD = 8
LANES = 128
F32 = jnp.float32
BF16 = jnp.bfloat16
MIB = 1024 * 1024


def shifted(value, axis, steps):
    count = lax.axis_size(axis)
    return lax.ppermute(value, axis, [(source, source + steps) for source in range(count - steps)])


def swapped(value, axis, bits):
    count = lax.axis_size(axis)
    return lax.ppermute(value, axis, [(source, source ^ bits) for source in range(count)])


def crossed(value, axis, even_bits, odd_bits):
    count = lax.axis_size(axis)
    pairs = [(source, source ^ (odd_bits if source % 2 else even_bits)) for source in range(count)]
    return lax.ppermute(value, axis, pairs)


def steps_over(count):
    half = count // 2
    return tuple(range(half, count)) + tuple(range(1, half))


def rms_scale(values, gain):
    mean_sq = jnp.mean(values * values, axis=-1, keepdims=True)
    return values * lax.rsqrt(mean_sq + 1e-06) * gain


def quarter_of(block):
    core = lax.rem(block, 2)
    return (1 - core) * lax.rem(lax.div(block, 2), 2) + core * (2 + lax.rem(lax.div(block, 4), 2))


def row_sum(value):
    return jnp.sum(value, axis=0, keepdims=True)


def norm_kernel(*refs):
    blocks, (gain_attn, normed) = refs[:-2], refs[-2:]
    steps, zone_rows, _ = blocks[0].shape
    gain = gain_attn[...]
    for index, block in enumerate(blocks):
        for step in range(steps):
            row = (index * steps + step) * zone_rows
            normed[row : row + zone_rows, :] = rms_scale(block[step].astype(F32), gain).astype(BF16)


def group_kernel(zones, place, w_in, w_out, own_in, packed):
    in_shard, hidden = w_in.shape
    out_rows = w_out.shape[0] // SPREAD
    in_cols = hidden // SPREAD
    width = w_out.shape[1]
    for index in range(SPREAD):
        for source in range(zones):
            low = (source * SPREAD + index) * out_rows
            to = slice(source * out_rows, (source + 1) * out_rows)
            own_in[index, :, to] = w_in[:, low : low + out_rows]
    slot = lax.rem(place[0], SPREAD)
    packed[:in_shard, :] = own_in[slot]
    rows = pl.ds(pl.multiple_of(slot * out_rows, out_rows), out_rows)
    for fold in range(width // in_cols):
        low = in_shard + fold * out_rows
        packed[low : low + out_rows, :] = w_out[rows, fold * in_cols : (fold + 1) * in_cols]


def split_kernel(place, packed, beside, states, before, *refs):
    arrived, (direct, upper, lower, doubled, last) = refs[:-5], refs[-5:]
    half = upper.shape[1]
    for index, piece in enumerate(arrived):
        direct[index] = piece[...]
        upper[index] = piece[:half, :]
        lower[index] = piece[half:, :]
    doubled[0] = packed[...]
    doubled[1] = beside[...]
    last[...] = jnp.where(lax.rem(place[0], 2) == 1, before[...], states[...])


def stack_kernel(doubled, arrived, *refs):
    out = refs[-1]
    near = doubled.shape[0]
    out[: near - 1] = doubled[1:]
    out[near - 1 :] = arrived[...]


def attention_kernel(zones, reach, steps, place, pattern, normed, own_qkv, own_attn, *refs):
    pieces, (context_out, attn_out, weights, w_turned, projected, context, sems) = refs[:-7], refs[-7:]
    key_count = (reach + 1) * steps
    zone_rows = normed.shape[0] // key_count
    width = normed.shape[1]
    head_size = width // HEADS
    my_block, my_zone = place[0], place[1]
    shard = own_qkv.shape[0]

    own_rows = pl.ds(pl.multiple_of(my_zone * shard, shard), shard)
    copies = [
        pltpu.make_async_copy(
            own_qkv.at[:, index * width : (index + 1) * width],
            weights.at[index, own_rows, :],
            sems.at[index],
        )
        for index in range(3)
    ]
    copies.append(pltpu.make_async_copy(own_attn, weights.at[3, own_rows, :], sems.at[3]))
    for copy in copies:
        copy.start()
    half = shard // 2
    mine, other = quarter_of(my_block), quarter_of(my_block ^ 1)
    for place_in, step in enumerate(steps_over(zones)):
        start = (my_zone ^ step) * shard
        for piece, quarter, low in zip(
            pieces, (mine, mine ^ 1, mine ^ 1, other, other ^ 1, other ^ 1), (0, 0, half, 0, 0, half)
        ):
            rows = pl.ds(pl.multiple_of(start + low, half), piece.shape[1])
            weights[quarter, rows, :] = piece[place_in]
    for copy in copies:
        copy.wait()
    attn_out[...] = weights[3]
    group = 3 * head_size
    def turn(head):
        for kind in range(3):
            rows = slice(head * group + kind * head_size, head * group + (kind + 1) * head_size)
            w_turned[rows, :] = weights[kind, :, head * head_size : (head + 1) * head_size].T

    def project(head, first, span):
        skip = 0 if first >= reach * steps * zone_rows else head_size
        projected[head, skip:, first : first + span] = lax.dot_general(
            w_turned[head * group + skip : (head + 1) * group, :],
            normed[first : first + span, :],
            (((1,), (1,)), ((), ())),
            preferred_element_type=F32,
        )

    span = 2 * zone_rows
    pending = [(head, first) for head in range(HEADS) for first in range(0, key_count * zone_rows, span)]

    def project_some(count):
        for _ in range(min(count, len(pending))):
            head, first = pending.pop(0)
            if first == 0:
                turn(head)
            project(head, first, span)

    allowed_back = [
        (pattern[0, back - 1] == 1) & (my_block >= back) for back in range(reach, 0, -1)
    ]
    chunks = head_size // 8

    def usable(query):
        return range(reach * steps + query + 1)

    def attend(head, queries):
        def tile(kind, chunk, key):
            row = kind * head_size + chunk * 8
            return projected[head, row : row + 8, key * zone_rows : (key + 1) * zone_rows]

        sums = {}
        for chunk in range(chunks):
            q_tiles = {q: tile(0, chunk, reach * steps + q) for q in queries}
            for key in usable(queries[-1]):
                k_tile = tile(1, chunk, key)
                for q in queries:
                    if key in usable(q):
                        term = q_tiles[q] * k_tile
                        sums[q, key] = term if chunk == 0 else sums[q, key] + term
        weights_of, scales = {}, {}
        for q in queries:
            scores = jnp.concatenate([row_sum(sums[q, key]) for key in usable(q)], axis=0)
            scores = scores * head_size ** (-0.5)
            row_id = lax.broadcasted_iota(jnp.int32, scores.shape, 0)
            allowed = row_id >= reach * steps
            for index, live in enumerate(allowed_back):
                inside = (row_id >= index * steps) & (row_id < (index + 1) * steps)
                allowed = allowed | (inside & live)
            masked = jnp.where(allowed, scores, -1e30)
            top = jnp.max(masked, axis=0, keepdims=True)
            expw = jnp.where(allowed, jnp.exp(masked - top), 0.0)
            scales[q] = jnp.broadcast_to(1.0 / row_sum(expw), (8, zone_rows))
            probs = expw.astype(BF16).astype(F32)
            for key in usable(q):
                weights_of[q, key] = jnp.broadcast_to(probs[key : key + 1, :], (8, zone_rows))
        for chunk in range(chunks):
            sums = {}
            for key in usable(queries[-1]):
                v_tile = tile(2, chunk, key)
                for q in queries:
                    if key in usable(q):
                        term = weights_of[q, key] * v_tile
                        sums[q] = term if key == 0 else sums[q] + term
            for q in queries:
                row = head * head_size + chunk * 8
                context[row : row + 8, q * zone_rows : (q + 1) * zone_rows] = sums[q] * scales[q]

    spans = key_count * zone_rows // span
    project_some(spans)
    pairs = range(0, steps, 2)
    for head in range(HEADS):
        for pair in pairs:
            project_some(-(-spans // len(pairs)))
            attend(head, range(pair, min(pair + 2, steps)))

    for step in range(steps):
        rows = slice(step * zone_rows, (step + 1) * zone_rows)
        context_out[rows, :] = context[:, rows].T.astype(BF16)


def project_kernel(place, states, context, w_attn, gain_mix, after_out, *refs):
    *outs, parts = refs
    steps, zone_rows, _ = states.shape
    zones, _, part = parts.shape
    my_zone = place[1]
    gain = gain_mix[...]
    for step in range(steps):
        rows = slice(step * zone_rows, (step + 1) * zone_rows)
        after = states[step].astype(F32) + jnp.dot(
            context[rows, :], w_attn[...], preferred_element_type=F32
        )
        after_out[rows, :] = after
        mixin = rms_scale(after, gain).astype(BF16)
        for index in range(zones):
            parts[index, rows, :] = mixin[:, index * part : (index + 1) * part]
    for index, step in enumerate((0,) + steps_over(zones)):
        outs[index][...] = parts[my_zone ^ step]


def mixing_kernel(steps, zones, place, neighbours, degree, mix, *refs):
    arrived, halves, (*outs, pair, items) = refs[:zones], refs[zones : zones + 2], refs[zones + 2 :]
    for index, value in enumerate(halves):
        pair[index] = value[...]
    _, slots, zone_rows, _ = mix.shape
    part = items.shape[-1]
    my_zone = place[1]
    group = 2 if part % LANES == 0 and steps % 2 == 0 else 1
    for index, step in enumerate((0,) + steps_over(zones)):
        items[my_zone ^ step] = arrived[index][...]

    for target, target_step in enumerate((0,) + steps_over(zones)):
        block = my_zone ^ target_step
        left = []
        for slot in range(slots):
            tile = mix[block, slot]
            left.append(jnp.where(degree[block] > slot, tile, jnp.zeros_like(tile)))
        left = jnp.concatenate(left, axis=1)
        for step in range(0, steps, group):
            right = []
            for slot in range(slots):
                source = neighbours[block, slot]
                right.append(
                    jnp.concatenate(
                        [
                            items[source, (step + index) * zone_rows : (step + index + 1) * zone_rows, :]
                            for index in range(group)
                        ],
                        axis=1,
                    )
                )
            result = jnp.dot(left, jnp.concatenate(right, axis=0), preferred_element_type=F32)
            for index in range(group):
                rows = slice((step + index) * zone_rows, (step + index + 1) * zone_rows)
                outs[target][rows, :] = result[:, index * part : (index + 1) * part].astype(BF16)


def slots_of(block):
    near = 2 + 2 * lax.rem(block, 2)
    return [lax.rem(block, SPREAD) ^ bits for bits in (0, near, 6 - near, 6)]


def fill_slots(zones, place, own_in, own_out, slots, pieces, w_in, w_out):
    my_zone = place[1]
    in_shard = own_in.shape[1]
    out_rows = own_out.shape[0] // SPREAD
    in_cols, width = own_in.shape[2], own_out.shape[1]
    own_rows = pl.ds(pl.multiple_of(my_zone * in_shard, in_shard), in_shard)
    own_out_rows = pl.ds(pl.multiple_of(my_zone * out_rows, out_rows), out_rows)
    for index, (slot, piece) in enumerate(zip(slots, pieces)):
        from_rows = pl.ds(pl.multiple_of(slot * out_rows, out_rows), out_rows)
        w_in[index, own_rows, :] = own_in[slot]
        w_out[index, own_out_rows, :] = own_out[from_rows, :]
        for step in range(1, zones):
            source = my_zone ^ step
            part = piece[step - 1]
            rows = pl.ds(pl.multiple_of(source * in_shard, in_shard), in_shard)
            w_in[index, rows, :] = part[:in_shard, :]
            rows = pl.ds(pl.multiple_of(source * out_rows, out_rows), out_rows)
            for fold in range(width // in_cols):
                low = in_shard + fold * out_rows
                w_out[index, rows, fold * in_cols : (fold + 1) * in_cols] = part[low : low + out_rows, :]


def order_kernel(zones, place, own_in, own_out, pair, far, swapped_pair, w_in, w_out):
    my_block = place[0]
    slots = slots_of(my_block) + slots_of(my_block ^ 1)[:2]
    pieces = [group.at[index] for group in (pair, far, swapped_pair) for index in range(2)]
    fill_slots(zones, place, own_in, own_out, slots, pieces, w_in, w_out)


def after_kernel(zones, place, after_attn, gain_ffn, ready, far, *refs):
    arrived, (after_mix, ffn_in, far_out, parts) = refs[:zones], refs[zones:]
    rows_all, width = after_attn.shape
    my_zone = place[1]
    far_out[...] = far[...]
    for index, step in enumerate((0,) + steps_over(zones)):
        parts[my_zone ^ step] = arrived[index][...]
    gain = gain_ffn[...]
    span = 128
    part = parts.shape[-1]
    for first in range(0, rows_all, span):
        rows = slice(first, first + span)
        for index in range(zones):
            cols = slice(index * part, (index + 1) * part)
            after_mix[rows, cols] = after_attn[rows, cols] + parts[index, rows, :].astype(F32)
        ffn_in[rows, :] = rms_scale(after_mix[rows, :], gain).astype(BF16)


def grow(ffn_in, w_in, hidden):
    in_cols = w_in.shape[2]
    for index in range(w_in.shape[0]):
        grown = jnp.dot(ffn_in[...], w_in[index], preferred_element_type=F32)
        hidden[:, index * in_cols : (index + 1) * in_cols] = jax.nn.gelu(
            grown, approximate=True
        ).astype(BF16)


def ffn_kernel(after_mix, ffn_in, w_in, w_out, out, hidden):
    grow(ffn_in, w_in, hidden)
    weights = w_out[...].reshape(hidden.shape[1], w_out.shape[2])
    out[...] = after_mix[...] + jnp.dot(hidden[...], weights, preferred_element_type=F32)


def last_kernel(
    zones, place, own_in, own_out, total, ffn_in, swapped_far, out, w_in, w_out, hidden, rows_out, sems
):
    slots = slots_of(place[0] ^ 1)[2:]
    pieces = [swapped_far.at[index] for index in range(2)]
    fill_slots(zones, place, own_in, own_out, slots, pieces, w_in, w_out)
    grow(ffn_in, w_in, hidden)
    weights = w_out[...].reshape(hidden.shape[1], w_out.shape[2])
    span = total.shape[0] // sems.shape[0]
    copies = []
    for index in range(sems.shape[0]):
        rows = slice(index * span, (index + 1) * span)
        shrunk = jnp.dot(hidden[rows, :], weights, preferred_element_type=F32)
        rows_out[rows, :] = (total[rows, :] + shrunk).astype(BF16)
        copies.append(pltpu.make_async_copy(rows_out.at[rows, :], out.at[rows, :], sems.at[index]))
        copies[-1].start()
    for copy in copies:
        copy.wait()


def call(kernel, out_shape, scratch, smem, hbm, limit, args, out_space=pltpu.VMEM):
    spaces = {index: pltpu.SMEM for index in smem} | {index: pltpu.HBM for index in hbm}
    return pl.pallas_call(
        kernel,
        out_shape=out_shape,
        in_specs=[
            pl.BlockSpec(memory_space=spaces.get(index, pltpu.VMEM)) for index in range(len(args))
        ],
        out_specs=jax.tree.map(lambda _: pl.BlockSpec(memory_space=out_space), out_shape),
        scratch_shapes=scratch,
        cost_estimate=pl.CostEstimate(flops=0, bytes_accessed=0, transcendentals=0),
        compiler_params=pltpu.CompilerParams(vmem_limit_bytes=limit * MIB),
    )(*args)


def on_device(
    states,
    gain_attn,
    w_qkv,
    w_out_attn,
    pattern,
    gain_mix,
    neighbours,
    degree,
    mix,
    gain_ffn,
    w_in,
    w_out,
):
    steps, zone_rows, width = states.shape
    rows = steps * zone_rows
    reach = pattern.shape[1]
    zones = lax.axis_size("zone")
    my_block, my_zone = lax.axis_index("tm"), lax.axis_index("zone")
    place = jnp.stack([my_block, my_zone]).astype(jnp.int32)
    key_count = (reach + 1) * steps
    hidden = w_in.shape[1]
    in_cols = hidden // SPREAD
    out_rows = w_out.shape[0] // SPREAD
    part = width // zones
    exchanges = steps_over(zones)

    before = shifted(states, "tm", 2)
    first = lax.dynamic_slice_in_dim(
        jnp.concatenate([w_qkv, w_out_attn], axis=1), quarter_of(my_block) * width, width, axis=1
    )
    direct = [swapped(first, "zone", step) for step in exchanges]
    packed_rows = w_in.shape[0] + out_rows * (width // in_cols)
    own_in, packed = call(
        functools.partial(group_kernel, zones),
        (
            jax.ShapeDtypeStruct((SPREAD, w_in.shape[0], in_cols), BF16),
            jax.ShapeDtypeStruct((packed_rows, in_cols), BF16),
        ),
        [],
        (0,),
        (),
        4,
        [place, w_in, w_out],
    )
    beside = swapped(packed, "zone", 1)
    half_shape = jax.ShapeDtypeStruct((zones - 1, first.shape[0] // 2, width), BF16)
    direct, upper, lower, doubled, last = call(
        split_kernel,
        (
            jax.ShapeDtypeStruct((zones - 1,) + first.shape, BF16),
            half_shape,
            half_shape,
            jax.ShapeDtypeStruct((2,) + packed.shape, BF16),
            jax.ShapeDtypeStruct(states.shape, BF16),
        ),
        [],
        (0,),
        (),
        4,
        [place, packed, beside, states, before] + direct,
    )
    over = [crossed(value, "tm", 2, 4) for value in (upper, lower)]
    last = swapped(last, "tm", 1)
    pieces = [direct] + over + [swapped(value, "tm", 1) for value in [direct] + over]
    normed = call(
        norm_kernel,
        jax.ShapeDtypeStruct((key_count * zone_rows, width), BF16),
        [],
        (),
        (),
        4,
        [before, last, states, gain_attn.reshape(1, -1)],
    )
    bits = 2
    while 2 * bits < zones:
        doubled = jnp.concatenate([doubled, swapped(doubled, "zone", bits)], axis=0)
        bits *= 2
    context, w_attn = call(
        functools.partial(attention_kernel, zones, reach, steps),
        (
            jax.ShapeDtypeStruct((rows, width), BF16),
            jax.ShapeDtypeStruct((width, width), BF16),
        ),
        [
            pltpu.VMEM((4, width, width), BF16),
            pltpu.VMEM((3 * width, width), BF16),
            pltpu.VMEM((HEADS, 3 * (width // HEADS), key_count * zone_rows), F32),
            pltpu.VMEM((width, rows), F32),
            pltpu.SemaphoreType.DMA((4,)),
        ],
        (0, 1),
        (3, 4),
        22,
        [place, pattern, normed, w_qkv, w_out_attn] + pieces,
    )

    chunk = jax.ShapeDtypeStruct((rows, part), BF16)
    after_attn, *chunks = call(
        project_kernel,
        (jax.ShapeDtypeStruct((rows, width), F32),)
        + (chunk,) * zones,
        [pltpu.VMEM((zones, rows, part), BF16)],
        (0,),
        (),
        8,
        [place, states, context, w_attn, gain_mix.reshape(1, -1)],
    )
    across = call(
        stack_kernel,
        jax.ShapeDtypeStruct((zones - 1,) + packed.shape, BF16),
        [],
        (),
        (),
        4,
        [doubled, swapped(doubled, "zone", bits), after_attn],
    )
    nearest = crossed(across, "tm", 2, 4)

    arrived = [chunks[0]] + [
        swapped(value, "zone", step) for value, step in zip(chunks[1:], exchanges)
    ]

    *spatial, pair = call(
        functools.partial(mixing_kernel, steps, zones),
        (chunk,) * zones
        + (jax.ShapeDtypeStruct((2,) + across.shape, BF16),),
        [pltpu.VMEM((zones, rows, part), BF16)],
        (0, 1, 2),
        (),
        8,
        [place, neighbours, degree, mix] + arrived + [across, nearest],
    )
    far = crossed(pair, "tm", 4, 2)
    full_in, full_out = call(
        functools.partial(order_kernel, zones),
        (
            jax.ShapeDtypeStruct((6, width, in_cols), BF16),
            jax.ShapeDtypeStruct((6, in_cols, width), BF16),
        ),
        [],
        (0,),
        (),
        8,
        [place, own_in, w_out, pair, far, swapped(pair, "tm", 1)],
    )
    arrived = [spatial[0]] + [
        swapped(value, "zone", step) for value, step in zip(spatial[1:], exchanges)
    ]
    after_mix, ffn_in, far = call(
        functools.partial(after_kernel, zones),
        (
            jax.ShapeDtypeStruct((rows, width), F32),
            jax.ShapeDtypeStruct((rows, width), BF16),
            jax.ShapeDtypeStruct(far.shape, BF16),
        ),
        [pltpu.VMEM((zones, rows, part), BF16)],
        (0,),
        (),
        8,
        [place, after_attn, gain_ffn.reshape(1, -1), full_out, far] + arrived,
    )
    total = call(
        ffn_kernel,
        jax.ShapeDtypeStruct((rows, width), F32),
        [pltpu.VMEM((rows, 6 * in_cols), BF16)],
        (),
        (),
        12,
        [after_mix, ffn_in, full_in, full_out],
    )
    evolved = call(
        functools.partial(last_kernel, zones),
        jax.ShapeDtypeStruct((rows, width), BF16),
        [
            pltpu.VMEM((2, width, in_cols), BF16),
            pltpu.VMEM((2, in_cols, width), BF16),
            pltpu.VMEM((rows, 2 * in_cols), BF16),
            pltpu.VMEM((rows, width), BF16),
            pltpu.SemaphoreType.DMA((2,)),
        ],
        (0,),
        (),
        12,
        [place, own_in, w_out, total, ffn_in, swapped(far, "tm", 1)],
        pl.ANY,
    )
    return evolved.reshape(steps, zone_rows, width)


def solution(mesh):
    return jax.shard_map(
        on_device,
        mesh=mesh,
        in_specs=(
            P("tm", "zone", None),
            P(),
            P("zone", None),
            P("zone", None),
            P("tm", None),
            P(),
            P(),
            P(),
            P(),
            P(),
            P("zone", None),
            P("zone", None),
        ),
        out_specs=P("tm", "zone", None),
        check_vma=False,
    )
```

```python
import functools

import jax
import jax.numpy as jnp
from jax import lax
from jax.experimental import pallas as pl
from jax.experimental.pallas import tpu as pltpu
from jax.sharding import PartitionSpec as P

HEADS = 4
SPREAD = 8
LANES = 128
F32 = jnp.float32
BF16 = jnp.bfloat16
MIB = 1024 * 1024


def shifted(value, axis, steps):
    count = lax.axis_size(axis)
    return lax.ppermute(value, axis, [(source, source + steps) for source in range(count - steps)])


def swapped(value, axis, bits):
    count = lax.axis_size(axis)
    return lax.ppermute(value, axis, [(source, source ^ bits) for source in range(count)])


def crossed(value, axis, even_bits, odd_bits):
    count = lax.axis_size(axis)
    pairs = [(source, source ^ (odd_bits if source % 2 else even_bits)) for source in range(count)]
    return lax.ppermute(value, axis, pairs)


def steps_over(count):
    half = count // 2
    return tuple(range(half, count)) + tuple(range(1, half))


def rms_scale(values, gain):
    mean_sq = jnp.mean(values * values, axis=-1, keepdims=True)
    return values * lax.rsqrt(mean_sq + 1e-06) * gain


def quarter_of(block):
    core = lax.rem(block, 2)
    return (1 - core) * lax.rem(lax.div(block, 2), 2) + core * (2 + lax.rem(lax.div(block, 4), 2))


def row_sum(value):
    return jnp.sum(value, axis=0, keepdims=True)


def norm_kernel(*refs):
    blocks, (gain_attn, normed) = refs[:-2], refs[-2:]
    steps, zone_rows, _ = blocks[0].shape
    gain = gain_attn[...]
    for index, block in enumerate(blocks):
        for step in range(steps):
            row = (index * steps + step) * zone_rows
            normed[row : row + zone_rows, :] = rms_scale(block[step].astype(F32), gain).astype(BF16)


def group_kernel(zones, place, w_in, w_out, own_in, packed):
    in_shard, hidden = w_in.shape
    out_rows = w_out.shape[0] // SPREAD
    in_cols = hidden // SPREAD
    width = w_out.shape[1]
    for index in range(SPREAD):
        for source in range(zones):
            low = (source * SPREAD + index) * out_rows
            to = slice(source * out_rows, (source + 1) * out_rows)
            own_in[index, :, to] = w_in[:, low : low + out_rows]
    slot = lax.rem(place[0], SPREAD)
    packed[:in_shard, :] = own_in[slot]
    rows = pl.ds(pl.multiple_of(slot * out_rows, out_rows), out_rows)
    for fold in range(width // in_cols):
        low = in_shard + fold * out_rows
        packed[low : low + out_rows, :] = w_out[rows, fold * in_cols : (fold + 1) * in_cols]


def split_kernel(place, packed, beside, states, before, *refs):
    arrived, (direct, upper, lower, doubled, last) = refs[:-5], refs[-5:]
    half = upper.shape[1]
    for index, piece in enumerate(arrived):
        direct[index] = piece[...]
        upper[index] = piece[:half, :]
        lower[index] = piece[half:, :]
    doubled[0] = packed[...]
    doubled[1] = beside[...]
    last[...] = jnp.where(lax.rem(place[0], 2) == 1, before[...], states[...])


def stack_kernel(doubled, arrived, *refs):
    out = refs[-1]
    near = doubled.shape[0]
    out[: near - 1] = doubled[1:]
    out[near - 1 :] = arrived[...]


def attention_kernel(zones, reach, steps, place, pattern, normed, own_qkv, own_attn, *refs):
    pieces, (context_out, attn_out, weights, w_turned, projected, context) = refs[:-6], refs[-6:]
    key_count = (reach + 1) * steps
    zone_rows = normed.shape[0] // key_count
    width = normed.shape[1]
    head_size = width // HEADS
    my_block, my_zone = place[0], place[1]
    shard = own_qkv.shape[0]

    own_rows = pl.ds(pl.multiple_of(my_zone * shard, shard), shard)
    for index in range(3):
        weights[index, own_rows, :] = own_qkv[:, index * width : (index + 1) * width]
    weights[3, own_rows, :] = own_attn[...]
    half = shard // 2
    mine, other = quarter_of(my_block), quarter_of(my_block ^ 1)
    for place_in, step in enumerate(steps_over(zones)):
        start = (my_zone ^ step) * shard
        for piece, quarter, low in zip(
            pieces, (mine, mine ^ 1, mine ^ 1, other, other ^ 1, other ^ 1), (0, 0, half, 0, 0, half)
        ):
            rows = pl.ds(pl.multiple_of(start + low, half), piece.shape[1])
            weights[quarter, rows, :] = piece[place_in]
    attn_out[...] = weights[3]
    group = 3 * head_size
    def turn(head):
        for kind in range(3):
            rows = slice(head * group + kind * head_size, head * group + (kind + 1) * head_size)
            w_turned[rows, :] = weights[kind, :, head * head_size : (head + 1) * head_size].T

    def project(head, first, span):
        skip = 0 if first >= reach * steps * zone_rows else head_size
        projected[head, skip:, first : first + span] = lax.dot_general(
            w_turned[head * group + skip : (head + 1) * group, :],
            normed[first : first + span, :],
            (((1,), (1,)), ((), ())),
            preferred_element_type=F32,
        )

    span = 2 * zone_rows
    pending = [(head, first) for head in range(HEADS) for first in range(0, key_count * zone_rows, span)]

    def project_some(count):
        for _ in range(min(count, len(pending))):
            head, first = pending.pop(0)
            if first == 0:
                turn(head)
            project(head, first, span)

    allowed_back = [
        (pattern[0, back - 1] == 1) & (my_block >= back) for back in range(reach, 0, -1)
    ]
    chunks = head_size // 8

    def usable(query):
        return range(reach * steps + query + 1)

    def attend(head, queries):
        def tile(kind, chunk, key):
            row = kind * head_size + chunk * 8
            return projected[head, row : row + 8, key * zone_rows : (key + 1) * zone_rows]

        sums = {}
        for chunk in range(chunks):
            q_tiles = {q: tile(0, chunk, reach * steps + q) for q in queries}
            for key in usable(queries[-1]):
                k_tile = tile(1, chunk, key)
                for q in queries:
                    if key in usable(q):
                        term = q_tiles[q] * k_tile
                        sums[q, key] = term if chunk == 0 else sums[q, key] + term
        weights_of, scales = {}, {}
        for q in queries:
            scores = jnp.concatenate([row_sum(sums[q, key]) for key in usable(q)], axis=0)
            scores = scores * head_size ** (-0.5)
            row_id = lax.broadcasted_iota(jnp.int32, scores.shape, 0)
            allowed = row_id >= reach * steps
            for index, live in enumerate(allowed_back):
                inside = (row_id >= index * steps) & (row_id < (index + 1) * steps)
                allowed = allowed | (inside & live)
            masked = jnp.where(allowed, scores, -1e30)
            top = jnp.max(masked, axis=0, keepdims=True)
            expw = jnp.where(allowed, jnp.exp(masked - top), 0.0)
            scales[q] = jnp.broadcast_to(1.0 / row_sum(expw), (8, zone_rows))
            probs = expw.astype(BF16).astype(F32)
            for key in usable(q):
                weights_of[q, key] = jnp.broadcast_to(probs[key : key + 1, :], (8, zone_rows))
        for chunk in range(chunks):
            sums = {}
            for key in usable(queries[-1]):
                v_tile = tile(2, chunk, key)
                for q in queries:
                    if key in usable(q):
                        term = weights_of[q, key] * v_tile
                        sums[q] = term if key == 0 else sums[q] + term
            for q in queries:
                row = head * head_size + chunk * 8
                context[row : row + 8, q * zone_rows : (q + 1) * zone_rows] = sums[q] * scales[q]

    spans = key_count * zone_rows // span
    project_some(spans)
    pairs = range(0, steps, 2)
    for head in range(HEADS):
        for pair in pairs:
            project_some(-(-spans // len(pairs)))
            attend(head, range(pair, min(pair + 2, steps)))

    for step in range(steps):
        rows = slice(step * zone_rows, (step + 1) * zone_rows)
        context_out[rows, :] = context[:, rows].T.astype(BF16)


def project_kernel(place, states, context, w_attn, gain_mix, after_out, *refs):
    *outs, parts = refs
    steps, zone_rows, _ = states.shape
    zones, _, part = parts.shape
    my_zone = place[1]
    gain = gain_mix[...]
    for step in range(steps):
        rows = slice(step * zone_rows, (step + 1) * zone_rows)
        after = states[step].astype(F32) + jnp.dot(
            context[rows, :], w_attn[...], preferred_element_type=F32
        )
        after_out[rows, :] = after
        mixin = rms_scale(after, gain).astype(BF16)
        for index in range(zones):
            parts[index, rows, :] = mixin[:, index * part : (index + 1) * part]
    for index, step in enumerate((0,) + steps_over(zones)):
        outs[index][...] = parts[my_zone ^ step]


def mixing_kernel(steps, zones, place, neighbours, degree, mix, *refs):
    arrived, halves, (*outs, pair, items) = refs[:zones], refs[zones : zones + 2], refs[zones + 2 :]
    for index, value in enumerate(halves):
        pair[index] = value[...]
    _, slots, zone_rows, _ = mix.shape
    part = items.shape[-1]
    my_zone = place[1]
    group = 2 if part % LANES == 0 and steps % 2 == 0 else 1
    for index, step in enumerate((0,) + steps_over(zones)):
        items[my_zone ^ step] = arrived[index][...]

    for target, target_step in enumerate((0,) + steps_over(zones)):
        block = my_zone ^ target_step
        left = []
        for slot in range(slots):
            tile = mix[block, slot]
            left.append(jnp.where(degree[block] > slot, tile, jnp.zeros_like(tile)))
        left = jnp.concatenate(left, axis=1)
        for step in range(0, steps, group):
            right = []
            for slot in range(slots):
                source = neighbours[block, slot]
                right.append(
                    jnp.concatenate(
                        [
                            items[source, (step + index) * zone_rows : (step + index + 1) * zone_rows, :]
                            for index in range(group)
                        ],
                        axis=1,
                    )
                )
            result = jnp.dot(left, jnp.concatenate(right, axis=0), preferred_element_type=F32)
            for index in range(group):
                rows = slice((step + index) * zone_rows, (step + index + 1) * zone_rows)
                outs[target][rows, :] = result[:, index * part : (index + 1) * part].astype(BF16)


def slots_of(block):
    near = 2 + 2 * lax.rem(block, 2)
    return [lax.rem(block, SPREAD) ^ bits for bits in (0, near, 6 - near, 6)]


def fill_slots(zones, place, own_in, own_out, slots, pieces, w_in, w_out):
    my_zone = place[1]
    in_shard = own_in.shape[1]
    out_rows = own_out.shape[0] // SPREAD
    in_cols, width = own_in.shape[2], own_out.shape[1]
    own_rows = pl.ds(pl.multiple_of(my_zone * in_shard, in_shard), in_shard)
    own_out_rows = pl.ds(pl.multiple_of(my_zone * out_rows, out_rows), out_rows)
    for index, (slot, piece) in enumerate(zip(slots, pieces)):
        from_rows = pl.ds(pl.multiple_of(slot * out_rows, out_rows), out_rows)
        w_in[index, own_rows, :] = own_in[slot]
        w_out[index, own_out_rows, :] = own_out[from_rows, :]
        for step in range(1, zones):
            source = my_zone ^ step
            part = piece[step - 1]
            rows = pl.ds(pl.multiple_of(source * in_shard, in_shard), in_shard)
            w_in[index, rows, :] = part[:in_shard, :]
            rows = pl.ds(pl.multiple_of(source * out_rows, out_rows), out_rows)
            for fold in range(width // in_cols):
                low = in_shard + fold * out_rows
                w_out[index, rows, fold * in_cols : (fold + 1) * in_cols] = part[low : low + out_rows, :]


def order_kernel(zones, place, own_in, own_out, pair, far, swapped_pair, w_in, w_out):
    my_block = place[0]
    slots = slots_of(my_block) + slots_of(my_block ^ 1)[:2]
    pieces = [group.at[index] for group in (pair, far, swapped_pair) for index in range(2)]
    fill_slots(zones, place, own_in, own_out, slots, pieces, w_in, w_out)


def after_kernel(zones, place, after_attn, gain_ffn, ready, far, *refs):
    arrived, (after_mix, ffn_in, far_out, parts) = refs[:zones], refs[zones:]
    rows_all, width = after_attn.shape
    my_zone = place[1]
    far_out[...] = far[...]
    for index, step in enumerate((0,) + steps_over(zones)):
        parts[my_zone ^ step] = arrived[index][...]
    gain = gain_ffn[...]
    span = 128
    part = parts.shape[-1]
    for first in range(0, rows_all, span):
        rows = slice(first, first + span)
        for index in range(zones):
            cols = slice(index * part, (index + 1) * part)
            after_mix[rows, cols] = after_attn[rows, cols] + parts[index, rows, :].astype(F32)
        ffn_in[rows, :] = rms_scale(after_mix[rows, :], gain).astype(BF16)


def grow(ffn_in, w_in, hidden):
    in_cols = w_in.shape[2]
    for index in range(w_in.shape[0]):
        grown = jnp.dot(ffn_in[...], w_in[index], preferred_element_type=F32)
        hidden[:, index * in_cols : (index + 1) * in_cols] = jax.nn.gelu(
            grown, approximate=True
        ).astype(BF16)


def ffn_kernel(after_mix, ffn_in, w_in, w_out, out, hidden):
    grow(ffn_in, w_in, hidden)
    weights = w_out[...].reshape(hidden.shape[1], w_out.shape[2])
    out[...] = after_mix[...] + jnp.dot(hidden[...], weights, preferred_element_type=F32)


def last_kernel(
    zones, place, own_in, own_out, total, ffn_in, swapped_far, out, w_in, w_out, hidden, rows_out, sems
):
    slots = slots_of(place[0] ^ 1)[2:]
    pieces = [swapped_far.at[index] for index in range(2)]
    fill_slots(zones, place, own_in, own_out, slots, pieces, w_in, w_out)
    grow(ffn_in, w_in, hidden)
    weights = w_out[...].reshape(hidden.shape[1], w_out.shape[2])
    span = total.shape[0] // sems.shape[0]
    copies = []
    for index in range(sems.shape[0]):
        rows = slice(index * span, (index + 1) * span)
        shrunk = jnp.dot(hidden[rows, :], weights, preferred_element_type=F32)
        rows_out[rows, :] = (total[rows, :] + shrunk).astype(BF16)
        copies.append(pltpu.make_async_copy(rows_out.at[rows, :], out.at[rows, :], sems.at[index]))
        copies[-1].start()
    for copy in copies:
        copy.wait()


def call(kernel, out_shape, scratch, smem, hbm, limit, args, out_space=pltpu.VMEM):
    spaces = {index: pltpu.SMEM for index in smem} | {index: pltpu.HBM for index in hbm}
    return pl.pallas_call(
        kernel,
        out_shape=out_shape,
        in_specs=[
            pl.BlockSpec(memory_space=spaces.get(index, pltpu.VMEM)) for index in range(len(args))
        ],
        out_specs=jax.tree.map(lambda _: pl.BlockSpec(memory_space=out_space), out_shape),
        scratch_shapes=scratch,
        cost_estimate=pl.CostEstimate(flops=0, bytes_accessed=0, transcendentals=0),
        compiler_params=pltpu.CompilerParams(vmem_limit_bytes=limit * MIB),
    )(*args)


def on_device(
    states,
    gain_attn,
    w_qkv,
    w_out_attn,
    pattern,
    gain_mix,
    neighbours,
    degree,
    mix,
    gain_ffn,
    w_in,
    w_out,
):
    steps, zone_rows, width = states.shape
    rows = steps * zone_rows
    reach = pattern.shape[1]
    zones = lax.axis_size("zone")
    my_block, my_zone = lax.axis_index("tm"), lax.axis_index("zone")
    place = jnp.stack([my_block, my_zone]).astype(jnp.int32)
    key_count = (reach + 1) * steps
    hidden = w_in.shape[1]
    in_cols = hidden // SPREAD
    out_rows = w_out.shape[0] // SPREAD
    part = width // zones
    exchanges = steps_over(zones)

    before = shifted(states, "tm", 2)
    first = lax.dynamic_slice_in_dim(
        jnp.concatenate([w_qkv, w_out_attn], axis=1), quarter_of(my_block) * width, width, axis=1
    )
    direct = [swapped(first, "zone", step) for step in exchanges]
    packed_rows = w_in.shape[0] + out_rows * (width // in_cols)
    own_in, packed = call(
        functools.partial(group_kernel, zones),
        (
            jax.ShapeDtypeStruct((SPREAD, w_in.shape[0], in_cols), BF16),
            jax.ShapeDtypeStruct((packed_rows, in_cols), BF16),
        ),
        [],
        (0,),
        (),
        4,
        [place, w_in, w_out],
    )
    beside = swapped(packed, "zone", 1)
    half_shape = jax.ShapeDtypeStruct((zones - 1, first.shape[0] // 2, width), BF16)
    direct, upper, lower, doubled, last = call(
        split_kernel,
        (
            jax.ShapeDtypeStruct((zones - 1,) + first.shape, BF16),
            half_shape,
            half_shape,
            jax.ShapeDtypeStruct((2,) + packed.shape, BF16),
            jax.ShapeDtypeStruct(states.shape, BF16),
        ),
        [],
        (0,),
        (),
        4,
        [place, packed, beside, states, before] + direct,
    )
    over = [crossed(value, "tm", 2, 4) for value in (upper, lower)]
    last = swapped(last, "tm", 1)
    pieces = [direct] + over + [swapped(value, "tm", 1) for value in [direct] + over]
    normed = call(
        norm_kernel,
        jax.ShapeDtypeStruct((key_count * zone_rows, width), BF16),
        [],
        (),
        (),
        4,
        [before, last, states, gain_attn.reshape(1, -1)],
    )
    bits = 2
    while 2 * bits < zones:
        doubled = jnp.concatenate([doubled, swapped(doubled, "zone", bits)], axis=0)
        bits *= 2
    context, w_attn = call(
        functools.partial(attention_kernel, zones, reach, steps),
        (
            jax.ShapeDtypeStruct((rows, width), BF16),
            jax.ShapeDtypeStruct((width, width), BF16),
        ),
        [
            pltpu.VMEM((4, width, width), BF16),
            pltpu.VMEM((3 * width, width), BF16),
            pltpu.VMEM((HEADS, 3 * (width // HEADS), key_count * zone_rows), F32),
            pltpu.VMEM((width, rows), F32),
        ],
        (0, 1),
        (),
        22,
        [place, pattern, normed, w_qkv, w_out_attn] + pieces,
    )

    chunk = jax.ShapeDtypeStruct((rows, part), BF16)
    after_attn, *chunks = call(
        project_kernel,
        (jax.ShapeDtypeStruct((rows, width), F32),)
        + (chunk,) * zones,
        [pltpu.VMEM((zones, rows, part), BF16)],
        (0,),
        (),
        8,
        [place, states, context, w_attn, gain_mix.reshape(1, -1)],
    )
    across = call(
        stack_kernel,
        jax.ShapeDtypeStruct((zones - 1,) + packed.shape, BF16),
        [],
        (),
        (),
        4,
        [doubled, swapped(doubled, "zone", bits), after_attn],
    )
    nearest = crossed(across, "tm", 2, 4)

    arrived = [chunks[0]] + [
        swapped(value, "zone", step) for value, step in zip(chunks[1:], exchanges)
    ]

    *spatial, pair = call(
        functools.partial(mixing_kernel, steps, zones),
        (chunk,) * zones
        + (jax.ShapeDtypeStruct((2,) + across.shape, BF16),),
        [pltpu.VMEM((zones, rows, part), BF16)],
        (0, 1, 2),
        (),
        8,
        [place, neighbours, degree, mix] + arrived + [across, nearest],
    )
    far = crossed(pair, "tm", 4, 2)
    full_in, full_out = call(
        functools.partial(order_kernel, zones),
        (
            jax.ShapeDtypeStruct((6, width, in_cols), BF16),
            jax.ShapeDtypeStruct((6, in_cols, width), BF16),
        ),
        [],
        (0,),
        (),
        8,
        [place, own_in, w_out, pair, far, swapped(pair, "tm", 1)],
    )
    arrived = [spatial[0]] + [
        swapped(value, "zone", step) for value, step in zip(spatial[1:], exchanges)
    ]
    after_mix, ffn_in, far = call(
        functools.partial(after_kernel, zones),
        (
            jax.ShapeDtypeStruct((rows, width), F32),
            jax.ShapeDtypeStruct((rows, width), BF16),
            jax.ShapeDtypeStruct(far.shape, BF16),
        ),
        [pltpu.VMEM((zones, rows, part), BF16)],
        (0,),
        (),
        8,
        [place, after_attn, gain_ffn.reshape(1, -1), full_out, far] + arrived,
    )
    total = call(
        ffn_kernel,
        jax.ShapeDtypeStruct((rows, width), F32),
        [pltpu.VMEM((rows, 6 * in_cols), BF16)],
        (),
        (),
        12,
        [after_mix, ffn_in, full_in, full_out],
    )
    evolved = call(
        functools.partial(last_kernel, zones),
        jax.ShapeDtypeStruct((rows, width), BF16),
        [
            pltpu.VMEM((2, width, in_cols), BF16),
            pltpu.VMEM((2, in_cols, width), BF16),
            pltpu.VMEM((rows, 2 * in_cols), BF16),
            pltpu.VMEM((rows, width), BF16),
            pltpu.SemaphoreType.DMA((2,)),
        ],
        (0,),
        (),
        12,
        [place, own_in, w_out, total, ffn_in, swapped(far, "tm", 1)],
        pl.ANY,
    )
    return evolved.reshape(steps, zone_rows, width)


def solution(mesh):
    return jax.shard_map(
        on_device,
        mesh=mesh,
        in_specs=(
            P("tm", "zone", None),
            P(),
            P("zone", None),
            P("zone", None),
            P("tm", None),
            P(),
            P(),
            P(),
            P(),
            P(),
            P("zone", None),
            P("zone", None),
        ),
        out_specs=P("tm", "zone", None),
        check_vma=False,
    )
```

```python
import functools

import jax
import jax.numpy as jnp
from jax import lax
from jax.experimental import pallas as pl
from jax.experimental.pallas import tpu as pltpu
from jax.sharding import PartitionSpec as P

HEADS = 4
SPREAD = 8
LANES = 128
F32 = jnp.float32
BF16 = jnp.bfloat16
MIB = 1024 * 1024


def shifted(value, axis, steps):
    count = lax.axis_size(axis)
    return lax.ppermute(value, axis, [(source, source + steps) for source in range(count - steps)])


def swapped(value, axis, bits):
    count = lax.axis_size(axis)
    return lax.ppermute(value, axis, [(source, source ^ bits) for source in range(count)])


def crossed(value, axis, even_bits, odd_bits):
    count = lax.axis_size(axis)
    pairs = [(source, source ^ (odd_bits if source % 2 else even_bits)) for source in range(count)]
    return lax.ppermute(value, axis, pairs)


def steps_over(count):
    half = count // 2
    return tuple(range(half, count)) + tuple(range(1, half))


def rms_scale(values, gain):
    mean_sq = jnp.mean(values * values, axis=-1, keepdims=True)
    return values * lax.rsqrt(mean_sq + 1e-06) * gain


def quarter_of(block):
    core = lax.rem(block, 2)
    return (1 - core) * lax.rem(lax.div(block, 2), 2) + core * (2 + lax.rem(lax.div(block, 4), 2))


def row_sum(value):
    return jnp.sum(value, axis=0, keepdims=True)


def norm_kernel(*refs):
    blocks, (gain_attn, normed) = refs[:-2], refs[-2:]
    steps, zone_rows, _ = blocks[0].shape
    gain = gain_attn[...]
    for index, block in enumerate(blocks):
        for step in range(steps):
            row = (index * steps + step) * zone_rows
            normed[row : row + zone_rows, :] = rms_scale(block[step].astype(F32), gain).astype(BF16)


def open_kernel(place, states, w_qkv, w_attn, states_out, first):
    states_out[...] = states[...]
    width = w_attn.shape[1]
    quarter = quarter_of(place[0])
    for index in range(4):

        @pl.when(quarter == index)
        def _():
            first[...] = w_attn[...] if index == 3 else w_qkv[:, index * width : (index + 1) * width]


def group_kernel(zones, place, w_in, w_out, own_in, packed):
    in_shard, hidden = w_in.shape
    out_rows = w_out.shape[0] // SPREAD
    in_cols = hidden // SPREAD
    width = w_out.shape[1]
    for index in range(SPREAD):
        for source in range(zones):
            low = (source * SPREAD + index) * out_rows
            to = slice(source * out_rows, (source + 1) * out_rows)
            own_in[index, :, to] = w_in[:, low : low + out_rows]
    slot = lax.rem(place[0], SPREAD)
    packed[:in_shard, :] = own_in[slot]
    rows = pl.ds(pl.multiple_of(slot * out_rows, out_rows), out_rows)
    for fold in range(width // in_cols):
        low = in_shard + fold * out_rows
        packed[low : low + out_rows, :] = w_out[rows, fold * in_cols : (fold + 1) * in_cols]


def split_kernel(place, packed, beside, states, before, *refs):
    arrived, (direct, upper, lower, doubled, last) = refs[:-5], refs[-5:]
    half = upper.shape[1]
    for index, piece in enumerate(arrived):
        direct[index] = piece[...]
        upper[index] = piece[:half, :]
        lower[index] = piece[half:, :]
    doubled[0] = packed[...]
    doubled[1] = beside[...]
    last[...] = jnp.where(lax.rem(place[0], 2) == 1, before[...], states[...])


def stack_kernel(doubled, arrived, *refs):
    out = refs[-1]
    near = doubled.shape[0]
    out[: near - 1] = doubled[1:]
    out[near - 1 :] = arrived[...]


def attention_kernel(zones, reach, steps, place, pattern, normed, own_qkv, own_attn, *refs):
    pieces, (context_out, attn_out, weights, w_turned, projected, context) = refs[:-6], refs[-6:]
    key_count = (reach + 1) * steps
    zone_rows = normed.shape[0] // key_count
    width = normed.shape[1]
    head_size = width // HEADS
    my_block, my_zone = place[0], place[1]
    shard = own_qkv.shape[0]

    own_rows = pl.ds(pl.multiple_of(my_zone * shard, shard), shard)
    for index in range(3):
        weights[index, own_rows, :] = own_qkv[:, index * width : (index + 1) * width]
    weights[3, own_rows, :] = own_attn[...]
    half = shard // 2
    mine, other = quarter_of(my_block), quarter_of(my_block ^ 1)
    for place_in, step in enumerate(steps_over(zones)):
        start = (my_zone ^ step) * shard
        for piece, quarter, low in zip(
            pieces, (mine, mine ^ 1, mine ^ 1, other, other ^ 1, other ^ 1), (0, 0, half, 0, 0, half)
        ):
            rows = pl.ds(pl.multiple_of(start + low, half), piece.shape[1])
            weights[quarter, rows, :] = piece[place_in]
    attn_out[...] = weights[3]
    group = 3 * head_size
    def turn(head):
        for kind in range(3):
            rows = slice(head * group + kind * head_size, head * group + (kind + 1) * head_size)
            w_turned[rows, :] = weights[kind, :, head * head_size : (head + 1) * head_size].T

    def project(head, first, span):
        skip = 0 if first >= reach * steps * zone_rows else head_size
        projected[head, skip:, first : first + span] = lax.dot_general(
            w_turned[head * group + skip : (head + 1) * group, :],
            normed[first : first + span, :],
            (((1,), (1,)), ((), ())),
            preferred_element_type=F32,
        )

    span = 2 * zone_rows
    pending = [(head, first) for head in range(HEADS) for first in range(0, key_count * zone_rows, span)]

    def project_some(count):
        for _ in range(min(count, len(pending))):
            head, first = pending.pop(0)
            if first == 0:
                turn(head)
            project(head, first, span)

    allowed_back = [
        (pattern[0, back - 1] == 1) & (my_block >= back) for back in range(reach, 0, -1)
    ]
    chunks = head_size // 8

    def usable(query):
        return range(reach * steps + query + 1)

    def attend(head, queries):
        def tile(kind, chunk, key):
            row = kind * head_size + chunk * 8
            return projected[head, row : row + 8, key * zone_rows : (key + 1) * zone_rows]

        sums = {}
        for chunk in range(chunks):
            q_tiles = {q: tile(0, chunk, reach * steps + q) for q in queries}
            for key in usable(queries[-1]):
                k_tile = tile(1, chunk, key)
                for q in queries:
                    if key in usable(q):
                        term = q_tiles[q] * k_tile
                        sums[q, key] = term if chunk == 0 else sums[q, key] + term
        weights_of, scales = {}, {}
        for q in queries:
            scores = jnp.concatenate([row_sum(sums[q, key]) for key in usable(q)], axis=0)
            scores = scores * head_size ** (-0.5)
            row_id = lax.broadcasted_iota(jnp.int32, scores.shape, 0)
            allowed = row_id >= reach * steps
            for index, live in enumerate(allowed_back):
                inside = (row_id >= index * steps) & (row_id < (index + 1) * steps)
                allowed = allowed | (inside & live)
            masked = jnp.where(allowed, scores, -1e30)
            top = jnp.max(masked, axis=0, keepdims=True)
            expw = jnp.where(allowed, jnp.exp(masked - top), 0.0)
            scales[q] = jnp.broadcast_to(1.0 / row_sum(expw), (8, zone_rows))
            probs = expw.astype(BF16).astype(F32)
            for key in usable(q):
                weights_of[q, key] = jnp.broadcast_to(probs[key : key + 1, :], (8, zone_rows))
        for chunk in range(chunks):
            sums = {}
            for key in usable(queries[-1]):
                v_tile = tile(2, chunk, key)
                for q in queries:
                    if key in usable(q):
                        term = weights_of[q, key] * v_tile
                        sums[q] = term if key == 0 else sums[q] + term
            for q in queries:
                row = head * head_size + chunk * 8
                context[row : row + 8, q * zone_rows : (q + 1) * zone_rows] = sums[q] * scales[q]

    spans = key_count * zone_rows // span
    project_some(spans)
    pairs = range(0, steps, 2)
    for head in range(HEADS):
        for pair in pairs:
            project_some(-(-spans // len(pairs)))
            attend(head, range(pair, min(pair + 2, steps)))

    for step in range(steps):
        rows = slice(step * zone_rows, (step + 1) * zone_rows)
        context_out[rows, :] = context[:, rows].T.astype(BF16)


def project_kernel(place, states, context, w_attn, gain_mix, after_out, *refs):
    *outs, parts = refs
    steps, zone_rows, _ = states.shape
    zones, _, part = parts.shape
    my_zone = place[1]
    gain = gain_mix[...]
    for step in range(steps):
        rows = slice(step * zone_rows, (step + 1) * zone_rows)
        after = states[step].astype(F32) + jnp.dot(
            context[rows, :], w_attn[...], preferred_element_type=F32
        )
        after_out[rows, :] = after
        mixin = rms_scale(after, gain).astype(BF16)
        for index in range(zones):
            parts[index, rows, :] = mixin[:, index * part : (index + 1) * part]
    for index, step in enumerate((0,) + steps_over(zones)):
        outs[index][...] = parts[my_zone ^ step]


def mixing_kernel(steps, zones, place, neighbours, degree, mix, *refs):
    arrived, halves, (*outs, pair, items) = refs[:zones], refs[zones : zones + 2], refs[zones + 2 :]
    for index, value in enumerate(halves):
        pair[index] = value[...]
    _, slots, zone_rows, _ = mix.shape
    part = items.shape[-1]
    my_zone = place[1]
    group = 2 if part % LANES == 0 and steps % 2 == 0 else 1
    for index, step in enumerate((0,) + steps_over(zones)):
        items[my_zone ^ step] = arrived[index][...]

    for target, target_step in enumerate((0,) + steps_over(zones)):
        block = my_zone ^ target_step
        left = []
        for slot in range(slots):
            tile = mix[block, slot]
            left.append(jnp.where(degree[block] > slot, tile, jnp.zeros_like(tile)))
        left = jnp.concatenate(left, axis=1)
        for step in range(0, steps, group):
            right = []
            for slot in range(slots):
                source = neighbours[block, slot]
                right.append(
                    jnp.concatenate(
                        [
                            items[source, (step + index) * zone_rows : (step + index + 1) * zone_rows, :]
                            for index in range(group)
                        ],
                        axis=1,
                    )
                )
            result = jnp.dot(left, jnp.concatenate(right, axis=0), preferred_element_type=F32)
            for index in range(group):
                rows = slice((step + index) * zone_rows, (step + index + 1) * zone_rows)
                outs[target][rows, :] = result[:, index * part : (index + 1) * part].astype(BF16)


def slots_of(block):
    near = 2 + 2 * lax.rem(block, 2)
    return [lax.rem(block, SPREAD) ^ bits for bits in (0, near, 6 - near, 6)]


def fill_slots(zones, place, own_in, own_out, slots, pieces, w_in, w_out):
    my_zone = place[1]
    in_shard = own_in.shape[1]
    out_rows = own_out.shape[0] // SPREAD
    in_cols, width = own_in.shape[2], own_out.shape[1]
    own_rows = pl.ds(pl.multiple_of(my_zone * in_shard, in_shard), in_shard)
    own_out_rows = pl.ds(pl.multiple_of(my_zone * out_rows, out_rows), out_rows)
    for index, (slot, piece) in enumerate(zip(slots, pieces)):
        from_rows = pl.ds(pl.multiple_of(slot * out_rows, out_rows), out_rows)
        w_in[index, own_rows, :] = own_in[slot]
        w_out[index, own_out_rows, :] = own_out[from_rows, :]
        for step in range(1, zones):
            source = my_zone ^ step
            part = piece[step - 1]
            rows = pl.ds(pl.multiple_of(source * in_shard, in_shard), in_shard)
            w_in[index, rows, :] = part[:in_shard, :]
            rows = pl.ds(pl.multiple_of(source * out_rows, out_rows), out_rows)
            for fold in range(width // in_cols):
                low = in_shard + fold * out_rows
                w_out[index, rows, fold * in_cols : (fold + 1) * in_cols] = part[low : low + out_rows, :]


def order_kernel(zones, place, own_in, own_out, pair, far, swapped_pair, w_in, w_out):
    my_block = place[0]
    slots = slots_of(my_block) + slots_of(my_block ^ 1)[:2]
    pieces = [group.at[index] for group in (pair, far, swapped_pair) for index in range(2)]
    fill_slots(zones, place, own_in, own_out, slots, pieces, w_in, w_out)


def after_kernel(zones, place, after_attn, gain_ffn, ready, far, *refs):
    arrived, (after_mix, ffn_in, far_out, parts) = refs[:zones], refs[zones:]
    rows_all, width = after_attn.shape
    my_zone = place[1]
    far_out[...] = far[...]
    for index, step in enumerate((0,) + steps_over(zones)):
        parts[my_zone ^ step] = arrived[index][...]
    gain = gain_ffn[...]
    span = 128
    part = parts.shape[-1]
    for first in range(0, rows_all, span):
        rows = slice(first, first + span)
        for index in range(zones):
            cols = slice(index * part, (index + 1) * part)
            after_mix[rows, cols] = after_attn[rows, cols] + parts[index, rows, :].astype(F32)
        ffn_in[rows, :] = rms_scale(after_mix[rows, :], gain).astype(BF16)


def grow(ffn_in, w_in, hidden):
    in_cols = w_in.shape[2]
    for index in range(w_in.shape[0]):
        grown = jnp.dot(ffn_in[...], w_in[index], preferred_element_type=F32)
        hidden[:, index * in_cols : (index + 1) * in_cols] = jax.nn.gelu(
            grown, approximate=True
        ).astype(BF16)


def ffn_kernel(after_mix, ffn_in, w_in, w_out, out, hidden):
    grow(ffn_in, w_in, hidden)
    weights = w_out[...].reshape(hidden.shape[1], w_out.shape[2])
    out[...] = after_mix[...] + jnp.dot(hidden[...], weights, preferred_element_type=F32)


def last_kernel(
    zones, place, own_in, own_out, total, ffn_in, swapped_far, out, w_in, w_out, hidden, rows_out, sems
):
    slots = slots_of(place[0] ^ 1)[2:]
    pieces = [swapped_far.at[index] for index in range(2)]
    fill_slots(zones, place, own_in, own_out, slots, pieces, w_in, w_out)
    grow(ffn_in, w_in, hidden)
    weights = w_out[...].reshape(hidden.shape[1], w_out.shape[2])
    span = total.shape[0] // sems.shape[0]
    copies = []
    for index in range(sems.shape[0]):
        rows = slice(index * span, (index + 1) * span)
        shrunk = jnp.dot(hidden[rows, :], weights, preferred_element_type=F32)
        rows_out[rows, :] = (total[rows, :] + shrunk).astype(BF16)
        copies.append(pltpu.make_async_copy(rows_out.at[rows, :], out.at[rows, :], sems.at[index]))
        copies[-1].start()
    for copy in copies:
        copy.wait()


def call(kernel, out_shape, scratch, smem, hbm, limit, args, out_space=pltpu.VMEM):
    spaces = {index: pltpu.SMEM for index in smem} | {index: pltpu.HBM for index in hbm}
    return pl.pallas_call(
        kernel,
        out_shape=out_shape,
        in_specs=[
            pl.BlockSpec(memory_space=spaces.get(index, pltpu.VMEM)) for index in range(len(args))
        ],
        out_specs=jax.tree.map(lambda _: pl.BlockSpec(memory_space=out_space), out_shape),
        scratch_shapes=scratch,
        cost_estimate=pl.CostEstimate(flops=0, bytes_accessed=0, transcendentals=0),
        compiler_params=pltpu.CompilerParams(vmem_limit_bytes=limit * MIB),
    )(*args)


def on_device(
    states,
    gain_attn,
    w_qkv,
    w_out_attn,
    pattern,
    gain_mix,
    neighbours,
    degree,
    mix,
    gain_ffn,
    w_in,
    w_out,
):
    steps, zone_rows, width = states.shape
    rows = steps * zone_rows
    reach = pattern.shape[1]
    zones = lax.axis_size("zone")
    my_block, my_zone = lax.axis_index("tm"), lax.axis_index("zone")
    place = jnp.stack([my_block, my_zone]).astype(jnp.int32)
    key_count = (reach + 1) * steps
    hidden = w_in.shape[1]
    in_cols = hidden // SPREAD
    out_rows = w_out.shape[0] // SPREAD
    part = width // zones
    exchanges = steps_over(zones)

    states, first = call(
        open_kernel,
        (
            jax.ShapeDtypeStruct(states.shape, BF16),
            jax.ShapeDtypeStruct(w_out_attn.shape, BF16),
        ),
        [],
        (0,),
        (),
        6,
        [place, states, w_qkv, w_out_attn],
    )
    before = shifted(states, "tm", 2)
    direct = [swapped(first, "zone", step) for step in exchanges]
    packed_rows = w_in.shape[0] + out_rows * (width // in_cols)
    own_in, packed = call(
        functools.partial(group_kernel, zones),
        (
            jax.ShapeDtypeStruct((SPREAD, w_in.shape[0], in_cols), BF16),
            jax.ShapeDtypeStruct((packed_rows, in_cols), BF16),
        ),
        [],
        (0,),
        (),
        4,
        [place, w_in, w_out],
    )
    beside = swapped(packed, "zone", 1)
    half_shape = jax.ShapeDtypeStruct((zones - 1, first.shape[0] // 2, width), BF16)
    direct, upper, lower, doubled, last = call(
        split_kernel,
        (
            jax.ShapeDtypeStruct((zones - 1,) + first.shape, BF16),
            half_shape,
            half_shape,
            jax.ShapeDtypeStruct((2,) + packed.shape, BF16),
            jax.ShapeDtypeStruct(states.shape, BF16),
        ),
        [],
        (0,),
        (),
        4,
        [place, packed, beside, states, before] + direct,
    )
    over = [crossed(value, "tm", 2, 4) for value in (upper, lower)]
    last = swapped(last, "tm", 1)
    pieces = [direct] + over + [swapped(value, "tm", 1) for value in [direct] + over]
    normed = call(
        norm_kernel,
        jax.ShapeDtypeStruct((key_count * zone_rows, width), BF16),
        [],
        (),
        (),
        4,
        [before, last, states, gain_attn.reshape(1, -1)],
    )
    bits = 2
    while 2 * bits < zones:
        doubled = jnp.concatenate([doubled, swapped(doubled, "zone", bits)], axis=0)
        bits *= 2
    context, w_attn = call(
        functools.partial(attention_kernel, zones, reach, steps),
        (
            jax.ShapeDtypeStruct((rows, width), BF16),
            jax.ShapeDtypeStruct((width, width), BF16),
        ),
        [
            pltpu.VMEM((4, width, width), BF16),
            pltpu.VMEM((3 * width, width), BF16),
            pltpu.VMEM((HEADS, 3 * (width // HEADS), key_count * zone_rows), F32),
            pltpu.VMEM((width, rows), F32),
        ],
        (0, 1),
        (),
        22,
        [place, pattern, normed, w_qkv, w_out_attn] + pieces,
    )

    chunk = jax.ShapeDtypeStruct((rows, part), BF16)
    after_attn, *chunks = call(
        project_kernel,
        (jax.ShapeDtypeStruct((rows, width), F32),)
        + (chunk,) * zones,
        [pltpu.VMEM((zones, rows, part), BF16)],
        (0,),
        (),
        8,
        [place, states, context, w_attn, gain_mix.reshape(1, -1)],
    )
    across = call(
        stack_kernel,
        jax.ShapeDtypeStruct((zones - 1,) + packed.shape, BF16),
        [],
        (),
        (),
        4,
        [doubled, swapped(doubled, "zone", bits), after_attn],
    )
    nearest = crossed(across, "tm", 2, 4)

    arrived = [chunks[0]] + [
        swapped(value, "zone", step) for value, step in zip(chunks[1:], exchanges)
    ]

    *spatial, pair = call(
        functools.partial(mixing_kernel, steps, zones),
        (chunk,) * zones
        + (jax.ShapeDtypeStruct((2,) + across.shape, BF16),),
        [pltpu.VMEM((zones, rows, part), BF16)],
        (0, 1, 2),
        (),
        8,
        [place, neighbours, degree, mix] + arrived + [across, nearest],
    )
    far = crossed(pair, "tm", 4, 2)
    full_in, full_out = call(
        functools.partial(order_kernel, zones),
        (
            jax.ShapeDtypeStruct((6, width, in_cols), BF16),
            jax.ShapeDtypeStruct((6, in_cols, width), BF16),
        ),
        [],
        (0,),
        (),
        8,
        [place, own_in, w_out, pair, far, swapped(pair, "tm", 1)],
    )
    arrived = [spatial[0]] + [
        swapped(value, "zone", step) for value, step in zip(spatial[1:], exchanges)
    ]
    after_mix, ffn_in, far = call(
        functools.partial(after_kernel, zones),
        (
            jax.ShapeDtypeStruct((rows, width), F32),
            jax.ShapeDtypeStruct((rows, width), BF16),
            jax.ShapeDtypeStruct(far.shape, BF16),
        ),
        [pltpu.VMEM((zones, rows, part), BF16)],
        (0,),
        (),
        8,
        [place, after_attn, gain_ffn.reshape(1, -1), full_out, far] + arrived,
    )
    total = call(
        ffn_kernel,
        jax.ShapeDtypeStruct((rows, width), F32),
        [pltpu.VMEM((rows, 6 * in_cols), BF16)],
        (),
        (),
        12,
        [after_mix, ffn_in, full_in, full_out],
    )
    evolved = call(
        functools.partial(last_kernel, zones),
        jax.ShapeDtypeStruct((rows, width), BF16),
        [
            pltpu.VMEM((2, width, in_cols), BF16),
            pltpu.VMEM((2, in_cols, width), BF16),
            pltpu.VMEM((rows, 2 * in_cols), BF16),
            pltpu.VMEM((rows, width), BF16),
            pltpu.SemaphoreType.DMA((2,)),
        ],
        (0,),
        (),
        12,
        [place, own_in, w_out, total, ffn_in, swapped(far, "tm", 1)],
        pl.ANY,
    )
    return evolved.reshape(steps, zone_rows, width)


def solution(mesh):
    return jax.shard_map(
        on_device,
        mesh=mesh,
        in_specs=(
            P("tm", "zone", None),
            P(),
            P("zone", None),
            P("zone", None),
            P("tm", None),
            P(),
            P(),
            P(),
            P(),
            P(),
            P("zone", None),
            P("zone", None),
        ),
        out_specs=P("tm", "zone", None),
        check_vma=False,
    )
```

```python
import functools

import jax
import jax.numpy as jnp
from jax import lax
from jax.experimental import pallas as pl
from jax.experimental.pallas import tpu as pltpu
from jax.sharding import PartitionSpec as P

HEADS = 4
SPREAD = 8
LANES = 128
F32 = jnp.float32
BF16 = jnp.bfloat16
MIB = 1024 * 1024


def shifted(value, axis, steps):
    count = lax.axis_size(axis)
    return lax.ppermute(value, axis, [(source, source + steps) for source in range(count - steps)])


def swapped(value, axis, bits):
    count = lax.axis_size(axis)
    return lax.ppermute(value, axis, [(source, source ^ bits) for source in range(count)])


def crossed(value, axis, even_bits, odd_bits):
    count = lax.axis_size(axis)
    pairs = [(source, source ^ (odd_bits if source % 2 else even_bits)) for source in range(count)]
    return lax.ppermute(value, axis, pairs)


def steps_over(count):
    half = count // 2
    return tuple(range(half, count)) + tuple(range(1, half))


def rms_scale(values, gain):
    mean_sq = jnp.mean(values * values, axis=-1, keepdims=True)
    return values * lax.rsqrt(mean_sq + 1e-06) * gain


def quarter_of(block):
    core = lax.rem(block, 2)
    return (1 - core) * lax.rem(lax.div(block, 2), 2) + core * (2 + lax.rem(lax.div(block, 4), 2))


def row_sum(value):
    return jnp.sum(value, axis=0, keepdims=True)


def norm_kernel(*refs):
    blocks, (gain_attn, normed) = refs[:-2], refs[-2:]
    steps, zone_rows, _ = blocks[0].shape
    gain = gain_attn[...]
    for index, block in enumerate(blocks):
        for step in range(steps):
            row = (index * steps + step) * zone_rows
            normed[row : row + zone_rows, :] = rms_scale(block[step].astype(F32), gain).astype(BF16)


def group_kernel(zones, place, w_in, w_out, own_in, packed):
    in_shard, hidden = w_in.shape
    out_rows = w_out.shape[0] // SPREAD
    in_cols = hidden // SPREAD
    width = w_out.shape[1]
    for index in range(SPREAD):
        for source in range(zones):
            low = (source * SPREAD + index) * out_rows
            to = slice(source * out_rows, (source + 1) * out_rows)
            own_in[index, :, to] = w_in[:, low : low + out_rows]
    slot = lax.rem(place[0], SPREAD)
    packed[:in_shard, :] = own_in[slot]
    rows = pl.ds(pl.multiple_of(slot * out_rows, out_rows), out_rows)
    for fold in range(width // in_cols):
        low = in_shard + fold * out_rows
        packed[low : low + out_rows, :] = w_out[rows, fold * in_cols : (fold + 1) * in_cols]


def split_kernel(place, packed, beside, states, before, *refs):
    arrived, (direct, upper, lower, doubled, last) = refs[:-5], refs[-5:]
    half = upper.shape[1]
    for index, piece in enumerate(arrived):
        direct[index] = piece[...]
        upper[index] = piece[:half, :]
        lower[index] = piece[half:, :]
    doubled[0] = packed[...]
    doubled[1] = beside[...]
    last[...] = jnp.where(lax.rem(place[0], 2) == 1, before[...], states[...])


def stack_kernel(doubled, arrived, *refs):
    out = refs[-1]
    near = doubled.shape[0]
    out[: near - 1] = doubled[1:]
    out[near - 1 :] = arrived[...]


def attention_kernel(zones, reach, steps, place, pattern, normed, own_qkv, own_attn, *refs):
    pieces, (context_out, attn_out, weights, w_turned, projected, context) = refs[:-6], refs[-6:]
    key_count = (reach + 1) * steps
    zone_rows = normed.shape[0] // key_count
    width = normed.shape[1]
    head_size = width // HEADS
    my_block, my_zone = place[0], place[1]
    shard = own_qkv.shape[0]

    own_rows = pl.ds(pl.multiple_of(my_zone * shard, shard), shard)
    for index in range(3):
        weights[index, own_rows, :] = own_qkv[:, index * width : (index + 1) * width]
    weights[3, own_rows, :] = own_attn[...]
    half = shard // 2
    mine, other = quarter_of(my_block), quarter_of(my_block ^ 1)
    for place_in, step in enumerate(steps_over(zones)):
        start = (my_zone ^ step) * shard
        for piece, quarter, low in zip(
            pieces, (mine, mine ^ 1, mine ^ 1, other, other ^ 1, other ^ 1), (0, 0, half, 0, 0, half)
        ):
            rows = pl.ds(pl.multiple_of(start + low, half), piece.shape[1])
            weights[quarter, rows, :] = piece[place_in]
    attn_out[...] = weights[3]
    group = 3 * head_size
    def turn(head):
        for kind in range(3):
            rows = slice(head * group + kind * head_size, head * group + (kind + 1) * head_size)
            w_turned[rows, :] = weights[kind, :, head * head_size : (head + 1) * head_size].T

    def project(head, first, span):
        skip = 0 if first >= reach * steps * zone_rows else head_size
        projected[head, skip:, first : first + span] = lax.dot_general(
            w_turned[head * group + skip : (head + 1) * group, :],
            normed[first : first + span, :],
            (((1,), (1,)), ((), ())),
            preferred_element_type=F32,
        )

    span = 2 * zone_rows
    pending = [(head, first) for head in range(HEADS) for first in range(0, key_count * zone_rows, span)]

    def project_some(count):
        for _ in range(min(count, len(pending))):
            head, first = pending.pop(0)
            if first == 0:
                turn(head)
            project(head, first, span)

    allowed_back = [
        (pattern[0, back - 1] == 1) & (my_block >= back) for back in range(reach, 0, -1)
    ]
    chunks = head_size // 8

    def usable(query):
        return range(reach * steps + query + 1)

    def attend(head, queries):
        def tile(kind, chunk, key):
            row = kind * head_size + chunk * 8
            return projected[head, row : row + 8, key * zone_rows : (key + 1) * zone_rows]

        sums = {}
        for chunk in range(chunks):
            q_tiles = {q: tile(0, chunk, reach * steps + q) for q in queries}
            for key in usable(queries[-1]):
                k_tile = tile(1, chunk, key)
                for q in queries:
                    if key in usable(q):
                        term = q_tiles[q] * k_tile
                        sums[q, key] = term if chunk == 0 else sums[q, key] + term
        weights_of, scales = {}, {}
        for q in queries:
            scores = jnp.concatenate([row_sum(sums[q, key]) for key in usable(q)], axis=0)
            scores = scores * head_size ** (-0.5)
            row_id = lax.broadcasted_iota(jnp.int32, scores.shape, 0)
            allowed = row_id >= reach * steps
            for index, live in enumerate(allowed_back):
                inside = (row_id >= index * steps) & (row_id < (index + 1) * steps)
                allowed = allowed | (inside & live)
            masked = jnp.where(allowed, scores, -1e30)
            top = jnp.max(masked, axis=0, keepdims=True)
            expw = jnp.where(allowed, jnp.exp(masked - top), 0.0)
            scales[q] = jnp.broadcast_to(1.0 / row_sum(expw), (8, zone_rows))
            probs = expw.astype(BF16).astype(F32)
            for key in usable(q):
                weights_of[q, key] = jnp.broadcast_to(probs[key : key + 1, :], (8, zone_rows))
        for chunk in range(chunks):
            sums = {}
            for key in usable(queries[-1]):
                v_tile = tile(2, chunk, key)
                for q in queries:
                    if key in usable(q):
                        term = weights_of[q, key] * v_tile
                        sums[q] = term if key == 0 else sums[q] + term
            for q in queries:
                row = head * head_size + chunk * 8
                context[row : row + 8, q * zone_rows : (q + 1) * zone_rows] = sums[q] * scales[q]

    spans = key_count * zone_rows // span
    project_some(spans)
    pairs = range(0, steps, 2)
    for head in range(HEADS):
        for pair in pairs:
            project_some(-(-spans // len(pairs)))
            attend(head, range(pair, min(pair + 2, steps)))

    for step in range(steps):
        rows = slice(step * zone_rows, (step + 1) * zone_rows)
        context_out[rows, :] = context[:, rows].T.astype(BF16)


def project_kernel(place, states, context, w_attn, gain_mix, after_out, *refs):
    *outs, parts = refs
    steps, zone_rows, _ = states.shape
    zones, _, part = parts.shape
    my_zone = place[1]
    gain = gain_mix[...]
    for step in range(steps):
        rows = slice(step * zone_rows, (step + 1) * zone_rows)
        after = states[step].astype(F32) + jnp.dot(
            context[rows, :], w_attn[...], preferred_element_type=F32
        )
        after_out[rows, :] = after
        mixin = rms_scale(after, gain).astype(BF16)
        for index in range(zones):
            parts[index, rows, :] = mixin[:, index * part : (index + 1) * part]
    for index, step in enumerate((0,) + steps_over(zones)):
        outs[index][...] = parts[my_zone ^ step]


def mixing_kernel(steps, zones, place, neighbours, degree, mix, *refs):
    arrived, halves, (*outs, pair, items) = refs[:zones], refs[zones : zones + 2], refs[zones + 2 :]
    for index, value in enumerate(halves):
        pair[index] = value[...]
    _, slots, zone_rows, _ = mix.shape
    part = items.shape[-1]
    my_zone = place[1]
    group = 2 if part % LANES == 0 and steps % 2 == 0 else 1
    for index, step in enumerate((0,) + steps_over(zones)):
        items[my_zone ^ step] = arrived[index][...]

    for target, target_step in enumerate((0,) + steps_over(zones)):
        block = my_zone ^ target_step
        left = []
        for slot in range(slots):
            tile = mix[block, slot]
            left.append(jnp.where(degree[block] > slot, tile, jnp.zeros_like(tile)))
        left = jnp.concatenate(left, axis=1)
        for step in range(0, steps, group):
            right = []
            for slot in range(slots):
                source = neighbours[block, slot]
                right.append(
                    jnp.concatenate(
                        [
                            items[source, (step + index) * zone_rows : (step + index + 1) * zone_rows, :]
                            for index in range(group)
                        ],
                        axis=1,
                    )
                )
            result = jnp.dot(left, jnp.concatenate(right, axis=0), preferred_element_type=F32)
            for index in range(group):
                rows = slice((step + index) * zone_rows, (step + index + 1) * zone_rows)
                outs[target][rows, :] = result[:, index * part : (index + 1) * part].astype(BF16)


def slots_of(block):
    near = 2 + 2 * lax.rem(block, 2)
    return [lax.rem(block, SPREAD) ^ bits for bits in (0, near, 6 - near, 6)]


def fill_slots(zones, place, own_in, own_out, slots, pieces, w_in, w_out):
    my_zone = place[1]
    in_shard = own_in.shape[1]
    out_rows = own_out.shape[0] // SPREAD
    in_cols, width = own_in.shape[2], own_out.shape[1]
    own_rows = pl.ds(pl.multiple_of(my_zone * in_shard, in_shard), in_shard)
    own_out_rows = pl.ds(pl.multiple_of(my_zone * out_rows, out_rows), out_rows)
    for index, (slot, piece) in enumerate(zip(slots, pieces)):
        from_rows = pl.ds(pl.multiple_of(slot * out_rows, out_rows), out_rows)
        w_in[index, own_rows, :] = own_in[slot]
        w_out[index, own_out_rows, :] = own_out[from_rows, :]
        for step in range(1, zones):
            source = my_zone ^ step
            part = piece[step - 1]
            rows = pl.ds(pl.multiple_of(source * in_shard, in_shard), in_shard)
            w_in[index, rows, :] = part[:in_shard, :]
            rows = pl.ds(pl.multiple_of(source * out_rows, out_rows), out_rows)
            for fold in range(width // in_cols):
                low = in_shard + fold * out_rows
                w_out[index, rows, fold * in_cols : (fold + 1) * in_cols] = part[low : low + out_rows, :]


def order_kernel(zones, place, own_in, own_out, pair, far, swapped_pair, w_in, w_out):
    my_block = place[0]
    slots = slots_of(my_block) + slots_of(my_block ^ 1)[:2]
    pieces = [group.at[index] for group in (pair, far, swapped_pair) for index in range(2)]
    fill_slots(zones, place, own_in, own_out, slots, pieces, w_in, w_out)


def relay_kernel(ready, far, *refs):
    refs[-1][...] = far[...]


def grow(ffn_in, w_in, hidden):
    in_cols = w_in.shape[2]
    for index in range(w_in.shape[0]):
        grown = jnp.dot(ffn_in[...], w_in[index], preferred_element_type=F32)
        hidden[:, index * in_cols : (index + 1) * in_cols] = jax.nn.gelu(
            grown, approximate=True
        ).astype(BF16)


def ffn_kernel(zones, place, after_attn, gain_ffn, w_in, w_out, *refs):
    arrived, (total, ffn_in, parts, hidden) = refs[:zones], refs[zones:]
    rows_all, width = after_attn.shape
    my_zone = place[1]
    for index, step in enumerate((0,) + steps_over(zones)):
        parts[my_zone ^ step] = arrived[index][...]
    gain = gain_ffn[...]
    span = 128
    part = parts.shape[-1]
    for first in range(0, rows_all, span):
        rows = slice(first, first + span)
        for index in range(zones):
            cols = slice(index * part, (index + 1) * part)
            total[rows, cols] = after_attn[rows, cols] + parts[index, rows, :].astype(F32)
        ffn_in[rows, :] = rms_scale(total[rows, :], gain).astype(BF16)
    grow(ffn_in, w_in, hidden)
    weights = w_out[...].reshape(hidden.shape[1], w_out.shape[2])
    total[...] += jnp.dot(hidden[...], weights, preferred_element_type=F32)


def last_kernel(
    zones, place, own_in, own_out, total, ffn_in, swapped_far, out, w_in, w_out, hidden, rows_out, sems
):
    slots = slots_of(place[0] ^ 1)[2:]
    pieces = [swapped_far.at[index] for index in range(2)]
    fill_slots(zones, place, own_in, own_out, slots, pieces, w_in, w_out)
    grow(ffn_in, w_in, hidden)
    weights = w_out[...].reshape(hidden.shape[1], w_out.shape[2])
    span = total.shape[0] // sems.shape[0]
    copies = []
    for index in range(sems.shape[0]):
        rows = slice(index * span, (index + 1) * span)
        shrunk = jnp.dot(hidden[rows, :], weights, preferred_element_type=F32)
        rows_out[rows, :] = (total[rows, :] + shrunk).astype(BF16)
        copies.append(pltpu.make_async_copy(rows_out.at[rows, :], out.at[rows, :], sems.at[index]))
        copies[-1].start()
    for copy in copies:
        copy.wait()


def call(kernel, out_shape, scratch, smem, hbm, limit, args, out_space=pltpu.VMEM):
    spaces = {index: pltpu.SMEM for index in smem} | {index: pltpu.HBM for index in hbm}
    return pl.pallas_call(
        kernel,
        out_shape=out_shape,
        in_specs=[
            pl.BlockSpec(memory_space=spaces.get(index, pltpu.VMEM)) for index in range(len(args))
        ],
        out_specs=jax.tree.map(lambda _: pl.BlockSpec(memory_space=out_space), out_shape),
        scratch_shapes=scratch,
        cost_estimate=pl.CostEstimate(flops=0, bytes_accessed=0, transcendentals=0),
        compiler_params=pltpu.CompilerParams(vmem_limit_bytes=limit * MIB),
    )(*args)


def on_device(
    states,
    gain_attn,
    w_qkv,
    w_out_attn,
    pattern,
    gain_mix,
    neighbours,
    degree,
    mix,
    gain_ffn,
    w_in,
    w_out,
):
    steps, zone_rows, width = states.shape
    rows = steps * zone_rows
    reach = pattern.shape[1]
    zones = lax.axis_size("zone")
    my_block, my_zone = lax.axis_index("tm"), lax.axis_index("zone")
    place = jnp.stack([my_block, my_zone]).astype(jnp.int32)
    key_count = (reach + 1) * steps
    hidden = w_in.shape[1]
    in_cols = hidden // SPREAD
    out_rows = w_out.shape[0] // SPREAD
    part = width // zones
    exchanges = steps_over(zones)

    before = shifted(states, "tm", 2)
    first = lax.dynamic_slice_in_dim(
        jnp.concatenate([w_qkv, w_out_attn], axis=1), quarter_of(my_block) * width, width, axis=1
    )
    direct = [swapped(first, "zone", step) for step in exchanges]
    packed_rows = w_in.shape[0] + out_rows * (width // in_cols)
    own_in, packed = call(
        functools.partial(group_kernel, zones),
        (
            jax.ShapeDtypeStruct((SPREAD, w_in.shape[0], in_cols), BF16),
            jax.ShapeDtypeStruct((packed_rows, in_cols), BF16),
        ),
        [],
        (0,),
        (),
        4,
        [place, w_in, w_out],
    )
    beside = swapped(packed, "zone", 1)
    half_shape = jax.ShapeDtypeStruct((zones - 1, first.shape[0] // 2, width), BF16)
    direct, upper, lower, doubled, last = call(
        split_kernel,
        (
            jax.ShapeDtypeStruct((zones - 1,) + first.shape, BF16),
            half_shape,
            half_shape,
            jax.ShapeDtypeStruct((2,) + packed.shape, BF16),
            jax.ShapeDtypeStruct(states.shape, BF16),
        ),
        [],
        (0,),
        (),
        4,
        [place, packed, beside, states, before] + direct,
    )
    over = [crossed(value, "tm", 2, 4) for value in (upper, lower)]
    last = swapped(last, "tm", 1)
    pieces = [direct] + over + [swapped(value, "tm", 1) for value in [direct] + over]
    normed = call(
        norm_kernel,
        jax.ShapeDtypeStruct((key_count * zone_rows, width), BF16),
        [],
        (),
        (),
        4,
        [before, last, states, gain_attn.reshape(1, -1)],
    )
    bits = 2
    while 2 * bits < zones:
        doubled = jnp.concatenate([doubled, swapped(doubled, "zone", bits)], axis=0)
        bits *= 2
    context, w_attn = call(
        functools.partial(attention_kernel, zones, reach, steps),
        (
            jax.ShapeDtypeStruct((rows, width), BF16),
            jax.ShapeDtypeStruct((width, width), BF16),
        ),
        [
            pltpu.VMEM((4, width, width), BF16),
            pltpu.VMEM((3 * width, width), BF16),
            pltpu.VMEM((HEADS, 3 * (width // HEADS), key_count * zone_rows), F32),
            pltpu.VMEM((width, rows), F32),
        ],
        (0, 1),
        (),
        22,
        [place, pattern, normed, w_qkv, w_out_attn] + pieces,
    )

    chunk = jax.ShapeDtypeStruct((rows, part), BF16)
    after_attn, *chunks = call(
        project_kernel,
        (jax.ShapeDtypeStruct((rows, width), F32),)
        + (chunk,) * zones,
        [pltpu.VMEM((zones, rows, part), BF16)],
        (0,),
        (),
        8,
        [place, states, context, w_attn, gain_mix.reshape(1, -1)],
    )
    across = call(
        stack_kernel,
        jax.ShapeDtypeStruct((zones - 1,) + packed.shape, BF16),
        [],
        (),
        (),
        4,
        [doubled, swapped(doubled, "zone", bits), after_attn],
    )
    nearest = crossed(across, "tm", 2, 4)

    arrived = [chunks[0]] + [
        swapped(value, "zone", step) for value, step in zip(chunks[1:], exchanges)
    ]

    *spatial, pair = call(
        functools.partial(mixing_kernel, steps, zones),
        (chunk,) * zones
        + (jax.ShapeDtypeStruct((2,) + across.shape, BF16),),
        [pltpu.VMEM((zones, rows, part), BF16)],
        (0, 1, 2),
        (),
        8,
        [place, neighbours, degree, mix] + arrived + [across, nearest],
    )
    far = crossed(pair, "tm", 4, 2)
    full_in, full_out = call(
        functools.partial(order_kernel, zones),
        (
            jax.ShapeDtypeStruct((6, width, in_cols), BF16),
            jax.ShapeDtypeStruct((6, in_cols, width), BF16),
        ),
        [],
        (0,),
        (),
        8,
        [place, own_in, w_out, pair, far, swapped(pair, "tm", 1)],
    )
    arrived = [spatial[0]] + [
        swapped(value, "zone", step) for value, step in zip(spatial[1:], exchanges)
    ]
    far = call(
        relay_kernel,
        jax.ShapeDtypeStruct(far.shape, BF16),
        [],
        (),
        (),
        4,
        [full_out, far] + arrived[1:],
    )
    total, ffn_in = call(
        functools.partial(ffn_kernel, zones),
        (jax.ShapeDtypeStruct((rows, width), F32), jax.ShapeDtypeStruct((rows, width), BF16)),
        [pltpu.VMEM((zones, rows, part), BF16), pltpu.VMEM((rows, 6 * in_cols), BF16)],
        (0,),
        (),
        12,
        [place, after_attn, gain_ffn.reshape(1, -1), full_in, full_out] + arrived,
    )
    evolved = call(
        functools.partial(last_kernel, zones),
        jax.ShapeDtypeStruct((rows, width), BF16),
        [
            pltpu.VMEM((2, width, in_cols), BF16),
            pltpu.VMEM((2, in_cols, width), BF16),
            pltpu.VMEM((rows, 2 * in_cols), BF16),
            pltpu.VMEM((rows, width), BF16),
            pltpu.SemaphoreType.DMA((4,)),
        ],
        (0,),
        (),
        12,
        [place, own_in, w_out, total, ffn_in, swapped(far, "tm", 1)],
        pl.ANY,
    )
    return evolved.reshape(steps, zone_rows, width)


def solution(mesh):
    return jax.shard_map(
        on_device,
        mesh=mesh,
        in_specs=(
            P("tm", "zone", None),
            P(),
            P("zone", None),
            P("zone", None),
            P("tm", None),
            P(),
            P(),
            P(),
            P(),
            P(),
            P("zone", None),
            P("zone", None),
        ),
        out_specs=P("tm", "zone", None),
        check_vma=False,
    )
```

```python
import functools

import jax
import jax.numpy as jnp
from jax import lax
from jax.experimental import pallas as pl
from jax.experimental.pallas import tpu as pltpu
from jax.sharding import PartitionSpec as P

HEADS = 4
SPREAD = 8
LANES = 128
F32 = jnp.float32
BF16 = jnp.bfloat16
MIB = 1024 * 1024


def shifted(value, axis, steps):
    count = lax.axis_size(axis)
    return lax.ppermute(value, axis, [(source, source + steps) for source in range(count - steps)])


def swapped(value, axis, bits):
    count = lax.axis_size(axis)
    return lax.ppermute(value, axis, [(source, source ^ bits) for source in range(count)])


def crossed(value, axis, even_bits, odd_bits):
    count = lax.axis_size(axis)
    pairs = [(source, source ^ (odd_bits if source % 2 else even_bits)) for source in range(count)]
    return lax.ppermute(value, axis, pairs)


def steps_over(count):
    half = count // 2
    return tuple(range(half, count)) + tuple(range(1, half))


def rms_scale(values, gain):
    mean_sq = jnp.mean(values * values, axis=-1, keepdims=True)
    return values * lax.rsqrt(mean_sq + 1e-06) * gain


def quarter_of(block):
    core = lax.rem(block, 2)
    return (1 - core) * lax.rem(lax.div(block, 2), 2) + core * (2 + lax.rem(lax.div(block, 4), 2))


def row_sum(value):
    return jnp.sum(value, axis=0, keepdims=True)


def norm_kernel(*refs):
    blocks, (gain_attn, normed) = refs[:-2], refs[-2:]
    steps, zone_rows, _ = blocks[0].shape
    gain = gain_attn[...]
    for index, block in enumerate(blocks):
        for step in range(steps):
            row = (index * steps + step) * zone_rows
            normed[row : row + zone_rows, :] = rms_scale(block[step].astype(F32), gain).astype(BF16)


def group_kernel(zones, place, w_in, w_out, own_in, packed):
    in_shard, hidden = w_in.shape
    out_rows = w_out.shape[0] // SPREAD
    in_cols = hidden // SPREAD
    width = w_out.shape[1]
    for index in range(SPREAD):
        for source in range(zones):
            low = (source * SPREAD + index) * out_rows
            to = slice(source * out_rows, (source + 1) * out_rows)
            own_in[index, :, to] = w_in[:, low : low + out_rows]
    slot = lax.rem(place[0], SPREAD)
    packed[:in_shard, :] = own_in[slot]
    rows = pl.ds(pl.multiple_of(slot * out_rows, out_rows), out_rows)
    for fold in range(width // in_cols):
        low = in_shard + fold * out_rows
        packed[low : low + out_rows, :] = w_out[rows, fold * in_cols : (fold + 1) * in_cols]


def split_kernel(place, packed, beside, states, before, *refs):
    arrived, (direct, upper, lower, doubled, last) = refs[:-5], refs[-5:]
    half = upper.shape[1]
    for index, piece in enumerate(arrived):
        direct[index] = piece[...]
        upper[index] = piece[:half, :]
        lower[index] = piece[half:, :]
    doubled[0] = packed[...]
    doubled[1] = beside[...]
    last[...] = jnp.where(lax.rem(place[0], 2) == 1, before[...], states[...])


def stack_kernel(doubled, arrived, *refs):
    out = refs[-1]
    near = doubled.shape[0]
    out[: near - 1] = doubled[1:]
    out[near - 1 :] = arrived[...]


def attention_kernel(zones, reach, steps, place, pattern, normed, own_qkv, own_attn, *refs):
    pieces, (context_out, attn_out, weights, w_turned, projected, context) = refs[:-6], refs[-6:]
    key_count = (reach + 1) * steps
    zone_rows = normed.shape[0] // key_count
    width = normed.shape[1]
    head_size = width // HEADS
    my_block, my_zone = place[0], place[1]
    shard = own_qkv.shape[0]

    own_rows = pl.ds(pl.multiple_of(my_zone * shard, shard), shard)
    for index in range(3):
        weights[index, own_rows, :] = own_qkv[:, index * width : (index + 1) * width]
    weights[3, own_rows, :] = own_attn[...]
    half = shard // 2
    mine, other = quarter_of(my_block), quarter_of(my_block ^ 1)
    for place_in, step in enumerate(steps_over(zones)):
        start = (my_zone ^ step) * shard
        for piece, quarter, low in zip(
            pieces, (mine, mine ^ 1, mine ^ 1, other, other ^ 1, other ^ 1), (0, 0, half, 0, 0, half)
        ):
            rows = pl.ds(pl.multiple_of(start + low, half), piece.shape[1])
            weights[quarter, rows, :] = piece[place_in]
    attn_out[...] = weights[3]
    group = 3 * head_size
    def turn(head):
        for kind in range(3):
            rows = slice(head * group + kind * head_size, head * group + (kind + 1) * head_size)
            w_turned[rows, :] = weights[kind, :, head * head_size : (head + 1) * head_size].T

    def project(head, first, span):
        skip = 0 if first >= reach * steps * zone_rows else head_size
        projected[head, skip:, first : first + span] = lax.dot_general(
            w_turned[head * group + skip : (head + 1) * group, :],
            normed[first : first + span, :],
            (((1,), (1,)), ((), ())),
            preferred_element_type=F32,
        )

    span = 2 * zone_rows
    pending = [(head, first) for head in range(HEADS) for first in range(0, key_count * zone_rows, span)]

    def project_some(count):
        for _ in range(min(count, len(pending))):
            head, first = pending.pop(0)
            if first == 0:
                turn(head)
            project(head, first, span)

    allowed_back = [
        (pattern[0, back - 1] == 1) & (my_block >= back) for back in range(reach, 0, -1)
    ]
    chunks = head_size // 8

    def usable(query):
        return range(reach * steps + query + 1)

    def attend(head, queries):
        def tile(kind, chunk, key):
            row = kind * head_size + chunk * 8
            return projected[head, row : row + 8, key * zone_rows : (key + 1) * zone_rows]

        sums = {}
        for chunk in range(chunks):
            q_tiles = {q: tile(0, chunk, reach * steps + q) for q in queries}
            for key in usable(queries[-1]):
                k_tile = tile(1, chunk, key)
                for q in queries:
                    if key in usable(q):
                        term = q_tiles[q] * k_tile
                        sums[q, key] = term if chunk == 0 else sums[q, key] + term
        weights_of, scales = {}, {}
        for q in queries:
            scores = jnp.concatenate([row_sum(sums[q, key]) for key in usable(q)], axis=0)
            scores = scores * head_size ** (-0.5)
            row_id = lax.broadcasted_iota(jnp.int32, scores.shape, 0)
            allowed = row_id >= reach * steps
            for index, live in enumerate(allowed_back):
                inside = (row_id >= index * steps) & (row_id < (index + 1) * steps)
                allowed = allowed | (inside & live)
            masked = jnp.where(allowed, scores, -1e30)
            top = jnp.max(masked, axis=0, keepdims=True)
            expw = jnp.where(allowed, jnp.exp(masked - top), 0.0)
            scales[q] = jnp.broadcast_to(1.0 / row_sum(expw), (8, zone_rows))
            probs = expw.astype(BF16).astype(F32)
            for key in usable(q):
                weights_of[q, key] = jnp.broadcast_to(probs[key : key + 1, :], (8, zone_rows))
        for chunk in range(chunks):
            sums = {}
            for key in usable(queries[-1]):
                v_tile = tile(2, chunk, key)
                for q in queries:
                    if key in usable(q):
                        term = weights_of[q, key] * v_tile
                        sums[q] = term if key == 0 else sums[q] + term
            for q in queries:
                row = head * head_size + chunk * 8
                context[row : row + 8, q * zone_rows : (q + 1) * zone_rows] = sums[q] * scales[q]

    spans = key_count * zone_rows // span
    project_some(spans)
    pairs = range(0, steps, 2)
    for head in range(HEADS):
        for pair in pairs:
            project_some(-(-spans // len(pairs)))
            attend(head, range(pair, min(pair + 2, steps)))

    for step in range(steps):
        rows = slice(step * zone_rows, (step + 1) * zone_rows)
        context_out[rows, :] = context[:, rows].T.astype(BF16)


def project_kernel(place, states, context, w_attn, gain_mix, after_out, *refs):
    *outs, parts = refs
    steps, zone_rows, _ = states.shape
    zones, _, part = parts.shape
    my_zone = place[1]
    gain = gain_mix[...]
    for step in range(steps):
        rows = slice(step * zone_rows, (step + 1) * zone_rows)
        after = states[step].astype(F32) + jnp.dot(
            context[rows, :], w_attn[...], preferred_element_type=F32
        )
        after_out[rows, :] = after
        mixin = rms_scale(after, gain).astype(BF16)
        for index in range(zones):
            parts[index, rows, :] = mixin[:, index * part : (index + 1) * part]
    for index, step in enumerate((0,) + steps_over(zones)):
        outs[index][...] = parts[my_zone ^ step]


def mixing_kernel(steps, zones, place, neighbours, degree, mix, *refs):
    arrived, halves, (*outs, pair, items) = refs[:zones], refs[zones : zones + 2], refs[zones + 2 :]
    for index, value in enumerate(halves):
        pair[index] = value[...]
    _, slots, zone_rows, _ = mix.shape
    part = items.shape[-1]
    my_zone = place[1]
    group = 2 if part % LANES == 0 and steps % 2 == 0 else 1
    for index, step in enumerate((0,) + steps_over(zones)):
        items[my_zone ^ step] = arrived[index][...]

    for target, target_step in enumerate((0,) + steps_over(zones)):
        block = my_zone ^ target_step
        left = []
        for slot in range(slots):
            tile = mix[block, slot]
            left.append(jnp.where(degree[block] > slot, tile, jnp.zeros_like(tile)))
        left = jnp.concatenate(left, axis=1)
        for step in range(0, steps, group):
            right = []
            for slot in range(slots):
                source = neighbours[block, slot]
                right.append(
                    jnp.concatenate(
                        [
                            items[source, (step + index) * zone_rows : (step + index + 1) * zone_rows, :]
                            for index in range(group)
                        ],
                        axis=1,
                    )
                )
            result = jnp.dot(left, jnp.concatenate(right, axis=0), preferred_element_type=F32)
            for index in range(group):
                rows = slice((step + index) * zone_rows, (step + index + 1) * zone_rows)
                outs[target][rows, :] = result[:, index * part : (index + 1) * part].astype(BF16)


def slots_of(block):
    near = 2 + 2 * lax.rem(block, 2)
    return [lax.rem(block, SPREAD) ^ bits for bits in (0, near, 6 - near, 6)]


def fill_slots(zones, place, own_in, own_out, slots, pieces, w_in, w_out):
    my_zone = place[1]
    in_shard = own_in.shape[1]
    out_rows = own_out.shape[0] // SPREAD
    in_cols, width = own_in.shape[2], own_out.shape[1]
    own_rows = pl.ds(pl.multiple_of(my_zone * in_shard, in_shard), in_shard)
    own_out_rows = pl.ds(pl.multiple_of(my_zone * out_rows, out_rows), out_rows)
    for index, (slot, piece) in enumerate(zip(slots, pieces)):
        from_rows = pl.ds(pl.multiple_of(slot * out_rows, out_rows), out_rows)
        w_in[index, own_rows, :] = own_in[slot]
        w_out[index, own_out_rows, :] = own_out[from_rows, :]
        for step in range(1, zones):
            source = my_zone ^ step
            part = piece[step - 1]
            rows = pl.ds(pl.multiple_of(source * in_shard, in_shard), in_shard)
            w_in[index, rows, :] = part[:in_shard, :]
            rows = pl.ds(pl.multiple_of(source * out_rows, out_rows), out_rows)
            for fold in range(width // in_cols):
                low = in_shard + fold * out_rows
                w_out[index, rows, fold * in_cols : (fold + 1) * in_cols] = part[low : low + out_rows, :]


def order_kernel(zones, place, gain, own_in, own_out, pair, far, swapped_pair, w_in, w_out, gain_out):
    gain_out[...] = gain[...]
    my_block = place[0]
    slots = slots_of(my_block) + slots_of(my_block ^ 1)[:2]
    pieces = [group.at[index] for group in (pair, far, swapped_pair) for index in range(2)]
    fill_slots(zones, place, own_in, own_out, slots, pieces, w_in, w_out)


def relay_kernel(ready, far, *refs):
    refs[-1][...] = far[...]


def grow(ffn_in, w_in, hidden):
    in_cols = w_in.shape[2]
    for index in range(w_in.shape[0]):
        grown = jnp.dot(ffn_in[...], w_in[index], preferred_element_type=F32)
        hidden[:, index * in_cols : (index + 1) * in_cols] = jax.nn.gelu(
            grown, approximate=True
        ).astype(BF16)


def ffn_kernel(zones, place, after_attn, gain_ffn, w_in, w_out, *refs):
    arrived, (total, ffn_in, parts, hidden) = refs[:zones], refs[zones:]
    rows_all, width = after_attn.shape
    my_zone = place[1]
    for index, step in enumerate((0,) + steps_over(zones)):
        parts[my_zone ^ step] = arrived[index][...]
    gain = gain_ffn[...]
    span = 128
    part = parts.shape[-1]
    for first in range(0, rows_all, span):
        rows = slice(first, first + span)
        for index in range(zones):
            cols = slice(index * part, (index + 1) * part)
            total[rows, cols] = after_attn[rows, cols] + parts[index, rows, :].astype(F32)
        ffn_in[rows, :] = rms_scale(total[rows, :], gain).astype(BF16)
    grow(ffn_in, w_in, hidden)
    weights = w_out[...].reshape(hidden.shape[1], w_out.shape[2])
    total[...] += jnp.dot(hidden[...], weights, preferred_element_type=F32)


def last_kernel(
    zones, place, own_in, own_out, total, ffn_in, swapped_far, out, w_in, w_out, hidden, rows_out, sems
):
    slots = slots_of(place[0] ^ 1)[2:]
    pieces = [swapped_far.at[index] for index in range(2)]
    fill_slots(zones, place, own_in, own_out, slots, pieces, w_in, w_out)
    grow(ffn_in, w_in, hidden)
    weights = w_out[...].reshape(hidden.shape[1], w_out.shape[2])
    span = total.shape[0] // sems.shape[0]
    copies = []
    for index in range(sems.shape[0]):
        rows = slice(index * span, (index + 1) * span)
        shrunk = jnp.dot(hidden[rows, :], weights, preferred_element_type=F32)
        rows_out[rows, :] = (total[rows, :] + shrunk).astype(BF16)
        copies.append(pltpu.make_async_copy(rows_out.at[rows, :], out.at[rows, :], sems.at[index]))
        copies[-1].start()
    for copy in copies:
        copy.wait()


def call(kernel, out_shape, scratch, smem, hbm, limit, args, out_space=pltpu.VMEM):
    spaces = {index: pltpu.SMEM for index in smem} | {index: pltpu.HBM for index in hbm}
    return pl.pallas_call(
        kernel,
        out_shape=out_shape,
        in_specs=[
            pl.BlockSpec(memory_space=spaces.get(index, pltpu.VMEM)) for index in range(len(args))
        ],
        out_specs=jax.tree.map(lambda _: pl.BlockSpec(memory_space=out_space), out_shape),
        scratch_shapes=scratch,
        cost_estimate=pl.CostEstimate(flops=0, bytes_accessed=0, transcendentals=0),
        compiler_params=pltpu.CompilerParams(vmem_limit_bytes=limit * MIB),
    )(*args)


def on_device(
    states,
    gain_attn,
    w_qkv,
    w_out_attn,
    pattern,
    gain_mix,
    neighbours,
    degree,
    mix,
    gain_ffn,
    w_in,
    w_out,
):
    steps, zone_rows, width = states.shape
    rows = steps * zone_rows
    reach = pattern.shape[1]
    zones = lax.axis_size("zone")
    my_block, my_zone = lax.axis_index("tm"), lax.axis_index("zone")
    place = jnp.stack([my_block, my_zone]).astype(jnp.int32)
    key_count = (reach + 1) * steps
    hidden = w_in.shape[1]
    in_cols = hidden // SPREAD
    out_rows = w_out.shape[0] // SPREAD
    part = width // zones
    exchanges = steps_over(zones)

    before = shifted(states, "tm", 2)
    first = lax.dynamic_slice_in_dim(
        jnp.concatenate([w_qkv, w_out_attn], axis=1), quarter_of(my_block) * width, width, axis=1
    )
    direct = [swapped(first, "zone", step) for step in exchanges]
    packed_rows = w_in.shape[0] + out_rows * (width // in_cols)
    own_in, packed = call(
        functools.partial(group_kernel, zones),
        (
            jax.ShapeDtypeStruct((SPREAD, w_in.shape[0], in_cols), BF16),
            jax.ShapeDtypeStruct((packed_rows, in_cols), BF16),
        ),
        [],
        (0,),
        (),
        4,
        [place, w_in, w_out],
    )
    beside = swapped(packed, "zone", 1)
    half_shape = jax.ShapeDtypeStruct((zones - 1, first.shape[0] // 2, width), BF16)
    direct, upper, lower, doubled, last = call(
        split_kernel,
        (
            jax.ShapeDtypeStruct((zones - 1,) + first.shape, BF16),
            half_shape,
            half_shape,
            jax.ShapeDtypeStruct((2,) + packed.shape, BF16),
            jax.ShapeDtypeStruct(states.shape, BF16),
        ),
        [],
        (0,),
        (),
        4,
        [place, packed, beside, states, before] + direct,
    )
    over = [crossed(value, "tm", 2, 4) for value in (upper, lower)]
    last = swapped(last, "tm", 1)
    pieces = [direct] + over + [swapped(value, "tm", 1) for value in [direct] + over]
    normed = call(
        norm_kernel,
        jax.ShapeDtypeStruct((key_count * zone_rows, width), BF16),
        [],
        (),
        (),
        4,
        [before, last, states, gain_attn.reshape(1, -1)],
    )
    bits = 2
    while 2 * bits < zones:
        doubled = jnp.concatenate([doubled, swapped(doubled, "zone", bits)], axis=0)
        bits *= 2
    context, w_attn = call(
        functools.partial(attention_kernel, zones, reach, steps),
        (
            jax.ShapeDtypeStruct((rows, width), BF16),
            jax.ShapeDtypeStruct((width, width), BF16),
        ),
        [
            pltpu.VMEM((4, width, width), BF16),
            pltpu.VMEM((3 * width, width), BF16),
            pltpu.VMEM((HEADS, 3 * (width // HEADS), key_count * zone_rows), F32),
            pltpu.VMEM((width, rows), F32),
        ],
        (0, 1),
        (),
        22,
        [place, pattern, normed, w_qkv, w_out_attn] + pieces,
    )

    chunk = jax.ShapeDtypeStruct((rows, part), BF16)
    after_attn, *chunks = call(
        project_kernel,
        (jax.ShapeDtypeStruct((rows, width), F32),)
        + (chunk,) * zones,
        [pltpu.VMEM((zones, rows, part), BF16)],
        (0,),
        (),
        8,
        [place, states, context, w_attn, gain_mix.reshape(1, -1)],
    )
    across = call(
        stack_kernel,
        jax.ShapeDtypeStruct((zones - 1,) + packed.shape, BF16),
        [],
        (),
        (),
        4,
        [doubled, swapped(doubled, "zone", bits), after_attn],
    )
    nearest = crossed(across, "tm", 2, 4)

    arrived = [chunks[0]] + [
        swapped(value, "zone", step) for value, step in zip(chunks[1:], exchanges)
    ]

    *spatial, pair = call(
        functools.partial(mixing_kernel, steps, zones),
        (chunk,) * zones
        + (jax.ShapeDtypeStruct((2,) + across.shape, BF16),),
        [pltpu.VMEM((zones, rows, part), BF16)],
        (0, 1, 2),
        (),
        8,
        [place, neighbours, degree, mix] + arrived + [across, nearest],
    )
    far = crossed(pair, "tm", 4, 2)
    full_in, full_out, gain = call(
        functools.partial(order_kernel, zones),
        (
            jax.ShapeDtypeStruct((6, width, in_cols), BF16),
            jax.ShapeDtypeStruct((6, in_cols, width), BF16),
            jax.ShapeDtypeStruct((1, width), F32),
        ),
        [],
        (0,),
        (),
        8,
        [place, gain_ffn.reshape(1, -1), own_in, w_out, pair, far, swapped(pair, "tm", 1)],
    )
    arrived = [spatial[0]] + [
        swapped(value, "zone", step) for value, step in zip(spatial[1:], exchanges)
    ]
    far = call(
        relay_kernel,
        jax.ShapeDtypeStruct(far.shape, BF16),
        [],
        (),
        (),
        4,
        [full_out, far] + arrived[1:],
    )
    total, ffn_in = call(
        functools.partial(ffn_kernel, zones),
        (jax.ShapeDtypeStruct((rows, width), F32), jax.ShapeDtypeStruct((rows, width), BF16)),
        [pltpu.VMEM((zones, rows, part), BF16), pltpu.VMEM((rows, 6 * in_cols), BF16)],
        (0,),
        (),
        12,
        [place, after_attn, gain, full_in, full_out] + arrived,
    )
    evolved = call(
        functools.partial(last_kernel, zones),
        jax.ShapeDtypeStruct((rows, width), BF16),
        [
            pltpu.VMEM((2, width, in_cols), BF16),
            pltpu.VMEM((2, in_cols, width), BF16),
            pltpu.VMEM((rows, 2 * in_cols), BF16),
            pltpu.VMEM((rows, width), BF16),
            pltpu.SemaphoreType.DMA((4,)),
        ],
        (0,),
        (),
        12,
        [place, own_in, w_out, total, ffn_in, swapped(far, "tm", 1)],
        pl.ANY,
    )
    return evolved.reshape(steps, zone_rows, width)


def solution(mesh):
    return jax.shard_map(
        on_device,
        mesh=mesh,
        in_specs=(
            P("tm", "zone", None),
            P(),
            P("zone", None),
            P("zone", None),
            P("tm", None),
            P(),
            P(),
            P(),
            P(),
            P(),
            P("zone", None),
            P("zone", None),
        ),
        out_specs=P("tm", "zone", None),
        check_vma=False,
    )
```

```python
import functools

import jax
import jax.numpy as jnp
from jax import lax
from jax.experimental import pallas as pl
from jax.experimental.pallas import tpu as pltpu
from jax.sharding import PartitionSpec as P

HEADS = 4
SPREAD = 8
LANES = 128
F32 = jnp.float32
BF16 = jnp.bfloat16
MIB = 1024 * 1024


def shifted(value, axis, steps):
    count = lax.axis_size(axis)
    return lax.ppermute(value, axis, [(source, source + steps) for source in range(count - steps)])


def swapped(value, axis, bits):
    count = lax.axis_size(axis)
    return lax.ppermute(value, axis, [(source, source ^ bits) for source in range(count)])


def crossed(value, axis, even_bits, odd_bits):
    count = lax.axis_size(axis)
    pairs = [(source, source ^ (odd_bits if source % 2 else even_bits)) for source in range(count)]
    return lax.ppermute(value, axis, pairs)


def steps_over(count):
    half = count // 2
    return tuple(range(half, count)) + tuple(range(1, half))


def rms_scale(values, gain):
    mean_sq = jnp.mean(values * values, axis=-1, keepdims=True)
    return values * lax.rsqrt(mean_sq + 1e-06) * gain


def quarter_of(block):
    core = lax.rem(block, 2)
    return (1 - core) * lax.rem(lax.div(block, 2), 2) + core * (2 + lax.rem(lax.div(block, 4), 2))


def row_sum(value):
    return jnp.sum(value, axis=0, keepdims=True)


def norm_kernel(*refs):
    blocks, (gain_attn, normed) = refs[:-2], refs[-2:]
    steps, zone_rows, _ = blocks[0].shape
    gain = gain_attn[...]
    for index, block in enumerate(blocks):
        for step in range(steps):
            row = (index * steps + step) * zone_rows
            normed[row : row + zone_rows, :] = rms_scale(block[step].astype(F32), gain).astype(BF16)


def group_kernel(zones, place, w_in, w_out, own_in, packed):
    in_shard, hidden = w_in.shape
    out_rows = w_out.shape[0] // SPREAD
    in_cols = hidden // SPREAD
    width = w_out.shape[1]
    for index in range(SPREAD):
        for source in range(zones):
            low = (source * SPREAD + index) * out_rows
            to = slice(source * out_rows, (source + 1) * out_rows)
            own_in[index, :, to] = w_in[:, low : low + out_rows]
    slot = lax.rem(place[0], SPREAD)
    packed[:in_shard, :] = own_in[slot]
    rows = pl.ds(pl.multiple_of(slot * out_rows, out_rows), out_rows)
    for fold in range(width // in_cols):
        low = in_shard + fold * out_rows
        packed[low : low + out_rows, :] = w_out[rows, fold * in_cols : (fold + 1) * in_cols]


def split_kernel(place, packed, beside, states, before, *refs):
    arrived, (direct, upper, lower, doubled, last) = refs[:-5], refs[-5:]
    half = upper.shape[1]
    for index, piece in enumerate(arrived):
        direct[index] = piece[...]
        upper[index] = piece[:half, :]
        lower[index] = piece[half:, :]
    doubled[0] = packed[...]
    doubled[1] = beside[...]
    last[...] = jnp.where(lax.rem(place[0], 2) == 1, before[...], states[...])


def stack_kernel(doubled, arrived, *refs):
    out = refs[-1]
    near = doubled.shape[0]
    out[: near - 1] = doubled[1:]
    out[near - 1 :] = arrived[...]


def attention_kernel(zones, reach, steps, place, pattern, normed, own_qkv, own_attn, *refs):
    pieces, (context_out, attn_out, weights, w_turned, projected, context) = refs[:-6], refs[-6:]
    key_count = (reach + 1) * steps
    zone_rows = normed.shape[0] // key_count
    width = normed.shape[1]
    head_size = width // HEADS
    my_block, my_zone = place[0], place[1]
    shard = own_qkv.shape[0]

    own_rows = pl.ds(pl.multiple_of(my_zone * shard, shard), shard)
    for index in range(3):
        weights[index, own_rows, :] = own_qkv[:, index * width : (index + 1) * width]
    weights[3, own_rows, :] = own_attn[...]
    half = shard // 2
    mine, other = quarter_of(my_block), quarter_of(my_block ^ 1)
    for place_in, step in enumerate(steps_over(zones)):
        start = (my_zone ^ step) * shard
        for piece, quarter, low in zip(
            pieces, (mine, mine ^ 1, mine ^ 1, other, other ^ 1, other ^ 1), (0, 0, half, 0, 0, half)
        ):
            rows = pl.ds(pl.multiple_of(start + low, half), piece.shape[1])
            weights[quarter, rows, :] = piece[place_in]
    attn_out[...] = weights[3]
    group = 3 * head_size
    def turn(head):
        for kind in range(3):
            rows = slice(head * group + kind * head_size, head * group + (kind + 1) * head_size)
            w_turned[rows, :] = weights[kind, :, head * head_size : (head + 1) * head_size].T

    def project(head, first, span):
        skip = 0 if first >= reach * steps * zone_rows else head_size
        projected[head, skip:, first : first + span] = lax.dot_general(
            w_turned[head * group + skip : (head + 1) * group, :],
            normed[first : first + span, :],
            (((1,), (1,)), ((), ())),
            preferred_element_type=F32,
        )

    span = 2 * zone_rows
    pending = [(head, first) for head in range(HEADS) for first in range(0, key_count * zone_rows, span)]

    def project_some(count):
        for _ in range(min(count, len(pending))):
            head, first = pending.pop(0)
            if first == 0:
                turn(head)
            project(head, first, span)

    allowed_back = [
        (pattern[0, back - 1] == 1) & (my_block >= back) for back in range(reach, 0, -1)
    ]
    chunks = head_size // 8

    def usable(query):
        return range(reach * steps + query + 1)

    spans = key_count * zone_rows // span
    pairs = range(0, steps, 2)
    every = 2 * chunks * len(pairs) // spans
    ticks = [0]

    def tick(head):
        ticks[0] += 1
        if ticks[0] % every == 0 and pending and pending[0][0] <= head + 1:
            project_some(1)

    def attend(head, queries):
        def tile(kind, chunk, key):
            row = kind * head_size + chunk * 8
            return projected[head, row : row + 8, key * zone_rows : (key + 1) * zone_rows]

        sums = {}
        for chunk in range(chunks):
            q_tiles = {q: tile(0, chunk, reach * steps + q) for q in queries}
            for key in usable(queries[-1]):
                k_tile = tile(1, chunk, key)
                for q in queries:
                    if key in usable(q):
                        term = q_tiles[q] * k_tile
                        sums[q, key] = term if chunk == 0 else sums[q, key] + term
            tick(head)
        weights_of, scales = {}, {}
        for q in queries:
            scores = jnp.concatenate([row_sum(sums[q, key]) for key in usable(q)], axis=0)
            scores = scores * head_size ** (-0.5)
            row_id = lax.broadcasted_iota(jnp.int32, scores.shape, 0)
            allowed = row_id >= reach * steps
            for index, live in enumerate(allowed_back):
                inside = (row_id >= index * steps) & (row_id < (index + 1) * steps)
                allowed = allowed | (inside & live)
            masked = jnp.where(allowed, scores, -1e30)
            top = jnp.max(masked, axis=0, keepdims=True)
            expw = jnp.where(allowed, jnp.exp(masked - top), 0.0)
            scales[q] = jnp.broadcast_to(1.0 / row_sum(expw), (8, zone_rows))
            probs = expw.astype(BF16).astype(F32)
            for key in usable(q):
                weights_of[q, key] = jnp.broadcast_to(probs[key : key + 1, :], (8, zone_rows))
        for chunk in range(chunks):
            sums = {}
            for key in usable(queries[-1]):
                v_tile = tile(2, chunk, key)
                for q in queries:
                    if key in usable(q):
                        term = weights_of[q, key] * v_tile
                        sums[q] = term if key == 0 else sums[q] + term
            for q in queries:
                row = head * head_size + chunk * 8
                context[row : row + 8, q * zone_rows : (q + 1) * zone_rows] = sums[q] * scales[q]
            tick(head)

    for head in range(HEADS):
        while pending and pending[0][0] <= head:
            project_some(1)
        for pair in pairs:
            attend(head, range(pair, min(pair + 2, steps)))

    for step in range(steps):
        rows = slice(step * zone_rows, (step + 1) * zone_rows)
        context_out[rows, :] = context[:, rows].T.astype(BF16)


def project_kernel(place, states, context, w_attn, gain_mix, after_out, *refs):
    *outs, parts = refs
    steps, zone_rows, _ = states.shape
    zones, _, part = parts.shape
    my_zone = place[1]
    gain = gain_mix[...]
    for step in range(steps):
        rows = slice(step * zone_rows, (step + 1) * zone_rows)
        after = states[step].astype(F32) + jnp.dot(
            context[rows, :], w_attn[...], preferred_element_type=F32
        )
        after_out[rows, :] = after
        mixin = rms_scale(after, gain).astype(BF16)
        for index in range(zones):
            parts[index, rows, :] = mixin[:, index * part : (index + 1) * part]
    for index, step in enumerate((0,) + steps_over(zones)):
        outs[index][...] = parts[my_zone ^ step]


def mixing_kernel(steps, zones, place, neighbours, degree, mix, *refs):
    arrived, halves, (*outs, pair, items) = refs[:zones], refs[zones : zones + 2], refs[zones + 2 :]
    for index, value in enumerate(halves):
        pair[index] = value[...]
    _, slots, zone_rows, _ = mix.shape
    part = items.shape[-1]
    my_zone = place[1]
    group = 2 if part % LANES == 0 and steps % 2 == 0 else 1
    for index, step in enumerate((0,) + steps_over(zones)):
        items[my_zone ^ step] = arrived[index][...]

    for target, target_step in enumerate((0,) + steps_over(zones)):
        block = my_zone ^ target_step
        left = []
        for slot in range(slots):
            tile = mix[block, slot]
            left.append(jnp.where(degree[block] > slot, tile, jnp.zeros_like(tile)))
        left = jnp.concatenate(left, axis=1)
        for step in range(0, steps, group):
            right = []
            for slot in range(slots):
                source = neighbours[block, slot]
                right.append(
                    jnp.concatenate(
                        [
                            items[source, (step + index) * zone_rows : (step + index + 1) * zone_rows, :]
                            for index in range(group)
                        ],
                        axis=1,
                    )
                )
            result = jnp.dot(left, jnp.concatenate(right, axis=0), preferred_element_type=F32)
            for index in range(group):
                rows = slice((step + index) * zone_rows, (step + index + 1) * zone_rows)
                outs[target][rows, :] = result[:, index * part : (index + 1) * part].astype(BF16)


def slots_of(block):
    near = 2 + 2 * lax.rem(block, 2)
    return [lax.rem(block, SPREAD) ^ bits for bits in (0, near, 6 - near, 6)]


def fill_slots(zones, place, own_in, own_out, slots, pieces, w_in, w_out):
    my_zone = place[1]
    in_shard = own_in.shape[1]
    out_rows = own_out.shape[0] // SPREAD
    in_cols, width = own_in.shape[2], own_out.shape[1]
    own_rows = pl.ds(pl.multiple_of(my_zone * in_shard, in_shard), in_shard)
    own_out_rows = pl.ds(pl.multiple_of(my_zone * out_rows, out_rows), out_rows)
    for index, (slot, piece) in enumerate(zip(slots, pieces)):
        from_rows = pl.ds(pl.multiple_of(slot * out_rows, out_rows), out_rows)
        w_in[index, own_rows, :] = own_in[slot]
        w_out[index, own_out_rows, :] = own_out[from_rows, :]
        for step in range(1, zones):
            source = my_zone ^ step
            part = piece[step - 1]
            rows = pl.ds(pl.multiple_of(source * in_shard, in_shard), in_shard)
            w_in[index, rows, :] = part[:in_shard, :]
            rows = pl.ds(pl.multiple_of(source * out_rows, out_rows), out_rows)
            for fold in range(width // in_cols):
                low = in_shard + fold * out_rows
                w_out[index, rows, fold * in_cols : (fold + 1) * in_cols] = part[low : low + out_rows, :]


def order_kernel(zones, place, gain, own_in, own_out, pair, far, swapped_pair, w_in, w_out, gain_out):
    gain_out[...] = gain[...]
    my_block = place[0]
    slots = slots_of(my_block) + slots_of(my_block ^ 1)[:2]
    pieces = [group.at[index] for group in (pair, far, swapped_pair) for index in range(2)]
    fill_slots(zones, place, own_in, own_out, slots, pieces, w_in, w_out)


def relay_kernel(ready, far, *refs):
    refs[-1][...] = far[...]


def grow(ffn_in, w_in, hidden):
    in_cols = w_in.shape[2]
    for index in range(w_in.shape[0]):
        grown = jnp.dot(ffn_in[...], w_in[index], preferred_element_type=F32)
        hidden[:, index * in_cols : (index + 1) * in_cols] = jax.nn.gelu(
            grown, approximate=True
        ).astype(BF16)


def ffn_kernel(zones, place, after_attn, gain_ffn, w_in, w_out, *refs):
    arrived, (total, ffn_in, parts, hidden) = refs[:zones], refs[zones:]
    rows_all, width = after_attn.shape
    my_zone = place[1]
    for index, step in enumerate((0,) + steps_over(zones)):
        parts[my_zone ^ step] = arrived[index][...]
    gain = gain_ffn[...]
    span = 128
    part = parts.shape[-1]
    for first in range(0, rows_all, span):
        rows = slice(first, first + span)
        for index in range(zones):
            cols = slice(index * part, (index + 1) * part)
            total[rows, cols] = after_attn[rows, cols] + parts[index, rows, :].astype(F32)
        ffn_in[rows, :] = rms_scale(total[rows, :], gain).astype(BF16)
    grow(ffn_in, w_in, hidden)
    weights = w_out[...].reshape(hidden.shape[1], w_out.shape[2])
    total[...] += jnp.dot(hidden[...], weights, preferred_element_type=F32)


def last_kernel(
    zones, place, own_in, own_out, total, ffn_in, swapped_far, out, w_in, w_out, hidden, rows_out, sems
):
    slots = slots_of(place[0] ^ 1)[2:]
    pieces = [swapped_far.at[index] for index in range(2)]
    fill_slots(zones, place, own_in, own_out, slots, pieces, w_in, w_out)
    grow(ffn_in, w_in, hidden)
    weights = w_out[...].reshape(hidden.shape[1], w_out.shape[2])
    span = total.shape[0] // sems.shape[0]
    copies = []
    for index in range(sems.shape[0]):
        rows = slice(index * span, (index + 1) * span)
        shrunk = jnp.dot(hidden[rows, :], weights, preferred_element_type=F32)
        rows_out[rows, :] = (total[rows, :] + shrunk).astype(BF16)
        copies.append(pltpu.make_async_copy(rows_out.at[rows, :], out.at[rows, :], sems.at[index]))
        copies[-1].start()
    for copy in copies:
        copy.wait()


def call(kernel, out_shape, scratch, smem, hbm, limit, args, out_space=pltpu.VMEM):
    spaces = {index: pltpu.SMEM for index in smem} | {index: pltpu.HBM for index in hbm}
    return pl.pallas_call(
        kernel,
        out_shape=out_shape,
        in_specs=[
            pl.BlockSpec(memory_space=spaces.get(index, pltpu.VMEM)) for index in range(len(args))
        ],
        out_specs=jax.tree.map(lambda _: pl.BlockSpec(memory_space=out_space), out_shape),
        scratch_shapes=scratch,
        cost_estimate=pl.CostEstimate(flops=0, bytes_accessed=0, transcendentals=0),
        compiler_params=pltpu.CompilerParams(vmem_limit_bytes=limit * MIB),
    )(*args)


def on_device(
    states,
    gain_attn,
    w_qkv,
    w_out_attn,
    pattern,
    gain_mix,
    neighbours,
    degree,
    mix,
    gain_ffn,
    w_in,
    w_out,
):
    steps, zone_rows, width = states.shape
    rows = steps * zone_rows
    reach = pattern.shape[1]
    zones = lax.axis_size("zone")
    my_block, my_zone = lax.axis_index("tm"), lax.axis_index("zone")
    place = jnp.stack([my_block, my_zone]).astype(jnp.int32)
    key_count = (reach + 1) * steps
    hidden = w_in.shape[1]
    in_cols = hidden // SPREAD
    out_rows = w_out.shape[0] // SPREAD
    part = width // zones
    exchanges = steps_over(zones)

    before = shifted(states, "tm", 2)
    first = lax.dynamic_slice_in_dim(
        jnp.concatenate([w_qkv, w_out_attn], axis=1), quarter_of(my_block) * width, width, axis=1
    )
    direct = [swapped(first, "zone", step) for step in exchanges]
    packed_rows = w_in.shape[0] + out_rows * (width // in_cols)
    own_in, packed = call(
        functools.partial(group_kernel, zones),
        (
            jax.ShapeDtypeStruct((SPREAD, w_in.shape[0], in_cols), BF16),
            jax.ShapeDtypeStruct((packed_rows, in_cols), BF16),
        ),
        [],
        (0,),
        (),
        4,
        [place, w_in, w_out],
    )
    beside = swapped(packed, "zone", 1)
    half_shape = jax.ShapeDtypeStruct((zones - 1, first.shape[0] // 2, width), BF16)
    direct, upper, lower, doubled, last = call(
        split_kernel,
        (
            jax.ShapeDtypeStruct((zones - 1,) + first.shape, BF16),
            half_shape,
            half_shape,
            jax.ShapeDtypeStruct((2,) + packed.shape, BF16),
            jax.ShapeDtypeStruct(states.shape, BF16),
        ),
        [],
        (0,),
        (),
        4,
        [place, packed, beside, states, before] + direct,
    )
    over = [crossed(value, "tm", 2, 4) for value in (upper, lower)]
    last = swapped(last, "tm", 1)
    pieces = [direct] + over + [swapped(value, "tm", 1) for value in [direct] + over]
    normed = call(
        norm_kernel,
        jax.ShapeDtypeStruct((key_count * zone_rows, width), BF16),
        [],
        (),
        (),
        4,
        [before, last, states, gain_attn.reshape(1, -1)],
    )
    bits = 2
    while 2 * bits < zones:
        doubled = jnp.concatenate([doubled, swapped(doubled, "zone", bits)], axis=0)
        bits *= 2
    context, w_attn = call(
        functools.partial(attention_kernel, zones, reach, steps),
        (
            jax.ShapeDtypeStruct((rows, width), BF16),
            jax.ShapeDtypeStruct((width, width), BF16),
        ),
        [
            pltpu.VMEM((4, width, width), BF16),
            pltpu.VMEM((3 * width, width), BF16),
            pltpu.VMEM((HEADS, 3 * (width // HEADS), key_count * zone_rows), F32),
            pltpu.VMEM((width, rows), F32),
        ],
        (0, 1),
        (),
        22,
        [place, pattern, normed, w_qkv, w_out_attn] + pieces,
    )

    chunk = jax.ShapeDtypeStruct((rows, part), BF16)
    after_attn, *chunks = call(
        project_kernel,
        (jax.ShapeDtypeStruct((rows, width), F32),)
        + (chunk,) * zones,
        [pltpu.VMEM((zones, rows, part), BF16)],
        (0,),
        (),
        8,
        [place, states, context, w_attn, gain_mix.reshape(1, -1)],
    )
    across = call(
        stack_kernel,
        jax.ShapeDtypeStruct((zones - 1,) + packed.shape, BF16),
        [],
        (),
        (),
        4,
        [doubled, swapped(doubled, "zone", bits), after_attn],
    )
    nearest = crossed(across, "tm", 2, 4)

    arrived = [chunks[0]] + [
        swapped(value, "zone", step) for value, step in zip(chunks[1:], exchanges)
    ]

    *spatial, pair = call(
        functools.partial(mixing_kernel, steps, zones),
        (chunk,) * zones
        + (jax.ShapeDtypeStruct((2,) + across.shape, BF16),),
        [pltpu.VMEM((zones, rows, part), BF16)],
        (0, 1, 2),
        (),
        8,
        [place, neighbours, degree, mix] + arrived + [across, nearest],
    )
    far = crossed(pair, "tm", 4, 2)
    full_in, full_out, gain = call(
        functools.partial(order_kernel, zones),
        (
            jax.ShapeDtypeStruct((6, width, in_cols), BF16),
            jax.ShapeDtypeStruct((6, in_cols, width), BF16),
            jax.ShapeDtypeStruct((1, width), F32),
        ),
        [],
        (0,),
        (),
        8,
        [place, gain_ffn.reshape(1, -1), own_in, w_out, pair, far, swapped(pair, "tm", 1)],
    )
    arrived = [spatial[0]] + [
        swapped(value, "zone", step) for value, step in zip(spatial[1:], exchanges)
    ]
    far = call(
        relay_kernel,
        jax.ShapeDtypeStruct(far.shape, BF16),
        [],
        (),
        (),
        4,
        [full_out, far] + arrived[1:],
    )
    total, ffn_in = call(
        functools.partial(ffn_kernel, zones),
        (jax.ShapeDtypeStruct((rows, width), F32), jax.ShapeDtypeStruct((rows, width), BF16)),
        [pltpu.VMEM((zones, rows, part), BF16), pltpu.VMEM((rows, 6 * in_cols), BF16)],
        (0,),
        (),
        12,
        [place, after_attn, gain, full_in, full_out] + arrived,
    )
    evolved = call(
        functools.partial(last_kernel, zones),
        jax.ShapeDtypeStruct((rows, width), BF16),
        [
            pltpu.VMEM((2, width, in_cols), BF16),
            pltpu.VMEM((2, in_cols, width), BF16),
            pltpu.VMEM((rows, 2 * in_cols), BF16),
            pltpu.VMEM((rows, width), BF16),
            pltpu.SemaphoreType.DMA((4,)),
        ],
        (0,),
        (),
        12,
        [place, own_in, w_out, total, ffn_in, swapped(far, "tm", 1)],
        pl.ANY,
    )
    return evolved.reshape(steps, zone_rows, width)


def solution(mesh):
    return jax.shard_map(
        on_device,
        mesh=mesh,
        in_specs=(
            P("tm", "zone", None),
            P(),
            P("zone", None),
            P("zone", None),
            P("tm", None),
            P(),
            P(),
            P(),
            P(),
            P(),
            P("zone", None),
            P("zone", None),
        ),
        out_specs=P("tm", "zone", None),
        check_vma=False,
    )
```

```python
import functools

import jax
import jax.numpy as jnp
from jax import lax
from jax.experimental import pallas as pl
from jax.experimental.pallas import tpu as pltpu
from jax.sharding import PartitionSpec as P

HEADS = 4
SPREAD = 8
LANES = 128
F32 = jnp.float32
BF16 = jnp.bfloat16
MIB = 1024 * 1024


def shifted(value, axis, steps):
    count = lax.axis_size(axis)
    return lax.ppermute(value, axis, [(source, source + steps) for source in range(count - steps)])


def swapped(value, axis, bits):
    count = lax.axis_size(axis)
    return lax.ppermute(value, axis, [(source, source ^ bits) for source in range(count)])


def crossed(value, axis, even_bits, odd_bits):
    count = lax.axis_size(axis)
    pairs = [(source, source ^ (odd_bits if source % 2 else even_bits)) for source in range(count)]
    return lax.ppermute(value, axis, pairs)


def steps_over(count):
    half = count // 2
    return tuple(range(half, count)) + tuple(range(1, half))


def rms_scale(values, gain):
    mean_sq = jnp.mean(values * values, axis=-1, keepdims=True)
    return values * lax.rsqrt(mean_sq + 1e-06) * gain


def quarter_of(block):
    core = lax.rem(block, 2)
    return (1 - core) * lax.rem(lax.div(block, 2), 2) + core * (2 + lax.rem(lax.div(block, 4), 2))


def row_sum(value):
    return jnp.sum(value, axis=0, keepdims=True)


def norm_kernel(*refs):
    blocks, (gain_attn, normed) = refs[:-2], refs[-2:]
    steps, zone_rows, _ = blocks[0].shape
    gain = gain_attn[...]
    for index, block in enumerate(blocks):
        for step in range(steps):
            row = (index * steps + step) * zone_rows
            normed[row : row + zone_rows, :] = rms_scale(block[step].astype(F32), gain).astype(BF16)


def group_kernel(zones, place, w_in, w_out, own_in, packed):
    in_shard, hidden = w_in.shape
    out_rows = w_out.shape[0] // SPREAD
    in_cols = hidden // SPREAD
    width = w_out.shape[1]
    for index in range(SPREAD):
        for source in range(zones):
            low = (source * SPREAD + index) * out_rows
            to = slice(source * out_rows, (source + 1) * out_rows)
            own_in[index, :, to] = w_in[:, low : low + out_rows]
    slot = lax.rem(place[0], SPREAD)
    packed[:in_shard, :] = own_in[slot]
    rows = pl.ds(pl.multiple_of(slot * out_rows, out_rows), out_rows)
    for fold in range(width // in_cols):
        low = in_shard + fold * out_rows
        packed[low : low + out_rows, :] = w_out[rows, fold * in_cols : (fold + 1) * in_cols]


def split_kernel(place, packed, beside, states, before, *refs):
    arrived, (direct, upper, lower, doubled, last) = refs[:-5], refs[-5:]
    half = upper.shape[1]
    for index, piece in enumerate(arrived):
        direct[index] = piece[...]
        upper[index] = piece[:half, :]
        lower[index] = piece[half:, :]
    doubled[0] = packed[...]
    doubled[1] = beside[...]
    last[...] = jnp.where(lax.rem(place[0], 2) == 1, before[...], states[...])


def stack_kernel(doubled, arrived, *refs):
    out = refs[-1]
    near = doubled.shape[0]
    out[: near - 1] = doubled[1:]
    out[near - 1 :] = arrived[...]


def attention_kernel(zones, reach, steps, place, pattern, normed, own_qkv, own_attn, *refs):
    pieces, (context_out, attn_out, weights, w_turned, projected, context) = refs[:-6], refs[-6:]
    key_count = (reach + 1) * steps
    zone_rows = normed.shape[0] // key_count
    width = normed.shape[1]
    head_size = width // HEADS
    my_block, my_zone = place[0], place[1]
    shard = own_qkv.shape[0]

    own_rows = pl.ds(pl.multiple_of(my_zone * shard, shard), shard)
    for index in range(3):
        weights[index, own_rows, :] = own_qkv[:, index * width : (index + 1) * width]
    weights[3, own_rows, :] = own_attn[...]
    half = shard // 2
    mine, other = quarter_of(my_block), quarter_of(my_block ^ 1)
    for place_in, step in enumerate(steps_over(zones)):
        start = (my_zone ^ step) * shard
        for piece, quarter, low in zip(
            pieces, (mine, mine ^ 1, mine ^ 1, other, other ^ 1, other ^ 1), (0, 0, half, 0, 0, half)
        ):
            rows = pl.ds(pl.multiple_of(start + low, half), piece.shape[1])
            weights[quarter, rows, :] = piece[place_in]
    attn_out[...] = weights[3]
    group = 3 * head_size
    def turn(head):
        for kind in range(3):
            rows = slice(head * group + kind * head_size, head * group + (kind + 1) * head_size)
            w_turned[rows, :] = weights[kind, :, head * head_size : (head + 1) * head_size].T

    def project(head, first, span):
        skip = 0 if first >= reach * steps * zone_rows else head_size
        projected[head, skip:, first : first + span] = lax.dot_general(
            w_turned[head * group + skip : (head + 1) * group, :],
            normed[first : first + span, :],
            (((1,), (1,)), ((), ())),
            preferred_element_type=F32,
        ).astype(BF16).astype(F32)

    span = 2 * zone_rows
    pending = [(head, first) for head in range(HEADS) for first in range(0, key_count * zone_rows, span)]

    def project_some(count):
        for _ in range(min(count, len(pending))):
            head, first = pending.pop(0)
            if first == 0:
                turn(head)
            project(head, first, span)

    allowed_back = [
        (pattern[0, back - 1] == 1) & (my_block >= back) for back in range(reach, 0, -1)
    ]
    chunks = head_size // 8

    def usable(query):
        return range(reach * steps + query + 1)

    def attend(head, queries):
        def tile(kind, chunk, key):
            row = kind * head_size + chunk * 8
            return projected[head, row : row + 8, key * zone_rows : (key + 1) * zone_rows]

        sums = {}
        for chunk in range(chunks):
            q_tiles = {q: tile(0, chunk, reach * steps + q) for q in queries}
            for key in usable(queries[-1]):
                k_tile = tile(1, chunk, key)
                for q in queries:
                    if key in usable(q):
                        term = q_tiles[q] * k_tile
                        sums[q, key] = term if chunk == 0 else sums[q, key] + term
        weights_of, scales = {}, {}
        for q in queries:
            scores = jnp.concatenate([row_sum(sums[q, key]) for key in usable(q)], axis=0)
            scores = scores * head_size ** (-0.5)
            row_id = lax.broadcasted_iota(jnp.int32, scores.shape, 0)
            allowed = row_id >= reach * steps
            for index, live in enumerate(allowed_back):
                inside = (row_id >= index * steps) & (row_id < (index + 1) * steps)
                allowed = allowed | (inside & live)
            masked = jnp.where(allowed, scores, -1e30)
            top = jnp.max(masked, axis=0, keepdims=True)
            expw = jnp.where(allowed, jnp.exp(masked - top), 0.0)
            scales[q] = jnp.broadcast_to(1.0 / row_sum(expw), (8, zone_rows))
            probs = expw.astype(BF16).astype(F32)
            for key in usable(q):
                weights_of[q, key] = jnp.broadcast_to(probs[key : key + 1, :], (8, zone_rows))
        for chunk in range(chunks):
            sums = {}
            for key in usable(queries[-1]):
                v_tile = tile(2, chunk, key)
                for q in queries:
                    if key in usable(q):
                        term = weights_of[q, key] * v_tile
                        sums[q] = term if key == 0 else sums[q] + term
            for q in queries:
                row = head * head_size + chunk * 8
                context[row : row + 8, q * zone_rows : (q + 1) * zone_rows] = sums[q] * scales[q]

    spans = key_count * zone_rows // span
    project_some(spans)
    pairs = range(0, steps, 2)
    for head in range(HEADS):
        for pair in pairs:
            project_some(-(-spans // len(pairs)))
            attend(head, range(pair, min(pair + 2, steps)))

    for step in range(steps):
        rows = slice(step * zone_rows, (step + 1) * zone_rows)
        context_out[rows, :] = context[:, rows].T.astype(BF16)


def project_kernel(place, states, context, w_attn, gain_mix, after_out, *refs):
    *outs, parts = refs
    steps, zone_rows, _ = states.shape
    zones, _, part = parts.shape
    my_zone = place[1]
    gain = gain_mix[...]
    for step in range(steps):
        rows = slice(step * zone_rows, (step + 1) * zone_rows)
        after = states[step].astype(F32) + jnp.dot(
            context[rows, :], w_attn[...], preferred_element_type=F32
        )
        after_out[rows, :] = after
        mixin = rms_scale(after, gain).astype(BF16)
        for index in range(zones):
            parts[index, rows, :] = mixin[:, index * part : (index + 1) * part]
    for index, step in enumerate((0,) + steps_over(zones)):
        outs[index][...] = parts[my_zone ^ step]


def mixing_kernel(steps, zones, place, neighbours, degree, mix, *refs):
    arrived, halves, (*outs, pair, items) = refs[:zones], refs[zones : zones + 2], refs[zones + 2 :]
    for index, value in enumerate(halves):
        pair[index] = value[...]
    _, slots, zone_rows, _ = mix.shape
    part = items.shape[-1]
    my_zone = place[1]
    group = 2 if part % LANES == 0 and steps % 2 == 0 else 1
    for index, step in enumerate((0,) + steps_over(zones)):
        items[my_zone ^ step] = arrived[index][...]

    for target, target_step in enumerate((0,) + steps_over(zones)):
        block = my_zone ^ target_step
        left = []
        for slot in range(slots):
            tile = mix[block, slot]
            left.append(jnp.where(degree[block] > slot, tile, jnp.zeros_like(tile)))
        left = jnp.concatenate(left, axis=1)
        for step in range(0, steps, group):
            right = []
            for slot in range(slots):
                source = neighbours[block, slot]
                right.append(
                    jnp.concatenate(
                        [
                            items[source, (step + index) * zone_rows : (step + index + 1) * zone_rows, :]
                            for index in range(group)
                        ],
                        axis=1,
                    )
                )
            result = jnp.dot(left, jnp.concatenate(right, axis=0), preferred_element_type=F32)
            for index in range(group):
                rows = slice((step + index) * zone_rows, (step + index + 1) * zone_rows)
                outs[target][rows, :] = result[:, index * part : (index + 1) * part].astype(BF16)


def slots_of(block):
    near = 2 + 2 * lax.rem(block, 2)
    return [lax.rem(block, SPREAD) ^ bits for bits in (0, near, 6 - near, 6)]


def fill_slots(zones, place, own_in, own_out, slots, pieces, w_in, w_out):
    my_zone = place[1]
    in_shard = own_in.shape[1]
    out_rows = own_out.shape[0] // SPREAD
    in_cols, width = own_in.shape[2], own_out.shape[1]
    own_rows = pl.ds(pl.multiple_of(my_zone * in_shard, in_shard), in_shard)
    own_out_rows = pl.ds(pl.multiple_of(my_zone * out_rows, out_rows), out_rows)
    for index, (slot, piece) in enumerate(zip(slots, pieces)):
        from_rows = pl.ds(pl.multiple_of(slot * out_rows, out_rows), out_rows)
        w_in[index, own_rows, :] = own_in[slot]
        w_out[index, own_out_rows, :] = own_out[from_rows, :]
        for step in range(1, zones):
            source = my_zone ^ step
            part = piece[step - 1]
            rows = pl.ds(pl.multiple_of(source * in_shard, in_shard), in_shard)
            w_in[index, rows, :] = part[:in_shard, :]
            rows = pl.ds(pl.multiple_of(source * out_rows, out_rows), out_rows)
            for fold in range(width // in_cols):
                low = in_shard + fold * out_rows
                w_out[index, rows, fold * in_cols : (fold + 1) * in_cols] = part[low : low + out_rows, :]


def order_kernel(zones, place, gain, own_in, own_out, pair, far, swapped_pair, w_in, w_out, gain_out):
    gain_out[...] = gain[...]
    my_block = place[0]
    slots = slots_of(my_block) + slots_of(my_block ^ 1)[:2]
    pieces = [group.at[index] for group in (pair, far, swapped_pair) for index in range(2)]
    fill_slots(zones, place, own_in, own_out, slots, pieces, w_in, w_out)


def relay_kernel(ready, far, *refs):
    refs[-1][...] = far[...]


def grow(ffn_in, w_in, hidden):
    in_cols = w_in.shape[2]
    for index in range(w_in.shape[0]):
        grown = jnp.dot(ffn_in[...], w_in[index], preferred_element_type=F32)
        hidden[:, index * in_cols : (index + 1) * in_cols] = jax.nn.gelu(
            grown, approximate=True
        ).astype(BF16)


def ffn_kernel(zones, place, after_attn, gain_ffn, w_in, w_out, *refs):
    arrived, (total, ffn_in, parts, hidden) = refs[:zones], refs[zones:]
    rows_all, width = after_attn.shape
    my_zone = place[1]
    for index, step in enumerate((0,) + steps_over(zones)):
        parts[my_zone ^ step] = arrived[index][...]
    gain = gain_ffn[...]
    span = 128
    part = parts.shape[-1]
    for first in range(0, rows_all, span):
        rows = slice(first, first + span)
        for index in range(zones):
            cols = slice(index * part, (index + 1) * part)
            total[rows, cols] = after_attn[rows, cols] + parts[index, rows, :].astype(F32)
        ffn_in[rows, :] = rms_scale(total[rows, :], gain).astype(BF16)
    grow(ffn_in, w_in, hidden)
    weights = w_out[...].reshape(hidden.shape[1], w_out.shape[2])
    total[...] += jnp.dot(hidden[...], weights, preferred_element_type=F32)


def last_kernel(
    zones, place, own_in, own_out, total, ffn_in, swapped_far, out, w_in, w_out, hidden, rows_out, sems
):
    slots = slots_of(place[0] ^ 1)[2:]
    pieces = [swapped_far.at[index] for index in range(2)]
    fill_slots(zones, place, own_in, own_out, slots, pieces, w_in, w_out)
    grow(ffn_in, w_in, hidden)
    weights = w_out[...].reshape(hidden.shape[1], w_out.shape[2])
    span = total.shape[0] // sems.shape[0]
    copies = []
    for index in range(sems.shape[0]):
        rows = slice(index * span, (index + 1) * span)
        shrunk = jnp.dot(hidden[rows, :], weights, preferred_element_type=F32)
        rows_out[rows, :] = (total[rows, :] + shrunk).astype(BF16)
        copies.append(pltpu.make_async_copy(rows_out.at[rows, :], out.at[rows, :], sems.at[index]))
        copies[-1].start()
    for copy in copies:
        copy.wait()


def call(kernel, out_shape, scratch, smem, hbm, limit, args, out_space=pltpu.VMEM):
    spaces = {index: pltpu.SMEM for index in smem} | {index: pltpu.HBM for index in hbm}
    return pl.pallas_call(
        kernel,
        out_shape=out_shape,
        in_specs=[
            pl.BlockSpec(memory_space=spaces.get(index, pltpu.VMEM)) for index in range(len(args))
        ],
        out_specs=jax.tree.map(lambda _: pl.BlockSpec(memory_space=out_space), out_shape),
        scratch_shapes=scratch,
        cost_estimate=pl.CostEstimate(flops=0, bytes_accessed=0, transcendentals=0),
        compiler_params=pltpu.CompilerParams(vmem_limit_bytes=limit * MIB),
    )(*args)


def on_device(
    states,
    gain_attn,
    w_qkv,
    w_out_attn,
    pattern,
    gain_mix,
    neighbours,
    degree,
    mix,
    gain_ffn,
    w_in,
    w_out,
):
    steps, zone_rows, width = states.shape
    rows = steps * zone_rows
    reach = pattern.shape[1]
    zones = lax.axis_size("zone")
    my_block, my_zone = lax.axis_index("tm"), lax.axis_index("zone")
    place = jnp.stack([my_block, my_zone]).astype(jnp.int32)
    key_count = (reach + 1) * steps
    hidden = w_in.shape[1]
    in_cols = hidden // SPREAD
    out_rows = w_out.shape[0] // SPREAD
    part = width // zones
    exchanges = steps_over(zones)

    before = shifted(states, "tm", 2)
    first = lax.dynamic_slice_in_dim(
        jnp.concatenate([w_qkv, w_out_attn], axis=1), quarter_of(my_block) * width, width, axis=1
    )
    direct = [swapped(first, "zone", step) for step in exchanges]
    packed_rows = w_in.shape[0] + out_rows * (width // in_cols)
    own_in, packed = call(
        functools.partial(group_kernel, zones),
        (
            jax.ShapeDtypeStruct((SPREAD, w_in.shape[0], in_cols), BF16),
            jax.ShapeDtypeStruct((packed_rows, in_cols), BF16),
        ),
        [],
        (0,),
        (),
        4,
        [place, w_in, w_out],
    )
    beside = swapped(packed, "zone", 1)
    half_shape = jax.ShapeDtypeStruct((zones - 1, first.shape[0] // 2, width), BF16)
    direct, upper, lower, doubled, last = call(
        split_kernel,
        (
            jax.ShapeDtypeStruct((zones - 1,) + first.shape, BF16),
            half_shape,
            half_shape,
            jax.ShapeDtypeStruct((2,) + packed.shape, BF16),
            jax.ShapeDtypeStruct(states.shape, BF16),
        ),
        [],
        (0,),
        (),
        4,
        [place, packed, beside, states, before] + direct,
    )
    over = [crossed(value, "tm", 2, 4) for value in (upper, lower)]
    last = swapped(last, "tm", 1)
    pieces = [direct] + over + [swapped(value, "tm", 1) for value in [direct] + over]
    normed = call(
        norm_kernel,
        jax.ShapeDtypeStruct((key_count * zone_rows, width), BF16),
        [],
        (),
        (),
        4,
        [before, last, states, gain_attn.reshape(1, -1)],
    )
    bits = 2
    while 2 * bits < zones:
        doubled = jnp.concatenate([doubled, swapped(doubled, "zone", bits)], axis=0)
        bits *= 2
    context, w_attn = call(
        functools.partial(attention_kernel, zones, reach, steps),
        (
            jax.ShapeDtypeStruct((rows, width), BF16),
            jax.ShapeDtypeStruct((width, width), BF16),
        ),
        [
            pltpu.VMEM((4, width, width), BF16),
            pltpu.VMEM((3 * width, width), BF16),
            pltpu.VMEM((HEADS, 3 * (width // HEADS), key_count * zone_rows), F32),
            pltpu.VMEM((width, rows), F32),
        ],
        (0, 1),
        (),
        22,
        [place, pattern, normed, w_qkv, w_out_attn] + pieces,
    )

    chunk = jax.ShapeDtypeStruct((rows, part), BF16)
    after_attn, *chunks = call(
        project_kernel,
        (jax.ShapeDtypeStruct((rows, width), F32),)
        + (chunk,) * zones,
        [pltpu.VMEM((zones, rows, part), BF16)],
        (0,),
        (),
        8,
        [place, states, context, w_attn, gain_mix.reshape(1, -1)],
    )
    across = call(
        stack_kernel,
        jax.ShapeDtypeStruct((zones - 1,) + packed.shape, BF16),
        [],
        (),
        (),
        4,
        [doubled, swapped(doubled, "zone", bits), after_attn],
    )
    nearest = crossed(across, "tm", 2, 4)

    arrived = [chunks[0]] + [
        swapped(value, "zone", step) for value, step in zip(chunks[1:], exchanges)
    ]

    *spatial, pair = call(
        functools.partial(mixing_kernel, steps, zones),
        (chunk,) * zones
        + (jax.ShapeDtypeStruct((2,) + across.shape, BF16),),
        [pltpu.VMEM((zones, rows, part), BF16)],
        (0, 1, 2),
        (),
        8,
        [place, neighbours, degree, mix] + arrived + [across, nearest],
    )
    far = crossed(pair, "tm", 4, 2)
    full_in, full_out, gain = call(
        functools.partial(order_kernel, zones),
        (
            jax.ShapeDtypeStruct((6, width, in_cols), BF16),
            jax.ShapeDtypeStruct((6, in_cols, width), BF16),
            jax.ShapeDtypeStruct((1, width), F32),
        ),
        [],
        (0,),
        (),
        8,
        [place, gain_ffn.reshape(1, -1), own_in, w_out, pair, far, swapped(pair, "tm", 1)],
    )
    arrived = [spatial[0]] + [
        swapped(value, "zone", step) for value, step in zip(spatial[1:], exchanges)
    ]
    far = call(
        relay_kernel,
        jax.ShapeDtypeStruct(far.shape, BF16),
        [],
        (),
        (),
        4,
        [full_out, far] + arrived[1:],
    )
    total, ffn_in = call(
        functools.partial(ffn_kernel, zones),
        (jax.ShapeDtypeStruct((rows, width), F32), jax.ShapeDtypeStruct((rows, width), BF16)),
        [pltpu.VMEM((zones, rows, part), BF16), pltpu.VMEM((rows, 6 * in_cols), BF16)],
        (0,),
        (),
        12,
        [place, after_attn, gain, full_in, full_out] + arrived,
    )
    evolved = call(
        functools.partial(last_kernel, zones),
        jax.ShapeDtypeStruct((rows, width), BF16),
        [
            pltpu.VMEM((2, width, in_cols), BF16),
            pltpu.VMEM((2, in_cols, width), BF16),
            pltpu.VMEM((rows, 2 * in_cols), BF16),
            pltpu.VMEM((rows, width), BF16),
            pltpu.SemaphoreType.DMA((4,)),
        ],
        (0,),
        (),
        12,
        [place, own_in, w_out, total, ffn_in, swapped(far, "tm", 1)],
        pl.ANY,
    )
    return evolved.reshape(steps, zone_rows, width)


def solution(mesh):
    return jax.shard_map(
        on_device,
        mesh=mesh,
        in_specs=(
            P("tm", "zone", None),
            P(),
            P("zone", None),
            P("zone", None),
            P("tm", None),
            P(),
            P(),
            P(),
            P(),
            P(),
            P("zone", None),
            P("zone", None),
        ),
        out_specs=P("tm", "zone", None),
        check_vma=False,
    )
```

```python
import functools

import jax
import jax.numpy as jnp
from jax import lax
from jax.experimental import pallas as pl
from jax.experimental.pallas import tpu as pltpu
from jax.sharding import PartitionSpec as P

HEADS = 4
SPREAD = 8
LANES = 128
F32 = jnp.float32
BF16 = jnp.bfloat16
MIB = 1024 * 1024


def shifted(value, axis, steps):
    count = lax.axis_size(axis)
    return lax.ppermute(value, axis, [(source, source + steps) for source in range(count - steps)])


def swapped(value, axis, bits):
    count = lax.axis_size(axis)
    return lax.ppermute(value, axis, [(source, source ^ bits) for source in range(count)])


def crossed(value, axis, even_bits, odd_bits):
    count = lax.axis_size(axis)
    pairs = [(source, source ^ (odd_bits if source % 2 else even_bits)) for source in range(count)]
    return lax.ppermute(value, axis, pairs)


def steps_over(count):
    half = count // 2
    return tuple(range(half, count)) + tuple(range(1, half))


def rms_scale(values, gain):
    mean_sq = jnp.mean(values * values, axis=-1, keepdims=True)
    return values * lax.rsqrt(mean_sq + 1e-06) * gain


def quarter_of(block):
    core = lax.rem(block, 2)
    return (1 - core) * lax.rem(lax.div(block, 2), 2) + core * (2 + lax.rem(lax.div(block, 4), 2))


def row_sum(value):
    return jnp.sum(value, axis=0, keepdims=True)


def norm_kernel(*refs):
    blocks, (gain_attn, normed) = refs[:-2], refs[-2:]
    steps, zone_rows, _ = blocks[0].shape
    gain = gain_attn[...]
    for index, block in enumerate(blocks):
        for step in range(steps):
            row = (index * steps + step) * zone_rows
            normed[row : row + zone_rows, :] = rms_scale(block[step].astype(F32), gain).astype(BF16)


def group_kernel(zones, place, w_in, w_out, own_in, packed):
    in_shard, hidden = w_in.shape
    out_rows = w_out.shape[0] // SPREAD
    in_cols = hidden // SPREAD
    width = w_out.shape[1]
    for index in range(SPREAD):
        for source in range(zones):
            low = (source * SPREAD + index) * out_rows
            to = slice(source * out_rows, (source + 1) * out_rows)
            own_in[index, :, to] = w_in[:, low : low + out_rows]
    slot = lax.rem(place[0], SPREAD)
    packed[:in_shard, :] = own_in[slot]
    rows = pl.ds(pl.multiple_of(slot * out_rows, out_rows), out_rows)
    for fold in range(width // in_cols):
        low = in_shard + fold * out_rows
        packed[low : low + out_rows, :] = w_out[rows, fold * in_cols : (fold + 1) * in_cols]


def split_kernel(place, packed, beside, states, before, *refs):
    arrived, (direct, upper, lower, doubled, last) = refs[:-5], refs[-5:]
    half = upper.shape[1]
    for index, piece in enumerate(arrived):
        direct[index] = piece[...]
        upper[index] = piece[:half, :]
        lower[index] = piece[half:, :]
    doubled[0] = packed[...]
    doubled[1] = beside[...]
    last[...] = jnp.where(lax.rem(place[0], 2) == 1, before[...], states[...])


def stack_kernel(doubled, arrived, *refs):
    out = refs[-1]
    near = doubled.shape[0]
    out[: near - 1] = doubled[1:]
    for index in range(near):
        out[2 * near - 2 - index] = arrived[index]


def attention_kernel(zones, reach, steps, place, pattern, normed, own_qkv, own_attn, *refs):
    pieces, (context_out, attn_out, weights, w_turned, projected, context) = refs[:-6], refs[-6:]
    key_count = (reach + 1) * steps
    zone_rows = normed.shape[0] // key_count
    width = normed.shape[1]
    head_size = width // HEADS
    my_block, my_zone = place[0], place[1]
    shard = own_qkv.shape[0]

    own_rows = pl.ds(pl.multiple_of(my_zone * shard, shard), shard)
    for index in range(3):
        weights[index, own_rows, :] = own_qkv[:, index * width : (index + 1) * width]
    weights[3, own_rows, :] = own_attn[...]
    half = shard // 2
    mine, other = quarter_of(my_block), quarter_of(my_block ^ 1)
    for place_in, step in enumerate(steps_over(zones)):
        start = (my_zone ^ step) * shard
        for piece, quarter, low in zip(
            pieces, (mine, mine ^ 1, mine ^ 1, other, other ^ 1, other ^ 1), (0, 0, half, 0, 0, half)
        ):
            rows = pl.ds(pl.multiple_of(start + low, half), piece.shape[1])
            weights[quarter, rows, :] = piece[place_in]
    attn_out[...] = weights[3]
    group = 3 * head_size
    def turn(head):
        for kind in range(3):
            rows = slice(head * group + kind * head_size, head * group + (kind + 1) * head_size)
            w_turned[rows, :] = weights[kind, :, head * head_size : (head + 1) * head_size].T

    def project(head, first, span):
        skip = 0 if first >= reach * steps * zone_rows else head_size
        projected[head, skip:, first : first + span] = lax.dot_general(
            w_turned[head * group + skip : (head + 1) * group, :],
            normed[first : first + span, :],
            (((1,), (1,)), ((), ())),
            preferred_element_type=F32,
        ).astype(BF16).astype(F32)

    span = 2 * zone_rows
    pending = [(head, first) for head in range(HEADS) for first in range(0, key_count * zone_rows, span)]

    def project_some(count):
        for _ in range(min(count, len(pending))):
            head, first = pending.pop(0)
            if first == 0:
                turn(head)
            project(head, first, span)

    allowed_back = [
        (pattern[0, back - 1] == 1) & (my_block >= back) for back in range(reach, 0, -1)
    ]
    chunks = head_size // 8

    def usable(query):
        return range(reach * steps + query + 1)

    def attend(head, queries):
        def tile(kind, chunk, key):
            row = kind * head_size + chunk * 8
            return projected[head, row : row + 8, key * zone_rows : (key + 1) * zone_rows]

        sums = {}
        for chunk in range(chunks):
            q_tiles = {q: tile(0, chunk, reach * steps + q) for q in queries}
            for key in usable(queries[-1]):
                k_tile = tile(1, chunk, key)
                for q in queries:
                    if key in usable(q):
                        term = q_tiles[q] * k_tile
                        sums[q, key] = term if chunk == 0 else sums[q, key] + term
        weights_of, scales = {}, {}
        for q in queries:
            scores = jnp.concatenate([row_sum(sums[q, key]) for key in usable(q)], axis=0)
            scores = scores * head_size ** (-0.5)
            row_id = lax.broadcasted_iota(jnp.int32, scores.shape, 0)
            allowed = row_id >= reach * steps
            for index, live in enumerate(allowed_back):
                inside = (row_id >= index * steps) & (row_id < (index + 1) * steps)
                allowed = allowed | (inside & live)
            masked = jnp.where(allowed, scores, -1e30)
            top = jnp.max(masked, axis=0, keepdims=True)
            expw = jnp.where(allowed, jnp.exp(masked - top), 0.0)
            scales[q] = jnp.broadcast_to(1.0 / row_sum(expw), (8, zone_rows))
            probs = expw.astype(BF16).astype(F32)
            for key in usable(q):
                weights_of[q, key] = jnp.broadcast_to(probs[key : key + 1, :], (8, zone_rows))
        for chunk in range(chunks):
            sums = {}
            for key in usable(queries[-1]):
                v_tile = tile(2, chunk, key)
                for q in queries:
                    if key in usable(q):
                        term = weights_of[q, key] * v_tile
                        sums[q] = term if key == 0 else sums[q] + term
            for q in queries:
                row = head * head_size + chunk * 8
                context[row : row + 8, q * zone_rows : (q + 1) * zone_rows] = sums[q] * scales[q]

    spans = key_count * zone_rows // span
    project_some(spans)
    pairs = range(0, steps, 2)
    for head in range(HEADS):
        for pair in pairs:
            project_some(-(-spans // len(pairs)))
            attend(head, range(pair, min(pair + 2, steps)))

    for step in range(steps):
        rows = slice(step * zone_rows, (step + 1) * zone_rows)
        context_out[rows, :] = context[:, rows].T.astype(BF16)


def project_kernel(place, states, context, w_attn, gain_mix, after_out, *refs):
    *outs, parts = refs
    steps, zone_rows, _ = states.shape
    zones, _, part = parts.shape
    my_zone = place[1]
    gain = gain_mix[...]
    for step in range(steps):
        rows = slice(step * zone_rows, (step + 1) * zone_rows)
        after = states[step].astype(F32) + jnp.dot(
            context[rows, :], w_attn[...], preferred_element_type=F32
        )
        after_out[rows, :] = after
        mixin = rms_scale(after, gain).astype(BF16)
        for index in range(zones):
            parts[index, rows, :] = mixin[:, index * part : (index + 1) * part]
    for index, step in enumerate((0,) + steps_over(zones)):
        outs[index][...] = parts[my_zone ^ step]


def mixing_kernel(steps, zones, place, neighbours, degree, mix, *refs):
    arrived, halves, (*outs, pair, items) = refs[:zones], refs[zones : zones + 2], refs[zones + 2 :]
    for index, value in enumerate(halves):
        pair[index] = value[...]
    _, slots, zone_rows, _ = mix.shape
    part = items.shape[-1]
    my_zone = place[1]
    group = 2 if part % LANES == 0 and steps % 2 == 0 else 1
    for index, step in enumerate((0,) + steps_over(zones)):
        items[my_zone ^ step] = arrived[index][...]

    for target, target_step in enumerate((0,) + steps_over(zones)):
        block = my_zone ^ target_step
        left = []
        for slot in range(slots):
            tile = mix[block, slot]
            left.append(jnp.where(degree[block] > slot, tile, jnp.zeros_like(tile)))
        left = jnp.concatenate(left, axis=1)
        for step in range(0, steps, group):
            right = []
            for slot in range(slots):
                source = neighbours[block, slot]
                right.append(
                    jnp.concatenate(
                        [
                            items[source, (step + index) * zone_rows : (step + index + 1) * zone_rows, :]
                            for index in range(group)
                        ],
                        axis=1,
                    )
                )
            result = jnp.dot(left, jnp.concatenate(right, axis=0), preferred_element_type=F32)
            for index in range(group):
                rows = slice((step + index) * zone_rows, (step + index + 1) * zone_rows)
                outs[target][rows, :] = result[:, index * part : (index + 1) * part].astype(BF16)


def slots_of(block):
    near = 2 + 2 * lax.rem(block, 2)
    return [lax.rem(block, SPREAD) ^ bits for bits in (0, near, 6 - near, 6)]


def fill_slots(zones, place, own_in, own_out, slots, pieces, w_in, w_out):
    my_zone = place[1]
    in_shard = own_in.shape[1]
    out_rows = own_out.shape[0] // SPREAD
    in_cols, width = own_in.shape[2], own_out.shape[1]
    own_rows = pl.ds(pl.multiple_of(my_zone * in_shard, in_shard), in_shard)
    own_out_rows = pl.ds(pl.multiple_of(my_zone * out_rows, out_rows), out_rows)
    for index, (slot, piece) in enumerate(zip(slots, pieces)):
        from_rows = pl.ds(pl.multiple_of(slot * out_rows, out_rows), out_rows)
        w_in[index, own_rows, :] = own_in[slot]
        w_out[index, own_out_rows, :] = own_out[from_rows, :]
        for step in range(1, zones):
            source = my_zone ^ step
            part = piece[step - 1]
            rows = pl.ds(pl.multiple_of(source * in_shard, in_shard), in_shard)
            w_in[index, rows, :] = part[:in_shard, :]
            rows = pl.ds(pl.multiple_of(source * out_rows, out_rows), out_rows)
            for fold in range(width // in_cols):
                low = in_shard + fold * out_rows
                w_out[index, rows, fold * in_cols : (fold + 1) * in_cols] = part[low : low + out_rows, :]


def order_kernel(zones, place, gain, own_in, own_out, pair, far, swapped_pair, w_in, w_out, gain_out):
    gain_out[...] = gain[...]
    my_block = place[0]
    slots = slots_of(my_block) + slots_of(my_block ^ 1)[:2]
    pieces = [group.at[index] for group in (pair, far, swapped_pair) for index in range(2)]
    fill_slots(zones, place, own_in, own_out, slots, pieces, w_in, w_out)


def relay_kernel(ready, far, *refs):
    refs[-1][...] = far[...]


def grow(ffn_in, w_in, hidden):
    in_cols = w_in.shape[2]
    for index in range(w_in.shape[0]):
        grown = jnp.dot(ffn_in[...], w_in[index], preferred_element_type=F32)
        hidden[:, index * in_cols : (index + 1) * in_cols] = jax.nn.gelu(
            grown, approximate=True
        ).astype(BF16)


def ffn_kernel(zones, place, after_attn, gain_ffn, w_in, w_out, *refs):
    arrived, (total, ffn_in, parts, hidden) = refs[:zones], refs[zones:]
    rows_all, width = after_attn.shape
    my_zone = place[1]
    for index, step in enumerate((0,) + steps_over(zones)):
        parts[my_zone ^ step] = arrived[index][...]
    gain = gain_ffn[...]
    span = 128
    part = parts.shape[-1]
    for first in range(0, rows_all, span):
        rows = slice(first, first + span)
        for index in range(zones):
            cols = slice(index * part, (index + 1) * part)
            total[rows, cols] = after_attn[rows, cols] + parts[index, rows, :].astype(F32)
        ffn_in[rows, :] = rms_scale(total[rows, :], gain).astype(BF16)
    grow(ffn_in, w_in, hidden)
    weights = w_out[...].reshape(hidden.shape[1], w_out.shape[2])
    total[...] += jnp.dot(hidden[...], weights, preferred_element_type=F32)


def last_kernel(
    zones, place, own_in, own_out, total, ffn_in, swapped_far, out, w_in, w_out, hidden, rows_out, sems
):
    slots = slots_of(place[0] ^ 1)[2:]
    pieces = [swapped_far.at[index] for index in range(2)]
    fill_slots(zones, place, own_in, own_out, slots, pieces, w_in, w_out)
    grow(ffn_in, w_in, hidden)
    weights = w_out[...].reshape(hidden.shape[1], w_out.shape[2])
    span = total.shape[0] // sems.shape[0]
    copies = []
    for index in range(sems.shape[0]):
        rows = slice(index * span, (index + 1) * span)
        shrunk = jnp.dot(hidden[rows, :], weights, preferred_element_type=F32)
        rows_out[rows, :] = (total[rows, :] + shrunk).astype(BF16)
        copies.append(pltpu.make_async_copy(rows_out.at[rows, :], out.at[rows, :], sems.at[index]))
        copies[-1].start()
    for copy in copies:
        copy.wait()


def call(kernel, out_shape, scratch, smem, hbm, limit, args, out_space=pltpu.VMEM):
    spaces = {index: pltpu.SMEM for index in smem} | {index: pltpu.HBM for index in hbm}
    return pl.pallas_call(
        kernel,
        out_shape=out_shape,
        in_specs=[
            pl.BlockSpec(memory_space=spaces.get(index, pltpu.VMEM)) for index in range(len(args))
        ],
        out_specs=jax.tree.map(lambda _: pl.BlockSpec(memory_space=out_space), out_shape),
        scratch_shapes=scratch,
        cost_estimate=pl.CostEstimate(flops=0, bytes_accessed=0, transcendentals=0),
        compiler_params=pltpu.CompilerParams(vmem_limit_bytes=limit * MIB),
    )(*args)


def on_device(
    states,
    gain_attn,
    w_qkv,
    w_out_attn,
    pattern,
    gain_mix,
    neighbours,
    degree,
    mix,
    gain_ffn,
    w_in,
    w_out,
):
    steps, zone_rows, width = states.shape
    rows = steps * zone_rows
    reach = pattern.shape[1]
    zones = lax.axis_size("zone")
    my_block, my_zone = lax.axis_index("tm"), lax.axis_index("zone")
    place = jnp.stack([my_block, my_zone]).astype(jnp.int32)
    key_count = (reach + 1) * steps
    hidden = w_in.shape[1]
    in_cols = hidden // SPREAD
    out_rows = w_out.shape[0] // SPREAD
    part = width // zones
    exchanges = steps_over(zones)

    before = shifted(states, "tm", 2)
    first = lax.dynamic_slice_in_dim(
        jnp.concatenate([w_qkv, w_out_attn], axis=1), quarter_of(my_block) * width, width, axis=1
    )
    direct = [swapped(first, "zone", step) for step in exchanges]
    packed_rows = w_in.shape[0] + out_rows * (width // in_cols)
    own_in, packed = call(
        functools.partial(group_kernel, zones),
        (
            jax.ShapeDtypeStruct((SPREAD, w_in.shape[0], in_cols), BF16),
            jax.ShapeDtypeStruct((packed_rows, in_cols), BF16),
        ),
        [],
        (0,),
        (),
        4,
        [place, w_in, w_out],
    )
    beside = swapped(packed, "zone", 1)
    half_shape = jax.ShapeDtypeStruct((zones - 1, first.shape[0] // 2, width), BF16)
    direct, upper, lower, doubled, last = call(
        split_kernel,
        (
            jax.ShapeDtypeStruct((zones - 1,) + first.shape, BF16),
            half_shape,
            half_shape,
            jax.ShapeDtypeStruct((2,) + packed.shape, BF16),
            jax.ShapeDtypeStruct(states.shape, BF16),
        ),
        [],
        (0,),
        (),
        4,
        [place, packed, beside, states, before] + direct,
    )
    over = [crossed(value, "tm", 2, 4) for value in (upper, lower)]
    last = swapped(last, "tm", 1)
    pieces = [direct] + over + [swapped(value, "tm", 1) for value in [direct] + over]
    normed = call(
        norm_kernel,
        jax.ShapeDtypeStruct((key_count * zone_rows, width), BF16),
        [],
        (),
        (),
        4,
        [before, last, states, gain_attn.reshape(1, -1)],
    )
    bits = 2
    while 2 * bits < zones:
        doubled = jnp.concatenate([doubled, swapped(doubled, "zone", bits)], axis=0)
        bits *= 2
    context, w_attn = call(
        functools.partial(attention_kernel, zones, reach, steps),
        (
            jax.ShapeDtypeStruct((rows, width), BF16),
            jax.ShapeDtypeStruct((width, width), BF16),
        ),
        [
            pltpu.VMEM((4, width, width), BF16),
            pltpu.VMEM((3 * width, width), BF16),
            pltpu.VMEM((HEADS, 3 * (width // HEADS), key_count * zone_rows), F32),
            pltpu.VMEM((width, rows), F32),
        ],
        (0, 1),
        (),
        22,
        [place, pattern, normed, w_qkv, w_out_attn] + pieces,
    )

    chunk = jax.ShapeDtypeStruct((rows, part), BF16)
    after_attn, *chunks = call(
        project_kernel,
        (jax.ShapeDtypeStruct((rows, width), F32),)
        + (chunk,) * zones,
        [pltpu.VMEM((zones, rows, part), BF16)],
        (0,),
        (),
        8,
        [place, states, context, w_attn, gain_mix.reshape(1, -1)],
    )
    across = call(
        stack_kernel,
        jax.ShapeDtypeStruct((zones - 1,) + packed.shape, BF16),
        [],
        (),
        (),
        4,
        [doubled, swapped(doubled, "zone", 2 * bits - 1), after_attn],
    )
    nearest = crossed(across, "tm", 2, 4)

    arrived = [chunks[0]] + [
        swapped(value, "zone", step) for value, step in zip(chunks[1:], exchanges)
    ]

    *spatial, pair = call(
        functools.partial(mixing_kernel, steps, zones),
        (chunk,) * zones
        + (jax.ShapeDtypeStruct((2,) + across.shape, BF16),),
        [pltpu.VMEM((zones, rows, part), BF16)],
        (0, 1, 2),
        (),
        8,
        [place, neighbours, degree, mix] + arrived + [across, nearest],
    )
    far = crossed(pair, "tm", 4, 2)
    full_in, full_out, gain = call(
        functools.partial(order_kernel, zones),
        (
            jax.ShapeDtypeStruct((6, width, in_cols), BF16),
            jax.ShapeDtypeStruct((6, in_cols, width), BF16),
            jax.ShapeDtypeStruct((1, width), F32),
        ),
        [],
        (0,),
        (),
        8,
        [place, gain_ffn.reshape(1, -1), own_in, w_out, pair, far, swapped(pair, "tm", 1)],
    )
    arrived = [spatial[0]] + [
        swapped(value, "zone", step) for value, step in zip(spatial[1:], exchanges)
    ]
    far = call(
        relay_kernel,
        jax.ShapeDtypeStruct(far.shape, BF16),
        [],
        (),
        (),
        4,
        [full_out, far] + arrived[1:],
    )
    total, ffn_in = call(
        functools.partial(ffn_kernel, zones),
        (jax.ShapeDtypeStruct((rows, width), F32), jax.ShapeDtypeStruct((rows, width), BF16)),
        [pltpu.VMEM((zones, rows, part), BF16), pltpu.VMEM((rows, 6 * in_cols), BF16)],
        (0,),
        (),
        12,
        [place, after_attn, gain, full_in, full_out] + arrived,
    )
    evolved = call(
        functools.partial(last_kernel, zones),
        jax.ShapeDtypeStruct((rows, width), BF16),
        [
            pltpu.VMEM((2, width, in_cols), BF16),
            pltpu.VMEM((2, in_cols, width), BF16),
            pltpu.VMEM((rows, 2 * in_cols), BF16),
            pltpu.VMEM((rows, width), BF16),
            pltpu.SemaphoreType.DMA((4,)),
        ],
        (0,),
        (),
        12,
        [place, own_in, w_out, total, ffn_in, swapped(far, "tm", 1)],
        pl.ANY,
    )
    return evolved.reshape(steps, zone_rows, width)


def solution(mesh):
    return jax.shard_map(
        on_device,
        mesh=mesh,
        in_specs=(
            P("tm", "zone", None),
            P(),
            P("zone", None),
            P("zone", None),
            P("tm", None),
            P(),
            P(),
            P(),
            P(),
            P(),
            P("zone", None),
            P("zone", None),
        ),
        out_specs=P("tm", "zone", None),
        check_vma=False,
    )
```

```python
import functools

import jax
import jax.numpy as jnp
from jax import lax
from jax.experimental import pallas as pl
from jax.experimental.pallas import tpu as pltpu
from jax.sharding import PartitionSpec as P

HEADS = 4
SPREAD = 8
LANES = 128
F32 = jnp.float32
BF16 = jnp.bfloat16
MIB = 1024 * 1024


def shifted(value, axis, steps):
    count = lax.axis_size(axis)
    return lax.ppermute(value, axis, [(source, source + steps) for source in range(count - steps)])


def swapped(value, axis, bits):
    count = lax.axis_size(axis)
    return lax.ppermute(value, axis, [(source, source ^ bits) for source in range(count)])


def crossed(value, axis, even_bits, odd_bits):
    count = lax.axis_size(axis)
    pairs = [(source, source ^ (odd_bits if source % 2 else even_bits)) for source in range(count)]
    return lax.ppermute(value, axis, pairs)


def steps_over(count):
    half = count // 2
    return tuple(range(count - 1, 0, -1))


def rms_scale(values, gain):
    mean_sq = jnp.mean(values * values, axis=-1, keepdims=True)
    return values * lax.rsqrt(mean_sq + 1e-06) * gain


def quarter_of(block):
    core = lax.rem(block, 2)
    return (1 - core) * lax.rem(lax.div(block, 2), 2) + core * (2 + lax.rem(lax.div(block, 4), 2))


def row_sum(value):
    return jnp.sum(value, axis=0, keepdims=True)


def norm_kernel(*refs):
    blocks, (gain_attn, normed) = refs[:-2], refs[-2:]
    steps, zone_rows, _ = blocks[0].shape
    gain = gain_attn[...]
    for index, block in enumerate(blocks):
        for step in range(steps):
            row = (index * steps + step) * zone_rows
            normed[row : row + zone_rows, :] = rms_scale(block[step].astype(F32), gain).astype(BF16)


def group_kernel(zones, place, w_in, w_out, own_in, packed):
    in_shard, hidden = w_in.shape
    out_rows = w_out.shape[0] // SPREAD
    in_cols = hidden // SPREAD
    width = w_out.shape[1]
    for index in range(SPREAD):
        for source in range(zones):
            low = (source * SPREAD + index) * out_rows
            to = slice(source * out_rows, (source + 1) * out_rows)
            own_in[index, :, to] = w_in[:, low : low + out_rows]
    slot = lax.rem(place[0], SPREAD)
    packed[:in_shard, :] = own_in[slot]
    rows = pl.ds(pl.multiple_of(slot * out_rows, out_rows), out_rows)
    for fold in range(width // in_cols):
        low = in_shard + fold * out_rows
        packed[low : low + out_rows, :] = w_out[rows, fold * in_cols : (fold + 1) * in_cols]


def split_kernel(place, packed, beside, states, before, *refs):
    arrived, (direct, upper, lower, doubled, last) = refs[:-5], refs[-5:]
    half = upper.shape[1]
    for index, piece in enumerate(arrived):
        direct[index] = piece[...]
        upper[index] = piece[:half, :]
        lower[index] = piece[half:, :]
    doubled[0] = packed[...]
    doubled[1] = beside[...]
    last[...] = jnp.where(lax.rem(place[0], 2) == 1, before[...], states[...])


def stack_kernel(doubled, arrived, *refs):
    out = refs[-1]
    near = doubled.shape[0]
    out[: near - 1] = doubled[1:]
    for index in range(near):
        out[2 * near - 2 - index] = arrived[index]


def attention_kernel(zones, reach, steps, place, pattern, normed, own_qkv, own_attn, *refs):
    pieces, (context_out, attn_out, weights, w_turned, projected, context) = refs[:-6], refs[-6:]
    key_count = (reach + 1) * steps
    zone_rows = normed.shape[0] // key_count
    width = normed.shape[1]
    head_size = width // HEADS
    my_block, my_zone = place[0], place[1]
    shard = own_qkv.shape[0]

    own_rows = pl.ds(pl.multiple_of(my_zone * shard, shard), shard)
    for index in range(3):
        weights[index, own_rows, :] = own_qkv[:, index * width : (index + 1) * width]
    weights[3, own_rows, :] = own_attn[...]
    half = shard // 2
    mine, other = quarter_of(my_block), quarter_of(my_block ^ 1)
    for place_in, step in enumerate(steps_over(zones)):
        start = (my_zone ^ step) * shard
        for piece, quarter, low in zip(
            pieces, (mine, mine ^ 1, mine ^ 1, other, other ^ 1, other ^ 1), (0, 0, half, 0, 0, half)
        ):
            rows = pl.ds(pl.multiple_of(start + low, half), piece.shape[1])
            weights[quarter, rows, :] = piece[place_in]
    attn_out[...] = weights[3]
    group = 3 * head_size
    def turn(head):
        for kind in range(3):
            rows = slice(head * group + kind * head_size, head * group + (kind + 1) * head_size)
            w_turned[rows, :] = weights[kind, :, head * head_size : (head + 1) * head_size].T

    def project(head, first, span):
        skip = 0 if first >= reach * steps * zone_rows else head_size
        projected[head, skip:, first : first + span] = lax.dot_general(
            w_turned[head * group + skip : (head + 1) * group, :],
            normed[first : first + span, :],
            (((1,), (1,)), ((), ())),
            preferred_element_type=F32,
        ).astype(BF16).astype(F32)

    span = 2 * zone_rows
    pending = [(head, first) for head in range(HEADS) for first in range(0, key_count * zone_rows, span)]

    def project_some(count):
        for _ in range(min(count, len(pending))):
            head, first = pending.pop(0)
            if first == 0:
                turn(head)
            project(head, first, span)

    allowed_back = [
        (pattern[0, back - 1] == 1) & (my_block >= back) for back in range(reach, 0, -1)
    ]
    chunks = head_size // 8

    def usable(query):
        return range(reach * steps + query + 1)

    def attend(head, queries):
        def tile(kind, chunk, key):
            row = kind * head_size + chunk * 8
            return projected[head, row : row + 8, key * zone_rows : (key + 1) * zone_rows]

        sums = {}
        for chunk in range(chunks):
            q_tiles = {q: tile(0, chunk, reach * steps + q) for q in queries}
            for key in usable(queries[-1]):
                k_tile = tile(1, chunk, key)
                for q in queries:
                    if key in usable(q):
                        term = q_tiles[q] * k_tile
                        sums[q, key] = term if chunk == 0 else sums[q, key] + term
        weights_of, scales = {}, {}
        for q in queries:
            scores = jnp.concatenate([row_sum(sums[q, key]) for key in usable(q)], axis=0)
            scores = scores * head_size ** (-0.5)
            row_id = lax.broadcasted_iota(jnp.int32, scores.shape, 0)
            allowed = row_id >= reach * steps
            for index, live in enumerate(allowed_back):
                inside = (row_id >= index * steps) & (row_id < (index + 1) * steps)
                allowed = allowed | (inside & live)
            masked = jnp.where(allowed, scores, -1e30)
            top = jnp.max(masked, axis=0, keepdims=True)
            expw = jnp.where(allowed, jnp.exp(masked - top), 0.0)
            scales[q] = jnp.broadcast_to(1.0 / row_sum(expw), (8, zone_rows))
            probs = expw.astype(BF16).astype(F32)
            for key in usable(q):
                weights_of[q, key] = jnp.broadcast_to(probs[key : key + 1, :], (8, zone_rows))
        for chunk in range(chunks):
            sums = {}
            for key in usable(queries[-1]):
                v_tile = tile(2, chunk, key)
                for q in queries:
                    if key in usable(q):
                        term = weights_of[q, key] * v_tile
                        sums[q] = term if key == 0 else sums[q] + term
            for q in queries:
                row = head * head_size + chunk * 8
                context[row : row + 8, q * zone_rows : (q + 1) * zone_rows] = sums[q] * scales[q]

    spans = key_count * zone_rows // span
    project_some(spans)
    pairs = range(0, steps, 2)
    for head in range(HEADS):
        for pair in pairs:
            project_some(-(-spans // len(pairs)))
            attend(head, range(pair, min(pair + 2, steps)))

    for step in range(steps):
        rows = slice(step * zone_rows, (step + 1) * zone_rows)
        context_out[rows, :] = context[:, rows].T.astype(BF16)


def project_kernel(place, states, context, w_attn, gain_mix, after_out, *refs):
    *outs, parts = refs
    steps, zone_rows, _ = states.shape
    zones, _, part = parts.shape
    my_zone = place[1]
    gain = gain_mix[...]
    for step in range(steps):
        rows = slice(step * zone_rows, (step + 1) * zone_rows)
        after = states[step].astype(F32) + jnp.dot(
            context[rows, :], w_attn[...], preferred_element_type=F32
        )
        after_out[rows, :] = after
        mixin = rms_scale(after, gain).astype(BF16)
        for index in range(zones):
            parts[index, rows, :] = mixin[:, index * part : (index + 1) * part]
    for index, step in enumerate((0,) + steps_over(zones)):
        outs[index][...] = parts[my_zone ^ step]


def mixing_kernel(steps, zones, place, neighbours, degree, mix, *refs):
    arrived, halves, (*outs, pair, items) = refs[:zones], refs[zones : zones + 2], refs[zones + 2 :]
    for index, value in enumerate(halves):
        pair[index] = value[...]
    _, slots, zone_rows, _ = mix.shape
    part = items.shape[-1]
    my_zone = place[1]
    group = 2 if part % LANES == 0 and steps % 2 == 0 else 1
    for index, step in enumerate((0,) + steps_over(zones)):
        items[my_zone ^ step] = arrived[index][...]

    for target, target_step in enumerate((0,) + steps_over(zones)):
        block = my_zone ^ target_step
        left = []
        for slot in range(slots):
            tile = mix[block, slot]
            left.append(jnp.where(degree[block] > slot, tile, jnp.zeros_like(tile)))
        left = jnp.concatenate(left, axis=1)
        for step in range(0, steps, group):
            right = []
            for slot in range(slots):
                source = neighbours[block, slot]
                right.append(
                    jnp.concatenate(
                        [
                            items[source, (step + index) * zone_rows : (step + index + 1) * zone_rows, :]
                            for index in range(group)
                        ],
                        axis=1,
                    )
                )
            result = jnp.dot(left, jnp.concatenate(right, axis=0), preferred_element_type=F32)
            for index in range(group):
                rows = slice((step + index) * zone_rows, (step + index + 1) * zone_rows)
                outs[target][rows, :] = result[:, index * part : (index + 1) * part].astype(BF16)


def slots_of(block):
    near = 2 + 2 * lax.rem(block, 2)
    return [lax.rem(block, SPREAD) ^ bits for bits in (0, near, 6 - near, 6)]


def fill_slots(zones, place, own_in, own_out, slots, pieces, w_in, w_out):
    my_zone = place[1]
    in_shard = own_in.shape[1]
    out_rows = own_out.shape[0] // SPREAD
    in_cols, width = own_in.shape[2], own_out.shape[1]
    own_rows = pl.ds(pl.multiple_of(my_zone * in_shard, in_shard), in_shard)
    own_out_rows = pl.ds(pl.multiple_of(my_zone * out_rows, out_rows), out_rows)
    for index, (slot, piece) in enumerate(zip(slots, pieces)):
        from_rows = pl.ds(pl.multiple_of(slot * out_rows, out_rows), out_rows)
        w_in[index, own_rows, :] = own_in[slot]
        w_out[index, own_out_rows, :] = own_out[from_rows, :]
        for step in range(1, zones):
            source = my_zone ^ step
            part = piece[step - 1]
            rows = pl.ds(pl.multiple_of(source * in_shard, in_shard), in_shard)
            w_in[index, rows, :] = part[:in_shard, :]
            rows = pl.ds(pl.multiple_of(source * out_rows, out_rows), out_rows)
            for fold in range(width // in_cols):
                low = in_shard + fold * out_rows
                w_out[index, rows, fold * in_cols : (fold + 1) * in_cols] = part[low : low + out_rows, :]


def order_kernel(zones, place, gain, own_in, own_out, pair, far, swapped_pair, w_in, w_out, gain_out):
    gain_out[...] = gain[...]
    my_block = place[0]
    slots = slots_of(my_block) + slots_of(my_block ^ 1)[:2]
    pieces = [group.at[index] for group in (pair, far, swapped_pair) for index in range(2)]
    fill_slots(zones, place, own_in, own_out, slots, pieces, w_in, w_out)


def relay_kernel(ready, far, *refs):
    refs[-1][...] = far[...]


def grow(ffn_in, w_in, hidden):
    in_cols = w_in.shape[2]
    for index in range(w_in.shape[0]):
        grown = jnp.dot(ffn_in[...], w_in[index], preferred_element_type=F32)
        hidden[:, index * in_cols : (index + 1) * in_cols] = jax.nn.gelu(
            grown, approximate=True
        ).astype(BF16)


def ffn_kernel(zones, place, after_attn, gain_ffn, w_in, w_out, *refs):
    arrived, (total, ffn_in, parts, hidden) = refs[:zones], refs[zones:]
    rows_all, width = after_attn.shape
    my_zone = place[1]
    for index, step in enumerate((0,) + steps_over(zones)):
        parts[my_zone ^ step] = arrived[index][...]
    gain = gain_ffn[...]
    span = 128
    part = parts.shape[-1]
    for first in range(0, rows_all, span):
        rows = slice(first, first + span)
        for index in range(zones):
            cols = slice(index * part, (index + 1) * part)
            total[rows, cols] = after_attn[rows, cols] + parts[index, rows, :].astype(F32)
        ffn_in[rows, :] = rms_scale(total[rows, :], gain).astype(BF16)
    grow(ffn_in, w_in, hidden)
    weights = w_out[...].reshape(hidden.shape[1], w_out.shape[2])
    total[...] += jnp.dot(hidden[...], weights, preferred_element_type=F32)


def last_kernel(
    zones, place, own_in, own_out, total, ffn_in, swapped_far, out, w_in, w_out, hidden, rows_out, sems
):
    slots = slots_of(place[0] ^ 1)[2:]
    pieces = [swapped_far.at[index] for index in range(2)]
    fill_slots(zones, place, own_in, own_out, slots, pieces, w_in, w_out)
    grow(ffn_in, w_in, hidden)
    weights = w_out[...].reshape(hidden.shape[1], w_out.shape[2])
    span = total.shape[0] // sems.shape[0]
    copies = []
    for index in range(sems.shape[0]):
        rows = slice(index * span, (index + 1) * span)
        shrunk = jnp.dot(hidden[rows, :], weights, preferred_element_type=F32)
        rows_out[rows, :] = (total[rows, :] + shrunk).astype(BF16)
        copies.append(pltpu.make_async_copy(rows_out.at[rows, :], out.at[rows, :], sems.at[index]))
        copies[-1].start()
    for copy in copies:
        copy.wait()


def call(kernel, out_shape, scratch, smem, hbm, limit, args, out_space=pltpu.VMEM):
    spaces = {index: pltpu.SMEM for index in smem} | {index: pltpu.HBM for index in hbm}
    return pl.pallas_call(
        kernel,
        out_shape=out_shape,
        in_specs=[
            pl.BlockSpec(memory_space=spaces.get(index, pltpu.VMEM)) for index in range(len(args))
        ],
        out_specs=jax.tree.map(lambda _: pl.BlockSpec(memory_space=out_space), out_shape),
        scratch_shapes=scratch,
        cost_estimate=pl.CostEstimate(flops=0, bytes_accessed=0, transcendentals=0),
        compiler_params=pltpu.CompilerParams(vmem_limit_bytes=limit * MIB),
    )(*args)


def on_device(
    states,
    gain_attn,
    w_qkv,
    w_out_attn,
    pattern,
    gain_mix,
    neighbours,
    degree,
    mix,
    gain_ffn,
    w_in,
    w_out,
):
    steps, zone_rows, width = states.shape
    rows = steps * zone_rows
    reach = pattern.shape[1]
    zones = lax.axis_size("zone")
    my_block, my_zone = lax.axis_index("tm"), lax.axis_index("zone")
    place = jnp.stack([my_block, my_zone]).astype(jnp.int32)
    key_count = (reach + 1) * steps
    hidden = w_in.shape[1]
    in_cols = hidden // SPREAD
    out_rows = w_out.shape[0] // SPREAD
    part = width // zones
    exchanges = steps_over(zones)

    before = shifted(states, "tm", 2)
    first = lax.dynamic_slice_in_dim(
        jnp.concatenate([w_qkv, w_out_attn], axis=1), quarter_of(my_block) * width, width, axis=1
    )
    direct = [swapped(first, "zone", step) for step in exchanges]
    packed_rows = w_in.shape[0] + out_rows * (width // in_cols)
    own_in, packed = call(
        functools.partial(group_kernel, zones),
        (
            jax.ShapeDtypeStruct((SPREAD, w_in.shape[0], in_cols), BF16),
            jax.ShapeDtypeStruct((packed_rows, in_cols), BF16),
        ),
        [],
        (0,),
        (),
        4,
        [place, w_in, w_out],
    )
    beside = swapped(packed, "zone", 1)
    half_shape = jax.ShapeDtypeStruct((zones - 1, first.shape[0] // 2, width), BF16)
    direct, upper, lower, doubled, last = call(
        split_kernel,
        (
            jax.ShapeDtypeStruct((zones - 1,) + first.shape, BF16),
            half_shape,
            half_shape,
            jax.ShapeDtypeStruct((2,) + packed.shape, BF16),
            jax.ShapeDtypeStruct(states.shape, BF16),
        ),
        [],
        (0,),
        (),
        4,
        [place, packed, beside, states, before] + direct,
    )
    over = [crossed(value, "tm", 2, 4) for value in (upper, lower)]
    last = swapped(last, "tm", 1)
    pieces = [direct] + over + [swapped(value, "tm", 1) for value in [direct] + over]
    normed = call(
        norm_kernel,
        jax.ShapeDtypeStruct((key_count * zone_rows, width), BF16),
        [],
        (),
        (),
        4,
        [before, last, states, gain_attn.reshape(1, -1)],
    )
    bits = 2
    while 2 * bits < zones:
        doubled = jnp.concatenate([doubled, swapped(doubled, "zone", bits)], axis=0)
        bits *= 2
    context, w_attn = call(
        functools.partial(attention_kernel, zones, reach, steps),
        (
            jax.ShapeDtypeStruct((rows, width), BF16),
            jax.ShapeDtypeStruct((width, width), BF16),
        ),
        [
            pltpu.VMEM((4, width, width), BF16),
            pltpu.VMEM((3 * width, width), BF16),
            pltpu.VMEM((HEADS, 3 * (width // HEADS), key_count * zone_rows), F32),
            pltpu.VMEM((width, rows), F32),
        ],
        (0, 1),
        (),
        22,
        [place, pattern, normed, w_qkv, w_out_attn] + pieces,
    )

    chunk = jax.ShapeDtypeStruct((rows, part), BF16)
    after_attn, *chunks = call(
        project_kernel,
        (jax.ShapeDtypeStruct((rows, width), F32),)
        + (chunk,) * zones,
        [pltpu.VMEM((zones, rows, part), BF16)],
        (0,),
        (),
        8,
        [place, states, context, w_attn, gain_mix.reshape(1, -1)],
    )
    across = call(
        stack_kernel,
        jax.ShapeDtypeStruct((zones - 1,) + packed.shape, BF16),
        [],
        (),
        (),
        4,
        [doubled, swapped(doubled, "zone", 2 * bits - 1), after_attn],
    )
    nearest = crossed(across, "tm", 2, 4)

    arrived = [chunks[0]] + [
        swapped(value, "zone", step) for value, step in zip(chunks[1:], exchanges)
    ]

    *spatial, pair = call(
        functools.partial(mixing_kernel, steps, zones),
        (chunk,) * zones
        + (jax.ShapeDtypeStruct((2,) + across.shape, BF16),),
        [pltpu.VMEM((zones, rows, part), BF16)],
        (0, 1, 2),
        (),
        8,
        [place, neighbours, degree, mix] + arrived + [across, nearest],
    )
    far = crossed(pair, "tm", 4, 2)
    full_in, full_out, gain = call(
        functools.partial(order_kernel, zones),
        (
            jax.ShapeDtypeStruct((6, width, in_cols), BF16),
            jax.ShapeDtypeStruct((6, in_cols, width), BF16),
            jax.ShapeDtypeStruct((1, width), F32),
        ),
        [],
        (0,),
        (),
        8,
        [place, gain_ffn.reshape(1, -1), own_in, w_out, pair, far, swapped(pair, "tm", 1)],
    )
    arrived = [spatial[0]] + [
        swapped(value, "zone", step) for value, step in zip(spatial[1:], exchanges)
    ]
    far = call(
        relay_kernel,
        jax.ShapeDtypeStruct(far.shape, BF16),
        [],
        (),
        (),
        4,
        [full_out, far] + arrived[1:],
    )
    total, ffn_in = call(
        functools.partial(ffn_kernel, zones),
        (jax.ShapeDtypeStruct((rows, width), F32), jax.ShapeDtypeStruct((rows, width), BF16)),
        [pltpu.VMEM((zones, rows, part), BF16), pltpu.VMEM((rows, 6 * in_cols), BF16)],
        (0,),
        (),
        12,
        [place, after_attn, gain, full_in, full_out] + arrived,
    )
    evolved = call(
        functools.partial(last_kernel, zones),
        jax.ShapeDtypeStruct((rows, width), BF16),
        [
            pltpu.VMEM((2, width, in_cols), BF16),
            pltpu.VMEM((2, in_cols, width), BF16),
            pltpu.VMEM((rows, 2 * in_cols), BF16),
            pltpu.VMEM((rows, width), BF16),
            pltpu.SemaphoreType.DMA((4,)),
        ],
        (0,),
        (),
        12,
        [place, own_in, w_out, total, ffn_in, swapped(far, "tm", 1)],
        pl.ANY,
    )
    return evolved.reshape(steps, zone_rows, width)


def solution(mesh):
    return jax.shard_map(
        on_device,
        mesh=mesh,
        in_specs=(
            P("tm", "zone", None),
            P(),
            P("zone", None),
            P("zone", None),
            P("tm", None),
            P(),
            P(),
            P(),
            P(),
            P(),
            P("zone", None),
            P("zone", None),
        ),
        out_specs=P("tm", "zone", None),
        check_vma=False,
    )
```
